32 devices in a mesh: dp: 8 (over y, x, core), tensor: 4 (over z).
Axes of the slice: x: 2, y: 2, z: 4, core: 2. Of those that a mesh axis runs over, the one named last changes fastest.
Arguments:
- tokens: bfloat16 [8192, 2048], P(('dp', 'tensor')), may hold values from -6 to 6
- positions: int32 [8192], P('dp'), may hold values from 0 to 1023, as said below
- cotangent: bfloat16 [8192, 2048], P(('dp', 'tensor')), may hold values from -6 to 6
- query_weight: bfloat16 [2048, 2048], P('dp', 'tensor'), may hold values from -0.125 to 0.125
- key_weight: bfloat16 [2048, 2048], P('dp', 'tensor'), may hold values from -0.125 to 0.125
- value_weight: bfloat16 [2048, 2048], P('dp', 'tensor'), may hold values from -0.125 to 0.125
- output_weight: bfloat16 [2048, 2048], P('tensor', 'dp'), may hold values from -0.125 to 0.125
- gate_weight: bfloat16 [2048, 8192], P('dp', 'tensor'), may hold values from -0.125 to 0.125
- up_weight: bfloat16 [2048, 8192], P('dp', 'tensor'), may hold values from -0.125 to 0.125
- down_weight: bfloat16 [8192, 2048], P('tensor', 'dp'), may hold values from -0.0625 to 0.0625
- query_gain: bfloat16 [128, 16], P('dp', 'tensor'), may hold values from 0.5 to 1.5
- key_gain: bfloat16 [128, 16], P('dp', 'tensor'), may hold values from 0.5 to 1.5
- attention_gain: bfloat16 [2048], P('dp'), may hold values from 0.5 to 1.5
- feedforward_gain: bfloat16 [2048], P('dp'), may hold values from 0.5 to 1.5
Outputs:
- block_output: float32 [8192, 2048], P(('dp', 'tensor'))
- grad_tokens: float32 [8192, 2048], P(('dp', 'tensor'))
- grad_query_weight: float32 [2048, 2048], P('dp', 'tensor')
- grad_key_weight: float32 [2048, 2048], P('dp', 'tensor')
- grad_value_weight: float32 [2048, 2048], P('dp', 'tensor')
- grad_output_weight: float32 [2048, 2048], P('tensor', 'dp')
- grad_gate_weight: float32 [2048, 8192], P('dp', 'tensor')
- grad_up_weight: float32 [2048, 8192], P('dp', 'tensor')
- grad_down_weight: float32 [8192, 2048], P('tensor', 'dp')
- grad_query_gain: float32 [128, 16], P('dp', 'tensor')
- grad_key_gain: float32 [128, 16], P('dp', 'tensor')
- grad_attention_gain: float32 [2048], P('dp')
- grad_feedforward_gain: float32 [2048], P('dp')
The draws below stay inside these ranges and needn't reach their ends.
Inputs may be any that keep to these rules, and one draw needn't show every extreme that they name: Each sequence packs documents: positions start at 0 on a sequence's first row and rise by one, except at a document's first row, where they are 0 again. The first sequence is one document.
All inputs are finite; a program needn't handle non-finite values.
Results may differ from the reference program's by a relative error of at most 0.028.
Values may be sent and summed in bfloat16 or wider, within the bound.
A program may use at most 256 MiB of HBM per device.

```python
import jax
import jax.numpy as jnp
from jax import lax

D = 2048
HEADS = 16
HD = 128
FF = 8192
LENGTH = 1024
TOKENS = 8192


def draw_positions(key, part):
    key = jax.random.fold_in(key, 7)
    seq_count = TOKENS // LENGTH
    picks = jax.random.randint(key, (seq_count, LENGTH), 0, LENGTH)
    row_index = lax.broadcasted_iota(jnp.int32, (seq_count, LENGTH), 1)
    seq_index = lax.broadcasted_iota(jnp.int32, (seq_count, LENGTH), 0)
    restart = jnp.logical_or(row_index == 0, jnp.logical_and(seq_index > 0, picks < 4))
    starts = lax.cummax(jnp.where(restart, row_index, 0), axis=1)
    return (row_index - starts).reshape(-1).astype(jnp.int32)


def steps_of(rng, dims, split, least, high):
    loudness = 1.0
    for axis_at, blocks in split:
        heights = jax.random.uniform(jax.random.fold_in(jax.random.fold_in(rng, 6), axis_at), (blocks,), jnp.float32, least / len(split), high / len(split))
        loudness = loudness * jnp.repeat(jnp.exp(heights), dims[axis_at] // blocks).reshape((-1,) + (1,) * (len(dims) - 1 - axis_at))
    return loudness


def noise(rng, extent, deviation, reach, shards=(), held_as=jnp.bfloat16):
    loudness = steps_of(rng, extent, shards, -0.22, 0.18) if shards else 1.0
    drawn = jax.random.normal(rng, extent, jnp.float32) * deviation * loudness
    return jnp.minimum(jnp.maximum(drawn, -reach), reach).astype(held_as)


def setup_inputs(seed: int = 0) -> dict:
    key_of = jax.random.split(jax.random.key(seed), 15)
    tokens = noise(key_of[0], (TOKENS, D), 1.0, 6.0, ((0, 32),))
    positions = draw_positions(jax.random.fold_in(key_of[14], 71), 0)
    cotangent = noise(key_of[2], (TOKENS, D), 1.0, 6.0, ((0, 32),))
    query_weight = noise(key_of[3], (D, D), D ** -0.5, 0.125, ((0, 8), (1, 4)))
    key_weight = noise(key_of[4], (D, D), D ** -0.5, 0.125, ((0, 8), (1, 4)))
    value_weight = noise(key_of[5], (D, D), D ** -0.5, 0.125, ((0, 8), (1, 4)))
    output_weight = noise(key_of[6], (D, D), D ** -0.5, 0.125, ((0, 4), (1, 8)))
    gate_weight = noise(key_of[7], (D, FF), D ** -0.5, 0.125, ((0, 8), (1, 4)))
    up_weight = noise(key_of[8], (D, FF), D ** -0.5, 0.125, ((0, 8), (1, 4)))
    down_weight = noise(key_of[9], (FF, D), FF ** -0.5, 0.0625, ((0, 4), (1, 8)))
    query_gain = jnp.clip(1.0 + 0.1 * jax.random.normal(key_of[10], (HD, HEADS), jnp.float32), 0.5, 1.5).astype(jnp.bfloat16)
    key_gain = jnp.clip(1.0 + 0.1 * jax.random.normal(key_of[11], (HD, HEADS), jnp.float32), 0.5, 1.5).astype(jnp.bfloat16)
    attention_gain = jnp.clip(1.0 + 0.1 * jax.random.normal(key_of[12], (D,), jnp.float32), 0.5, 1.5).astype(jnp.bfloat16)
    feedforward_gain = jnp.clip(1.0 + 0.1 * jax.random.normal(key_of[13], (D,), jnp.float32), 0.5, 1.5).astype(jnp.bfloat16)
    return {"tokens": tokens, "positions": positions, "cotangent": cotangent, "query_weight": query_weight, "key_weight": key_weight, "value_weight": value_weight, "output_weight": output_weight, "gate_weight": gate_weight, "up_weight": up_weight, "down_weight": down_weight, "query_gain": query_gain, "key_gain": key_gain, "attention_gain": attention_gain, "feedforward_gain": feedforward_gain}


EPS = 1e-06
THETA = 500000.0
MASKED = -1e+30

@jax.custom_vjp
def low(v):
    return lax.optimization_barrier(v.astype(jnp.bfloat16)).astype(jnp.float32)

@jax.custom_vjp
def low_back(v):
    return v

def low_keep(v):
    return (low(v), None)

def low_pass(kept, grad):
    return (grad,)

def back_keep(v):
    return (v, None)

def back_low(kept, grad):
    return (low(grad),)
low.defvjp(low_keep, low_pass)
low_back.defvjp(back_keep, back_low)

def rope_tables(positions, head_size):
    half_size = head_size // 2
    frequency = THETA ** (-(jnp.arange(half_size, dtype=jnp.float32) * 2.0 / head_size))
    angles = positions.astype(jnp.float32)[:, None] * frequency[None, :]
    return (jnp.cos(angles)[:, None, :], jnp.sin(angles)[:, None, :])

def rotate(values, cosine_table, sine_table):
    half_size = values.shape[-1] // 2
    first_half = values[..., :half_size]
    second_half = values[..., half_size:]
    return jnp.concatenate([first_half * cosine_table - second_half * sine_table, second_half * cosine_table + first_half * sine_table], -1)

def rms_norm(values, gain):
    return values * lax.rsqrt(lax.optimization_barrier(jnp.mean(values * values, -1, keepdims=True)) + EPS) * gain

def matmul_high(left_side, right_side):
    return jnp.dot(left_side, right_side, precision=lax.Precision.HIGHEST, preferred_element_type=jnp.float32)

def layer(rows_in, positions, params):
    query_weight, key_weight, value_weight, output_weight, gate_weight, up_weight, down_weight, query_gain, key_gain, attention_gain, feedforward_gain = params
    length = rows_in.shape[0]
    cosine_table, sine_table = rope_tables(positions, HD)
    query_scale = query_gain.T.reshape(D)
    key_scale = key_gain.T.reshape(D)
    queries = low_back(matmul_high(rows_in, query_weight))
    key_rows = low_back(matmul_high(rows_in, key_weight))
    value_rows = low_back(low(matmul_high(rows_in, value_weight))).reshape(length, HEADS, HD)
    queries = low_back(low(rotate(rms_norm(queries, query_scale).reshape(length, HEADS, HD), cosine_table, sine_table)))
    key_rows = low_back(low(rotate(rms_norm(key_rows, key_scale).reshape(length, HEADS, HD), cosine_table, sine_table)))
    scores = low_back(jnp.einsum('qhc,khc->hqk', queries, key_rows, precision=lax.Precision.HIGHEST) * HD ** (-0.5))
    row_index = lax.broadcasted_iota(jnp.int32, (length, length), 0)
    col_index = lax.broadcasted_iota(jnp.int32, (length, length), 1)
    scores = jnp.where((col_index <= row_index)[None], scores, MASKED)
    exponent = jnp.exp(scores - lax.optimization_barrier(jnp.max(scores, -1, keepdims=True)))
    probabilities = low(exponent / lax.optimization_barrier(jnp.sum(exponent, -1, keepdims=True)))
    attended = jnp.einsum('hqk,khc->qhc', probabilities, value_rows, precision=lax.Precision.HIGHEST).reshape(length, D)
    attended = low_back(low(attended))
    branch = low_back(matmul_high(attended, output_weight))
    hidden_state = rows_in + rms_norm(branch, attention_gain)
    mlp_in = low(hidden_state)
    gate_act = low_back(matmul_high(mlp_in, gate_weight))
    up_act = low_back(matmul_high(mlp_in, up_weight))
    inner_act = low(jax.nn.silu(gate_act) * up_act)
    mixed = low_back(matmul_high(inner_act, down_weight))
    return hidden_state + rms_norm(mixed, feedforward_gain)

def reference(tokens, positions, cotangent, query_weight, key_weight, value_weight, output_weight, gate_weight, up_weight, down_weight, query_gain, key_gain, attention_gain, feedforward_gain):
    params = tuple((weight.astype(jnp.float32) for weight in (query_weight, key_weight, value_weight, output_weight, gate_weight, up_weight, down_weight, query_gain, key_gain, attention_gain, feedforward_gain)))
    seq_count = tokens.shape[0] // LENGTH
    token_seqs = tokens.astype(jnp.float32).reshape(seq_count, LENGTH, D)
    position_seqs = positions.reshape(seq_count, LENGTH)
    cot_seqs = cotangent.astype(jnp.float32).reshape(seq_count, LENGTH, D)

    def scan_step(totals, sequence_item):
        rows_in, seq_positions, cot_rows = sequence_item
        block_out, pullback = jax.vjp(lambda inputs, weights: layer(inputs, seq_positions, weights), rows_in, params)
        grad_rows, grad_params = pullback(cot_rows)
        return (tuple((left_term + right_term for left_term, right_term in zip(totals, grad_params))), (block_out, grad_rows))
    zero_grads = tuple((jnp.zeros_like(weight) for weight in params))
    totals, (outputs_all, grads_all) = lax.scan(scan_step, zero_grads, (token_seqs, position_seqs, cot_seqs))
    return (outputs_all.reshape(-1, D), grads_all.reshape(-1, D), totals[0], totals[1], totals[2], totals[3], totals[4], totals[5], totals[6], totals[7], totals[8], totals[9], totals[10])
```

```python
import jax
import jax.numpy as jnp
from jax import lax
from jax.sharding import PartitionSpec as P

LENGTH = 1024


EPS = 1e-06
THETA = 500000.0
MASKED = -1e30


def rope_tables(positions, head_size):
    half_size = head_size // 2
    frequency = THETA ** (-(jnp.arange(half_size, dtype=jnp.float32) * 2.0 / head_size))
    angles = positions.astype(jnp.float32)[:, None] * frequency[None, :]
    return (jnp.cos(angles)[:, None, :], jnp.sin(angles)[:, None, :])


def rotate(values, cosine_table, sine_table):
    half_size = values.shape[-1] // 2
    first_half = values[..., :half_size]
    second_half = values[..., half_size:]
    return jnp.concatenate(
        [
            first_half * cosine_table - second_half * sine_table,
            second_half * cosine_table + first_half * sine_table,
        ],
        -1,
    )


def unrotate(gradient, cosine_table, sine_table):
    half_size = gradient.shape[-1] // 2
    first_half = gradient[..., :half_size]
    second_half = gradient[..., half_size:]
    return jnp.concatenate(
        [
            first_half * cosine_table + second_half * sine_table,
            second_half * cosine_table - first_half * sine_table,
        ],
        -1,
    )


def channel_scale(gain_block):
    return gain_block.astype(jnp.float32).T.reshape(-1)


def masked_scores(queries, key_rows, first_row, block_rows):
    last_row = first_row + block_rows
    score_scale = queries.shape[-1] ** (-0.5)
    scores = (
        jnp.einsum(
            "qhc,khc->hqk",
            queries[first_row:last_row],
            key_rows[:last_row],
            preferred_element_type=jnp.float32,
        )
        * score_scale
    )
    row_index = first_row + lax.broadcasted_iota(jnp.int32, (block_rows, last_row), 0)
    col_index = lax.broadcasted_iota(jnp.int32, (block_rows, last_row), 1)
    return jnp.where((col_index <= row_index)[None], scores, MASKED)


def attend_forward(queries, key_rows, value_rows, block_rows):
    length = queries.shape[0]
    output_list = []
    lse_list = []
    for first_row in range(0, length, block_rows):
        last_row = first_row + block_rows
        scores = masked_scores(queries, key_rows, first_row, block_rows)
        row_max = jnp.max(scores, -1, keepdims=True)
        exponent = jnp.exp(scores - row_max)
        row_total = jnp.sum(exponent, -1, keepdims=True)
        low_probs = (exponent / row_total).astype(jnp.bfloat16)
        output_list.append(
            jnp.einsum(
                "hqk,khc->qhc", low_probs, value_rows[:last_row], preferred_element_type=jnp.float32
            )
        )
        lse_list.append(row_max + jnp.log(row_total))
    return (jnp.concatenate(output_list, 0), jnp.concatenate(lse_list, 1))


def attend_backward(queries, key_rows, value_rows, grad_out, row_lse, block_rows):
    length = queries.shape[0]
    score_scale = queries.shape[-1] ** (-0.5)
    grad_keys = jnp.zeros(key_rows.shape, jnp.float32)
    grad_values = jnp.zeros(value_rows.shape, jnp.float32)
    query_list = []
    for first_row in range(0, length, block_rows):
        last_row = first_row + block_rows
        padding = ((0, length - last_row), (0, 0), (0, 0))
        scores = masked_scores(queries, key_rows, first_row, block_rows)
        probabilities = jnp.exp(scores - row_lse[:, first_row:last_row])
        low_probs = probabilities.astype(jnp.bfloat16)
        grad_block = grad_out[first_row:last_row]
        grad_values = grad_values + jnp.pad(
            jnp.einsum("hqk,qhc->khc", low_probs, grad_block, preferred_element_type=jnp.float32),
            padding,
        )
        grad_probs = jnp.einsum(
            "qhc,khc->hqk", grad_block, value_rows[:last_row], preferred_element_type=jnp.float32
        )
        row_delta = jnp.sum(grad_probs * probabilities, -1, keepdims=True)
        grad_scores = (probabilities * (grad_probs - row_delta)).astype(jnp.bfloat16)
        query_list.append(
            jnp.einsum(
                "hqk,khc->qhc", grad_scores, key_rows[:last_row], preferred_element_type=jnp.float32
            )
            * score_scale
        )
        grad_keys = grad_keys + jnp.pad(
            jnp.einsum(
                "hqk,qhc->khc",
                grad_scores,
                queries[first_row:last_row],
                preferred_element_type=jnp.float32,
            )
            * score_scale,
            padding,
        )
    return (jnp.concatenate(query_list, 0), grad_keys, grad_values)


def norm_backward(grad_in, normalized, inverse_rms, gain_values):
    scaled = grad_in * gain_values
    return inverse_rms * (scaled - normalized * jnp.mean(scaled * normalized, -1, keepdims=True))


def bits_of(size):
    return size.bit_length() - 1


def mask_order(size):
    evens = [mask for mask in range(size) if mask % 2 == 0]
    return evens + [mask + 1 for mask in evens]


def swap(array_in, mask):
    size = lax.axis_size("dp")
    return lax.ppermute(array_in, "dp", [(index, index ^ mask) for index in range(size)])


def gather_shards(shard, axis):
    size = lax.axis_size("dp")
    held = {0: shard}
    if size >= 8:
        held[2] = swap(shard, 2)
        held[4] = swap(shard, 4)
        half = shard.shape[0] // 2
        held[6] = jnp.concatenate([swap(held[2][:half], 4), swap(held[4][half:], 2)], 0)
        first_bit = 3
    else:
        first_bit = 1
    for bit in range(first_bit, bits_of(size)):
        for mask in list(held):
            held[mask | (1 << bit)] = swap(held[mask], 1 << bit)
    for mask in list(held):
        held[mask | 1] = swap(held[mask], 1)
    return jnp.concatenate([held[mask] for mask in mask_order(size)], axis)


def low(array_in):
    return array_in.astype(jnp.bfloat16)


def wide(array_in):
    return array_in.astype(jnp.float32)


def scatter_shards(near_part, far_part, axis):
    size = lax.axis_size("dp")
    total = low(near_part + wide(swap(low(far_part), 1)))
    evens = [mask for mask in range(size) if mask % 2 == 0]
    width = total.shape[axis] // len(evens)
    held = {
        mask: lax.slice_in_dim(total, place * width, (place + 1) * width, axis=axis)
        for place, mask in enumerate(evens)
    }
    first_bit = 3 if size >= 8 else 1
    for bit in reversed(range(first_bit, bits_of(size))):
        for mask in [mask for mask in held if mask >> bit & 1]:
            arrived = swap(held.pop(mask), 1 << bit)
            base = mask ^ (1 << bit)
            held[base] = low(wide(held[base]) + wide(arrived))
    if size >= 8:
        half = held[6].shape[0] // 2
        by_four = swap(held[6][:half], 4)
        by_two = swap(held[6][half:], 2)
        two = jnp.concatenate(
            [low(wide(held[2][:half]) + wide(by_four)), held[2][half:]], 0
        )
        four = jnp.concatenate(
            [held[4][:half], low(wide(held[4][half:]) + wide(by_two))], 0
        )
        return wide(held[0]) + wide(swap(two, 2)) + wide(swap(four, 4))
    return wide(held[0])


def step_up(array_in, first=0, last=None):
    size = lax.axis_size("tensor")
    return lax.ppermute(
        array_in, "tensor", [(index, index + 1) for index in range(first, size - 1)]
    )


def step_down(array_in, first=0):
    size = lax.axis_size("tensor")
    return lax.ppermute(
        array_in, "tensor", [(index, index - 1) for index in range(1, size - first)]
    )


def gather_rows(own):
    size = lax.axis_size("tensor")
    me = lax.axis_index("tensor")
    rows = own.shape[0]
    ups, downs = [], []
    up, down = own, own
    for step in range(size - 1):
        up = step_up(up, step)
        down = step_down(down, step)
        ups.append(up)
        downs.append(down)
    line = jnp.concatenate(ups[::-1] + [own] + downs, 0)
    return lax.dynamic_slice_in_dim(line, (size - 1 - me) * rows, size * rows, 0)


def scatter_rows(partial):
    size = lax.axis_size("tensor")
    me = lax.axis_index("tensor")
    rows = partial.shape[0] // size

    def block(index):
        place = jnp.clip(index, 0, size - 1)
        return wide(lax.dynamic_slice_in_dim(partial, place * rows, rows, 0))

    up = None
    down = None
    for step in range(1, size):
        term_up = block(me + size - step)
        term_down = block(me - size + step)
        if up is not None:
            term_up = term_up + wide(up)
            term_down = term_down + wide(down)
        up = lax.ppermute(
            low(term_up), "tensor", [(index, index + 1) for index in range(0, step)]
        )
        down = lax.ppermute(
            low(term_down),
            "tensor",
            [(index, index - 1) for index in range(size - step, size)],
        )
    return block(me) + wide(up) + wide(down)


def local(
    tokens,
    positions,
    cotangent,
    query_weight,
    key_weight,
    value_weight,
    output_weight,
    gate_weight,
    up_weight,
    down_weight,
    query_gain,
    key_gain,
    attention_gain,
    feedforward_gain,
):
    model_width = tokens.shape[1]
    data_size = lax.axis_size("dp")
    data_index = lax.axis_index("dp")
    head_size = query_gain.shape[0] * data_size
    local_heads = query_gain.shape[1]
    local_width = query_weight.shape[1]
    local_units = gate_weight.shape[1]
    block_rows = min(512, LENGTH)
    order = mask_order(data_size)
    place_of = jnp.array([order.index(mask) for mask in range(data_size)], jnp.int32)
    width = model_width // data_size
    half_width = model_width // 2

    def shuffle(array_in):
        return jnp.concatenate(
            [
                lax.dynamic_slice_in_dim(array_in, (data_index ^ mask) * width, width, -1)
                for mask in order
            ],
            -1,
        )

    def unshuffle(array_in):
        return jnp.concatenate(
            [
                lax.dynamic_slice_in_dim(
                    array_in, place_of[data_index ^ block] * width, width, -1
                )
                for block in range(data_size)
            ],
            -1,
        )

    small = jnp.concatenate(
        [query_gain.reshape(-1), key_gain.reshape(-1), attention_gain, feedforward_gain]
    )
    small_all = lax.all_gather(small, "dp", axis=0, tiled=False)
    gain_count = query_gain.size
    query_gain_full = small_all[:, :gain_count].reshape(head_size, local_heads)
    key_gain_full = small_all[:, gain_count : 2 * gain_count].reshape(head_size, local_heads)
    attention_scale = wide(
        shuffle(small_all[:, 2 * gain_count : 2 * gain_count + width].reshape(-1))
    )
    feedforward_scale = wide(shuffle(small_all[:, 2 * gain_count + width :].reshape(-1)))
    query_scale = channel_scale(query_gain_full)
    key_scale = channel_scale(key_gain_full)

    attention_full = gather_shards(
        jnp.concatenate([query_weight, key_weight, value_weight], 1), 0
    )
    tokens_here = shuffle(tokens)
    rows_all = gather_rows(tokens_here)
    output_late, gate_late, up_late, down_late, _ = lax.optimization_barrier(
        (output_weight, gate_weight, up_weight, down_weight, attention_full[:8, :128])
    )
    output_full = gather_shards(output_late, 1)
    gate_full = gather_shards(gate_late, 0)
    up_full = gather_shards(up_late, 0)
    down_full = gather_shards(down_late, 1)

    group_rows = rows_all.shape[0]
    seq_count = group_rows // LENGTH

    def per_sequence(array_in):
        return array_in.reshape((seq_count, LENGTH) + array_in.shape[1:])

    projected = jnp.dot(rows_all, attention_full, preferred_element_type=jnp.float32)
    queries = projected[:, :local_width]
    key_rows = projected[:, local_width : 2 * local_width]
    squares = lax.psum(
        jnp.stack([jnp.sum(queries * queries, -1), jnp.sum(key_rows * key_rows, -1)]), "tensor"
    )
    inverse_q = lax.rsqrt(squares[0] / model_width + EPS)[:, None]
    inverse_k = lax.rsqrt(squares[1] / model_width + EPS)[:, None]
    query_hat = queries * inverse_q
    key_hat = key_rows * inverse_k
    cosine_table, sine_table = rope_tables(positions, head_size)
    query_rot = low(
        rotate(
            (query_hat * query_scale).reshape(group_rows, local_heads, head_size),
            cosine_table,
            sine_table,
        )
    )
    key_rot = low(
        rotate(
            (key_hat * key_scale).reshape(group_rows, local_heads, head_size),
            cosine_table,
            sine_table,
        )
    )
    value_rows = low(projected[:, 2 * local_width :]).reshape(group_rows, local_heads, head_size)
    attended, row_lse = lax.map(
        lambda sequence_item: attend_forward(
            sequence_item[0], sequence_item[1], sequence_item[2], block_rows
        ),
        (per_sequence(query_rot), per_sequence(key_rot), per_sequence(value_rows)),
    )
    attended = low(attended.reshape(group_rows, -1))
    branch = scatter_rows(jnp.dot(attended, output_full, preferred_element_type=jnp.float32))
    inverse_a = lax.rsqrt(jnp.mean(branch * branch, -1, keepdims=True) + EPS)
    branch_hat = branch * inverse_a
    hidden_state = wide(tokens_here) + branch_hat * attention_scale
    mlp_all = gather_rows(low(hidden_state))
    gate_act = jnp.dot(mlp_all, gate_full, preferred_element_type=jnp.float32)
    up_act = jnp.dot(mlp_all, up_full, preferred_element_type=jnp.float32)
    sigmoid_gate = jax.nn.sigmoid(gate_act)
    silu_gate = gate_act * sigmoid_gate
    inner_act = low(silu_gate * up_act)
    mixed = scatter_rows(jnp.dot(inner_act, down_full, preferred_element_type=jnp.float32))
    inverse_m = lax.rsqrt(jnp.mean(mixed * mixed, -1, keepdims=True) + EPS)
    mixed_hat = mixed * inverse_m
    block_output = unshuffle(hidden_state + mixed_hat * feedforward_scale)

    grad_output = wide(shuffle(cotangent))
    partial_feedforward_gain = jnp.sum(grad_output * mixed_hat, 0)
    grad_mixed = low(norm_backward(grad_output, mixed_hat, inverse_m, feedforward_scale))
    mixed_cot = gather_rows(grad_mixed)
    grad_inner = jnp.einsum("td,fd->tf", mixed_cot, down_full, preferred_element_type=jnp.float32)
    grad_gate_act = low(
        grad_inner * up_act * sigmoid_gate * (1.0 + gate_act * (1.0 - sigmoid_gate))
    )
    grad_up_act = low(grad_inner * silu_gate)
    mlp_input_part = jnp.einsum(
        "tf,df->td", grad_gate_act, gate_full, preferred_element_type=jnp.float32
    ) + jnp.einsum("tf,df->td", grad_up_act, up_full, preferred_element_type=jnp.float32)
    grad_hidden = grad_output + scatter_rows(mlp_input_part)

    def weight_grad(rows_in, grad_in, axis):
        if axis == 0:
            near, far = rows_in[:, :half_width], rows_in[:, half_width:]
            return scatter_shards(
                jnp.einsum("td,tf->df", near, grad_in, preferred_element_type=jnp.float32),
                jnp.einsum("td,tf->df", far, grad_in, preferred_element_type=jnp.float32),
                0,
            )
        near, far = grad_in[:, :half_width], grad_in[:, half_width:]
        return scatter_shards(
            jnp.einsum("tf,td->fd", rows_in, near, preferred_element_type=jnp.float32),
            jnp.einsum("tf,td->fd", rows_in, far, preferred_element_type=jnp.float32),
            1,
        )

    grad_down = weight_grad(inner_act, mixed_cot, 1)
    grad_gate = weight_grad(mlp_all, grad_gate_act, 0)
    grad_up = weight_grad(mlp_all, grad_up_act, 0)
    partial_attention_gain = jnp.sum(grad_hidden * branch_hat, 0)
    grad_branch = low(norm_backward(grad_hidden, branch_hat, inverse_a, attention_scale))
    branch_cot = gather_rows(grad_branch)
    grad_output_proj = weight_grad(attended, branch_cot, 1)
    grad_attended = low(
        jnp.einsum("td,cd->tc", branch_cot, output_full, preferred_element_type=jnp.float32)
    )
    grad_query_rot, grad_key_rot, grad_value_rows = lax.map(
        lambda sequence_item: attend_backward(
            sequence_item[0],
            sequence_item[1],
            sequence_item[2],
            sequence_item[3],
            sequence_item[4],
            block_rows,
        ),
        (
            per_sequence(query_rot),
            per_sequence(key_rot),
            per_sequence(value_rows),
            per_sequence(grad_attended.reshape(group_rows, local_heads, head_size)),
            row_lse,
        ),
    )
    grad_query_rot = wide(low(grad_query_rot.reshape(group_rows, local_heads, head_size)))
    grad_key_rot = wide(low(grad_key_rot.reshape(group_rows, local_heads, head_size)))
    grad_values_low = low(grad_value_rows.reshape(group_rows, -1))
    grad_query_norm = unrotate(grad_query_rot, cosine_table, sine_table).reshape(group_rows, -1)
    grad_key_norm = unrotate(grad_key_rot, cosine_table, sine_table).reshape(group_rows, -1)
    grad_query_scale = jnp.sum(grad_query_norm * query_hat, 0)
    grad_key_scale = jnp.sum(grad_key_norm * key_hat, 0)
    scaled_query = grad_query_norm * query_scale
    scaled_key = grad_key_norm * key_scale
    inner_query, inner_key, total_attention_gain, total_feedforward_gain = lax.psum(
        (
            jnp.sum(scaled_query * query_hat, -1),
            jnp.sum(scaled_key * key_hat, -1),
            partial_attention_gain,
            partial_feedforward_gain,
        ),
        "tensor",
    )
    grad_queries = low(
        inverse_q * (scaled_query - query_hat * inner_query[:, None] / model_width)
    )
    grad_keys = low(inverse_k * (scaled_key - key_hat * inner_key[:, None] / model_width))
    grad_projected = jnp.concatenate([grad_queries, grad_keys, grad_values_low], 1)
    grad_attention = weight_grad(rows_all, grad_projected, 0)
    input_part = jnp.einsum(
        "tc,dc->td", grad_projected, attention_full, preferred_element_type=jnp.float32
    )
    grad_tokens = unshuffle(grad_hidden + scatter_rows(input_part))
    query_gain_grad = grad_query_scale.reshape(local_heads, head_size).T
    key_gain_grad = grad_key_scale.reshape(local_heads, head_size).T
    gain_grads = jnp.concatenate(
        [
            query_gain_grad.reshape(data_size, -1),
            key_gain_grad.reshape(data_size, -1),
            unshuffle(total_attention_gain).reshape(data_size, width),
            unshuffle(total_feedforward_gain).reshape(data_size, width),
        ],
        1,
    )
    gain_shard = wide(
        lax.psum_scatter(gain_grads, "dp", scatter_dimension=0, tiled=True)
    ).reshape(-1)
    return (
        block_output,
        grad_tokens,
        grad_attention[:, :local_width],
        grad_attention[:, local_width : 2 * local_width],
        grad_attention[:, 2 * local_width :],
        grad_output_proj,
        grad_gate,
        grad_up,
        grad_down,
        gain_shard[:gain_count].reshape(query_gain.shape),
        gain_shard[gain_count : 2 * gain_count].reshape(key_gain.shape),
        gain_shard[2 * gain_count : 2 * gain_count + width],
        gain_shard[2 * gain_count + width :],
    )


def solution(mesh):
    return jax.shard_map(
        local,
        mesh=mesh,
        in_specs=(
            P(("dp", "tensor"), None),
            P("dp"),
            P(("dp", "tensor"), None),
            P("dp", "tensor"),
            P("dp", "tensor"),
            P("dp", "tensor"),
            P("tensor", "dp"),
            P("dp", "tensor"),
            P("dp", "tensor"),
            P("tensor", "dp"),
            P("dp", "tensor"),
            P("dp", "tensor"),
            P("dp"),
            P("dp"),
        ),
        out_specs=(
            P(("dp", "tensor"), None),
            P(("dp", "tensor"), None),
            P("dp", "tensor"),
            P("dp", "tensor"),
            P("dp", "tensor"),
            P("tensor", "dp"),
            P("dp", "tensor"),
            P("dp", "tensor"),
            P("tensor", "dp"),
            P("dp", "tensor"),
            P("dp", "tensor"),
            P("dp"),
            P("dp"),
        ),
        check_vma=False,
    )
```

```python
import functools

import jax
import jax.numpy as jnp
from jax import lax
from jax.experimental import pallas as pl
from jax.experimental.pallas import tpu as pltpu
from jax.sharding import PartitionSpec as P

LENGTH = 1024


EPS = 1e-06
THETA = 500000.0
MASKED = -1e30
VMEM_BYTES = 64 * 1024 * 1024 - 128 * 1024


def rope_tables(positions, head_size):
    half_size = head_size // 2
    frequency = THETA ** (-(jnp.arange(half_size, dtype=jnp.float32) * 2.0 / head_size))
    angles = positions.astype(jnp.float32)[:, None] * frequency[None, :]
    return (jnp.cos(angles)[:, None, :], jnp.sin(angles)[:, None, :])


def rotate(values, cosine_table, sine_table):
    half_size = values.shape[-1] // 2
    first_half = values[..., :half_size]
    second_half = values[..., half_size:]
    return jnp.concatenate(
        [
            first_half * cosine_table - second_half * sine_table,
            second_half * cosine_table + first_half * sine_table,
        ],
        -1,
    )


def unrotate(gradient, cosine_table, sine_table):
    half_size = gradient.shape[-1] // 2
    first_half = gradient[..., :half_size]
    second_half = gradient[..., half_size:]
    return jnp.concatenate(
        [
            first_half * cosine_table + second_half * sine_table,
            second_half * cosine_table - first_half * sine_table,
        ],
        -1,
    )


def channel_scale(gain_block):
    return gain_block.astype(jnp.float32).T.reshape(-1)


def masked_scores(queries, key_rows, first_row, block_rows):
    last_row = first_row + block_rows
    score_scale = queries.shape[-1] ** (-0.5)
    scores = (
        jnp.einsum(
            "qhc,khc->hqk",
            queries[first_row:last_row],
            key_rows[:last_row],
            preferred_element_type=jnp.float32,
        )
        * score_scale
    )
    row_index = first_row + lax.broadcasted_iota(jnp.int32, (block_rows, last_row), 0)
    col_index = lax.broadcasted_iota(jnp.int32, (block_rows, last_row), 1)
    return jnp.where((col_index <= row_index)[None], scores, MASKED)


def attend_forward(queries, key_rows, value_rows, block_rows):
    length = queries.shape[0]
    output_list = []
    lse_list = []
    for first_row in range(0, length, block_rows):
        last_row = first_row + block_rows
        scores = masked_scores(queries, key_rows, first_row, block_rows)
        row_max = jnp.max(scores, -1, keepdims=True)
        exponent = jnp.exp(scores - row_max)
        row_total = jnp.sum(exponent, -1, keepdims=True)
        low_probs = (exponent / row_total).astype(jnp.bfloat16)
        output_list.append(
            jnp.einsum(
                "hqk,khc->qhc", low_probs, value_rows[:last_row], preferred_element_type=jnp.float32
            )
        )
        lse_list.append(row_max + jnp.log(row_total))
    return (jnp.concatenate(output_list, 0), jnp.concatenate(lse_list, 1))


def attend_backward(queries, key_rows, value_rows, grad_out, row_lse, block_rows):
    length = queries.shape[0]
    score_scale = queries.shape[-1] ** (-0.5)
    grad_keys = jnp.zeros(key_rows.shape, jnp.float32)
    grad_values = jnp.zeros(value_rows.shape, jnp.float32)
    query_list = []
    for first_row in range(0, length, block_rows):
        last_row = first_row + block_rows
        padding = ((0, length - last_row), (0, 0), (0, 0))
        scores = masked_scores(queries, key_rows, first_row, block_rows)
        probabilities = jnp.exp(scores - row_lse[:, first_row:last_row])
        low_probs = probabilities.astype(jnp.bfloat16)
        grad_block = grad_out[first_row:last_row]
        grad_values = grad_values + jnp.pad(
            jnp.einsum("hqk,qhc->khc", low_probs, grad_block, preferred_element_type=jnp.float32),
            padding,
        )
        grad_probs = jnp.einsum(
            "qhc,khc->hqk", grad_block, value_rows[:last_row], preferred_element_type=jnp.float32
        )
        row_delta = jnp.sum(grad_probs * probabilities, -1, keepdims=True)
        grad_scores = (probabilities * (grad_probs - row_delta)).astype(jnp.bfloat16)
        query_list.append(
            jnp.einsum(
                "hqk,khc->qhc", grad_scores, key_rows[:last_row], preferred_element_type=jnp.float32
            )
            * score_scale
        )
        grad_keys = grad_keys + jnp.pad(
            jnp.einsum(
                "hqk,qhc->khc",
                grad_scores,
                queries[first_row:last_row],
                preferred_element_type=jnp.float32,
            )
            * score_scale,
            padding,
        )
    return (jnp.concatenate(query_list, 0), grad_keys, grad_values)


def norm_backward(grad_in, normalized, inverse_rms, gain_values):
    scaled = grad_in * gain_values
    return inverse_rms * (scaled - normalized * jnp.mean(scaled * normalized, -1, keepdims=True))


def bits_of(size):
    return size.bit_length() - 1


def mask_order(size):
    evens = [mask for mask in range(size) if mask % 2 == 0]
    return evens + [mask + 1 for mask in evens]


def swap(array_in, mask):
    size = lax.axis_size("dp")
    return lax.ppermute(array_in, "dp", [(index, index ^ mask) for index in range(size)])


def gather_parts(shard):
    size = lax.axis_size("dp")
    held = {0: shard}
    if size >= 8:
        held[2] = swap(shard, 2)
        held[4] = swap(shard, 4)
        half = shard.shape[0] // 2
        held[6] = jnp.concatenate([swap(held[2][:half], 4), swap(held[4][half:], 2)], 0)
        first_bit = 3
    else:
        first_bit = 1
    for bit in range(first_bit, bits_of(size)):
        for mask in list(held):
            held[mask | (1 << bit)] = swap(held[mask], 1 << bit)
    for mask in list(held):
        held[mask | 1] = swap(held[mask], 1)
    return [held[mask] for mask in mask_order(size)]


def gather_shards(shard, axis):
    return jnp.concatenate(gather_parts(shard), axis)


def gather_eighths(shard, axis):
    parts = gather_parts(shard)
    run = max(1, len(parts) // 8)
    if run == 1:
        return parts
    return [
        jnp.concatenate(parts[first : first + run], axis) for first in range(0, len(parts), run)
    ]


def low(array_in):
    return array_in.astype(jnp.bfloat16)


def wide(array_in):
    return array_in.astype(jnp.float32)


def scatter_shards(near_part, far_part, axis):
    size = lax.axis_size("dp")
    total = low(near_part + wide(swap(low(far_part), 1)))
    evens = [mask for mask in range(size) if mask % 2 == 0]
    width = total.shape[axis] // len(evens)
    held = {
        mask: lax.slice_in_dim(total, place * width, (place + 1) * width, axis=axis)
        for place, mask in enumerate(evens)
    }
    first_bit = 3 if size >= 8 else 1
    for bit in reversed(range(first_bit, bits_of(size))):
        for mask in [mask for mask in held if mask >> bit & 1]:
            arrived = swap(held.pop(mask), 1 << bit)
            base = mask ^ (1 << bit)
            held[base] = low(wide(held[base]) + wide(arrived))
    if size >= 8:
        half = held[6].shape[0] // 2
        by_four = swap(held[6][:half], 4)
        by_two = swap(held[6][half:], 2)
        two = jnp.concatenate(
            [low(wide(held[2][:half]) + wide(by_four)), held[2][half:]], 0
        )
        four = jnp.concatenate(
            [held[4][:half], low(wide(held[4][half:]) + wide(by_two))], 0
        )
        return wide(held[0]) + wide(swap(two, 2)) + wide(swap(four, 4))
    return wide(held[0])


def step_up(array_in, first=0, last=None):
    size = lax.axis_size("tensor")
    return lax.ppermute(
        array_in, "tensor", [(index, index + 1) for index in range(first, size - 1)]
    )


def step_down(array_in, first=0):
    size = lax.axis_size("tensor")
    return lax.ppermute(
        array_in, "tensor", [(index, index - 1) for index in range(1, size - first)]
    )


def gather_rows(own):
    size = lax.axis_size("tensor")
    me = lax.axis_index("tensor")
    rows = own.shape[0]
    ups, downs = [], []
    up, down = own, own
    for step in range(size - 1):
        up = step_up(up, step)
        down = step_down(down, step)
        ups.append(up)
        downs.append(down)
    line = jnp.concatenate(ups[::-1] + [own] + downs, 0)
    return lax.dynamic_slice_in_dim(line, (size - 1 - me) * rows, size * rows, 0)


def scatter_rows(partial):
    size = lax.axis_size("tensor")
    me = lax.axis_index("tensor")
    rows = partial.shape[0] // size

    def block(index):
        place = jnp.clip(index, 0, size - 1)
        return wide(lax.dynamic_slice_in_dim(partial, place * rows, rows, 0))

    up = None
    down = None
    for step in range(1, size):
        term_up = block(me + size - step)
        term_down = block(me - size + step)
        if up is not None:
            term_up = term_up + wide(up)
            term_down = term_down + wide(down)
        up = lax.ppermute(
            low(term_up), "tensor", [(index, index + 1) for index in range(0, step)]
        )
        down = lax.ppermute(
            low(term_down),
            "tensor",
            [(index, index - 1) for index in range(size - step, size)],
        )
    return block(me) + wide(up) + wide(down)


TILE = 256
STRIP = 16
CHUNKS = 2
HALVES = 2


def rows_product(left, right):
    return lax.dot_general(
        left, right, (((1,), (1,)), ((), ())), preferred_element_type=jnp.float32
    )


def middle_kernel(size, parts, *refs):
    refs = list(refs)
    attended_hbm, tokens_hbm, cotangent_hbm, attention_scale, feedforward_scale = refs[:5]
    output_hbm = refs[5]
    gate_hbm = refs[6 : 6 + parts]
    up_hbm = refs[6 + parts : 6 + 2 * parts]
    down_hbm = refs[6 + 2 * parts : 6 + 3 * parts]
    refs = refs[6 + 3 * parts :]
    (
        mlp_out,
        inner_out,
        mixed_cot_out,
        grad_gate_out,
        grad_up_out,
        branch_cot_out,
        block_out,
        grad_hidden_out,
        attention_gain_out,
        feedforward_gain_out,
        attended,
        tokens,
        cotangent,
        output_weight,
        gate_weight,
        up_weight,
        down_weight,
        everyone,
        gate_act,
        up_act,
        inner,
        hidden,
        branch,
        arrived,
        partial,
        total,
        load_sem,
        weight_sem,
        store_sem,
        sum_send,
        sum_recv,
        hand_send,
        hand_recv,
    ) = refs
    me = lax.axis_index("tensor")
    last = size - 1
    chunk_rows, model_width = tokens.shape[1], tokens.shape[2]
    units = gate_weight.shape[1]
    half_rows = chunk_rows // HALVES
    all_rows = size * chunk_rows

    barrier = pltpu.get_barrier_semaphore()
    for there, offset in ((me < last, 1), (me > 0, -1)):

        @pl.when(there)
        def _():
            pl.semaphore_signal(
                barrier,
                inc=1,
                device_id={"tensor": me + offset},
                device_id_type=pl.DeviceIdType.MESH,
            )

    first_loads = [
        pltpu.make_async_copy(source, target, load_sem.at[place])
        for place, (source, target) in enumerate(
            (
                (attended_hbm, attended),
                (output_hbm, output_weight),
                (tokens_hbm, tokens),
                (cotangent_hbm, cotangent),
            )
        )
    ]
    for copy in first_loads:
        copy.start()
    weight_loads = []
    width = model_width // parts
    for place in range(parts):
        span = pl.ds(place * width, width)
        for kind, (source, target) in enumerate(
            (
                (gate_hbm[place], gate_weight.at[span, :]),
                (up_hbm[place], up_weight.at[span, :]),
                (down_hbm[place], down_weight.at[:, span]),
            )
        ):
            weight_loads.append(
                pltpu.make_async_copy(source, target, weight_sem.at[kind, place])
            )
    for copy in weight_loads:
        copy.start()
    pl.semaphore_wait(barrier, jnp.minimum(me, 1) + jnp.minimum(last - me, 1))

    attention_gain_out[...] = jnp.zeros_like(attention_gain_out)
    feedforward_gain_out[...] = jnp.zeros_like(feedforward_gain_out)

    def half_span(half):
        return pl.ds(half * half_rows, half_rows)

    def strips(half, body):
        def step(index, carry):
            body(
                pl.ds(pl.multiple_of(half * half_rows + index * STRIP, STRIP), STRIP),
                pl.ds(pl.multiple_of(index * STRIP, STRIP), STRIP),
            )
            return carry

        lax.fori_loop(0, half_rows // STRIP, step, 0)

    def sum_copy(chunk, step, half, way, dest):
        return pltpu.make_async_remote_copy(
            src_ref=partial.at[chunk, dest, half_span(half)],
            dst_ref=arrived.at[way, chunk, step - 1, half_span(half)],
            send_sem=sum_send.at[way, chunk, step - 1, half],
            recv_sem=sum_recv.at[way, chunk, step - 1, half],
            device_id={"tensor": me + 1 - 2 * way},
            device_id_type=pl.DeviceIdType.MESH,
        )

    def hand_copy(chunk, hop, half, way, origin):
        rows = everyone.at[origin, chunk, half_span(half)]
        return pltpu.make_async_remote_copy(
            src_ref=rows,
            dst_ref=rows,
            send_sem=hand_send.at[way, chunk, hop - 1, half],
            recv_sem=hand_recv.at[way, chunk, hop - 1, half],
            device_id={"tensor": me + 1 - 2 * way},
            device_id_type=pl.DeviceIdType.MESH,
        )

    def away(way):
        return me if way == 0 else last - me

    def sum_step(chunk, step, half):
        for way in range(2):
            distance = away(way)

            @pl.when(distance <= step - 1)
            def _():
                dest = me + size - step if way == 0 else me - size + step
                if step > 1:

                    @pl.when(distance >= 1)
                    def _():
                        sum_copy(chunk, step - 1, half, way, dest).wait_recv()

                        def add(rows, _):
                            partial[chunk, dest, rows] = low(
                                wide(partial[chunk, dest, rows])
                                + wide(arrived[way, chunk, step - 2, rows])
                            )

                        strips(half, add)

                sum_copy(chunk, step, half, way, dest).start()

    def sum_end(chunk, half):
        def begin(rows, here):
            total[here] = wide(partial[chunk, me, rows])

        strips(half, begin)
        for way in range(2):

            @pl.when(away(way) >= 1)
            def _():
                sum_copy(chunk, size - 1, half, way, me).wait_recv()

                def add(rows, here):
                    total[here] = total[here] + wide(arrived[way, chunk, size - 2, rows])

                strips(half, add)

    def sum_sent(chunk):
        for step in range(1, size):
            for way in range(2):

                @pl.when(away(way) <= step - 1)
                def _():
                    for half in range(HALVES):
                        sum_copy(chunk, step, half, way, 0).wait_send()

    def hand_first(chunk, half):
        for way in range(2):

            @pl.when(away(1 - way) >= 1)
            def _():
                hand_copy(chunk, 1, half, way, me).start()

    def hand_on(chunk, hop, half):
        for way in range(2):

            @pl.when(away(way) >= hop)
            def _():
                origin = me - hop if way == 0 else me + hop
                hand_copy(chunk, hop, half, way, origin).wait_recv()
                if hop < size - 1:

                    @pl.when(away(1 - way) >= 1)
                    def _():
                        hand_copy(chunk, hop + 1, half, way, origin).start()

    def hand_sent(chunk):
        for hop in range(1, size):
            for way in range(2):

                @pl.when(jnp.logical_and(away(way) >= hop - 1, away(1 - way) >= 1))
                def _():
                    for half in range(HALVES):
                        hand_copy(chunk, hop, half, way, 0).wait_send()

    def inverse_rms(values):
        return lax.rsqrt(jnp.mean(values * values, -1, keepdims=True) + EPS)

    def fold(values):
        return values[:8] + values[8:]

    def own_rows(chunk, stage, half):
        def after_branch(rows, here):
            value = total[here]
            branch[chunk, rows] = value
            state = wide(tokens[chunk, rows]) + value * inverse_rms(value) * attention_scale[...]
            hidden[chunk, rows] = state
            everyone[me, chunk, rows] = low(state)

        def after_mixed(rows, here):
            value = total[here]
            inverse = inverse_rms(value)
            normalized = value * inverse
            hidden[chunk, rows] = hidden[chunk, rows] + normalized * feedforward_scale[...]
            grad = wide(cotangent[chunk, rows])
            feedforward_gain_out[...] += fold(grad * normalized)
            everyone[me, chunk, rows] = low(
                norm_backward(grad, normalized, inverse, feedforward_scale[...])
            )

        def after_gradient(rows, here):
            grad = total[here] + wide(cotangent[chunk, rows])
            value = branch[chunk, rows]
            inverse = inverse_rms(value)
            normalized = value * inverse
            branch[chunk, rows] = grad
            attention_gain_out[...] += fold(grad * normalized)
            everyone[me, chunk, rows] = low(
                norm_backward(grad, normalized, inverse, attention_scale[...])
            )

        strips(half, (after_branch, after_mixed, after_gradient)[stage])

    def gathered(chunk):
        return everyone[:, chunk].reshape(all_rows, model_width)

    def tiles(first, end, body):
        def step(index, carry):
            body(pl.ds(pl.multiple_of(index * TILE, TILE), TILE))
            return carry

        lax.fori_loop(first, end, step, 0)

    def store(kind, chunk):
        source, target = (
            (everyone.at[:, chunk], mlp_out.at[chunk]),
            (inner, inner_out.at[chunk]),
            (everyone.at[:, chunk], mixed_cot_out.at[chunk]),
            (gate_act.at[chunk], grad_gate_out.at[chunk]),
            (up_act.at[chunk], grad_up_out.at[chunk]),
            (everyone.at[:, chunk], branch_cot_out.at[:, chunk]),
            (hidden.at[chunk], block_out.at[chunk]),
            (branch.at[chunk], grad_hidden_out.at[chunk]),
        )[kind]
        return pltpu.make_async_copy(source, target, store_sem.at[kind, chunk])

    def put_partial(chunk, columns, values):
        partial[chunk, :, :, columns] = low(values).reshape(size, chunk_rows, TILE)

    def branch_terms(chunk):
        def tile(columns):
            rows = attended[:, chunk].reshape(all_rows, attended.shape[-1])
            put_partial(
                chunk,
                columns,
                jnp.dot(rows, output_weight[:, columns], preferred_element_type=jnp.float32),
            )

        tiles(0, model_width // TILE, tile)

    def gate_tile(chunk):
        def tile(columns):
            rows = gathered(chunk)
            gate = jnp.dot(rows, gate_weight[:, columns], preferred_element_type=jnp.float32)
            up = jnp.dot(rows, up_weight[:, columns], preferred_element_type=jnp.float32)
            gate_act[chunk, :, columns] = low(gate)
            up_act[chunk, :, columns] = low(up)
            inner[:, columns] = low(gate * jax.nn.sigmoid(gate) * up)

        return tile

    def down_tile(chunk):
        def tile(columns):
            put_partial(
                chunk,
                columns,
                jnp.dot(inner[...], down_weight[:, columns], preferred_element_type=jnp.float32),
            )

        return tile

    def grad_inner_tile(chunk):
        def tile(columns):
            grad = rows_product(gathered(chunk), down_weight[columns, :])
            gate = wide(gate_act[chunk, :, columns])
            up = wide(up_act[chunk, :, columns])
            sigmoid = jax.nn.sigmoid(gate)
            gate_act[chunk, :, columns] = low(
                grad * up * sigmoid * (1.0 + gate * (1.0 - sigmoid))
            )
            up_act[chunk, :, columns] = low(grad * gate * sigmoid)

        return tile

    def grad_input_tile(chunk):
        def tile(columns):
            put_partial(
                chunk,
                columns,
                rows_product(gate_act[chunk], gate_weight[columns, :])
                + rows_product(up_act[chunk], up_weight[columns, :]),
            )

        return tile

    unit_tiles, width_tiles = units // TILE, model_width // TILE

    def forward_piece(chunk, piece):
        if piece == 0:
            if chunk == 0:
                for copy in weight_loads:
                    copy.wait()
            store(0, chunk).start()
            tiles(0, unit_tiles // 2, gate_tile(chunk))
        elif piece == 1:
            tiles(unit_tiles // 2, unit_tiles, gate_tile(chunk))
            store(1, chunk).start()
            sum_sent(chunk)
            hand_sent(chunk)
        else:
            tiles(0, width_tiles, down_tile(chunk))
            store(0, chunk).wait()
            store(1, chunk).wait()

    def backward_piece(chunk, piece):
        if piece == 0:
            store(2, chunk).start()
            store(6, chunk).start()
            tiles(0, unit_tiles, grad_inner_tile(chunk))
            store(3, chunk).start()
            store(4, chunk).start()
        elif piece == 1:
            sum_sent(chunk)
            hand_sent(chunk)
            tiles(0, width_tiles // 2, grad_input_tile(chunk))
        else:
            tiles(width_tiles // 2, width_tiles, grad_input_tile(chunk))
            store(2, chunk).wait()

    def end_piece(chunk, piece):
        if piece == 0:
            store(5, chunk).start()
            store(7, chunk).start()

    first_loads[0].wait()
    first_loads[1].wait()
    branch_terms(0)
    first_loads[2].wait()
    first_loads[3].wait()
    bases = {
        (chunk, stage): (CHUNKS * stage + chunk) * size
        for stage in range(3)
        for chunk in range(CHUNKS)
    }
    ticks = max(bases.values()) + 2 * size
    for tick in range(1, ticks + 1):
        for half in range(HALVES):
            for (chunk, stage), base in bases.items():
                at = tick - base
                if size < at < 2 * size:
                    hand_on(chunk, at - size, half)
            for (chunk, stage), base in bases.items():
                at = tick - base
                if 1 <= at < size:
                    sum_step(chunk, at, half)
                elif at == size:
                    sum_end(chunk, half)
                    own_rows(chunk, stage, half)
                    hand_first(chunk, half)
            if tick == 1 and half == 1:
                branch_terms(1)
            for (chunk, stage), base in bases.items():
                piece = (tick - base - 2 * size + 1) * HALVES + half - 1
                if 0 <= piece < 3:
                    (forward_piece, backward_piece, end_piece)[stage](chunk, piece)
    for chunk in range(CHUNKS):
        sum_sent(chunk)
        hand_sent(chunk)
        for kind in range(3, 8):
            store(kind, chunk).wait()


def middle(
    attended,
    tokens_here,
    cotangent_here,
    attention_scale,
    feedforward_scale,
    output_full,
    gate_parts,
    up_parts,
    down_parts,
):
    size = lax.axis_size("tensor")
    parts = len(gate_parts)
    own_rows, model_width = tokens_here.shape
    chunk_rows = own_rows // CHUNKS
    all_rows = size * chunk_rows
    half_rows = chunk_rows // HALVES
    heads_width = attended.shape[1]
    units = gate_parts[0].shape[1]
    chunked = (CHUNKS, chunk_rows, model_width)
    lined = (CHUNKS, size, chunk_rows, model_width)
    low_type, wide_type = jnp.bfloat16, jnp.float32

    def shape(dims, kind=low_type):
        return jax.ShapeDtypeStruct(dims, kind)

    anywhere = pl.BlockSpec(memory_space=pl.ANY)
    inside = pl.BlockSpec(memory_space=pltpu.VMEM)
    dma = pltpu.SemaphoreType.DMA
    flops = 2 * CHUNKS * all_rows * model_width * (2 * heads_width + 6 * units)
    outs = pl.pallas_call(
        functools.partial(middle_kernel, size, parts),
        out_shape=[
            shape(lined),
            shape((CHUNKS, all_rows, units)),
            shape(lined),
            shape((CHUNKS, all_rows, units)),
            shape((CHUNKS, all_rows, units)),
            shape((size, CHUNKS, chunk_rows, model_width)),
            shape(chunked, wide_type),
            shape(chunked, wide_type),
            shape((8, model_width), wide_type),
            shape((8, model_width), wide_type),
        ],
        in_specs=[anywhere] * 3 + [inside] * 2 + [anywhere] * (1 + 3 * parts),
        out_specs=[anywhere] * 8 + [inside] * 2,
        scratch_shapes=[
            pltpu.VMEM((size, CHUNKS, chunk_rows, heads_width), low_type),
            pltpu.VMEM(chunked, low_type),
            pltpu.VMEM(chunked, low_type),
            pltpu.VMEM((heads_width, model_width), low_type),
            pltpu.VMEM((model_width, units), low_type),
            pltpu.VMEM((model_width, units), low_type),
            pltpu.VMEM((units, model_width), low_type),
            pltpu.VMEM((size, CHUNKS, chunk_rows, model_width), low_type),
            pltpu.VMEM((CHUNKS, all_rows, units), low_type),
            pltpu.VMEM((CHUNKS, all_rows, units), low_type),
            pltpu.VMEM((all_rows, units), low_type),
            pltpu.VMEM(chunked, wide_type),
            pltpu.VMEM(chunked, wide_type),
            pltpu.VMEM((2, CHUNKS, size - 1, chunk_rows, model_width), low_type),
            pltpu.VMEM(lined, low_type),
            pltpu.VMEM((half_rows, model_width), wide_type),
            dma((4,)),
            dma((3, parts)),
            dma((8, CHUNKS)),
            dma((2, CHUNKS, size - 1, HALVES)),
            dma((2, CHUNKS, size - 1, HALVES)),
            dma((2, CHUNKS, size - 1, HALVES)),
            dma((2, CHUNKS, size - 1, HALVES)),
        ],
        compiler_params=pltpu.CompilerParams(
            collective_id=0, has_side_effects=True, vmem_limit_bytes=VMEM_BYTES
        ),
        cost_estimate=pl.CostEstimate(
            flops=flops, bytes_accessed=64 << 20, transcendentals=0
        ),
        name="middle",
    )(
        attended.reshape(size, CHUNKS, chunk_rows, heads_width),
        tokens_here.reshape(chunked),
        cotangent_here.reshape(chunked),
        attention_scale.reshape(1, model_width),
        feedforward_scale.reshape(1, model_width),
        output_full,
        *gate_parts,
        *up_parts,
        *down_parts,
    )
    mlp_all, inner, mixed_cot, grad_gate, grad_up, branch_cot, block, grad_hidden = outs[:8]
    rows = CHUNKS * all_rows
    return (
        mlp_all.reshape(rows, model_width),
        inner.reshape(rows, units),
        mixed_cot.reshape(rows, model_width),
        grad_gate.reshape(rows, units),
        grad_up.reshape(rows, units),
        branch_cot.reshape(rows, model_width),
        block.reshape(own_rows, model_width),
        grad_hidden.reshape(own_rows, model_width),
        jnp.sum(outs[8], 0),
        jnp.sum(outs[9], 0),
    )


def local(
    tokens,
    positions,
    cotangent,
    query_weight,
    key_weight,
    value_weight,
    output_weight,
    gate_weight,
    up_weight,
    down_weight,
    query_gain,
    key_gain,
    attention_gain,
    feedforward_gain,
):
    model_width = tokens.shape[1]
    data_size = lax.axis_size("dp")
    data_index = lax.axis_index("dp")
    head_size = query_gain.shape[0] * data_size
    local_heads = query_gain.shape[1]
    local_width = query_weight.shape[1]
    local_units = gate_weight.shape[1]
    block_rows = min(512, LENGTH)
    order = mask_order(data_size)
    place_of = jnp.array([order.index(mask) for mask in range(data_size)], jnp.int32)
    width = model_width // data_size
    half_width = model_width // 2

    def shuffle(array_in):
        return jnp.concatenate(
            [
                lax.dynamic_slice_in_dim(array_in, (data_index ^ mask) * width, width, -1)
                for mask in order
            ],
            -1,
        )

    def unshuffle(array_in):
        return jnp.concatenate(
            [
                lax.dynamic_slice_in_dim(
                    array_in, place_of[data_index ^ block] * width, width, -1
                )
                for block in range(data_size)
            ],
            -1,
        )

    small = jnp.concatenate(
        [query_gain.reshape(-1), key_gain.reshape(-1), attention_gain, feedforward_gain]
    )
    small_all = lax.all_gather(small, "dp", axis=0, tiled=False)
    gain_count = query_gain.size
    query_gain_full = small_all[:, :gain_count].reshape(head_size, local_heads)
    key_gain_full = small_all[:, gain_count : 2 * gain_count].reshape(head_size, local_heads)
    attention_scale = wide(
        shuffle(small_all[:, 2 * gain_count : 2 * gain_count + width].reshape(-1))
    )
    feedforward_scale = wide(shuffle(small_all[:, 2 * gain_count + width :].reshape(-1)))
    query_scale = channel_scale(query_gain_full)
    key_scale = channel_scale(key_gain_full)

    attention_full = gather_shards(
        jnp.concatenate([query_weight, key_weight, value_weight], 1), 0
    )
    tokens_here = shuffle(tokens)
    rows_all = gather_rows(tokens_here)
    output_late, gate_late, up_late, down_late, _ = lax.optimization_barrier(
        (output_weight, gate_weight, up_weight, down_weight, attention_full[:8, :128])
    )
    output_full = gather_shards(output_late, 1)
    gate_parts = gather_eighths(gate_late, 0)
    up_parts = gather_eighths(up_late, 0)
    down_parts = gather_eighths(down_late, 1)

    group_rows = rows_all.shape[0]
    seq_count = group_rows // LENGTH

    def per_sequence(array_in):
        return array_in.reshape((seq_count, LENGTH) + array_in.shape[1:])

    projected = jnp.dot(rows_all, attention_full, preferred_element_type=jnp.float32)
    queries = projected[:, :local_width]
    key_rows = projected[:, local_width : 2 * local_width]
    squares = lax.psum(
        jnp.stack([jnp.sum(queries * queries, -1), jnp.sum(key_rows * key_rows, -1)]), "tensor"
    )
    inverse_q = lax.rsqrt(squares[0] / model_width + EPS)[:, None]
    inverse_k = lax.rsqrt(squares[1] / model_width + EPS)[:, None]
    query_hat = queries * inverse_q
    key_hat = key_rows * inverse_k
    cosine_table, sine_table = rope_tables(positions, head_size)
    query_rot = low(
        rotate(
            (query_hat * query_scale).reshape(group_rows, local_heads, head_size),
            cosine_table,
            sine_table,
        )
    )
    key_rot = low(
        rotate(
            (key_hat * key_scale).reshape(group_rows, local_heads, head_size),
            cosine_table,
            sine_table,
        )
    )
    value_rows = low(projected[:, 2 * local_width :]).reshape(group_rows, local_heads, head_size)
    attended, row_lse = lax.map(
        lambda sequence_item: attend_forward(
            sequence_item[0], sequence_item[1], sequence_item[2], block_rows
        ),
        (per_sequence(query_rot), per_sequence(key_rot), per_sequence(value_rows)),
    )
    attended = low(attended.reshape(group_rows, -1))
    (
        mlp_all,
        inner_act,
        mixed_cot,
        grad_gate_act,
        grad_up_act,
        branch_cot,
        block_here,
        grad_hidden,
        partial_attention_gain,
        partial_feedforward_gain,
    ) = middle(
        attended,
        tokens_here,
        shuffle(cotangent),
        attention_scale,
        feedforward_scale,
        output_full,
        gate_parts,
        up_parts,
        down_parts,
    )
    block_output = unshuffle(block_here)

    def weight_grad(rows_in, grad_in, axis):
        if axis == 0:
            near, far = rows_in[:, :half_width], rows_in[:, half_width:]
            return scatter_shards(
                jnp.einsum("td,tf->df", near, grad_in, preferred_element_type=jnp.float32),
                jnp.einsum("td,tf->df", far, grad_in, preferred_element_type=jnp.float32),
                0,
            )
        near, far = grad_in[:, :half_width], grad_in[:, half_width:]
        return scatter_shards(
            jnp.einsum("tf,td->fd", rows_in, near, preferred_element_type=jnp.float32),
            jnp.einsum("tf,td->fd", rows_in, far, preferred_element_type=jnp.float32),
            1,
        )

    grad_down = weight_grad(inner_act, mixed_cot, 1)
    grad_gate = weight_grad(mlp_all, grad_gate_act, 0)
    grad_up = weight_grad(mlp_all, grad_up_act, 0)
    grad_output_proj = weight_grad(attended, branch_cot, 1)
    grad_attended = low(
        jnp.einsum("td,cd->tc", branch_cot, output_full, preferred_element_type=jnp.float32)
    )
    grad_query_rot, grad_key_rot, grad_value_rows = lax.map(
        lambda sequence_item: attend_backward(
            sequence_item[0],
            sequence_item[1],
            sequence_item[2],
            sequence_item[3],
            sequence_item[4],
            block_rows,
        ),
        (
            per_sequence(query_rot),
            per_sequence(key_rot),
            per_sequence(value_rows),
            per_sequence(grad_attended.reshape(group_rows, local_heads, head_size)),
            row_lse,
        ),
    )
    grad_query_rot = wide(low(grad_query_rot.reshape(group_rows, local_heads, head_size)))
    grad_key_rot = wide(low(grad_key_rot.reshape(group_rows, local_heads, head_size)))
    grad_values_low = low(grad_value_rows.reshape(group_rows, -1))
    grad_query_norm = unrotate(grad_query_rot, cosine_table, sine_table).reshape(group_rows, -1)
    grad_key_norm = unrotate(grad_key_rot, cosine_table, sine_table).reshape(group_rows, -1)
    grad_query_scale = jnp.sum(grad_query_norm * query_hat, 0)
    grad_key_scale = jnp.sum(grad_key_norm * key_hat, 0)
    scaled_query = grad_query_norm * query_scale
    scaled_key = grad_key_norm * key_scale
    inner_query, inner_key, total_attention_gain, total_feedforward_gain = lax.psum(
        (
            jnp.sum(scaled_query * query_hat, -1),
            jnp.sum(scaled_key * key_hat, -1),
            partial_attention_gain,
            partial_feedforward_gain,
        ),
        "tensor",
    )
    grad_queries = low(
        inverse_q * (scaled_query - query_hat * inner_query[:, None] / model_width)
    )
    grad_keys = low(inverse_k * (scaled_key - key_hat * inner_key[:, None] / model_width))
    grad_projected = jnp.concatenate([grad_queries, grad_keys, grad_values_low], 1)
    grad_attention = weight_grad(rows_all, grad_projected, 0)
    input_part = jnp.einsum(
        "tc,dc->td", grad_projected, attention_full, preferred_element_type=jnp.float32
    )
    grad_tokens = unshuffle(grad_hidden + scatter_rows(input_part))
    query_gain_grad = grad_query_scale.reshape(local_heads, head_size).T
    key_gain_grad = grad_key_scale.reshape(local_heads, head_size).T
    gain_grads = jnp.concatenate(
        [
            query_gain_grad.reshape(data_size, -1),
            key_gain_grad.reshape(data_size, -1),
            unshuffle(total_attention_gain).reshape(data_size, width),
            unshuffle(total_feedforward_gain).reshape(data_size, width),
        ],
        1,
    )
    gain_shard = wide(
        lax.psum_scatter(gain_grads, "dp", scatter_dimension=0, tiled=True)
    ).reshape(-1)
    return (
        block_output,
        grad_tokens,
        grad_attention[:, :local_width],
        grad_attention[:, local_width : 2 * local_width],
        grad_attention[:, 2 * local_width :],
        grad_output_proj,
        grad_gate,
        grad_up,
        grad_down,
        gain_shard[:gain_count].reshape(query_gain.shape),
        gain_shard[gain_count : 2 * gain_count].reshape(key_gain.shape),
        gain_shard[2 * gain_count : 2 * gain_count + width],
        gain_shard[2 * gain_count + width :],
    )


def solution(mesh):
    return jax.shard_map(
        local,
        mesh=mesh,
        in_specs=(
            P(("dp", "tensor"), None),
            P("dp"),
            P(("dp", "tensor"), None),
            P("dp", "tensor"),
            P("dp", "tensor"),
            P("dp", "tensor"),
            P("tensor", "dp"),
            P("dp", "tensor"),
            P("dp", "tensor"),
            P("tensor", "dp"),
            P("dp", "tensor"),
            P("dp", "tensor"),
            P("dp"),
            P("dp"),
        ),
        out_specs=(
            P(("dp", "tensor"), None),
            P(("dp", "tensor"), None),
            P("dp", "tensor"),
            P("dp", "tensor"),
            P("dp", "tensor"),
            P("tensor", "dp"),
            P("dp", "tensor"),
            P("dp", "tensor"),
            P("tensor", "dp"),
            P("dp", "tensor"),
            P("dp", "tensor"),
            P("dp"),
            P("dp"),
        ),
        check_vma=False,
    )
```

```python
import functools

import jax
import jax.numpy as jnp
from jax import lax
from jax.experimental import pallas as pl
from jax.experimental.pallas import tpu as pltpu
from jax.sharding import PartitionSpec as P

LENGTH = 1024


EPS = 1e-06
THETA = 500000.0
MASKED = -1e30
VMEM_BYTES = 64 * 1024 * 1024 - 128 * 1024


def rope_tables(positions, head_size):
    half_size = head_size // 2
    frequency = THETA ** (-(jnp.arange(half_size, dtype=jnp.float32) * 2.0 / head_size))
    angles = positions.astype(jnp.float32)[:, None] * frequency[None, :]
    return (jnp.cos(angles)[:, None, :], jnp.sin(angles)[:, None, :])


def rotate(values, cosine_table, sine_table):
    half_size = values.shape[-1] // 2
    first_half = values[..., :half_size]
    second_half = values[..., half_size:]
    return jnp.concatenate(
        [
            first_half * cosine_table - second_half * sine_table,
            second_half * cosine_table + first_half * sine_table,
        ],
        -1,
    )


def unrotate(gradient, cosine_table, sine_table):
    half_size = gradient.shape[-1] // 2
    first_half = gradient[..., :half_size]
    second_half = gradient[..., half_size:]
    return jnp.concatenate(
        [
            first_half * cosine_table + second_half * sine_table,
            second_half * cosine_table - first_half * sine_table,
        ],
        -1,
    )


def channel_scale(gain_block):
    return gain_block.astype(jnp.float32).T.reshape(-1)


def masked_scores(queries, key_rows, first_row, block_rows):
    last_row = first_row + block_rows
    score_scale = queries.shape[-1] ** (-0.5)
    scores = (
        jnp.einsum(
            "qhc,khc->hqk",
            queries[first_row:last_row],
            key_rows[:last_row],
            preferred_element_type=jnp.float32,
        )
        * score_scale
    )
    row_index = first_row + lax.broadcasted_iota(jnp.int32, (block_rows, last_row), 0)
    col_index = lax.broadcasted_iota(jnp.int32, (block_rows, last_row), 1)
    return jnp.where((col_index <= row_index)[None], scores, MASKED)


def attend_forward(queries, key_rows, value_rows, block_rows):
    length = queries.shape[0]
    output_list = []
    lse_list = []
    for first_row in range(0, length, block_rows):
        last_row = first_row + block_rows
        scores = masked_scores(queries, key_rows, first_row, block_rows)
        row_max = jnp.max(scores, -1, keepdims=True)
        exponent = jnp.exp(scores - row_max)
        row_total = jnp.sum(exponent, -1, keepdims=True)
        low_probs = (exponent / row_total).astype(jnp.bfloat16)
        output_list.append(
            jnp.einsum(
                "hqk,khc->qhc", low_probs, value_rows[:last_row], preferred_element_type=jnp.float32
            )
        )
        lse_list.append(row_max + jnp.log(row_total))
    return (jnp.concatenate(output_list, 0), jnp.concatenate(lse_list, 1))


def attend_backward(queries, key_rows, value_rows, grad_out, row_lse, block_rows):
    length = queries.shape[0]
    score_scale = queries.shape[-1] ** (-0.5)
    grad_keys = jnp.zeros(key_rows.shape, jnp.float32)
    grad_values = jnp.zeros(value_rows.shape, jnp.float32)
    query_list = []
    for first_row in range(0, length, block_rows):
        last_row = first_row + block_rows
        padding = ((0, length - last_row), (0, 0), (0, 0))
        scores = masked_scores(queries, key_rows, first_row, block_rows)
        probabilities = jnp.exp(scores - row_lse[:, first_row:last_row])
        low_probs = probabilities.astype(jnp.bfloat16)
        grad_block = grad_out[first_row:last_row]
        grad_values = grad_values + jnp.pad(
            jnp.einsum("hqk,qhc->khc", low_probs, grad_block, preferred_element_type=jnp.float32),
            padding,
        )
        grad_probs = jnp.einsum(
            "qhc,khc->hqk", grad_block, value_rows[:last_row], preferred_element_type=jnp.float32
        )
        row_delta = jnp.sum(grad_probs * probabilities, -1, keepdims=True)
        grad_scores = (probabilities * (grad_probs - row_delta)).astype(jnp.bfloat16)
        query_list.append(
            jnp.einsum(
                "hqk,khc->qhc", grad_scores, key_rows[:last_row], preferred_element_type=jnp.float32
            )
            * score_scale
        )
        grad_keys = grad_keys + jnp.pad(
            jnp.einsum(
                "hqk,qhc->khc",
                grad_scores,
                queries[first_row:last_row],
                preferred_element_type=jnp.float32,
            )
            * score_scale,
            padding,
        )
    return (jnp.concatenate(query_list, 0), grad_keys, grad_values)


def norm_backward(grad_in, normalized, inverse_rms, gain_values):
    scaled = grad_in * gain_values
    return inverse_rms * (scaled - normalized * jnp.mean(scaled * normalized, -1, keepdims=True))


def bits_of(size):
    return size.bit_length() - 1


def mask_order(size):
    return [
        low_bits + 8 * high_bits
        for low_bits in (0, 2, 4, 6, 1, 3, 5, 7)
        for high_bits in range(size // 8)
    ]


def swap(array_in, mask):
    size = lax.axis_size("dp")
    return lax.ppermute(array_in, "dp", [(index, index ^ mask) for index in range(size)])


def gather_high(shard, axis):
    for bit in range(3, bits_of(lax.axis_size("dp"))):
        shard = jnp.concatenate([shard, swap(shard, 1 << bit)], axis)
    return shard


def scatter_high(total, axis):
    for bit in reversed(range(3, bits_of(lax.axis_size("dp")))):
        kept, sent = jnp.split(total, 2, axis)
        total = low(wide(kept) + wide(swap(low(sent), 1 << bit)))
    return total


def low(array_in):
    return array_in.astype(jnp.bfloat16)


def wide(array_in):
    return array_in.astype(jnp.float32)


def scatter_shards(near_part, far_part, axis):
    total = low(near_part + wide(swap(low(far_part), 1)))
    own, two, four, six = jnp.split(total, 4, axis)
    half = six.shape[0] // 2
    by_four = swap(six[:half], 4)
    by_two = swap(six[half:], 2)
    two = jnp.concatenate([low(wide(two[:half]) + wide(by_four)), two[half:]], 0)
    four = jnp.concatenate([four[:half], low(wide(four[half:]) + wide(by_two))], 0)
    total = wide(own) + wide(swap(two, 2)) + wide(swap(four, 4))
    return wide(scatter_high(total, axis))


def scatter_rows(partial):
    size = lax.axis_size("tensor")
    me = lax.axis_index("tensor")
    rows = partial.shape[0] // size

    def block(index):
        place = jnp.clip(index, 0, size - 1)
        return wide(lax.dynamic_slice_in_dim(partial, place * rows, rows, 0))

    up = None
    down = None
    for step in range(1, size):
        term_up = block(me + size - step)
        term_down = block(me - size + step)
        if up is not None:
            term_up = term_up + wide(up)
            term_down = term_down + wide(down)
        up = lax.ppermute(
            low(term_up), "tensor", [(index, index + 1) for index in range(0, step)]
        )
        down = lax.ppermute(
            low(term_down),
            "tensor",
            [(index, index - 1) for index in range(size - step, size)],
        )
    return block(me) + wide(up) + wide(down)


TILE = 256
STRIP = 16
CHUNKS = 2
HALVES = 2


def rows_product(left, right):
    return lax.dot_general(
        left, right, (((1,), (1,)), ((), ())), preferred_element_type=jnp.float32
    )


def shard_peer(mask):
    index = lax.axis_index("dp")
    return index + mask - 2 * mask * ((index // mask) % 2)


ROUTE = {1: (1, 1), 2: (2, 2), 3: (1, 1), 4: (4, 4), 5: (1, 1), 6: (4, 2), 7: (1, 1)}
PLACES = {mask: place for place, mask in enumerate((0, 2, 4, 6, 1, 3, 5, 7))}


class ShardGather:
    def __init__(self, own, target, send_sem, recv_sem):
        self.own, self.target, self.send_sem, self.recv_sem = own, target, send_sem, recv_sem

    def copy(self, mask, half):
        route = ROUTE[mask][half]
        before = mask ^ route
        return pltpu.make_async_remote_copy(
            src_ref=self.target(PLACES[before], half) if before else self.own(half),
            dst_ref=self.target(PLACES[mask], half),
            send_sem=self.send_sem.at[mask - 1, half],
            recv_sem=self.recv_sem.at[mask - 1, half],
            device_id={"dp": shard_peer(route)},
            device_id_type=pl.DeviceIdType.MESH,
        )

    def start(self, *masks):
        for half in range(2):
            for mask in masks:
                self.copy(mask, half).start()

    def arrive(self, mask, halves=(0, 1)):
        for half in halves:
            self.copy(mask, half).wait_recv()
            for after, route in ROUTE.items():
                if after != mask and after ^ route[half] == mask:
                    self.copy(after, half).start()

    def sent(self):
        for mask in ROUTE:
            for half in range(2):
                self.copy(mask, half).wait_send()


def row_halves(buffer, height):
    def target(place, half):
        return buffer.at[pl.ds(place * height + half * (height // 2), height // 2), :]

    return target


def column_halves(buffer, width):
    height = buffer.shape[0] // 2

    def target(place, half):
        return buffer.at[pl.ds(half * height, height), pl.ds(place * width, width)]

    return target


def own_halves(shard):
    height = shard.shape[0] // 2
    return lambda half: shard.at[pl.ds(half * height, height), :]


def greet(line_devices):
    barrier = pltpu.get_barrier_semaphore()
    for mask in (1, 2, 4):
        pl.semaphore_signal(
            barrier,
            inc=1,
            device_id={"dp": shard_peer(mask)},
            device_id_type=pl.DeviceIdType.MESH,
        )
    for there, index in line_devices:

        @pl.when(there)
        def _():
            pl.semaphore_signal(
                barrier,
                inc=1,
                device_id={"tensor": index},
                device_id_type=pl.DeviceIdType.MESH,
            )


PIECES = 4


def front_kernel(
    size,
    tokens_hbm,
    attention_hbm,
    output_hbm,
    gate_hbm,
    gain_hbm,
    rows_out,
    projected_out,
    attention_out,
    output_out,
    gate_out,
    gain_out,
    rows,
    weight,
    projected,
    load_sem,
    store_sem,
    hand_send,
    hand_recv,
    shard_send,
    shard_recv,
):
    me = lax.axis_index("tensor")
    last = size - 1
    piece_rows = rows.shape[1] // PIECES
    greet(((me < last, me + 1), (me > 0, me - 1)))
    loads = [
        pltpu.make_async_copy(source, target, load_sem.at[place])
        for place, (source, target) in enumerate(
            (
                (tokens_hbm, rows.at[me]),
                (attention_hbm, weight.at[pl.ds(0, attention_hbm.shape[0]), :]),
                (output_hbm, output_out.at[:, pl.ds(0, output_hbm.shape[1])]),
                (gate_hbm, gate_out.at[pl.ds(0, gate_hbm.shape[0]), :]),
                (gain_hbm, gain_out.at[pl.ds(0, gain_hbm.shape[0]), :]),
            )
        )
    ]
    for copy in loads:
        copy.start()
    attention_flow, output_flow, gate_flow, gain_flow = (
        ShardGather(own_halves(shard), target, shard_send.at[kind], shard_recv.at[kind])
        for kind, (shard, target) in enumerate(
            (
                (attention_hbm, row_halves(weight, attention_hbm.shape[0])),
                (output_hbm, column_halves(output_out, output_hbm.shape[1])),
                (gate_hbm, row_halves(gate_out, gate_hbm.shape[0])),
                (gain_hbm, row_halves(gain_out, gain_hbm.shape[0])),
            )
        )
    )
    pl.semaphore_wait(
        pltpu.get_barrier_semaphore(), 3 + jnp.minimum(me, 1) + jnp.minimum(last - me, 1)
    )

    def away(way):
        return me if way == 0 else last - me

    def hand_copy(hop, piece, way, origin):
        span = pl.ds(piece * piece_rows, piece_rows)
        return pltpu.make_async_remote_copy(
            src_ref=tokens_hbm.at[span] if hop == 1 else rows.at[origin, span],
            dst_ref=rows.at[origin, span],
            send_sem=hand_send.at[way, hop - 1, piece],
            recv_sem=hand_recv.at[way, hop - 1, piece],
            device_id={"tensor": me + 1 - 2 * way},
            device_id_type=pl.DeviceIdType.MESH,
        )

    for piece in range(PIECES):
        for way in range(2):

            @pl.when(away(1 - way) >= 1)
            def _():
                hand_copy(1, piece, way, me).start()

        if piece == 0:
            attention_flow.start(2, 4, 1)
            gain_flow.start(2, 4, 1)

    def hand_on(hop, piece):
        for way in range(2):

            @pl.when(away(way) >= hop)
            def _():
                origin = me - hop if way == 0 else me + hop
                hand_copy(hop, piece, way, origin).wait_recv()
                if hop < size - 1:

                    @pl.when(away(1 - way) >= 1)
                    def _():
                        hand_copy(hop + 1, piece, way, origin).start()

    def row_store(origin):
        return pltpu.make_async_copy(rows.at[origin], rows_out.at[origin], store_sem.at[0, origin])

    def projected_store(origin):
        return pltpu.make_async_copy(
            projected.at[origin], projected_out.at[origin], store_sem.at[1, origin]
        )

    weight_store = pltpu.make_async_copy(weight, attention_out, store_sem.at[2, 0])

    def project(origin):
        def step(index, carry):
            columns = pl.ds(pl.multiple_of(index * TILE, TILE), TILE)
            projected[origin, :, columns] = jnp.dot(
                rows[origin], weight[:, columns], preferred_element_type=jnp.float32
            )
            return carry

        row_store(origin).start()
        lax.fori_loop(0, weight.shape[1] // TILE, step, 0)
        projected_store(origin).start()

    def project_from(hop, way):
        @pl.when(away(way) >= hop)
        def _():
            project(me - hop if way == 0 else me + hop)

    def turns(beat):
        if beat == 2:
            attention_flow.arrive(2, (0,))
            attention_flow.arrive(4, (0,))
        elif beat == 3:
            attention_flow.arrive(2, (1,))
            attention_flow.arrive(4, (1,))
            output_flow.start(2, 4, 1)
            gain_flow.arrive(2)
            gain_flow.arrive(4)
        elif beat == 5:
            attention_flow.arrive(6)
            gate_flow.start(2, 4, 1)
            gain_flow.arrive(6)
        elif beat == 6:
            output_flow.arrive(2)
            output_flow.arrive(4)
            for mask in (1, 3, 5, 7):
                attention_flow.arrive(mask)
            loads[0].wait()
            loads[1].wait()
            weight_store.start()
            project(me)
        elif beat == 7:
            project_from(1, 0)
        elif beat == 8:
            project_from(1, 1)
            output_flow.arrive(6)
        elif beat == 9:
            gate_flow.arrive(2, (0,))
            gate_flow.arrive(4, (0,))
        elif beat == 10:
            project_from(2, 0)
        elif beat == 11:
            project_from(2, 1)
            gate_flow.arrive(2, (1,))
            gate_flow.arrive(4, (1,))

    for beat in range(1, (size - 1) * PIECES + 1):
        hand_on((beat - 1) // PIECES + 1, (beat - 1) % PIECES)
        turns(beat)
    project_from(3, 0)
    project_from(3, 1)
    gate_flow.arrive(6)
    for flow in (output_flow, gate_flow, gain_flow):
        for mask in (1, 3, 5, 7):
            flow.arrive(mask)
    for hop in range(1, size):
        for way in range(2):

            @pl.when(jnp.logical_and(away(way) >= hop - 1, away(1 - way) >= 1))
            def _():
                for piece in range(PIECES):
                    hand_copy(hop, piece, way, 0).wait_send()

    for flow in (attention_flow, output_flow, gate_flow, gain_flow):
        flow.sent()
    for copy in loads[2:]:
        copy.wait()
    for origin in range(size):
        row_store(origin).wait()
        projected_store(origin).wait()
    weight_store.wait()


def front(tokens_here, attention_shard, output_shard, gate_shard, gain_shard):
    size = lax.axis_size("tensor")
    own_rows, model_width = tokens_here.shape
    width = attention_shard.shape[1]
    low_type, wide_type = jnp.bfloat16, jnp.float32
    anywhere = pl.BlockSpec(memory_space=pl.ANY)
    dma = pltpu.SemaphoreType.DMA
    hands = (2, size - 1, PIECES)
    outs = pl.pallas_call(
        functools.partial(front_kernel, size),
        out_shape=[
            jax.ShapeDtypeStruct((size, own_rows, model_width), low_type),
            jax.ShapeDtypeStruct((size, own_rows, width), wide_type),
            jax.ShapeDtypeStruct((model_width, width), low_type),
            jax.ShapeDtypeStruct((output_shard.shape[0], model_width), low_type),
            jax.ShapeDtypeStruct((model_width, gate_shard.shape[1]), low_type),
            jax.ShapeDtypeStruct((8 * gain_shard.shape[0], gain_shard.shape[1]), low_type),
        ],
        in_specs=[anywhere] * 5,
        out_specs=[anywhere] * 6,
        scratch_shapes=[
            pltpu.VMEM((size, own_rows, model_width), low_type),
            pltpu.VMEM((model_width, width), low_type),
            pltpu.VMEM((size, own_rows, width), wide_type),
            dma((5,)),
            dma((3, size)),
            dma(hands),
            dma(hands),
            dma((4, 7, 2)),
            dma((4, 7, 2)),
        ],
        compiler_params=pltpu.CompilerParams(
            collective_id=0, has_side_effects=True, vmem_limit_bytes=VMEM_BYTES
        ),
        cost_estimate=pl.CostEstimate(
            flops=2 * size * own_rows * model_width * width,
            bytes_accessed=32 << 20,
            transcendentals=0,
        ),
        name="front",
    )(tokens_here, attention_shard, output_shard, gate_shard, gain_shard)
    rows = size * own_rows
    return (
        outs[0].reshape(rows, model_width),
        outs[1].reshape(rows, width),
        *outs[2:],
    )


def middle_kernel(size, *refs):
    (
        attended_hbm,
        tokens_hbm,
        cotangent_hbm,
        attention_scale,
        feedforward_scale,
        output_hbm,
        gate_hbm,
        up_hbm,
        down_hbm,
        mlp_out,
        inner_out,
        mixed_cot_out,
        grad_gate_out,
        grad_up_out,
        branch_cot_out,
        block_out,
        grad_hidden_out,
        attention_gain_out,
        feedforward_gain_out,
        attended,
        tokens,
        cotangent,
        output_weight,
        gate_weight,
        up_weight,
        down_weight,
        everyone,
        gate_act,
        up_act,
        inner,
        hidden,
        branch,
        arrived,
        partial,
        total,
        load_sem,
        store_sem,
        sum_send,
        sum_recv,
        hand_send,
        hand_recv,
        shard_send,
        shard_recv,
    ) = refs
    me = lax.axis_index("tensor")
    last = size - 1
    chunk_rows, model_width = tokens.shape[1], tokens.shape[2]
    units = gate_weight.shape[1]
    half_rows = chunk_rows // HALVES
    all_rows = size * chunk_rows

    greet(((me < last, me + 1), (me > 0, me - 1)))
    first_loads = [
        pltpu.make_async_copy(source, target, load_sem.at[place])
        for place, (source, target) in enumerate(
            (
                (attended_hbm, attended),
                (output_hbm, output_weight),
                (tokens_hbm, tokens),
                (cotangent_hbm, cotangent),
                (gate_hbm, gate_weight),
                (up_hbm, up_weight.at[pl.ds(0, up_hbm.shape[0]), :]),
                (down_hbm, down_weight.at[:, pl.ds(0, down_hbm.shape[1])]),
            )
        )
    ]
    for copy in first_loads:
        copy.start()
    up_flow = ShardGather(
        own_halves(up_hbm),
        row_halves(up_weight, up_hbm.shape[0]),
        shard_send.at[0],
        shard_recv.at[0],
    )
    down_flow = ShardGather(
        own_halves(down_hbm),
        column_halves(down_weight, down_hbm.shape[1]),
        shard_send.at[1],
        shard_recv.at[1],
    )
    pl.semaphore_wait(
        pltpu.get_barrier_semaphore(), 3 + jnp.minimum(me, 1) + jnp.minimum(last - me, 1)
    )
    up_flow.start(2, 4, 1)
    down_flow.start(1)

    def turns(tick, half):
        if (tick, half) == (2, 1):
            up_flow.arrive(2, (0,))
            up_flow.arrive(4, (0,))
        elif (tick, half) == (3, 0):
            up_flow.arrive(2, (1,))
            up_flow.arrive(4, (1,))
            down_flow.start(2, 4)
        elif (tick, half) == (4, 1):
            up_flow.arrive(6)
        elif (tick, half) == (5, 0):
            down_flow.arrive(2, (0,))
            down_flow.arrive(4, (0,))
        elif (tick, half) == (6, 0):
            down_flow.arrive(2, (1,))
            down_flow.arrive(4, (1,))
        elif (tick, half) == (7, 0):
            down_flow.arrive(6)

    attention_gain_out[...] = jnp.zeros_like(attention_gain_out)
    feedforward_gain_out[...] = jnp.zeros_like(feedforward_gain_out)

    def half_span(half):
        return pl.ds(half * half_rows, half_rows)

    def strips(half, body):
        def step(index, carry):
            body(
                pl.ds(pl.multiple_of(half * half_rows + index * STRIP, STRIP), STRIP),
                pl.ds(pl.multiple_of(index * STRIP, STRIP), STRIP),
            )
            return carry

        lax.fori_loop(0, half_rows // STRIP, step, 0)

    def sum_copy(chunk, step, half, way, dest):
        return pltpu.make_async_remote_copy(
            src_ref=partial.at[chunk, dest, half_span(half)],
            dst_ref=arrived.at[way, chunk, step - 1, half_span(half)],
            send_sem=sum_send.at[way, chunk, step - 1, half],
            recv_sem=sum_recv.at[way, chunk, step - 1, half],
            device_id={"tensor": me + 1 - 2 * way},
            device_id_type=pl.DeviceIdType.MESH,
        )

    def hand_copy(chunk, hop, half, way, origin):
        rows = everyone.at[origin, chunk, half_span(half)]
        return pltpu.make_async_remote_copy(
            src_ref=rows,
            dst_ref=rows,
            send_sem=hand_send.at[way, chunk, hop - 1, half],
            recv_sem=hand_recv.at[way, chunk, hop - 1, half],
            device_id={"tensor": me + 1 - 2 * way},
            device_id_type=pl.DeviceIdType.MESH,
        )

    def away(way):
        return me if way == 0 else last - me

    def sum_step(chunk, step, half):
        for way in range(2):
            distance = away(way)

            @pl.when(distance <= step - 1)
            def _():
                dest = me + size - step if way == 0 else me - size + step
                if step > 1:

                    @pl.when(distance >= 1)
                    def _():
                        sum_copy(chunk, step - 1, half, way, dest).wait_recv()

                        def add(rows, _):
                            partial[chunk, dest, rows] = low(
                                wide(partial[chunk, dest, rows])
                                + wide(arrived[way, chunk, step - 2, rows])
                            )

                        strips(half, add)

                sum_copy(chunk, step, half, way, dest).start()

    def sum_end(chunk, half):
        def begin(rows, here):
            total[here] = wide(partial[chunk, me, rows])

        strips(half, begin)
        for way in range(2):

            @pl.when(away(way) >= 1)
            def _():
                sum_copy(chunk, size - 1, half, way, me).wait_recv()

                def add(rows, here):
                    total[here] = total[here] + wide(arrived[way, chunk, size - 2, rows])

                strips(half, add)

    def sum_sent(chunk):
        for step in range(1, size):
            for way in range(2):

                @pl.when(away(way) <= step - 1)
                def _():
                    for half in range(HALVES):
                        sum_copy(chunk, step, half, way, 0).wait_send()

    def hand_first(chunk, half):
        for way in range(2):

            @pl.when(away(1 - way) >= 1)
            def _():
                hand_copy(chunk, 1, half, way, me).start()

    def hand_on(chunk, hop, half):
        for way in range(2):

            @pl.when(away(way) >= hop)
            def _():
                origin = me - hop if way == 0 else me + hop
                hand_copy(chunk, hop, half, way, origin).wait_recv()
                if hop < size - 1:

                    @pl.when(away(1 - way) >= 1)
                    def _():
                        hand_copy(chunk, hop + 1, half, way, origin).start()

    def hand_sent(chunk):
        for hop in range(1, size):
            for way in range(2):

                @pl.when(jnp.logical_and(away(way) >= hop - 1, away(1 - way) >= 1))
                def _():
                    for half in range(HALVES):
                        hand_copy(chunk, hop, half, way, 0).wait_send()

    def inverse_rms(values):
        return lax.rsqrt(jnp.mean(values * values, -1, keepdims=True) + EPS)

    def fold(values):
        return values[:8] + values[8:]

    def own_rows(chunk, stage, half):
        def after_branch(rows, here):
            value = total[here]
            branch[chunk, rows] = value
            state = wide(tokens[chunk, rows]) + value * inverse_rms(value) * attention_scale[...]
            hidden[chunk, rows] = state
            everyone[me, chunk, rows] = low(state)

        def after_mixed(rows, here):
            value = total[here]
            inverse = inverse_rms(value)
            normalized = value * inverse
            hidden[chunk, rows] = hidden[chunk, rows] + normalized * feedforward_scale[...]
            grad = wide(cotangent[chunk, rows])
            feedforward_gain_out[...] += fold(grad * normalized)
            everyone[me, chunk, rows] = low(
                norm_backward(grad, normalized, inverse, feedforward_scale[...])
            )

        def after_gradient(rows, here):
            grad = total[here] + wide(cotangent[chunk, rows])
            value = branch[chunk, rows]
            inverse = inverse_rms(value)
            normalized = value * inverse
            branch[chunk, rows] = grad
            attention_gain_out[...] += fold(grad * normalized)
            everyone[me, chunk, rows] = low(
                norm_backward(grad, normalized, inverse, attention_scale[...])
            )

        strips(half, (after_branch, after_mixed, after_gradient)[stage])

    def gathered(chunk):
        return everyone[:, chunk].reshape(all_rows, model_width)

    def tiles(first, end, body):
        def step(index, carry):
            body(pl.ds(pl.multiple_of(index * TILE, TILE), TILE))
            return carry

        lax.fori_loop(first, end, step, 0)

    def store(kind, chunk):
        source, target = (
            (everyone.at[:, chunk], mlp_out.at[chunk]),
            (inner, inner_out.at[chunk]),
            (everyone.at[:, chunk], mixed_cot_out.at[chunk]),
            (gate_act.at[chunk], grad_gate_out.at[chunk]),
            (up_act.at[chunk], grad_up_out.at[chunk]),
            (everyone.at[:, chunk], branch_cot_out.at[:, chunk]),
            (hidden.at[chunk], block_out.at[chunk]),
            (branch.at[chunk], grad_hidden_out.at[chunk]),
        )[kind]
        return pltpu.make_async_copy(source, target, store_sem.at[kind, chunk])

    def put_partial(chunk, columns, values):
        partial[chunk, :, :, columns] = low(values).reshape(size, chunk_rows, TILE)

    def branch_terms(chunk):
        def tile(columns):
            rows = attended[:, chunk].reshape(all_rows, attended.shape[-1])
            put_partial(
                chunk,
                columns,
                jnp.dot(rows, output_weight[:, columns], preferred_element_type=jnp.float32),
            )

        tiles(0, model_width // TILE, tile)

    def gate_tile(chunk):
        def tile(columns):
            rows = gathered(chunk)
            gate = jnp.dot(rows, gate_weight[:, columns], preferred_element_type=jnp.float32)
            up = jnp.dot(rows, up_weight[:, columns], preferred_element_type=jnp.float32)
            gate_act[chunk, :, columns] = low(gate)
            up_act[chunk, :, columns] = low(up)
            inner[:, columns] = low(gate * jax.nn.sigmoid(gate) * up)

        return tile

    def down_tile(chunk):
        def tile(columns):
            put_partial(
                chunk,
                columns,
                jnp.dot(inner[...], down_weight[:, columns], preferred_element_type=jnp.float32),
            )

        return tile

    def grad_inner_tile(chunk):
        def tile(columns):
            grad = rows_product(gathered(chunk), down_weight[columns, :])
            gate = wide(gate_act[chunk, :, columns])
            up = wide(up_act[chunk, :, columns])
            sigmoid = jax.nn.sigmoid(gate)
            gate_act[chunk, :, columns] = low(
                grad * up * sigmoid * (1.0 + gate * (1.0 - sigmoid))
            )
            up_act[chunk, :, columns] = low(grad * gate * sigmoid)

        return tile

    def grad_input_tile(chunk):
        def tile(columns):
            put_partial(
                chunk,
                columns,
                rows_product(gate_act[chunk], gate_weight[columns, :])
                + rows_product(up_act[chunk], up_weight[columns, :]),
            )

        return tile

    unit_tiles, width_tiles = units // TILE, model_width // TILE

    def forward_piece(chunk, piece):
        if piece == 0:
            if chunk == 0:
                for mask in (1, 3, 5, 7):
                    up_flow.arrive(mask)
                for copy in first_loads[4:]:
                    copy.wait()
            store(0, chunk).start()
            tiles(0, unit_tiles // 2, gate_tile(chunk))
        elif piece == 1:
            tiles(unit_tiles // 2, unit_tiles, gate_tile(chunk))
            store(1, chunk).start()
            sum_sent(chunk)
            hand_sent(chunk)
        else:
            if chunk == 0:
                for mask in (1, 3, 5, 7):
                    down_flow.arrive(mask)
            tiles(0, width_tiles, down_tile(chunk))
            store(0, chunk).wait()
            store(1, chunk).wait()

    def backward_piece(chunk, piece):
        if piece == 0:
            store(2, chunk).start()
            store(6, chunk).start()
            tiles(0, unit_tiles, grad_inner_tile(chunk))
            store(3, chunk).start()
            store(4, chunk).start()
        elif piece == 1:
            sum_sent(chunk)
            hand_sent(chunk)
            tiles(0, width_tiles // 2, grad_input_tile(chunk))
        else:
            tiles(width_tiles // 2, width_tiles, grad_input_tile(chunk))
            store(2, chunk).wait()

    def end_piece(chunk, piece):
        if piece == 0:
            store(5, chunk).start()
            store(7, chunk).start()

    first_loads[0].wait()
    first_loads[1].wait()
    branch_terms(0)
    first_loads[2].wait()
    first_loads[3].wait()
    bases = {
        (chunk, stage): (CHUNKS * stage + chunk) * size
        for stage in range(3)
        for chunk in range(CHUNKS)
    }
    ticks = max(bases.values()) + 2 * size
    for tick in range(1, ticks + 1):
        for half in range(HALVES):
            for (chunk, stage), base in bases.items():
                at = tick - base
                if size < at < 2 * size:
                    hand_on(chunk, at - size, half)
            for (chunk, stage), base in bases.items():
                at = tick - base
                if 1 <= at < size:
                    sum_step(chunk, at, half)
                elif at == size:
                    sum_end(chunk, half)
                    own_rows(chunk, stage, half)
                    hand_first(chunk, half)
            turns(tick, half)
            if tick == 1 and half == 1:
                branch_terms(1)
            for (chunk, stage), base in bases.items():
                piece = (tick - base - 2 * size + 1) * HALVES + half - 1
                if 0 <= piece < 3:
                    (forward_piece, backward_piece, end_piece)[stage](chunk, piece)
    up_flow.sent()
    down_flow.sent()
    for chunk in range(CHUNKS):
        sum_sent(chunk)
        hand_sent(chunk)
        for kind in range(3, 8):
            store(kind, chunk).wait()


def middle(
    attended,
    tokens_here,
    cotangent_here,
    attention_scale,
    feedforward_scale,
    output_full,
    gate_full,
    up_shard,
    down_shard,
):
    size = lax.axis_size("tensor")
    own_rows, model_width = tokens_here.shape
    chunk_rows = own_rows // CHUNKS
    all_rows = size * chunk_rows
    half_rows = chunk_rows // HALVES
    heads_width = attended.shape[1]
    units = gate_full.shape[1]
    chunked = (CHUNKS, chunk_rows, model_width)
    lined = (CHUNKS, size, chunk_rows, model_width)
    low_type, wide_type = jnp.bfloat16, jnp.float32

    def shape(dims, kind=low_type):
        return jax.ShapeDtypeStruct(dims, kind)

    anywhere = pl.BlockSpec(memory_space=pl.ANY)
    inside = pl.BlockSpec(memory_space=pltpu.VMEM)
    dma = pltpu.SemaphoreType.DMA
    flops = 2 * CHUNKS * all_rows * model_width * (2 * heads_width + 6 * units)
    outs = pl.pallas_call(
        functools.partial(middle_kernel, size),
        out_shape=[
            shape(lined),
            shape((CHUNKS, all_rows, units)),
            shape(lined),
            shape((CHUNKS, all_rows, units)),
            shape((CHUNKS, all_rows, units)),
            shape((size, CHUNKS, chunk_rows, model_width)),
            shape(chunked, wide_type),
            shape(chunked, wide_type),
            shape((8, model_width), wide_type),
            shape((8, model_width), wide_type),
        ],
        in_specs=[anywhere] * 3 + [inside] * 2 + [anywhere] * 4,
        out_specs=[anywhere] * 8 + [inside] * 2,
        scratch_shapes=[
            pltpu.VMEM((size, CHUNKS, chunk_rows, heads_width), low_type),
            pltpu.VMEM(chunked, low_type),
            pltpu.VMEM(chunked, low_type),
            pltpu.VMEM((heads_width, model_width), low_type),
            pltpu.VMEM((model_width, units), low_type),
            pltpu.VMEM((model_width, units), low_type),
            pltpu.VMEM((units, model_width), low_type),
            pltpu.VMEM((size, CHUNKS, chunk_rows, model_width), low_type),
            pltpu.VMEM((CHUNKS, all_rows, units), low_type),
            pltpu.VMEM((CHUNKS, all_rows, units), low_type),
            pltpu.VMEM((all_rows, units), low_type),
            pltpu.VMEM(chunked, wide_type),
            pltpu.VMEM(chunked, wide_type),
            pltpu.VMEM((2, CHUNKS, size - 1, chunk_rows, model_width), low_type),
            pltpu.VMEM(lined, low_type),
            pltpu.VMEM((half_rows, model_width), wide_type),
            dma((7,)),
            dma((8, CHUNKS)),
            dma((2, CHUNKS, size - 1, HALVES)),
            dma((2, CHUNKS, size - 1, HALVES)),
            dma((2, CHUNKS, size - 1, HALVES)),
            dma((2, CHUNKS, size - 1, HALVES)),
            dma((2, 7, 2)),
            dma((2, 7, 2)),
        ],
        compiler_params=pltpu.CompilerParams(
            collective_id=1, has_side_effects=True, vmem_limit_bytes=VMEM_BYTES
        ),
        cost_estimate=pl.CostEstimate(
            flops=flops, bytes_accessed=64 << 20, transcendentals=0
        ),
        name="middle",
    )(
        attended.reshape(size, CHUNKS, chunk_rows, heads_width),
        tokens_here.reshape(chunked),
        cotangent_here.reshape(chunked),
        attention_scale.reshape(1, model_width),
        feedforward_scale.reshape(1, model_width),
        output_full,
        gate_full,
        up_shard,
        down_shard,
    )
    mlp_all, inner, mixed_cot, grad_gate, grad_up, branch_cot, block, grad_hidden = outs[:8]
    rows = CHUNKS * all_rows
    return (
        mlp_all.reshape(rows, model_width),
        inner.reshape(rows, units),
        mixed_cot.reshape(rows, model_width),
        grad_gate.reshape(rows, units),
        grad_up.reshape(rows, units),
        branch_cot.reshape(rows, model_width),
        block.reshape(own_rows, model_width),
        grad_hidden.reshape(own_rows, model_width),
        jnp.sum(outs[8], 0),
        jnp.sum(outs[9], 0),
    )


def local(
    tokens,
    positions,
    cotangent,
    query_weight,
    key_weight,
    value_weight,
    output_weight,
    gate_weight,
    up_weight,
    down_weight,
    query_gain,
    key_gain,
    attention_gain,
    feedforward_gain,
):
    model_width = tokens.shape[1]
    data_size = lax.axis_size("dp")
    data_index = lax.axis_index("dp")
    head_size = query_gain.shape[0] * data_size
    local_heads = query_gain.shape[1]
    local_width = query_weight.shape[1]
    local_units = gate_weight.shape[1]
    block_rows = min(512, LENGTH)
    order = mask_order(data_size)
    place_of = jnp.array([order.index(mask) for mask in range(data_size)], jnp.int32)
    width = model_width // data_size
    half_width = model_width // 2

    def shuffle(array_in):
        return jnp.concatenate(
            [
                lax.dynamic_slice_in_dim(array_in, (data_index ^ mask) * width, width, -1)
                for mask in order
            ],
            -1,
        )

    def unshuffle(array_in):
        return jnp.concatenate(
            [
                lax.dynamic_slice_in_dim(
                    array_in, place_of[data_index ^ block] * width, width, -1
                )
                for block in range(data_size)
            ],
            -1,
        )

    small = jnp.concatenate(
        [query_gain.reshape(-1), key_gain.reshape(-1), attention_gain, feedforward_gain]
    )
    small = gather_high(small[None], 0)
    small_count = small.size
    small = jnp.pad(small.reshape(-1), (0, 32 * 128 - small_count)).reshape(32, 128)
    tokens_here = shuffle(tokens)
    rows_all, projected, attention_full, output_full, gate_full, small_all = front(
        tokens_here,
        gather_high(jnp.concatenate([query_weight, key_weight, value_weight], 1), 0),
        gather_high(output_weight, 1),
        gather_high(gate_weight, 0),
        small,
    )
    small_all = small_all.reshape(8, -1)[:, :small_count].reshape(data_size, -1)
    gain_count = query_gain.size
    natural = jnp.concatenate(
        [
            lax.dynamic_slice_in_dim(
                small_all[:, : 2 * gain_count], place_of[data_index ^ block], 1, 0
            )
            for block in range(data_size)
        ],
        0,
    )
    query_gain_full = natural[:, :gain_count].reshape(head_size, local_heads)
    key_gain_full = natural[:, gain_count:].reshape(head_size, local_heads)
    attention_scale = wide(small_all[:, 2 * gain_count : 2 * gain_count + width].reshape(-1))
    feedforward_scale = wide(small_all[:, 2 * gain_count + width :].reshape(-1))
    query_scale = channel_scale(query_gain_full)
    key_scale = channel_scale(key_gain_full)
    group_rows = rows_all.shape[0]
    seq_count = group_rows // LENGTH

    def per_sequence(array_in):
        return array_in.reshape((seq_count, LENGTH) + array_in.shape[1:])

    queries = projected[:, :local_width]
    key_rows = projected[:, local_width : 2 * local_width]
    squares = lax.psum(
        jnp.stack([jnp.sum(queries * queries, -1), jnp.sum(key_rows * key_rows, -1)]), "tensor"
    )
    inverse_q = lax.rsqrt(squares[0] / model_width + EPS)[:, None]
    inverse_k = lax.rsqrt(squares[1] / model_width + EPS)[:, None]
    query_hat = queries * inverse_q
    key_hat = key_rows * inverse_k
    cosine_table, sine_table = rope_tables(positions, head_size)
    query_rot = low(
        rotate(
            (query_hat * query_scale).reshape(group_rows, local_heads, head_size),
            cosine_table,
            sine_table,
        )
    )
    key_rot = low(
        rotate(
            (key_hat * key_scale).reshape(group_rows, local_heads, head_size),
            cosine_table,
            sine_table,
        )
    )
    value_rows = low(projected[:, 2 * local_width :]).reshape(group_rows, local_heads, head_size)
    attended, row_lse = lax.map(
        lambda sequence_item: attend_forward(
            sequence_item[0], sequence_item[1], sequence_item[2], block_rows
        ),
        (per_sequence(query_rot), per_sequence(key_rot), per_sequence(value_rows)),
    )
    attended = low(attended.reshape(group_rows, -1))
    (
        mlp_all,
        inner_act,
        mixed_cot,
        grad_gate_act,
        grad_up_act,
        branch_cot,
        block_here,
        grad_hidden,
        partial_attention_gain,
        partial_feedforward_gain,
    ) = middle(
        attended,
        tokens_here,
        shuffle(cotangent),
        attention_scale,
        feedforward_scale,
        output_full,
        gate_full,
        gather_high(up_weight, 0),
        gather_high(down_weight, 1),
    )
    block_output = unshuffle(block_here)

    def weight_grad(rows_in, grad_in, axis):
        if axis == 0:
            near, far = rows_in[:, :half_width], rows_in[:, half_width:]
            return scatter_shards(
                jnp.einsum("td,tf->df", near, grad_in, preferred_element_type=jnp.float32),
                jnp.einsum("td,tf->df", far, grad_in, preferred_element_type=jnp.float32),
                0,
            )
        near, far = grad_in[:, :half_width], grad_in[:, half_width:]
        return scatter_shards(
            jnp.einsum("tf,td->fd", rows_in, near, preferred_element_type=jnp.float32),
            jnp.einsum("tf,td->fd", rows_in, far, preferred_element_type=jnp.float32),
            1,
        )

    grad_down = weight_grad(inner_act, mixed_cot, 1)
    grad_gate = weight_grad(mlp_all, grad_gate_act, 0)
    grad_up = weight_grad(mlp_all, grad_up_act, 0)
    grad_output_proj = weight_grad(attended, branch_cot, 1)
    grad_attended = low(
        jnp.einsum("td,cd->tc", branch_cot, output_full, preferred_element_type=jnp.float32)
    )
    grad_query_rot, grad_key_rot, grad_value_rows = lax.map(
        lambda sequence_item: attend_backward(
            sequence_item[0],
            sequence_item[1],
            sequence_item[2],
            sequence_item[3],
            sequence_item[4],
            block_rows,
        ),
        (
            per_sequence(query_rot),
            per_sequence(key_rot),
            per_sequence(value_rows),
            per_sequence(grad_attended.reshape(group_rows, local_heads, head_size)),
            row_lse,
        ),
    )
    grad_query_rot = wide(low(grad_query_rot.reshape(group_rows, local_heads, head_size)))
    grad_key_rot = wide(low(grad_key_rot.reshape(group_rows, local_heads, head_size)))
    grad_values_low = low(grad_value_rows.reshape(group_rows, -1))
    grad_query_norm = unrotate(grad_query_rot, cosine_table, sine_table).reshape(group_rows, -1)
    grad_key_norm = unrotate(grad_key_rot, cosine_table, sine_table).reshape(group_rows, -1)
    grad_query_scale = jnp.sum(grad_query_norm * query_hat, 0)
    grad_key_scale = jnp.sum(grad_key_norm * key_hat, 0)
    scaled_query = grad_query_norm * query_scale
    scaled_key = grad_key_norm * key_scale
    inner_query, inner_key, total_attention_gain, total_feedforward_gain = lax.psum(
        (
            jnp.sum(scaled_query * query_hat, -1),
            jnp.sum(scaled_key * key_hat, -1),
            partial_attention_gain,
            partial_feedforward_gain,
        ),
        "tensor",
    )
    grad_queries = low(
        inverse_q * (scaled_query - query_hat * inner_query[:, None] / model_width)
    )
    grad_keys = low(inverse_k * (scaled_key - key_hat * inner_key[:, None] / model_width))
    grad_projected = jnp.concatenate([grad_queries, grad_keys, grad_values_low], 1)
    grad_attention = weight_grad(rows_all, grad_projected, 0)
    input_part = jnp.einsum(
        "tc,dc->td", grad_projected, attention_full, preferred_element_type=jnp.float32
    )
    grad_tokens = unshuffle(grad_hidden + scatter_rows(input_part))
    query_gain_grad = grad_query_scale.reshape(local_heads, head_size).T
    key_gain_grad = grad_key_scale.reshape(local_heads, head_size).T
    gain_grads = jnp.concatenate(
        [
            query_gain_grad.reshape(data_size, -1),
            key_gain_grad.reshape(data_size, -1),
            unshuffle(total_attention_gain).reshape(data_size, width),
            unshuffle(total_feedforward_gain).reshape(data_size, width),
        ],
        1,
    )
    gain_shard = wide(
        lax.psum_scatter(gain_grads, "dp", scatter_dimension=0, tiled=True)
    ).reshape(-1)
    return (
        block_output,
        grad_tokens,
        grad_attention[:, :local_width],
        grad_attention[:, local_width : 2 * local_width],
        grad_attention[:, 2 * local_width :],
        grad_output_proj,
        grad_gate,
        grad_up,
        grad_down,
        gain_shard[:gain_count].reshape(query_gain.shape),
        gain_shard[gain_count : 2 * gain_count].reshape(key_gain.shape),
        gain_shard[2 * gain_count : 2 * gain_count + width],
        gain_shard[2 * gain_count + width :],
    )


def solution(mesh):
    return jax.shard_map(
        local,
        mesh=mesh,
        in_specs=(
            P(("dp", "tensor"), None),
            P("dp"),
            P(("dp", "tensor"), None),
            P("dp", "tensor"),
            P("dp", "tensor"),
            P("dp", "tensor"),
            P("tensor", "dp"),
            P("dp", "tensor"),
            P("dp", "tensor"),
            P("tensor", "dp"),
            P("dp", "tensor"),
            P("dp", "tensor"),
            P("dp"),
            P("dp"),
        ),
        out_specs=(
            P(("dp", "tensor"), None),
            P(("dp", "tensor"), None),
            P("dp", "tensor"),
            P("dp", "tensor"),
            P("dp", "tensor"),
            P("tensor", "dp"),
            P("dp", "tensor"),
            P("dp", "tensor"),
            P("tensor", "dp"),
            P("dp", "tensor"),
            P("dp", "tensor"),
            P("dp"),
            P("dp"),
        ),
        check_vma=False,
    )
```

```python
import functools

import jax
import jax.numpy as jnp
from jax import lax
from jax.experimental import pallas as pl
from jax.experimental.pallas import tpu as pltpu
from jax.sharding import PartitionSpec as P

LENGTH = 1024


EPS = 1e-06
THETA = 500000.0
MASKED = -1e30
VMEM_BYTES = 64 * 1024 * 1024 - 128 * 1024


def rope_tables(positions, head_size):
    half_size = head_size // 2
    frequency = THETA ** (-(jnp.arange(half_size, dtype=jnp.float32) * 2.0 / head_size))
    angles = positions.astype(jnp.float32)[:, None] * frequency[None, :]
    return (jnp.cos(angles)[:, None, :], jnp.sin(angles)[:, None, :])


def rotate(values, cosine_table, sine_table):
    half_size = values.shape[-1] // 2
    first_half = values[..., :half_size]
    second_half = values[..., half_size:]
    return jnp.concatenate(
        [
            first_half * cosine_table - second_half * sine_table,
            second_half * cosine_table + first_half * sine_table,
        ],
        -1,
    )


def unrotate(gradient, cosine_table, sine_table):
    half_size = gradient.shape[-1] // 2
    first_half = gradient[..., :half_size]
    second_half = gradient[..., half_size:]
    return jnp.concatenate(
        [
            first_half * cosine_table + second_half * sine_table,
            second_half * cosine_table - first_half * sine_table,
        ],
        -1,
    )


def channel_scale(gain_block):
    return gain_block.astype(jnp.float32).T.reshape(-1)


def masked_scores(queries, key_rows, first_row, block_rows):
    last_row = first_row + block_rows
    score_scale = queries.shape[-1] ** (-0.5)
    scores = (
        jnp.einsum(
            "qhc,khc->hqk",
            queries[first_row:last_row],
            key_rows[:last_row],
            preferred_element_type=jnp.float32,
        )
        * score_scale
    )
    row_index = first_row + lax.broadcasted_iota(jnp.int32, (block_rows, last_row), 0)
    col_index = lax.broadcasted_iota(jnp.int32, (block_rows, last_row), 1)
    return jnp.where((col_index <= row_index)[None], scores, MASKED)


def attend_forward(queries, key_rows, value_rows, block_rows):
    length = queries.shape[0]
    output_list = []
    lse_list = []
    for first_row in range(0, length, block_rows):
        last_row = first_row + block_rows
        scores = masked_scores(queries, key_rows, first_row, block_rows)
        row_max = jnp.max(scores, -1, keepdims=True)
        exponent = jnp.exp(scores - row_max)
        row_total = jnp.sum(exponent, -1, keepdims=True)
        low_probs = (exponent / row_total).astype(jnp.bfloat16)
        output_list.append(
            jnp.einsum(
                "hqk,khc->qhc", low_probs, value_rows[:last_row], preferred_element_type=jnp.float32
            )
        )
        lse_list.append(row_max + jnp.log(row_total))
    return (jnp.concatenate(output_list, 0), jnp.concatenate(lse_list, 1))


def attend_backward(queries, key_rows, value_rows, grad_out, row_lse, block_rows):
    length = queries.shape[0]
    score_scale = queries.shape[-1] ** (-0.5)
    grad_keys = jnp.zeros(key_rows.shape, jnp.float32)
    grad_values = jnp.zeros(value_rows.shape, jnp.float32)
    query_list = []
    for first_row in range(0, length, block_rows):
        last_row = first_row + block_rows
        padding = ((0, length - last_row), (0, 0), (0, 0))
        scores = masked_scores(queries, key_rows, first_row, block_rows)
        probabilities = jnp.exp(scores - row_lse[:, first_row:last_row])
        low_probs = probabilities.astype(jnp.bfloat16)
        grad_block = grad_out[first_row:last_row]
        grad_values = grad_values + jnp.pad(
            jnp.einsum("hqk,qhc->khc", low_probs, grad_block, preferred_element_type=jnp.float32),
            padding,
        )
        grad_probs = jnp.einsum(
            "qhc,khc->hqk", grad_block, value_rows[:last_row], preferred_element_type=jnp.float32
        )
        row_delta = jnp.sum(grad_probs * probabilities, -1, keepdims=True)
        grad_scores = (probabilities * (grad_probs - row_delta)).astype(jnp.bfloat16)
        query_list.append(
            jnp.einsum(
                "hqk,khc->qhc", grad_scores, key_rows[:last_row], preferred_element_type=jnp.float32
            )
            * score_scale
        )
        grad_keys = grad_keys + jnp.pad(
            jnp.einsum(
                "hqk,qhc->khc",
                grad_scores,
                queries[first_row:last_row],
                preferred_element_type=jnp.float32,
            )
            * score_scale,
            padding,
        )
    return (jnp.concatenate(query_list, 0), grad_keys, grad_values)


def norm_backward(grad_in, normalized, inverse_rms, gain_values):
    scaled = grad_in * gain_values
    return inverse_rms * (scaled - normalized * jnp.mean(scaled * normalized, -1, keepdims=True))


def bits_of(size):
    return size.bit_length() - 1


def mask_order(size):
    return [
        low_bits + 8 * high_bits
        for low_bits in (0, 2, 4, 6, 1, 3, 5, 7)
        for high_bits in range(size // 8)
    ]


def swap(array_in, mask):
    size = lax.axis_size("dp")
    return lax.ppermute(array_in, "dp", [(index, index ^ mask) for index in range(size)])


def gather_high(shard, axis):
    for bit in range(3, bits_of(lax.axis_size("dp"))):
        shard = jnp.concatenate([shard, swap(shard, 1 << bit)], axis)
    return shard


def scatter_high(total, axis):
    for bit in reversed(range(3, bits_of(lax.axis_size("dp")))):
        kept, sent = jnp.split(total, 2, axis)
        total = low(wide(kept) + wide(swap(low(sent), 1 << bit)))
    return total


def low(array_in):
    return array_in.astype(jnp.bfloat16)


def wide(array_in):
    return array_in.astype(jnp.float32)


def rows_product(left, right):
    return lax.dot_general(
        left, right, (((1,), (1,)), ((), ())), preferred_element_type=jnp.float32
    )


TILE = 256
STRIP = 16
CHUNKS = 2
HALVES = 2
PIECES = 4


def shard_peer(mask):
    index = lax.axis_index("dp")
    return index + mask - 2 * mask * ((index // mask) % 2)


ROUTE = {1: (1, 1), 2: (2, 2), 3: (1, 1), 4: (4, 4), 5: (1, 1), 6: (4, 2), 7: (1, 1)}
PLACES = {mask: place for place, mask in enumerate((0, 2, 4, 6, 1, 3, 5, 7))}


class ShardGather:
    def __init__(self, own, target, send_sem, recv_sem):
        self.own, self.target, self.send_sem, self.recv_sem = own, target, send_sem, recv_sem

    def copy(self, mask, half):
        route = ROUTE[mask][half]
        before = mask ^ route
        return pltpu.make_async_remote_copy(
            src_ref=self.target(PLACES[before], half) if before else self.own(half),
            dst_ref=self.target(PLACES[mask], half),
            send_sem=self.send_sem.at[mask - 1, half],
            recv_sem=self.recv_sem.at[mask - 1, half],
            device_id={"dp": shard_peer(route)},
            device_id_type=pl.DeviceIdType.MESH,
        )

    def start(self, *masks):
        for half in range(2):
            for mask in masks:
                self.copy(mask, half).start()

    def arrive(self, mask, halves=(0, 1)):
        for half in halves:
            self.copy(mask, half).wait_recv()
            for after, route in ROUTE.items():
                if after != mask and after ^ route[half] == mask:
                    self.copy(after, half).start()

    def sent(self):
        for mask in ROUTE:
            for half in range(2):
                self.copy(mask, half).wait_send()


def row_halves(buffer, height):
    def target(place, half):
        return buffer.at[pl.ds(place * height + half * (height // 2), height // 2), :]

    return target


def column_halves(buffer, width):
    height = buffer.shape[0] // 2

    def target(place, half):
        return buffer.at[pl.ds(half * height, height), pl.ds(place * width, width)]

    return target


def own_halves(shard):
    height = shard.shape[0] // 2
    return lambda half: shard.at[pl.ds(half * height, height), :]


def greet(line_devices):
    barrier = pltpu.get_barrier_semaphore()
    for mask in (1, 2, 4):
        pl.semaphore_signal(
            barrier,
            inc=1,
            device_id={"dp": shard_peer(mask)},
            device_id_type=pl.DeviceIdType.MESH,
        )
    for there, index in line_devices:

        @pl.when(there)
        def _():
            pl.semaphore_signal(
                barrier,
                inc=1,
                device_id={"tensor": index},
                device_id_type=pl.DeviceIdType.MESH,
            )


def front_kernel(
    size,
    tokens_hbm,
    attention_hbm,
    output_hbm,
    gate_hbm,
    gain_hbm,
    rows_out,
    projected_out,
    attention_out,
    output_out,
    gate_out,
    gain_out,
    rows,
    weight,
    projected,
    load_sem,
    store_sem,
    hand_send,
    hand_recv,
    shard_send,
    shard_recv,
):
    me = lax.axis_index("tensor")
    last = size - 1
    piece_rows = rows.shape[1] // PIECES
    greet(((me < last, me + 1), (me > 0, me - 1)))
    loads = [
        pltpu.make_async_copy(source, target, load_sem.at[place])
        for place, (source, target) in enumerate(
            (
                (tokens_hbm, rows.at[me]),
                (attention_hbm, weight.at[pl.ds(0, attention_hbm.shape[0]), :]),
                (output_hbm, output_out.at[:, pl.ds(0, output_hbm.shape[1])]),
                (gate_hbm, gate_out.at[pl.ds(0, gate_hbm.shape[0]), :]),
                (gain_hbm, gain_out.at[pl.ds(0, gain_hbm.shape[0]), :]),
            )
        )
    ]
    for copy in loads:
        copy.start()
    attention_flow, output_flow, gate_flow, gain_flow = (
        ShardGather(own_halves(shard), target, shard_send.at[kind], shard_recv.at[kind])
        for kind, (shard, target) in enumerate(
            (
                (attention_hbm, row_halves(weight, attention_hbm.shape[0])),
                (output_hbm, column_halves(output_out, output_hbm.shape[1])),
                (gate_hbm, row_halves(gate_out, gate_hbm.shape[0])),
                (gain_hbm, row_halves(gain_out, gain_hbm.shape[0])),
            )
        )
    )
    pl.semaphore_wait(
        pltpu.get_barrier_semaphore(), 3 + jnp.minimum(me, 1) + jnp.minimum(last - me, 1)
    )

    def away(way):
        return me if way == 0 else last - me

    def hand_copy(hop, piece, way, origin):
        span = pl.ds(piece * piece_rows, piece_rows)
        return pltpu.make_async_remote_copy(
            src_ref=tokens_hbm.at[span] if hop == 1 else rows.at[origin, span],
            dst_ref=rows.at[origin, span],
            send_sem=hand_send.at[way, hop - 1, piece],
            recv_sem=hand_recv.at[way, hop - 1, piece],
            device_id={"tensor": me + 1 - 2 * way},
            device_id_type=pl.DeviceIdType.MESH,
        )

    for piece in range(PIECES):
        for way in range(2):

            @pl.when(away(1 - way) >= 1)
            def _():
                hand_copy(1, piece, way, me).start()

        if piece == 0:
            attention_flow.start(2, 4, 1)
            gain_flow.start(2, 4, 1)

    def hand_on(hop, piece):
        for way in range(2):

            @pl.when(away(way) >= hop)
            def _():
                origin = me - hop if way == 0 else me + hop
                hand_copy(hop, piece, way, origin).wait_recv()
                if hop < size - 1:

                    @pl.when(away(1 - way) >= 1)
                    def _():
                        hand_copy(hop + 1, piece, way, origin).start()

    def row_store(origin):
        return pltpu.make_async_copy(rows.at[origin], rows_out.at[origin], store_sem.at[0, origin])

    def projected_store(origin):
        return pltpu.make_async_copy(
            projected.at[origin], projected_out.at[origin], store_sem.at[1, origin]
        )

    weight_store = pltpu.make_async_copy(weight, attention_out, store_sem.at[2, 0])

    def project(origin):
        def step(index, carry):
            columns = pl.ds(pl.multiple_of(index * TILE, TILE), TILE)
            projected[origin, :, columns] = jnp.dot(
                rows[origin], weight[:, columns], preferred_element_type=jnp.float32
            )
            return carry

        row_store(origin).start()
        lax.fori_loop(0, weight.shape[1] // TILE, step, 0)
        projected_store(origin).start()

    def project_from(hop, way):
        @pl.when(away(way) >= hop)
        def _():
            project(me - hop if way == 0 else me + hop)

    def turns(beat):
        if beat == 2:
            attention_flow.arrive(2, (0,))
            attention_flow.arrive(4, (0,))
        elif beat == 3:
            attention_flow.arrive(2, (1,))
            attention_flow.arrive(4, (1,))
            output_flow.start(2, 4, 1)
            gain_flow.arrive(2)
            gain_flow.arrive(4)
        elif beat == 5:
            attention_flow.arrive(6)
            gate_flow.start(2, 4, 1)
            gain_flow.arrive(6)
        elif beat == 6:
            output_flow.arrive(2)
            output_flow.arrive(4)
            for mask in (1, 3, 5, 7):
                attention_flow.arrive(mask)
            loads[0].wait()
            loads[1].wait()
            weight_store.start()
            project(me)
        elif beat == 7:
            project_from(1, 0)
        elif beat == 8:
            project_from(1, 1)
            output_flow.arrive(6)
        elif beat == 9:
            gate_flow.arrive(2, (0,))
            gate_flow.arrive(4, (0,))
        elif beat == 10:
            project_from(2, 0)
        elif beat == 11:
            project_from(2, 1)
            gate_flow.arrive(2, (1,))
            gate_flow.arrive(4, (1,))

    for beat in range(1, (size - 1) * PIECES + 1):
        hand_on((beat - 1) // PIECES + 1, (beat - 1) % PIECES)
        turns(beat)
    project_from(3, 0)
    project_from(3, 1)
    gate_flow.arrive(6)
    for flow in (output_flow, gate_flow, gain_flow):
        for mask in (1, 3, 5, 7):
            flow.arrive(mask)
    for hop in range(1, size):
        for way in range(2):

            @pl.when(jnp.logical_and(away(way) >= hop - 1, away(1 - way) >= 1))
            def _():
                for piece in range(PIECES):
                    hand_copy(hop, piece, way, 0).wait_send()

    for flow in (attention_flow, output_flow, gate_flow, gain_flow):
        flow.sent()
    for copy in loads[2:]:
        copy.wait()
    for origin in range(size):
        row_store(origin).wait()
        projected_store(origin).wait()
    weight_store.wait()


def front(tokens_here, attention_shard, output_shard, gate_shard, gain_shard):
    size = lax.axis_size("tensor")
    own_rows, model_width = tokens_here.shape
    width = attention_shard.shape[1]
    low_type, wide_type = jnp.bfloat16, jnp.float32
    anywhere = pl.BlockSpec(memory_space=pl.ANY)
    dma = pltpu.SemaphoreType.DMA
    hands = (2, size - 1, PIECES)
    outs = pl.pallas_call(
        functools.partial(front_kernel, size),
        out_shape=[
            jax.ShapeDtypeStruct((size, own_rows, model_width), low_type),
            jax.ShapeDtypeStruct((size, own_rows, width), wide_type),
            jax.ShapeDtypeStruct((model_width, width), low_type),
            jax.ShapeDtypeStruct((output_shard.shape[0], model_width), low_type),
            jax.ShapeDtypeStruct((model_width, gate_shard.shape[1]), low_type),
            jax.ShapeDtypeStruct((8 * gain_shard.shape[0], gain_shard.shape[1]), low_type),
        ],
        in_specs=[anywhere] * 5,
        out_specs=[anywhere] * 6,
        scratch_shapes=[
            pltpu.VMEM((size, own_rows, model_width), low_type),
            pltpu.VMEM((model_width, width), low_type),
            pltpu.VMEM((size, own_rows, width), wide_type),
            dma((5,)),
            dma((3, size)),
            dma(hands),
            dma(hands),
            dma((4, 7, 2)),
            dma((4, 7, 2)),
        ],
        compiler_params=pltpu.CompilerParams(
            collective_id=0, has_side_effects=True, vmem_limit_bytes=VMEM_BYTES
        ),
        cost_estimate=pl.CostEstimate(
            flops=2 * size * own_rows * model_width * width,
            bytes_accessed=32 << 20,
            transcendentals=0,
        ),
        name="front",
    )(tokens_here, attention_shard, output_shard, gate_shard, gain_shard)
    rows = size * own_rows
    return (
        outs[0].reshape(rows, model_width),
        outs[1].reshape(rows, width),
        *outs[2:],
    )


class ShardSum:
    def __init__(self, near, far, corner, final, send_sem, recv_sem):
        self.near, self.far, self.corner, self.final = near, far, corner, final
        self.send_sem, self.recv_sem = send_sem, recv_sem

    def remote(self, source, target, place, route):
        return pltpu.make_async_remote_copy(
            src_ref=source,
            dst_ref=target,
            send_sem=self.send_sem.at[place],
            recv_sem=self.recv_sem.at[place],
            device_id={"dp": shard_peer(route)},
            device_id_type=pl.DeviceIdType.MESH,
        )

    def core_copy(self, place):
        return self.remote(self.far(place), self.near(place), place, 1)

    def corner_copy(self, half):
        return self.remote(self.near(3, half), self.corner(half), 4 + half, (4, 2)[half])

    def final_copy(self, way, half):
        return self.remote(
            self.near(1 + way, half), self.final(way, half), 6 + 2 * way + half, (2, 4)[way]
        )

    def far_terms(self, term):
        for place in (3, 1, 2, 0):
            term(4 + place, self.far(place), False)
            self.core_copy(place).start()

    def near_terms(self, term, allowed=None):
        for place in (3, 1, 2, 0):
            self.core_copy(place).wait_recv()
            term(place, self.near(place), True)
            if place == 3:
                if allowed is not None:
                    allowed()
                for half in range(2):
                    self.corner_copy(half).start()
            elif place:
                self.final_copy(place - 1, 2 - place).start()

    def take_corner(self):
        for half in range(2):
            self.corner_copy(half).wait_recv()
            add_into(self.near(1 + half, half), self.corner(half))
            self.final_copy(half, half).start()

    def take_final(self, target):
        for half in range(2):
            for way in range(2):
                self.final_copy(way, half).wait_recv()
            own, first, second = self.near(0, half), self.final(0, half), self.final(1, half)
            out = target(half)

            def step(index, carry):
                span = pl.ds(pl.multiple_of(index * STRIP, STRIP), STRIP)
                out[span, :] = wide(own[span, :]) + wide(first[span, :]) + wide(second[span, :])
                return carry

            lax.fori_loop(0, own.shape[0] // STRIP, step, 0)

    def sent(self, core=True):
        for place in range(4) if core else ():
            self.core_copy(place).wait_send()
        for half in range(2):
            self.corner_copy(half).wait_send()
            for way in range(2):
                self.final_copy(way, half).wait_send()


def add_into(target, source):
    def step(index, carry):
        span = pl.ds(pl.multiple_of(index * STRIP, STRIP), STRIP)
        target[span, :] = (wide(target[span, :]) + wide(source[span, :])).astype(target.dtype)
        return carry

    lax.fori_loop(0, target.shape[0] // STRIP, step, 0)


def product_term(left, right, tile):
    def term(place, target, adds):
        height = target.shape[0]
        turned = left(place, height).T

        def step(index, carry):
            columns = pl.ds(pl.multiple_of(index * tile, tile), tile)
            value = jnp.dot(turned, right(columns), preferred_element_type=jnp.float32)
            if adds:
                value = value + wide(target[:, columns])
            target[:, columns] = value.astype(target.dtype)
            return carry

        lax.fori_loop(0, target.shape[1] // tile, step, 0)

    return term


def stacked(buffer, first, height):
    def view(place, half=None):
        at = first + place * height
        if half is None:
            return buffer.at[pl.ds(at, height), :]
        return buffer.at[pl.ds(at + half * (height // 2), height // 2), :]

    return view


def middle_kernel(size, *refs):
    (
        attended_hbm,
        tokens_hbm,
        cotangent_hbm,
        attention_scale,
        feedforward_scale,
        output_hbm,
        gate_hbm,
        up_hbm,
        down_hbm,
        mlp_out,
        inner_out,
        mixed_cot_out,
        branch_cot_out,
        block_out,
        grad_hidden_out,
        gate_grad_out,
        up_grad_out,
        attention_gain_out,
        feedforward_gain_out,
        attended,
        tokens,
        cotangent,
        output_weight,
        gate_weight,
        up_weight,
        down_weight,
        everyone,
        gate_act,
        up_act,
        inner,
        hidden,
        branch,
        arrived,
        partial,
        total,
        load_sem,
        store_sem,
        sum_send,
        sum_recv,
        hand_send,
        hand_recv,
        shard_send,
        shard_recv,
        grad_send,
        grad_recv,
        again_sem,
        free_sem,
    ) = refs
    me = lax.axis_index("tensor")
    last = size - 1
    chunk_rows, model_width = tokens.shape[1], tokens.shape[2]
    units = gate_weight.shape[1]
    half_rows = chunk_rows // HALVES
    all_rows = size * chunk_rows

    greet(((me < last, me + 1), (me > 0, me - 1)))
    first_loads = [
        pltpu.make_async_copy(source, target, load_sem.at[place])
        for place, (source, target) in enumerate(
            (
                (attended_hbm, attended),
                (output_hbm, output_weight),
                (tokens_hbm, tokens),
                (cotangent_hbm, cotangent),
                (gate_hbm, gate_weight),
                (up_hbm, up_weight.at[pl.ds(0, up_hbm.shape[0]), :]),
                (down_hbm, down_weight.at[:, pl.ds(0, down_hbm.shape[1])]),
            )
        )
    ]
    for copy in first_loads:
        copy.start()
    up_flow = ShardGather(
        own_halves(up_hbm),
        row_halves(up_weight, up_hbm.shape[0]),
        shard_send.at[0],
        shard_recv.at[0],
    )
    down_flow = ShardGather(
        own_halves(down_hbm),
        column_halves(down_weight, down_hbm.shape[1]),
        shard_send.at[1],
        shard_recv.at[1],
    )
    pl.semaphore_wait(
        pltpu.get_barrier_semaphore(), 3 + jnp.minimum(me, 1) + jnp.minimum(last - me, 1)
    )
    up_flow.start(2, 4, 1)
    down_flow.start(1)

    height = model_width // 8
    again = [
        pltpu.make_async_copy(
            mlp_out.at[chunk, origin],
            down_weight.at[pl.ds((chunk * size + origin) * chunk_rows, chunk_rows), :],
            again_sem.at[chunk, origin],
        )
        for chunk in range(CHUNKS)
        for origin in range(size)
    ]
    gate_grads, up_grads = (
        ShardSum(
            stacked(buffer, 0, height),
            stacked(down_weight, 4 * height, height),
            functools.partial(stacked(buffer, 4 * height, height), 0),
            stacked(buffer, 5 * height, height),
            grad_send.at[kind],
            grad_recv.at[kind],
        )
        for kind, buffer in enumerate((gate_weight, up_weight))
    )

    def rows_again(place, shard_width):
        return down_weight[pl.ds(0, CHUNKS * all_rows), pl.ds(place * shard_width, shard_width)]

    def grad_term(act):
        def columns_of(columns):
            return act[:, :, columns].reshape(CHUNKS * all_rows, 512)

        return product_term(rows_again, columns_of, 512)

    def weights_free():
        for place, mask in enumerate((1, 2, 4)):
            pl.semaphore_signal(
                free_sem.at[place],
                inc=1,
                device_id={"dp": shard_peer(mask)},
                device_id_type=pl.DeviceIdType.MESH,
            )
        for copy in again:
            copy.start()

    def neighbours_free():
        pl.semaphore_wait(free_sem.at[1], 1)
        pl.semaphore_wait(free_sem.at[2], 1)

    def grad_turns(tick, half):
        if (tick, half) == (21, 0):
            for copy in again:
                copy.wait()
            pl.semaphore_wait(free_sem.at[0], 1)
            gate_grads.far_terms(grad_term(gate_act))
        elif (tick, half) == (21, 1):
            gate_grads.near_terms(grad_term(gate_act), neighbours_free)
        elif (tick, half) == (22, 0):
            for place in range(4):
                gate_grads.core_copy(place).wait_send()
            up_grads.far_terms(grad_term(up_act))
        elif (tick, half) == (22, 1):
            up_grads.near_terms(grad_term(up_act))
        elif (tick, half) == (23, 1):
            gate_grads.take_corner()
        elif (tick, half) == (25, 1):
            up_grads.take_corner()
        elif (tick, half) == (27, 1):
            gate_grads.take_final(lambda half: hidden.at[half])
            for half in range(HALVES):
                store(6, half).start()
            for half in range(HALVES):
                store(6, half).wait()

    def turns(tick, half):
        if (tick, half) == (2, 1):
            up_flow.arrive(2, (0,))
            up_flow.arrive(4, (0,))
        elif (tick, half) == (3, 0):
            up_flow.arrive(2, (1,))
            up_flow.arrive(4, (1,))
            down_flow.start(2, 4)
        elif (tick, half) == (4, 1):
            up_flow.arrive(6)
        elif (tick, half) == (5, 0):
            down_flow.arrive(2, (0,))
            down_flow.arrive(4, (0,))
        elif (tick, half) == (6, 0):
            down_flow.arrive(2, (1,))
            down_flow.arrive(4, (1,))
        elif (tick, half) == (7, 0):
            down_flow.arrive(6)

    attention_gain_out[...] = jnp.zeros_like(attention_gain_out)
    feedforward_gain_out[...] = jnp.zeros_like(feedforward_gain_out)

    def half_span(half):
        return pl.ds(half * half_rows, half_rows)

    def strips(half, body):
        def step(index, carry):
            body(
                pl.ds(pl.multiple_of(half * half_rows + index * STRIP, STRIP), STRIP),
                pl.ds(pl.multiple_of(index * STRIP, STRIP), STRIP),
            )
            return carry

        lax.fori_loop(0, half_rows // STRIP, step, 0)

    def sum_copy(chunk, step, half, way, dest):
        return pltpu.make_async_remote_copy(
            src_ref=partial.at[chunk, dest, half_span(half)],
            dst_ref=arrived.at[way, chunk, step - 1, half_span(half)],
            send_sem=sum_send.at[way, chunk, step - 1, half],
            recv_sem=sum_recv.at[way, chunk, step - 1, half],
            device_id={"tensor": me + 1 - 2 * way},
            device_id_type=pl.DeviceIdType.MESH,
        )

    def hand_copy(chunk, hop, half, way, origin):
        rows = everyone.at[origin, chunk, half_span(half)]
        return pltpu.make_async_remote_copy(
            src_ref=rows,
            dst_ref=rows,
            send_sem=hand_send.at[way, chunk, hop - 1, half],
            recv_sem=hand_recv.at[way, chunk, hop - 1, half],
            device_id={"tensor": me + 1 - 2 * way},
            device_id_type=pl.DeviceIdType.MESH,
        )

    def away(way):
        return me if way == 0 else last - me

    def sum_step(chunk, step, half):
        for way in range(2):
            distance = away(way)

            @pl.when(distance <= step - 1)
            def _():
                dest = me + size - step if way == 0 else me - size + step
                if step > 1:

                    @pl.when(distance >= 1)
                    def _():
                        sum_copy(chunk, step - 1, half, way, dest).wait_recv()

                        def add(rows, _):
                            partial[chunk, dest, rows] = low(
                                wide(partial[chunk, dest, rows])
                                + wide(arrived[way, chunk, step - 2, rows])
                            )

                        strips(half, add)

                sum_copy(chunk, step, half, way, dest).start()

    def sum_end(chunk, half):
        def begin(rows, here):
            total[here] = wide(partial[chunk, me, rows])

        strips(half, begin)
        for way in range(2):

            @pl.when(away(way) >= 1)
            def _():
                sum_copy(chunk, size - 1, half, way, me).wait_recv()

                def add(rows, here):
                    total[here] = total[here] + wide(arrived[way, chunk, size - 2, rows])

                strips(half, add)

    def sum_sent(chunk):
        for step in range(1, size):
            for way in range(2):

                @pl.when(away(way) <= step - 1)
                def _():
                    for half in range(HALVES):
                        sum_copy(chunk, step, half, way, 0).wait_send()

    def hand_first(chunk, half):
        for way in range(2):

            @pl.when(away(1 - way) >= 1)
            def _():
                hand_copy(chunk, 1, half, way, me).start()

    def hand_on(chunk, hop, half):
        for way in range(2):

            @pl.when(away(way) >= hop)
            def _():
                origin = me - hop if way == 0 else me + hop
                hand_copy(chunk, hop, half, way, origin).wait_recv()
                if hop < size - 1:

                    @pl.when(away(1 - way) >= 1)
                    def _():
                        hand_copy(chunk, hop + 1, half, way, origin).start()

    def hand_sent(chunk):
        for hop in range(1, size):
            for way in range(2):

                @pl.when(jnp.logical_and(away(way) >= hop - 1, away(1 - way) >= 1))
                def _():
                    for half in range(HALVES):
                        hand_copy(chunk, hop, half, way, 0).wait_send()

    def inverse_rms(values):
        return lax.rsqrt(jnp.mean(values * values, -1, keepdims=True) + EPS)

    def fold(values):
        return values[:8] + values[8:]

    def own_rows(chunk, stage, half):
        def after_branch(rows, here):
            value = total[here]
            branch[chunk, rows] = value
            state = wide(tokens[chunk, rows]) + value * inverse_rms(value) * attention_scale[...]
            hidden[chunk, rows] = state
            everyone[me, chunk, rows] = low(state)

        def after_mixed(rows, here):
            value = total[here]
            inverse = inverse_rms(value)
            normalized = value * inverse
            hidden[chunk, rows] = hidden[chunk, rows] + normalized * feedforward_scale[...]
            grad = wide(cotangent[chunk, rows])
            feedforward_gain_out[...] += fold(grad * normalized)
            everyone[me, chunk, rows] = low(
                norm_backward(grad, normalized, inverse, feedforward_scale[...])
            )

        def after_gradient(rows, here):
            grad = total[here] + wide(cotangent[chunk, rows])
            value = branch[chunk, rows]
            inverse = inverse_rms(value)
            normalized = value * inverse
            branch[chunk, rows] = grad
            attention_gain_out[...] += fold(grad * normalized)
            everyone[me, chunk, rows] = low(
                norm_backward(grad, normalized, inverse, attention_scale[...])
            )

        strips(half, (after_branch, after_mixed, after_gradient)[stage])

    def gathered(chunk):
        return everyone[:, chunk].reshape(all_rows, model_width)

    def tiles(first, end, body):
        def step(index, carry):
            body(pl.ds(pl.multiple_of(index * TILE, TILE), TILE))
            return carry

        lax.fori_loop(first, end, step, 0)

    def store(kind, chunk):
        source, target = (
            (everyone.at[:, chunk], mlp_out.at[chunk]),
            (inner, inner_out.at[chunk]),
            (everyone.at[:, chunk], mixed_cot_out.at[chunk]),
            (everyone.at[:, chunk], branch_cot_out.at[:, chunk]),
            (hidden.at[chunk], block_out.at[chunk]),
            (branch.at[chunk], grad_hidden_out.at[chunk]),
            (hidden.at[chunk], gate_grad_out.at[pl.ds(chunk * chunk_rows, chunk_rows), :]),
            (hidden.at[chunk], up_grad_out.at[pl.ds(chunk * chunk_rows, chunk_rows), :]),
        )[kind]
        return pltpu.make_async_copy(source, target, store_sem.at[kind, chunk])

    def put_partial(chunk, columns, values):
        partial[chunk, :, :, columns] = low(values).reshape(size, chunk_rows, TILE)

    def branch_terms(chunk):
        def tile(columns):
            rows = attended[:, chunk].reshape(all_rows, attended.shape[-1])
            put_partial(
                chunk,
                columns,
                jnp.dot(rows, output_weight[:, columns], preferred_element_type=jnp.float32),
            )

        tiles(0, model_width // TILE, tile)

    def gate_tile(chunk):
        def tile(columns):
            rows = gathered(chunk)
            gate = jnp.dot(rows, gate_weight[:, columns], preferred_element_type=jnp.float32)
            up = jnp.dot(rows, up_weight[:, columns], preferred_element_type=jnp.float32)
            gate_act[chunk, :, columns] = low(gate)
            up_act[chunk, :, columns] = low(up)
            inner[:, columns] = low(gate * jax.nn.sigmoid(gate) * up)

        return tile

    def down_tile(chunk):
        def tile(columns):
            put_partial(
                chunk,
                columns,
                jnp.dot(inner[...], down_weight[:, columns], preferred_element_type=jnp.float32),
            )

        return tile

    def grad_inner_tile(chunk):
        def tile(columns):
            grad = rows_product(gathered(chunk), down_weight[columns, :])
            gate = wide(gate_act[chunk, :, columns])
            up = wide(up_act[chunk, :, columns])
            sigmoid = jax.nn.sigmoid(gate)
            gate_act[chunk, :, columns] = low(
                grad * up * sigmoid * (1.0 + gate * (1.0 - sigmoid))
            )
            up_act[chunk, :, columns] = low(grad * gate * sigmoid)

        return tile

    def grad_input_tile(chunk):
        def tile(columns):
            put_partial(
                chunk,
                columns,
                rows_product(gate_act[chunk], gate_weight[columns, :])
                + rows_product(up_act[chunk], up_weight[columns, :]),
            )

        return tile

    unit_tiles, width_tiles = units // TILE, model_width // TILE

    def forward_piece(chunk, piece):
        if piece == 0:
            if chunk == 0:
                for mask in (1, 3, 5, 7):
                    up_flow.arrive(mask)
                for copy in first_loads[4:]:
                    copy.wait()
            store(0, chunk).start()
            tiles(0, unit_tiles // 2, gate_tile(chunk))
        elif piece == 1:
            tiles(unit_tiles // 2, unit_tiles, gate_tile(chunk))
            store(1, chunk).start()
            sum_sent(chunk)
            hand_sent(chunk)
        else:
            if chunk == 0:
                for mask in (1, 3, 5, 7):
                    down_flow.arrive(mask)
            tiles(0, width_tiles, down_tile(chunk))
            store(0, chunk).wait()
            store(1, chunk).wait()

    def backward_piece(chunk, piece):
        if piece == 0:
            store(2, chunk).start()
            store(4, chunk).start()
            tiles(0, unit_tiles, grad_inner_tile(chunk))
        elif piece == 1:
            sum_sent(chunk)
            hand_sent(chunk)
            tiles(0, width_tiles // 2, grad_input_tile(chunk))
        else:
            tiles(width_tiles // 2, width_tiles, grad_input_tile(chunk))
            store(2, chunk).wait()
            store(4, chunk).wait()
            if chunk == CHUNKS - 1:
                up_flow.sent()
                down_flow.sent()
                weights_free()

    def end_piece(chunk, piece):
        if piece == 0:
            store(3, chunk).start()
            store(5, chunk).start()

    first_loads[0].wait()
    first_loads[1].wait()
    branch_terms(0)
    first_loads[2].wait()
    first_loads[3].wait()
    bases = {
        (chunk, stage): (CHUNKS * stage + chunk) * size
        for stage in range(3)
        for chunk in range(CHUNKS)
    }
    ticks = max(bases.values()) + 2 * size
    for tick in range(1, ticks + 1):
        for half in range(HALVES):
            for (chunk, stage), base in bases.items():
                at = tick - base
                if size < at < 2 * size:
                    hand_on(chunk, at - size, half)
            for (chunk, stage), base in bases.items():
                at = tick - base
                if 1 <= at < size:
                    sum_step(chunk, at, half)
                elif at == size:
                    sum_end(chunk, half)
                    own_rows(chunk, stage, half)
                    hand_first(chunk, half)
            turns(tick, half)
            if tick == 1 and half == 1:
                branch_terms(1)
            for (chunk, stage), base in bases.items():
                piece = (tick - base - 2 * size + 1) * HALVES + half - 1
                if 0 <= piece < 3:
                    (forward_piece, backward_piece, end_piece)[stage](chunk, piece)
            grad_turns(tick, half)
    up_grads.take_final(lambda half: hidden.at[half])
    for half in range(HALVES):
        store(7, half).start()
    gate_grads.sent(False)
    up_grads.sent()
    for chunk in range(CHUNKS):
        sum_sent(chunk)
        hand_sent(chunk)
        store(3, chunk).wait()
        store(5, chunk).wait()
        store(7, chunk).wait()


def middle(
    attended,
    tokens_here,
    cotangent_here,
    attention_scale,
    feedforward_scale,
    output_full,
    gate_full,
    up_shard,
    down_shard,
):
    size = lax.axis_size("tensor")
    own_rows, model_width = tokens_here.shape
    chunk_rows = own_rows // CHUNKS
    all_rows = size * chunk_rows
    half_rows = chunk_rows // HALVES
    heads_width = attended.shape[1]
    units = gate_full.shape[1]
    chunked = (CHUNKS, chunk_rows, model_width)
    lined = (CHUNKS, size, chunk_rows, model_width)
    low_type, wide_type = jnp.bfloat16, jnp.float32

    def shape(dims, kind=low_type):
        return jax.ShapeDtypeStruct(dims, kind)

    anywhere = pl.BlockSpec(memory_space=pl.ANY)
    inside = pl.BlockSpec(memory_space=pltpu.VMEM)
    dma = pltpu.SemaphoreType.DMA
    flops = 2 * CHUNKS * all_rows * model_width * (2 * heads_width + 6 * units)
    outs = pl.pallas_call(
        functools.partial(middle_kernel, size),
        out_shape=[
            shape(lined),
            shape((CHUNKS, all_rows, units)),
            shape(lined),
            shape((size, CHUNKS, chunk_rows, model_width)),
            shape(chunked, wide_type),
            shape(chunked, wide_type),
            shape((model_width // 8, units), wide_type),
            shape((model_width // 8, units), wide_type),
            shape((8, model_width), wide_type),
            shape((8, model_width), wide_type),
        ],
        in_specs=[anywhere] * 3 + [inside] * 2 + [anywhere] * 4,
        out_specs=[anywhere] * 8 + [inside] * 2,
        scratch_shapes=[
            pltpu.VMEM((size, CHUNKS, chunk_rows, heads_width), low_type),
            pltpu.VMEM(chunked, low_type),
            pltpu.VMEM(chunked, low_type),
            pltpu.VMEM((heads_width, model_width), low_type),
            pltpu.VMEM((model_width, units), low_type),
            pltpu.VMEM((model_width, units), low_type),
            pltpu.VMEM((units, model_width), low_type),
            pltpu.VMEM((size, CHUNKS, chunk_rows, model_width), low_type),
            pltpu.VMEM((CHUNKS, all_rows, units), low_type),
            pltpu.VMEM((CHUNKS, all_rows, units), low_type),
            pltpu.VMEM((all_rows, units), low_type),
            pltpu.VMEM(chunked, wide_type),
            pltpu.VMEM(chunked, wide_type),
            pltpu.VMEM((2, CHUNKS, size - 1, chunk_rows, model_width), low_type),
            pltpu.VMEM(lined, low_type),
            pltpu.VMEM((half_rows, model_width), wide_type),
            dma((7,)),
            dma((8, CHUNKS)),
            dma((2, CHUNKS, size - 1, HALVES)),
            dma((2, CHUNKS, size - 1, HALVES)),
            dma((2, CHUNKS, size - 1, HALVES)),
            dma((2, CHUNKS, size - 1, HALVES)),
            dma((2, 7, 2)),
            dma((2, 7, 2)),
            dma((2, 10)),
            dma((2, 10)),
            dma((CHUNKS, size)),
            pltpu.SemaphoreType.REGULAR((3,)),
        ],
        compiler_params=pltpu.CompilerParams(
            collective_id=1, has_side_effects=True, vmem_limit_bytes=VMEM_BYTES
        ),
        cost_estimate=pl.CostEstimate(
            flops=flops, bytes_accessed=64 << 20, transcendentals=0
        ),
        name="middle",
    )(
        attended.reshape(size, CHUNKS, chunk_rows, heads_width),
        tokens_here.reshape(chunked),
        cotangent_here.reshape(chunked),
        attention_scale.reshape(1, model_width),
        feedforward_scale.reshape(1, model_width),
        output_full,
        gate_full,
        up_shard,
        down_shard,
    )
    rows = CHUNKS * all_rows
    return (
        outs[1].reshape(rows, units),
        outs[2].reshape(rows, model_width),
        outs[3].reshape(rows, model_width),
        outs[4].reshape(own_rows, model_width),
        outs[5].reshape(own_rows, model_width),
        outs[6],
        outs[7],
        jnp.sum(outs[8], 0),
        jnp.sum(outs[9], 0),
    )


def back_kernel(
    size,
    grad_hbm,
    weight_hbm,
    attended_hbm,
    branch_cot_hbm,
    mixed_cot_hbm,
    inner_hbm,
    rows_hbm,
    gain_hbm,
    hidden_hbm,
    tokens_out,
    down_out,
    output_out,
    attention_out,
    gain_out,
    grad,
    weight,
    attended,
    branch_cot,
    mixed_cot,
    inner,
    rows,
    gain,
    hidden,
    partial,
    arrived,
    down_far,
    down_near,
    output_far,
    output_near,
    attention_far,
    attention_near,
    gain_far,
    gain_near,
    down_total,
    output_total,
    load_sem,
    store_sem,
    sum_send,
    sum_recv,
    shard_send,
    shard_recv,
):
    me = lax.axis_index("tensor")
    last = size - 1
    own_rows, model_width = partial.shape[1:]
    piece_rows = own_rows // PIECES
    height = model_width // 8
    greet(((me < last, me + 1), (me > 0, me - 1)))
    loads = [
        pltpu.make_async_copy(source, target, load_sem.at[place])
        for place, (source, target) in enumerate(
            (
                (grad_hbm, grad),
                (weight_hbm, weight),
                (attended_hbm, attended),
                (branch_cot_hbm, branch_cot),
                (mixed_cot_hbm, mixed_cot),
                (inner_hbm, inner),
                (rows_hbm, rows),
                (gain_hbm, gain),
                (hidden_hbm, hidden),
            )
        )
    ]
    for copy in loads:
        copy.start()

    def flow(kind, near, far, shard_height):
        return ShardSum(
            stacked(near, 0, shard_height),
            stacked(far, 0, shard_height),
            lambda half: stacked(near, 4 * shard_height, shard_height)(0, half),
            lambda way, half: stacked(near, 5 * shard_height, shard_height)(way, half),
            shard_send.at[kind],
            shard_recv.at[kind],
        )

    down_flow = flow(0, down_near, down_far, height)
    output_flow = flow(1, output_near, output_far, height)
    attention_flow = flow(2, attention_near, attention_far, height)
    gain_flow = flow(3, gain_near, gain_far, gain.shape[0] // 8)
    flows = (down_flow, output_flow, attention_flow, gain_flow)

    def columns_of(source):
        return lambda place, width: source[:, pl.ds(place * width, width)]

    down_term = product_term(columns_of(mixed_cot), lambda columns: inner[:, columns], 512)
    output_term = product_term(columns_of(branch_cot), lambda columns: attended[:, columns], 512)
    attention_term = product_term(columns_of(rows), lambda columns: grad[:, columns], 512)

    def gain_term(place, target, adds):
        value = gain[pl.ds(place * target.shape[0], target.shape[0]), :]
        target[...] = value + target[...] if adds else value

    def terms(dest):
        def step(index, carry):
            columns = pl.ds(pl.multiple_of(index * TILE, TILE), TILE)
            span = pl.ds(pl.multiple_of(dest * own_rows, own_rows), own_rows)
            partial[dest, :, columns] = low(rows_product(grad[span, :], weight[columns, :]))
            return carry

        lax.fori_loop(0, model_width // TILE, step, 0)

    def terms_at(distance):
        for way in range(2):

            @pl.when(away(1 - way) >= distance)
            def _():
                terms(me + distance if way == 0 else me - distance)

    def away(way):
        return me if way == 0 else last - me

    def span_of(piece):
        return pl.ds(piece * piece_rows, piece_rows)

    def sum_copy(step, piece, way, dest):
        return pltpu.make_async_remote_copy(
            src_ref=partial.at[dest, span_of(piece)],
            dst_ref=arrived.at[way, step - 1, span_of(piece)],
            send_sem=sum_send.at[way, step - 1, piece],
            recv_sem=sum_recv.at[way, step - 1, piece],
            device_id={"tensor": me + 1 - 2 * way},
            device_id_type=pl.DeviceIdType.MESH,
        )

    def sum_step(step, *pieces):
        for piece in pieces:
            for way in range(2):
                distance = away(way)

                @pl.when(distance <= step - 1)
                def _():
                    dest = me + size - step if way == 0 else me - size + step
                    if step > 1:

                        @pl.when(distance >= 1)
                        def _():
                            sum_copy(step - 1, piece, way, dest).wait_recv()
                            add_into(
                                partial.at[dest, span_of(piece)],
                                arrived.at[way, step - 2, span_of(piece)],
                            )

                    sum_copy(step, piece, way, dest).start()

    def sum_end(*pieces):
        for piece in pieces:
            add_into(hidden.at[span_of(piece)], partial.at[me, span_of(piece)])
            for way in range(2):

                @pl.when(away(way) >= 1)
                def _():
                    sum_copy(size - 1, piece, way, me).wait_recv()
                    add_into(
                        hidden.at[span_of(piece)], arrived.at[way, size - 2, span_of(piece)]
                    )

            pltpu.make_async_copy(
                hidden.at[span_of(piece)], tokens_out.at[span_of(piece)], store_sem.at[3 + piece]
            ).start()

    def halves_of(total):
        rows_of_half = total.shape[0] // 2
        return lambda half: total.at[pl.ds(half * rows_of_half, rows_of_half), :]

    stores = [
        pltpu.make_async_copy(source, target, store_sem.at[place])
        for place, (source, target) in enumerate(
            (
                (down_total, down_out),
                (output_total, output_out),
                (down_total.at[:, pl.ds(0, grad.shape[1])], attention_out),
            )
        )
    ]

    pl.semaphore_wait(
        pltpu.get_barrier_semaphore(), 3 + jnp.minimum(me, 1) + jnp.minimum(last - me, 1)
    )
    loads[0].wait()
    loads[1].wait()
    terms_at(3)
    sum_step(1, *range(PIECES))
    loads[2].wait()
    loads[3].wait()
    output_flow.far_terms(output_term)
    loads[7].wait()
    gain_flow.far_terms(gain_term)
    loads[4].wait()
    loads[5].wait()
    down_flow.far_terms(down_term)
    output_flow.near_terms(output_term)
    gain_flow.near_terms(gain_term)
    terms_at(2)
    sum_step(2, 0)
    down_flow.near_terms(down_term)
    sum_step(2, 1)
    terms_at(1)
    loads[6].wait()
    sum_step(2, 2)
    attention_flow.far_terms(attention_term)
    output_flow.take_corner()
    gain_flow.take_corner()
    sum_step(2, 3)
    terms(me)
    sum_step(3, 0)
    attention_flow.near_terms(attention_term)
    sum_step(3, 1)
    down_flow.take_corner()
    sum_step(3, 2)
    sum_step(3, 3)
    loads[8].wait()
    output_flow.take_final(halves_of(output_total))
    stores[1].start()
    gain_flow.take_final(halves_of(gain_out))
    sum_end(0)
    attention_flow.take_corner()
    sum_end(1)
    down_flow.take_final(halves_of(down_total))
    stores[0].start()
    sum_end(2)
    sum_end(3)
    stores[0].wait()
    attention_flow.take_final(
        lambda half: down_total.at[
            pl.ds(half * (height // 2), height // 2), pl.ds(0, grad.shape[1])
        ]
    )
    stores[2].start()
    for shard_flow in flows:
        shard_flow.sent()
    for step in range(1, size):
        for way in range(2):

            @pl.when(away(way) <= step - 1)
            def _():
                for piece in range(PIECES):
                    sum_copy(step, piece, way, 0).wait_send()

    for copy in stores[1:]:
        copy.wait()
    for piece in range(PIECES):
        pltpu.make_async_copy(
            hidden.at[span_of(piece)], tokens_out.at[span_of(piece)], store_sem.at[3 + piece]
        ).wait()


def back(
    grad_projected,
    attention_full,
    attended,
    branch_cot,
    mixed_cot,
    inner,
    rows_all,
    gain_terms,
    grad_hidden,
):
    size = lax.axis_size("tensor")
    own_rows, model_width = grad_hidden.shape
    height = model_width // 8
    operands = (
        grad_projected,
        attention_full,
        attended,
        branch_cot,
        mixed_cot,
        inner,
        rows_all,
        gain_terms,
        grad_hidden,
    )
    widths = (inner.shape[1], attended.shape[1], grad_projected.shape[1])
    gain_height, gain_width = gain_terms.shape[0] // 8, gain_terms.shape[1]
    low_type, wide_type = jnp.bfloat16, jnp.float32
    anywhere = pl.BlockSpec(memory_space=pl.ANY)
    dma = pltpu.SemaphoreType.DMA
    buffers = []
    for width in widths:
        buffers.append(pltpu.VMEM((4 * height, width), low_type))
        buffers.append(pltpu.VMEM((7 * height, width), low_type))
    return pl.pallas_call(
        functools.partial(back_kernel, size),
        out_shape=[
            jax.ShapeDtypeStruct((own_rows, model_width), wide_type),
            *(jax.ShapeDtypeStruct((height, width), wide_type) for width in widths),
            jax.ShapeDtypeStruct((gain_height, gain_width), wide_type),
        ],
        in_specs=[anywhere] * 9,
        out_specs=[anywhere] * 4 + [pl.BlockSpec(memory_space=pltpu.VMEM)],
        scratch_shapes=[
            *(pltpu.VMEM(operand.shape, operand.dtype) for operand in operands),
            pltpu.VMEM((size, own_rows, model_width), low_type),
            pltpu.VMEM((2, size - 1, own_rows, model_width), low_type),
            *buffers,
            pltpu.VMEM((4 * gain_height, gain_width), wide_type),
            pltpu.VMEM((7 * gain_height, gain_width), wide_type),
            *(pltpu.VMEM((height, width), wide_type) for width in widths[:2]),
            dma((9,)),
            dma((3 + PIECES,)),
            dma((2, size - 1, PIECES)),
            dma((2, size - 1, PIECES)),
            dma((4, 10)),
            dma((4, 10)),
        ],
        compiler_params=pltpu.CompilerParams(
            collective_id=2, has_side_effects=True, vmem_limit_bytes=VMEM_BYTES
        ),
        cost_estimate=pl.CostEstimate(
            flops=2 * size * own_rows * model_width * (sum(widths) + widths[2]),
            bytes_accessed=48 << 20,
            transcendentals=0,
        ),
        name="back",
    )(*operands)


def local(
    tokens,
    positions,
    cotangent,
    query_weight,
    key_weight,
    value_weight,
    output_weight,
    gate_weight,
    up_weight,
    down_weight,
    query_gain,
    key_gain,
    attention_gain,
    feedforward_gain,
):
    model_width = tokens.shape[1]
    data_size = lax.axis_size("dp")
    data_index = lax.axis_index("dp")
    head_size = query_gain.shape[0] * data_size
    local_heads = query_gain.shape[1]
    local_width = query_weight.shape[1]
    block_rows = min(512, LENGTH)
    order = mask_order(data_size)
    place_of = jnp.array([order.index(mask) for mask in range(data_size)], jnp.int32)
    width = model_width // data_size

    def shuffle(array_in):
        return jnp.concatenate(
            [
                lax.dynamic_slice_in_dim(array_in, (data_index ^ mask) * width, width, -1)
                for mask in order
            ],
            -1,
        )

    def unshuffle(array_in):
        return jnp.concatenate(
            [
                lax.dynamic_slice_in_dim(
                    array_in, place_of[data_index ^ block] * width, width, -1
                )
                for block in range(data_size)
            ],
            -1,
        )

    small = jnp.concatenate(
        [query_gain.reshape(-1), key_gain.reshape(-1), attention_gain, feedforward_gain]
    )
    small = gather_high(small[None], 0)
    small_count = small.size
    small = jnp.pad(small.reshape(-1), (0, 32 * 128 - small_count)).reshape(32, 128)
    tokens_here = shuffle(tokens)
    rows_all, projected, attention_full, output_full, gate_full, small_all = front(
        tokens_here,
        gather_high(jnp.concatenate([query_weight, key_weight, value_weight], 1), 0),
        gather_high(output_weight, 1),
        gather_high(gate_weight, 0),
        small,
    )
    small_all = small_all.reshape(8, -1)[:, :small_count].reshape(data_size, -1)
    gain_count = query_gain.size
    natural = jnp.concatenate(
        [
            lax.dynamic_slice_in_dim(
                small_all[:, : 2 * gain_count], place_of[data_index ^ block], 1, 0
            )
            for block in range(data_size)
        ],
        0,
    )
    query_gain_full = natural[:, :gain_count].reshape(head_size, local_heads)
    key_gain_full = natural[:, gain_count:].reshape(head_size, local_heads)
    attention_scale = wide(small_all[:, 2 * gain_count : 2 * gain_count + width].reshape(-1))
    feedforward_scale = wide(small_all[:, 2 * gain_count + width :].reshape(-1))
    query_scale = channel_scale(query_gain_full)
    key_scale = channel_scale(key_gain_full)
    group_rows = rows_all.shape[0]
    seq_count = group_rows // LENGTH

    def per_sequence(array_in):
        return array_in.reshape((seq_count, LENGTH) + array_in.shape[1:])

    queries = projected[:, :local_width]
    key_rows = projected[:, local_width : 2 * local_width]
    squares = lax.psum(
        jnp.stack([jnp.sum(queries * queries, -1), jnp.sum(key_rows * key_rows, -1)]), "tensor"
    )
    inverse_q = lax.rsqrt(squares[0] / model_width + EPS)[:, None]
    inverse_k = lax.rsqrt(squares[1] / model_width + EPS)[:, None]
    query_hat = queries * inverse_q
    key_hat = key_rows * inverse_k
    cosine_table, sine_table = rope_tables(positions, head_size)
    query_rot = low(
        rotate(
            (query_hat * query_scale).reshape(group_rows, local_heads, head_size),
            cosine_table,
            sine_table,
        )
    )
    key_rot = low(
        rotate(
            (key_hat * key_scale).reshape(group_rows, local_heads, head_size),
            cosine_table,
            sine_table,
        )
    )
    value_rows = low(projected[:, 2 * local_width :]).reshape(group_rows, local_heads, head_size)
    attended, row_lse = lax.map(
        lambda sequence_item: attend_forward(
            sequence_item[0], sequence_item[1], sequence_item[2], block_rows
        ),
        (per_sequence(query_rot), per_sequence(key_rot), per_sequence(value_rows)),
    )
    attended = low(attended.reshape(group_rows, -1))
    (
        inner_act,
        mixed_cot,
        branch_cot,
        block_here,
        grad_hidden,
        grad_gate,
        grad_up,
        partial_attention_gain,
        partial_feedforward_gain,
    ) = middle(
        attended,
        tokens_here,
        shuffle(cotangent),
        attention_scale,
        feedforward_scale,
        output_full,
        gate_full,
        gather_high(up_weight, 0),
        gather_high(down_weight, 1),
    )
    block_output = unshuffle(block_here)

    grad_attended = low(
        jnp.einsum("td,cd->tc", branch_cot, output_full, preferred_element_type=jnp.float32)
    )
    grad_query_rot, grad_key_rot, grad_value_rows = lax.map(
        lambda sequence_item: attend_backward(
            sequence_item[0],
            sequence_item[1],
            sequence_item[2],
            sequence_item[3],
            sequence_item[4],
            block_rows,
        ),
        (
            per_sequence(query_rot),
            per_sequence(key_rot),
            per_sequence(value_rows),
            per_sequence(grad_attended.reshape(group_rows, local_heads, head_size)),
            row_lse,
        ),
    )
    grad_query_rot = wide(low(grad_query_rot.reshape(group_rows, local_heads, head_size)))
    grad_key_rot = wide(low(grad_key_rot.reshape(group_rows, local_heads, head_size)))
    grad_values_low = low(grad_value_rows.reshape(group_rows, -1))
    grad_query_norm = unrotate(grad_query_rot, cosine_table, sine_table).reshape(group_rows, -1)
    grad_key_norm = unrotate(grad_key_rot, cosine_table, sine_table).reshape(group_rows, -1)
    grad_query_scale = jnp.sum(grad_query_norm * query_hat, 0)
    grad_key_scale = jnp.sum(grad_key_norm * key_hat, 0)
    scaled_query = grad_query_norm * query_scale
    scaled_key = grad_key_norm * key_scale
    inner_query, inner_key, total_attention_gain, total_feedforward_gain = lax.psum(
        (
            jnp.sum(scaled_query * query_hat, -1),
            jnp.sum(scaled_key * key_hat, -1),
            partial_attention_gain,
            partial_feedforward_gain,
        ),
        "tensor",
    )
    grad_queries = low(
        inverse_q * (scaled_query - query_hat * inner_query[:, None] / model_width)
    )
    grad_keys = low(inverse_k * (scaled_key - key_hat * inner_key[:, None] / model_width))
    grad_projected = jnp.concatenate([grad_queries, grad_keys, grad_values_low], 1)
    query_gain_grad = grad_query_scale.reshape(local_heads, head_size).T
    key_gain_grad = grad_key_scale.reshape(local_heads, head_size).T

    def in_order(array_in):
        blocks = array_in.reshape(data_size, -1)
        return jnp.concatenate(
            [lax.dynamic_slice_in_dim(blocks, data_index ^ mask, 1, 0) for mask in order], 0
        )

    gain_terms = jnp.concatenate(
        [
            in_order(query_gain_grad),
            in_order(key_gain_grad),
            total_attention_gain.reshape(data_size, width),
            total_feedforward_gain.reshape(data_size, width),
        ],
        1,
    ).reshape(8, -1)
    gain_size = gain_terms.shape[1]
    gain_terms = jnp.pad(gain_terms, ((0, 0), (0, 32 * 128 - gain_size))).reshape(8 * 32, 128)
    tokens_part, grad_down, grad_output_proj, grad_attention, gain_part = back(
        grad_projected,
        attention_full,
        attended,
        branch_cot,
        mixed_cot,
        inner_act,
        rows_all,
        gain_terms,
        grad_hidden,
    )
    gain_shard = gain_part.reshape(-1)[:gain_size].reshape(data_size // 8, -1)
    for bit in reversed(range(3, bits_of(data_size))):
        kept, sent = jnp.split(gain_shard, 2, 0)
        gain_shard = kept + swap(sent, 1 << bit)
    gain_shard = gain_shard.reshape(-1)
    grad_attention = wide(scatter_high(grad_attention, 0))
    return (
        block_output,
        unshuffle(tokens_part),
        grad_attention[:, :local_width],
        grad_attention[:, local_width : 2 * local_width],
        grad_attention[:, 2 * local_width :],
        wide(scatter_high(grad_output_proj, 0)).T,
        wide(scatter_high(grad_gate, 0)),
        wide(scatter_high(grad_up, 0)),
        wide(scatter_high(grad_down, 0)).T,
        gain_shard[:gain_count].reshape(query_gain.shape),
        gain_shard[gain_count : 2 * gain_count].reshape(key_gain.shape),
        gain_shard[2 * gain_count : 2 * gain_count + width],
        gain_shard[2 * gain_count + width :],
    )


def solution(mesh):
    return jax.shard_map(
        local,
        mesh=mesh,
        in_specs=(
            P(("dp", "tensor"), None),
            P("dp"),
            P(("dp", "tensor"), None),
            P("dp", "tensor"),
            P("dp", "tensor"),
            P("dp", "tensor"),
            P("tensor", "dp"),
            P("dp", "tensor"),
            P("dp", "tensor"),
            P("tensor", "dp"),
            P("dp", "tensor"),
            P("dp", "tensor"),
            P("dp"),
            P("dp"),
        ),
        out_specs=(
            P(("dp", "tensor"), None),
            P(("dp", "tensor"), None),
            P("dp", "tensor"),
            P("dp", "tensor"),
            P("dp", "tensor"),
            P("tensor", "dp"),
            P("dp", "tensor"),
            P("dp", "tensor"),
            P("tensor", "dp"),
            P("dp", "tensor"),
            P("dp", "tensor"),
            P("dp"),
            P("dp"),
        ),
        check_vma=False,
    )
```

```python
import functools

import jax
import jax.numpy as jnp
from jax import lax
from jax.experimental import pallas as pl
from jax.experimental.pallas import tpu as pltpu
from jax.sharding import PartitionSpec as P

EPS = 1e-06
THETA = 500000.0
MASKED = -1e30
VMEM_BYTES = 64 * 1024 * 1024 - 128 * 1024


def norm_backward(grad_in, normalized, inverse_rms, gain_values):
    scaled = grad_in * gain_values
    return inverse_rms * (scaled - normalized * jnp.mean(scaled * normalized, -1, keepdims=True))


def bits_of(size):
    return size.bit_length() - 1


def swap(array_in, mask):
    size = lax.axis_size("dp")
    return lax.ppermute(array_in, "dp", [(index, index ^ mask) for index in range(size)])


def gather_high(shard, axis):
    for bit in range(3, bits_of(lax.axis_size("dp"))):
        shard = jnp.concatenate([shard, swap(shard, 1 << bit)], axis)
    return shard


def scatter_high(total, axis):
    for bit in reversed(range(3, bits_of(lax.axis_size("dp")))):
        kept, sent = jnp.split(total, 2, axis)
        total = low(wide(kept) + wide(swap(low(sent), 1 << bit)))
    return total


def low(array_in):
    return array_in.astype(jnp.bfloat16)


def wide(array_in):
    return array_in.astype(jnp.float32)


def rows_product(left, right):
    return lax.dot_general(
        left, right, (((1,), (1,)), ((), ())), preferred_element_type=jnp.float32
    )


TILE = 256
STRIP = 16
CHUNKS = 2
HALVES = 2
PIECES = 4


def shard_peer(mask):
    index = lax.axis_index("dp")
    return index + mask - 2 * mask * ((index // mask) % 2)


def low_place(mask):
    index = lax.axis_index("dp")
    total = 0
    for bit in (1, 2, 4):
        value = (index // bit) % 2
        total = total + bit * (1 - value if mask & bit else value)
    return total


ROUTE = {1: (1, 1), 2: (2, 2), 3: (1, 1), 4: (4, 4), 5: (1, 1), 6: (4, 2), 7: (1, 1)}
PLACES = {mask: place for place, mask in enumerate((0, 2, 4, 6, 1, 3, 5, 7))}


def column_blocks(width):
    return [
        (
            pl.ds(place * width, width),
            pl.ds(pl.multiple_of(low_place(mask) * width, width), width),
        )
        for mask, place in PLACES.items()
    ]


class ShardGather:
    def __init__(self, own, target, send_sem, recv_sem):
        self.own, self.target, self.send_sem, self.recv_sem = own, target, send_sem, recv_sem

    def copy(self, mask, half):
        route = ROUTE[mask][half]
        before = mask ^ route
        return pltpu.make_async_remote_copy(
            src_ref=self.target(PLACES[before], half) if before else self.own(half),
            dst_ref=self.target(PLACES[mask], half),
            send_sem=self.send_sem.at[mask - 1, half],
            recv_sem=self.recv_sem.at[mask - 1, half],
            device_id={"dp": shard_peer(route)},
            device_id_type=pl.DeviceIdType.MESH,
        )

    def start(self, *masks):
        for half in range(2):
            for mask in masks:
                self.copy(mask, half).start()

    def arrive(self, mask, halves=(0, 1)):
        for half in halves:
            self.copy(mask, half).wait_recv()
            for after, route in ROUTE.items():
                if after != mask and after ^ route[half] == mask:
                    self.copy(after, half).start()

    def sent(self):
        for mask in ROUTE:
            for half in range(2):
                self.copy(mask, half).wait_send()


def row_halves(buffer, height):
    def target(place, half):
        return buffer.at[pl.ds(place * height + half * (height // 2), height // 2), :]

    return target


def column_halves(buffer, width):
    height = buffer.shape[0] // 2

    def target(place, half):
        return buffer.at[pl.ds(half * height, height), pl.ds(place * width, width)]

    return target


def own_halves(shard):
    height = shard.shape[0] // 2
    return lambda half: shard.at[pl.ds(half * height, height), :]


def greet(line_devices):
    barrier = pltpu.get_barrier_semaphore()
    for mask in (1, 2, 4):
        pl.semaphore_signal(
            barrier,
            inc=1,
            device_id={"dp": shard_peer(mask)},
            device_id_type=pl.DeviceIdType.MESH,
        )
    for there, index in line_devices:

        @pl.when(there)
        def _():
            pl.semaphore_signal(
                barrier,
                inc=1,
                device_id={"tensor": index},
                device_id_type=pl.DeviceIdType.MESH,
            )


def turned_rows(row):
    return jnp.broadcast_to(row, (128, row.shape[1])).T


def column_sums(values):
    total = values[:, :128]
    for first in range(128, values.shape[1], 128):
        total = total + values[:, first : first + 128]
    return jnp.sum(total.T, 0, keepdims=True)


def ahead_of(values, first_key, first_query):
    key = first_key + lax.broadcasted_iota(jnp.int32, values.shape, 0)
    query = first_query + lax.broadcasted_iota(jnp.int32, values.shape, 1)
    return key > query


def head_span(head):
    return pl.ds(pl.multiple_of(head * 128, 128), 128)


def each(count, body):
    def step(index, carry):
        body(index)
        return carry

    lax.fori_loop(0, count, step, 0)


def front_kernel(
    size,
    tokens_hbm,
    query_hbm,
    key_hbm,
    value_hbm,
    output_hbm,
    gate_hbm,
    gain_hbm,
    positions,
    frequency,
    rows_out,
    attention_out,
    output_out,
    gate_out,
    attended_out,
    query_rot_out,
    key_rot_out,
    value_out,
    query_hat_out,
    key_hat_out,
    cosine_out,
    sine_out,
    stats,
    query_scale,
    key_scale,
    attention_scale,
    feedforward_scale,
    rows,
    weight,
    projected,
    gain,
    cosine,
    sine,
    squares,
    query_rot,
    key_rot,
    value,
    query_hat,
    key_hat,
    attended,
    load_sem,
    store_sem,
    hand_send,
    hand_recv,
    shard_send,
    shard_recv,
    square_send,
    square_recv,
):
    me = lax.axis_index("tensor")
    last = size - 1
    own_rows, model_width = rows.shape[1:]
    piece_rows = own_rows // PIECES
    local_width = query_hbm.shape[1]
    heads = local_width // 128
    everyone = True
    greet([(everyone, lax.rem(me + offset, size)) for offset in range(1, size)])
    block = model_width // 8
    token_loads = [
        pltpu.make_async_copy(
            tokens_hbm.at[:, natural], rows.at[me, :, here], load_sem.at[0, place]
        )
        for place, (here, natural) in enumerate(column_blocks(block))
    ]
    shard_rows = pl.ds(0, query_hbm.shape[0])
    loads = [
        pltpu.make_async_copy(source, target, load_sem.at[1, place])
        for place, (source, target) in enumerate(
            (
                (query_hbm, weight.at[shard_rows, pl.ds(0, local_width)]),
                (key_hbm, weight.at[shard_rows, pl.ds(local_width, local_width)]),
                (value_hbm, weight.at[shard_rows, pl.ds(2 * local_width, local_width)]),
                (gain_hbm, gain.at[pl.ds(0, gain_hbm.shape[0]), :]),
                (output_hbm, output_out.at[:, pl.ds(0, output_hbm.shape[1])]),
                (gate_hbm, gate_out.at[pl.ds(0, gate_hbm.shape[0]), :]),
            )
        )
    ]
    for copy in token_loads + loads:
        copy.start()
    attention_target = row_halves(weight, query_hbm.shape[0])
    attention_flow, output_flow, gate_flow, gain_flow = (
        ShardGather(own, target, shard_send.at[kind], shard_recv.at[kind])
        for kind, (own, target) in enumerate(
            (
                (functools.partial(attention_target, 0), attention_target),
                (own_halves(output_hbm), column_halves(output_out, output_hbm.shape[1])),
                (own_halves(gate_hbm), row_halves(gate_out, gate_hbm.shape[0])),
                (own_halves(gain_hbm), row_halves(gain, gain_hbm.shape[0])),
            )
        )
    )
    pl.semaphore_wait(pltpu.get_barrier_semaphore(), 3 + size - 1)

    def away(way):
        return me if way == 0 else last - me

    def hand_copy(hop, piece, way, origin):
        here = rows.at[origin, pl.ds(piece * piece_rows, piece_rows)]
        return pltpu.make_async_remote_copy(
            src_ref=here,
            dst_ref=here,
            send_sem=hand_send.at[way, hop - 1, piece],
            recv_sem=hand_recv.at[way, hop - 1, piece],
            device_id={"tensor": me + 1 - 2 * way},
            device_id_type=pl.DeviceIdType.MESH,
        )

    for copy in token_loads:
        copy.wait()
    for piece in range(PIECES):
        for way in range(2):

            @pl.when(away(1 - way) >= 1)
            def _():
                hand_copy(1, piece, way, me).start()

        if piece == 0:
            for copy in loads[:3]:
                copy.wait()
            attention_flow.start(2, 4, 1)
            gain_flow.start(2, 4, 1)

    def hand_on(hop, piece):
        for way in range(2):

            @pl.when(away(way) >= hop)
            def _():
                origin = me - hop if way == 0 else me + hop
                hand_copy(hop, piece, way, origin).wait_recv()
                if hop < size - 1:

                    @pl.when(away(1 - way) >= 1)
                    def _():
                        hand_copy(hop + 1, piece, way, origin).start()

    def row_store(origin):
        return pltpu.make_async_copy(rows.at[origin], rows_out.at[origin], store_sem.at[0, origin])

    whole_stores = [
        pltpu.make_async_copy(source, target, store_sem.at[1 + place // size, place % size])
        for place, (source, target) in enumerate(
            (
                (weight, attention_out),
                (cosine, cosine_out),
                (sine, sine_out),
                (query_hat, query_hat_out),
                (key_hat, key_hat_out),
                (query_rot, query_rot_out),
                (key_rot, key_rot_out),
                (value, value_out),
                (attended, attended_out),
            )
        )
    ]

    def span_of(origin):
        return pl.ds(pl.multiple_of(origin * own_rows, own_rows), own_rows)

    def square_copy(offset, origin):
        return pltpu.make_async_remote_copy(
            src_ref=squares.at[me, origin],
            dst_ref=squares.at[me, origin],
            send_sem=square_send.at[offset - 1, origin],
            recv_sem=square_recv.at[offset - 1, origin],
            device_id={"tensor": lax.rem(me + offset, size)},
            device_id_type=pl.DeviceIdType.MESH,
        )

    def project(origin):
        def step(index):
            columns = pl.ds(pl.multiple_of(index * TILE, TILE), TILE)
            projected[origin, :, columns] = jnp.dot(
                rows[origin], weight[:, columns], preferred_element_type=jnp.float32
            )

        row_store(origin).start()
        each(weight.shape[1] // TILE, step)
        queries = projected[origin, :, pl.ds(0, local_width)]
        keys = projected[origin, :, pl.ds(local_width, local_width)]
        squares[me, origin, pl.ds(0, 8), :] = jnp.concatenate(
            [
                column_sums(queries * queries),
                column_sums(keys * keys),
                jnp.zeros((6, own_rows), jnp.float32),
            ],
            0,
        )
        for offset in range(1, size):
            square_copy(offset, origin).start()

    def project_from(hop, way):
        @pl.when(away(way) >= hop)
        def _():
            project(me - hop if way == 0 else me + hop)

    def normalize(origin):
        for offset in range(1, size):
            square_copy(offset, origin).wait_recv()
        total = squares[0, origin]
        for device in range(1, size):
            total = total + squares[device, origin]
        inverse = lax.rsqrt(total / model_width + EPS)
        here = span_of(origin)
        stats[pl.ds(heads, 2), here] = inverse[:2]
        for kind, (hat, rot, scale) in enumerate(
            ((query_hat, query_rot, query_scale), (key_hat, key_rot, key_scale))
        ):
            column = turned_rows(inverse[kind : kind + 1])

            def step(head):
                span = head_span(head)
                source = head_span(head + kind * heads)
                normalized = projected[origin, :, source] * column
                hat[here, span] = low(normalized)
                scaled = normalized * scale[pl.ds(head, 1), :]
                rot[here, span] = low(
                    scaled * cosine[here, :] + pltpu.roll(scaled, 64, 1) * sine[here, :]
                )

            each(heads, step)
        value[here, :] = low(projected[origin, :, pl.ds(2 * local_width, local_width)])

    def tables():
        for origin in range(size):
            here = pl.ds(origin * own_rows, own_rows)
            angles = turned_rows(wide(positions[pl.ds(origin, 1), :])) * frequency[...]
            cosine[here, :] = jnp.cos(angles)
            lane = lax.broadcasted_iota(jnp.int32, angles.shape, 1)
            sine[here, :] = jnp.where(lane < 64, -1.0, 1.0) * jnp.sin(angles)

    def scales():
        for kind, scale in enumerate((query_scale, key_scale)):
            total = wide(gain[pl.ds(0, 16), :])
            for place in range(1, 8):
                total = total + wide(gain[pl.ds(place * gain_hbm.shape[0], 16), :])
            scale[...] = jnp.concatenate(
                [total[kind * heads : (kind + 1) * heads], jnp.zeros((8 - heads, 128), jnp.float32)],
                0,
            )
        for place in range(8):
            lines = wide(gain[pl.ds(place * gain_hbm.shape[0], 16), :])
            for kind, scale in enumerate((attention_scale, feedforward_scale)):
                for line in range(block // 128):
                    at = 2 * heads + kind * (block // 128) + line
                    scale[:, pl.ds(place * block + line * 128, 128)] = lines[at : at + 1]

    def attend(origin):
        count = (origin + 1) * own_rows
        here = pl.ds(origin * own_rows, own_rows)

        def step(head):
            span = head_span(head)
            scores = rows_product(key_rot[pl.ds(0, count), span], query_rot[here, span])
            scores = scores * (128**-0.5)
            near = scores[origin * own_rows :]
            near = jnp.where(ahead_of(near, 0, 0), MASKED, near)
            scores = jnp.concatenate([scores[: origin * own_rows], near], 0) if origin else near
            row_max = jnp.max(scores, 0, keepdims=True)
            exponent = jnp.exp(scores - row_max)
            row_total = jnp.sum(exponent, 0, keepdims=True)
            low_probs = low(exponent * (1.0 / row_total))
            result = jnp.dot(
                value[pl.ds(0, count), span].T, low_probs, preferred_element_type=jnp.float32
            )
            attended[here, span] = low(result.T)
            stats[pl.ds(head, 1), here] = row_max + jnp.log(row_total)

        each(heads, step)

    def turns(beat):
        if beat == 1:
            tables()
            for copy in whole_stores[1:3]:
                copy.start()
        elif beat == 2:
            attention_flow.arrive(2, (0,))
            attention_flow.arrive(4, (0,))
        elif beat == 3:
            attention_flow.arrive(2, (1,))
            attention_flow.arrive(4, (1,))
            output_flow.start(2, 4, 1)
            gain_flow.arrive(2)
            gain_flow.arrive(4)
        elif beat == 5:
            attention_flow.arrive(6)
            gate_flow.start(2, 4, 1)
            gain_flow.arrive(6)
        elif beat == 6:
            output_flow.arrive(2)
            output_flow.arrive(4)
            for mask in (1, 3, 5, 7):
                attention_flow.arrive(mask)
            whole_stores[0].start()
            project(me)
        elif beat == 7:
            project_from(1, 0)
        elif beat == 8:
            project_from(1, 1)
            output_flow.arrive(6)
            loads[3].wait()
            for mask in (1, 3, 5, 7):
                gain_flow.arrive(mask)
            scales()
        elif beat == 9:
            gate_flow.arrive(2, (0,))
            gate_flow.arrive(4, (0,))
        elif beat == 10:
            project_from(2, 0)
        elif beat == 11:
            project_from(2, 1)
            gate_flow.arrive(2, (1,))
            gate_flow.arrive(4, (1,))

    for beat in range(1, (size - 1) * PIECES + 1):
        hand_on((beat - 1) // PIECES + 1, (beat - 1) % PIECES)
        turns(beat)
    project_from(3, 0)
    project_from(3, 1)
    gate_flow.arrive(6)
    for offset in range(size):
        normalize(lax.rem(me + offset, size))
    for copy in whole_stores[3:8]:
        copy.start()
    for origin in range(size):
        attend(origin)
    whole_stores[8].start()
    for flow in (output_flow, gate_flow):
        for mask in (1, 3, 5, 7):
            flow.arrive(mask)
    for hop in range(1, size):
        for way in range(2):

            @pl.when(jnp.logical_and(away(way) >= hop - 1, away(1 - way) >= 1))
            def _():
                for piece in range(PIECES):
                    hand_copy(hop, piece, way, 0).wait_send()

    for flow in (attention_flow, output_flow, gate_flow, gain_flow):
        flow.sent()
    for offset in range(1, size):
        for origin in range(size):
            square_copy(offset, origin).wait_send()
    for copy in loads[4:]:
        copy.wait()
    for origin in range(size):
        row_store(origin).wait()
    for copy in whole_stores:
        copy.wait()


def front(
    tokens_grouped,
    query_shard,
    key_shard,
    value_shard,
    output_shard,
    gate_shard,
    gain_shard,
    positions,
):
    size = lax.axis_size("tensor")
    own_rows, model_width = tokens_grouped.shape
    local_width = query_shard.shape[1]
    group_rows = size * own_rows
    low_type, wide_type = jnp.bfloat16, jnp.float32
    anywhere = pl.BlockSpec(memory_space=pl.ANY)
    inside = pl.BlockSpec(memory_space=pltpu.VMEM)
    dma = pltpu.SemaphoreType.DMA
    hands = (2, size - 1, PIECES)
    half_head = jnp.arange(128, dtype=jnp.float32) % 64
    frequency = (THETA ** (-(half_head * 2.0 / 128)))[None]

    def shape(dims, kind=low_type):
        return jax.ShapeDtypeStruct(dims, kind)

    local_rows = (group_rows, local_width)
    tables = (group_rows, 128)
    return pl.pallas_call(
        functools.partial(front_kernel, size),
        out_shape=[
            shape((size, own_rows, model_width)),
            shape((model_width, 3 * local_width)),
            shape((output_shard.shape[0], model_width)),
            shape((model_width, gate_shard.shape[1])),
            *[shape(local_rows)] * 6,
            *[shape(tables, wide_type)] * 2,
            shape((8, group_rows), wide_type),
            *[shape((8, 128), wide_type)] * 2,
            *[shape((1, model_width), wide_type)] * 2,
        ],
        in_specs=[anywhere] * 7 + [inside] * 2,
        out_specs=[anywhere] * 12 + [inside] * 5,
        scratch_shapes=[
            pltpu.VMEM((size, own_rows, model_width), low_type),
            pltpu.VMEM((model_width, 3 * local_width), low_type),
            pltpu.VMEM((size, own_rows, 3 * local_width), wide_type),
            pltpu.VMEM((8 * gain_shard.shape[0], gain_shard.shape[1]), low_type),
            pltpu.VMEM(tables, wide_type),
            pltpu.VMEM(tables, wide_type),
            pltpu.VMEM((size, size, 8, own_rows), wide_type),
            *[pltpu.VMEM(local_rows, low_type)] * 6,
            dma((2, 8)),
            dma((4, size)),
            dma(hands),
            dma(hands),
            dma((4, 7, 2)),
            dma((4, 7, 2)),
            dma((size - 1, size)),
            dma((size - 1, size)),
        ],
        compiler_params=pltpu.CompilerParams(
            collective_id=0, has_side_effects=True, vmem_limit_bytes=VMEM_BYTES
        ),
        cost_estimate=pl.CostEstimate(
            flops=6 * group_rows * model_width * local_width,
            bytes_accessed=32 << 20,
            transcendentals=0,
        ),
        name="front",
    )(
        tokens_grouped,
        query_shard,
        key_shard,
        value_shard,
        output_shard,
        gate_shard,
        gain_shard,
        positions.reshape(size, own_rows),
        frequency,
    )


class ShardSum:
    def __init__(self, near, far, corner, final, send_sem, recv_sem):
        self.near, self.far, self.corner, self.final = near, far, corner, final
        self.send_sem, self.recv_sem = send_sem, recv_sem

    def remote(self, source, target, place, route):
        return pltpu.make_async_remote_copy(
            src_ref=source,
            dst_ref=target,
            send_sem=self.send_sem.at[place],
            recv_sem=self.recv_sem.at[place],
            device_id={"dp": shard_peer(route)},
            device_id_type=pl.DeviceIdType.MESH,
        )

    def core_copy(self, place):
        return self.remote(self.far(place), self.near(place), place, 1)

    def corner_copy(self, half):
        return self.remote(self.near(3, half), self.corner(half), 4 + half, (4, 2)[half])

    def final_copy(self, way, half):
        return self.remote(
            self.near(1 + way, half), self.final(way, half), 6 + 2 * way + half, (2, 4)[way]
        )

    def far_terms(self, term):
        for place in (3, 1, 2, 0):
            term(4 + place, self.far(place), False)
            self.core_copy(place).start()

    def near_terms(self, term, allowed=None):
        for place in (3, 1, 2, 0):
            self.core_copy(place).wait_recv()
            term(place, self.near(place), True)
            if place == 3:
                if allowed is not None:
                    allowed()
                for half in range(2):
                    self.corner_copy(half).start()
            elif place:
                self.final_copy(place - 1, 2 - place).start()

    def take_corner(self):
        for half in range(2):
            self.corner_copy(half).wait_recv()
            add_into(self.near(1 + half, half), self.corner(half))
            self.final_copy(half, half).start()

    def take_final(self, target):
        for half in range(2):
            for way in range(2):
                self.final_copy(way, half).wait_recv()
            own, first, second = self.near(0, half), self.final(0, half), self.final(1, half)
            out = target(half)
            rows = own.shape[0]

            def step(index):
                span = pl.ds(pl.multiple_of(index * STRIP, STRIP), STRIP)
                out[span, :] = wide(own[span, :]) + wide(first[span, :]) + wide(second[span, :])

            each(rows // STRIP, step)

    def take_final_tiles(self, out):
        for half in range(2):
            for way in range(2):
                self.final_copy(way, half).wait_recv()
            own, first, second = self.near(0, half), self.final(0, half), self.final(1, half)
            rows = own.shape[0]

            def step(index):
                span = pl.ds(pl.multiple_of(index * TILE, TILE), TILE)
                value = wide(own[:, span]) + wide(first[:, span]) + wide(second[:, span])
                out[pl.ds(pl.multiple_of(index * 2 * rows + half * rows, STRIP), rows), :] = value

            each(own.shape[1] // TILE, step)

    def take_final_turned(self, out):
        for half in range(2):
            for way in range(2):
                self.final_copy(way, half).wait_recv()
            own, first, second = self.near(0, half), self.final(0, half), self.final(1, half)
            rows = own.shape[0]

            def step(index):
                span = pl.ds(pl.multiple_of(index * TILE, TILE), TILE)
                value = wide(own[:, span]) + wide(first[:, span]) + wide(second[:, span])
                out[span, pl.ds(half * rows, rows)] = value.T

            each(own.shape[1] // TILE, step)

    def sent(self, core=True):
        for place in range(4) if core else ():
            self.core_copy(place).wait_send()
        for half in range(2):
            self.corner_copy(half).wait_send()
            for way in range(2):
                self.final_copy(way, half).wait_send()


def add_into(target, source):
    def step(index, carry):
        span = pl.ds(pl.multiple_of(index * STRIP, STRIP), STRIP)
        target[span, :] = (wide(target[span, :]) + wide(source[span, :])).astype(target.dtype)
        return carry

    lax.fori_loop(0, target.shape[0] // STRIP, step, 0)


def product_term(left, right, tile):
    def term(place, target, adds):
        height = target.shape[0]
        turned = left(place, height).T

        def step(index, carry):
            columns = pl.ds(pl.multiple_of(index * tile, tile), tile)
            value = jnp.dot(turned, right(columns), preferred_element_type=jnp.float32)
            if adds:
                value = value + wide(target[:, columns])
            target[:, columns] = value.astype(target.dtype)
            return carry

        lax.fori_loop(0, target.shape[1] // tile, step, 0)

    return term


def stacked(buffer, first, height):
    def view(place, half=None):
        at = first + place * height
        if half is None:
            return buffer.at[pl.ds(at, height), :]
        return buffer.at[pl.ds(at + half * (height // 2), height // 2), :]

    return view


def middle_kernel(size, *refs):
    (
        attended_hbm,
        rows_hbm,
        cotangent_hbm,
        attention_scale,
        feedforward_scale,
        output_hbm,
        gate_hbm,
        up_hbm,
        down_hbm,
        mlp_out,
        inner_out,
        mixed_cot_out,
        branch_cot_out,
        block_out,
        grad_hidden_out,
        gate_grad_out,
        up_grad_out,
        attention_gain_out,
        feedforward_gain_out,
        attended,
        tokens,
        cotangent,
        output_weight,
        gate_weight,
        up_weight,
        down_weight,
        everyone,
        gate_act,
        up_act,
        inner,
        hidden,
        branch,
        arrived,
        partial,
        total,
        load_sem,
        store_sem,
        sum_send,
        sum_recv,
        hand_send,
        hand_recv,
        shard_send,
        shard_recv,
        grad_send,
        grad_recv,
        again_sem,
        shuffle_sem,
        free_sem,
    ) = refs
    me = lax.axis_index("tensor")
    last = size - 1
    chunk_rows, model_width = tokens.shape[1], tokens.shape[2]
    units = gate_weight.shape[1]
    half_rows = chunk_rows // HALVES
    all_rows = size * chunk_rows

    greet(((me < last, me + 1), (me > 0, me - 1)))
    first_loads = [
        pltpu.make_async_copy(source, target, load_sem.at[place])
        for place, (source, target) in enumerate(
            (
                (attended_hbm, attended),
                (output_hbm, output_weight),
                (rows_hbm.at[me], tokens),
                (gate_hbm, gate_weight),
                (up_hbm, up_weight.at[pl.ds(0, up_hbm.shape[0]), :]),
                (down_hbm, down_weight.at[:, pl.ds(0, down_hbm.shape[1])]),
            )
        )
    ]
    first_loads += [
        pltpu.make_async_copy(
            cotangent_hbm.at[pl.ds(chunk * chunk_rows, chunk_rows), natural],
            cotangent.at[chunk, :, here],
            shuffle_sem.at[chunk, place],
        )
        for chunk in range(CHUNKS)
        for place, (here, natural) in enumerate(column_blocks(model_width // 8))
    ]
    for copy in first_loads:
        copy.start()
    up_flow = ShardGather(
        own_halves(up_hbm),
        row_halves(up_weight, up_hbm.shape[0]),
        shard_send.at[0],
        shard_recv.at[0],
    )
    down_flow = ShardGather(
        own_halves(down_hbm),
        column_halves(down_weight, down_hbm.shape[1]),
        shard_send.at[1],
        shard_recv.at[1],
    )
    pl.semaphore_wait(
        pltpu.get_barrier_semaphore(), 3 + jnp.minimum(me, 1) + jnp.minimum(last - me, 1)
    )
    up_flow.start(2, 4, 1)
    down_flow.start(1)

    height = model_width // 8
    again = [
        pltpu.make_async_copy(
            mlp_out.at[chunk, origin],
            down_weight.at[pl.ds((chunk * size + origin) * chunk_rows, chunk_rows), :],
            again_sem.at[chunk, origin],
        )
        for chunk in range(CHUNKS)
        for origin in range(size)
    ]
    gate_grads, up_grads = (
        ShardSum(
            stacked(buffer, 0, height),
            stacked(down_weight, 4 * height, height),
            functools.partial(stacked(buffer, 4 * height, height), 0),
            stacked(buffer, 5 * height, height),
            grad_send.at[kind],
            grad_recv.at[kind],
        )
        for kind, buffer in enumerate((gate_weight, up_weight))
    )

    def rows_again(place, shard_width):
        return down_weight[pl.ds(0, CHUNKS * all_rows), pl.ds(place * shard_width, shard_width)]

    def grad_term(act):
        def columns_of(columns):
            return act[:, :, columns].reshape(CHUNKS * all_rows, 512)

        return product_term(rows_again, columns_of, 512)

    def weights_free():
        for place, mask in enumerate((1, 2, 4)):
            pl.semaphore_signal(
                free_sem.at[place],
                inc=1,
                device_id={"dp": shard_peer(mask)},
                device_id_type=pl.DeviceIdType.MESH,
            )
        for copy in again:
            copy.start()

    def neighbours_free():
        pl.semaphore_wait(free_sem.at[1], 1)
        pl.semaphore_wait(free_sem.at[2], 1)

    def grad_turns(tick, half):
        if (tick, half) == (21, 0):
            for copy in again:
                copy.wait()
            pl.semaphore_wait(free_sem.at[0], 1)
            gate_grads.far_terms(grad_term(gate_act))
        elif (tick, half) == (21, 1):
            gate_grads.near_terms(grad_term(gate_act), neighbours_free)
        elif (tick, half) == (22, 0):
            for place in range(4):
                gate_grads.core_copy(place).wait_send()
            up_grads.far_terms(grad_term(up_act))
        elif (tick, half) == (22, 1):
            up_grads.near_terms(grad_term(up_act))
        elif (tick, half) == (23, 1):
            gate_grads.take_corner()
        elif (tick, half) == (25, 1):
            up_grads.take_corner()
        elif (tick, half) == (27, 1):
            gate_grads.take_final(lambda half: hidden.at[half])
            for half in range(HALVES):
                store(6, half).start()
            for half in range(HALVES):
                store(6, half).wait()

    def turns(tick, half):
        if (tick, half) == (2, 1):
            up_flow.arrive(2, (0,))
            up_flow.arrive(4, (0,))
        elif (tick, half) == (3, 0):
            up_flow.arrive(2, (1,))
            up_flow.arrive(4, (1,))
            down_flow.start(2, 4)
        elif (tick, half) == (4, 1):
            up_flow.arrive(6)
        elif (tick, half) == (5, 0):
            down_flow.arrive(2, (0,))
            down_flow.arrive(4, (0,))
        elif (tick, half) == (6, 0):
            down_flow.arrive(2, (1,))
            down_flow.arrive(4, (1,))
        elif (tick, half) == (7, 0):
            down_flow.arrive(6)

    attention_gain_out[...] = jnp.zeros_like(attention_gain_out)
    feedforward_gain_out[...] = jnp.zeros_like(feedforward_gain_out)

    def half_span(half):
        return pl.ds(half * half_rows, half_rows)

    def strips(half, body):
        def step(index, carry):
            body(
                pl.ds(pl.multiple_of(half * half_rows + index * STRIP, STRIP), STRIP),
                pl.ds(pl.multiple_of(index * STRIP, STRIP), STRIP),
            )
            return carry

        lax.fori_loop(0, half_rows // STRIP, step, 0)

    def sum_copy(chunk, step, half, way, dest):
        return pltpu.make_async_remote_copy(
            src_ref=partial.at[chunk, dest, half_span(half)],
            dst_ref=arrived.at[way, chunk, step - 1, half_span(half)],
            send_sem=sum_send.at[way, chunk, step - 1, half],
            recv_sem=sum_recv.at[way, chunk, step - 1, half],
            device_id={"tensor": me + 1 - 2 * way},
            device_id_type=pl.DeviceIdType.MESH,
        )

    def hand_copy(chunk, hop, half, way, origin):
        rows = everyone.at[origin, chunk, half_span(half)]
        return pltpu.make_async_remote_copy(
            src_ref=rows,
            dst_ref=rows,
            send_sem=hand_send.at[way, chunk, hop - 1, half],
            recv_sem=hand_recv.at[way, chunk, hop - 1, half],
            device_id={"tensor": me + 1 - 2 * way},
            device_id_type=pl.DeviceIdType.MESH,
        )

    def away(way):
        return me if way == 0 else last - me

    def sum_step(chunk, step, half):
        for way in range(2):
            distance = away(way)

            @pl.when(distance <= step - 1)
            def _():
                dest = me + size - step if way == 0 else me - size + step
                if step > 1:

                    @pl.when(distance >= 1)
                    def _():
                        sum_copy(chunk, step - 1, half, way, dest).wait_recv()

                        def add(rows, _):
                            partial[chunk, dest, rows] = low(
                                wide(partial[chunk, dest, rows])
                                + wide(arrived[way, chunk, step - 2, rows])
                            )

                        strips(half, add)

                sum_copy(chunk, step, half, way, dest).start()

    def sum_end(chunk, half):
        def begin(rows, here):
            total[here] = wide(partial[chunk, me, rows])

        strips(half, begin)
        for way in range(2):

            @pl.when(away(way) >= 1)
            def _():
                sum_copy(chunk, size - 1, half, way, me).wait_recv()

                def add(rows, here):
                    total[here] = total[here] + wide(arrived[way, chunk, size - 2, rows])

                strips(half, add)

    def sum_sent(chunk):
        for step in range(1, size):
            for way in range(2):

                @pl.when(away(way) <= step - 1)
                def _():
                    for half in range(HALVES):
                        sum_copy(chunk, step, half, way, 0).wait_send()

    def hand_first(chunk, half):
        for way in range(2):

            @pl.when(away(1 - way) >= 1)
            def _():
                hand_copy(chunk, 1, half, way, me).start()

    def hand_on(chunk, hop, half):
        for way in range(2):

            @pl.when(away(way) >= hop)
            def _():
                origin = me - hop if way == 0 else me + hop
                hand_copy(chunk, hop, half, way, origin).wait_recv()
                if hop < size - 1:

                    @pl.when(away(1 - way) >= 1)
                    def _():
                        hand_copy(chunk, hop + 1, half, way, origin).start()

    def hand_sent(chunk):
        for hop in range(1, size):
            for way in range(2):

                @pl.when(jnp.logical_and(away(way) >= hop - 1, away(1 - way) >= 1))
                def _():
                    for half in range(HALVES):
                        hand_copy(chunk, hop, half, way, 0).wait_send()

    def inverse_rms(values):
        return lax.rsqrt(jnp.mean(values * values, -1, keepdims=True) + EPS)

    def fold(values):
        return values[:8] + values[8:]

    def own_rows(chunk, stage, half):
        def after_branch(rows, here):
            value = total[here]
            branch[chunk, rows] = value
            state = wide(tokens[chunk, rows]) + value * inverse_rms(value) * attention_scale[...]
            hidden[chunk, rows] = state
            everyone[me, chunk, rows] = low(state)

        def after_mixed(rows, here):
            value = total[here]
            inverse = inverse_rms(value)
            normalized = value * inverse
            hidden[chunk, rows] = hidden[chunk, rows] + normalized * feedforward_scale[...]
            grad = wide(cotangent[chunk, rows])
            feedforward_gain_out[...] += fold(grad * normalized)
            everyone[me, chunk, rows] = low(
                norm_backward(grad, normalized, inverse, feedforward_scale[...])
            )

        def after_gradient(rows, here):
            grad = total[here] + wide(cotangent[chunk, rows])
            value = branch[chunk, rows]
            inverse = inverse_rms(value)
            normalized = value * inverse
            branch[chunk, rows] = grad
            attention_gain_out[...] += fold(grad * normalized)
            everyone[me, chunk, rows] = low(
                norm_backward(grad, normalized, inverse, attention_scale[...])
            )

        strips(half, (after_branch, after_mixed, after_gradient)[stage])

    def gathered(chunk):
        return everyone[:, chunk].reshape(all_rows, model_width)

    def tiles(first, end, body):
        def step(index, carry):
            body(pl.ds(pl.multiple_of(index * TILE, TILE), TILE))
            return carry

        lax.fori_loop(first, end, step, 0)

    def store(kind, chunk):
        source, target = (
            (everyone.at[:, chunk], mlp_out.at[chunk]),
            (inner, inner_out.at[chunk]),
            (everyone.at[:, chunk], mixed_cot_out.at[chunk]),
            (everyone.at[:, chunk], branch_cot_out.at[:, chunk]),
            None,
            (branch.at[chunk], grad_hidden_out.at[chunk]),
            (hidden.at[chunk], gate_grad_out.at[pl.ds(chunk * chunk_rows, chunk_rows), :]),
            (hidden.at[chunk], up_grad_out.at[pl.ds(chunk * chunk_rows, chunk_rows), :]),
        )[kind]
        return pltpu.make_async_copy(source, target, store_sem.at[kind, chunk])

    def block_stores(chunk):
        return [
            pltpu.make_async_copy(
                hidden.at[chunk, :, here],
                block_out.at[pl.ds(chunk * chunk_rows, chunk_rows), natural],
                shuffle_sem.at[chunk, place],
            )
            for place, (here, natural) in enumerate(column_blocks(model_width // 8))
        ]

    def put_partial(chunk, columns, values):
        partial[chunk, :, :, columns] = low(values).reshape(size, chunk_rows, TILE)

    def branch_terms(chunk):
        def tile(columns):
            rows = attended[:, chunk].reshape(all_rows, attended.shape[-1])
            put_partial(
                chunk,
                columns,
                jnp.dot(rows, output_weight[:, columns], preferred_element_type=jnp.float32),
            )

        tiles(0, model_width // TILE, tile)

    def gate_tile(chunk):
        def tile(columns):
            rows = gathered(chunk)
            gate = jnp.dot(rows, gate_weight[:, columns], preferred_element_type=jnp.float32)
            up = jnp.dot(rows, up_weight[:, columns], preferred_element_type=jnp.float32)
            gate_act[chunk, :, columns] = low(gate)
            up_act[chunk, :, columns] = low(up)
            inner[:, columns] = low(gate * jax.nn.sigmoid(gate) * up)

        return tile

    def down_tile(chunk):
        def tile(columns):
            put_partial(
                chunk,
                columns,
                jnp.dot(inner[...], down_weight[:, columns], preferred_element_type=jnp.float32),
            )

        return tile

    def grad_inner_tile(chunk):
        def tile(columns):
            grad = rows_product(gathered(chunk), down_weight[columns, :])
            gate = wide(gate_act[chunk, :, columns])
            up = wide(up_act[chunk, :, columns])
            sigmoid = jax.nn.sigmoid(gate)
            gate_act[chunk, :, columns] = low(
                grad * up * sigmoid * (1.0 + gate * (1.0 - sigmoid))
            )
            up_act[chunk, :, columns] = low(grad * gate * sigmoid)

        return tile

    def grad_input_tile(chunk):
        def tile(columns):
            put_partial(
                chunk,
                columns,
                rows_product(gate_act[chunk], gate_weight[columns, :])
                + rows_product(up_act[chunk], up_weight[columns, :]),
            )

        return tile

    unit_tiles, width_tiles = units // TILE, model_width // TILE

    def forward_piece(chunk, piece):
        if piece == 0:
            if chunk == 0:
                for mask in (1, 3, 5, 7):
                    up_flow.arrive(mask)
                for copy in first_loads[3:6]:
                    copy.wait()
            store(0, chunk).start()
            tiles(0, unit_tiles // 2, gate_tile(chunk))
        elif piece == 1:
            tiles(unit_tiles // 2, unit_tiles, gate_tile(chunk))
            store(1, chunk).start()
            sum_sent(chunk)
            hand_sent(chunk)
        else:
            if chunk == 0:
                for mask in (1, 3, 5, 7):
                    down_flow.arrive(mask)
            tiles(0, width_tiles, down_tile(chunk))
            store(0, chunk).wait()
            store(1, chunk).wait()

    def backward_piece(chunk, piece):
        if piece == 0:
            store(2, chunk).start()
            for copy in block_stores(chunk):
                copy.start()
            tiles(0, unit_tiles, grad_inner_tile(chunk))
        elif piece == 1:
            sum_sent(chunk)
            hand_sent(chunk)
            tiles(0, width_tiles // 2, grad_input_tile(chunk))
        else:
            tiles(width_tiles // 2, width_tiles, grad_input_tile(chunk))
            store(2, chunk).wait()
            for copy in block_stores(chunk):
                copy.wait()
            if chunk == CHUNKS - 1:
                up_flow.sent()
                down_flow.sent()
                weights_free()

    def end_piece(chunk, piece):
        if piece == 0:
            store(3, chunk).start()
            store(5, chunk).start()

    first_loads[0].wait()
    first_loads[1].wait()
    branch_terms(0)
    first_loads[2].wait()
    for copy in first_loads[6:]:
        copy.wait()
    bases = {
        (chunk, stage): (CHUNKS * stage + chunk) * size
        for stage in range(3)
        for chunk in range(CHUNKS)
    }
    ticks = max(bases.values()) + 2 * size
    for tick in range(1, ticks + 1):
        for half in range(HALVES):
            for (chunk, stage), base in bases.items():
                at = tick - base
                if size < at < 2 * size:
                    hand_on(chunk, at - size, half)
            for (chunk, stage), base in bases.items():
                at = tick - base
                if 1 <= at < size:
                    sum_step(chunk, at, half)
                elif at == size:
                    sum_end(chunk, half)
                    own_rows(chunk, stage, half)
                    hand_first(chunk, half)
            turns(tick, half)
            if tick == 1 and half == 1:
                branch_terms(1)
            for (chunk, stage), base in bases.items():
                piece = (tick - base - 2 * size + 1) * HALVES + half - 1
                if 0 <= piece < 3:
                    (forward_piece, backward_piece, end_piece)[stage](chunk, piece)
            grad_turns(tick, half)
    up_grads.take_final(lambda half: hidden.at[half])
    for half in range(HALVES):
        store(7, half).start()
    gate_grads.sent(False)
    up_grads.sent()
    for chunk in range(CHUNKS):
        sum_sent(chunk)
        hand_sent(chunk)
        store(3, chunk).wait()
        store(5, chunk).wait()
        store(7, chunk).wait()


def middle(
    attended,
    rows_all,
    cotangent_grouped,
    attention_scale,
    feedforward_scale,
    output_full,
    gate_full,
    up_shard,
    down_shard,
):
    size = lax.axis_size("tensor")
    own_rows, model_width = cotangent_grouped.shape
    chunk_rows = own_rows // CHUNKS
    all_rows = size * chunk_rows
    half_rows = chunk_rows // HALVES
    heads_width = attended.shape[1]
    units = gate_full.shape[1]
    chunked = (CHUNKS, chunk_rows, model_width)
    lined = (CHUNKS, size, chunk_rows, model_width)
    low_type, wide_type = jnp.bfloat16, jnp.float32

    def shape(dims, kind=low_type):
        return jax.ShapeDtypeStruct(dims, kind)

    anywhere = pl.BlockSpec(memory_space=pl.ANY)
    inside = pl.BlockSpec(memory_space=pltpu.VMEM)
    dma = pltpu.SemaphoreType.DMA
    flops = 2 * CHUNKS * all_rows * model_width * (2 * heads_width + 6 * units)
    outs = pl.pallas_call(
        functools.partial(middle_kernel, size),
        out_shape=[
            shape(lined),
            shape((CHUNKS, all_rows, units)),
            shape(lined),
            shape((size, CHUNKS, chunk_rows, model_width)),
            shape((own_rows, model_width), wide_type),
            shape(chunked, wide_type),
            shape((model_width // 8, units), wide_type),
            shape((model_width // 8, units), wide_type),
            shape((8, model_width), wide_type),
            shape((8, model_width), wide_type),
        ],
        in_specs=[anywhere] * 3 + [inside] * 2 + [anywhere] * 4,
        out_specs=[anywhere] * 8 + [inside] * 2,
        scratch_shapes=[
            pltpu.VMEM((size, CHUNKS, chunk_rows, heads_width), low_type),
            pltpu.VMEM(chunked, low_type),
            pltpu.VMEM(chunked, low_type),
            pltpu.VMEM((heads_width, model_width), low_type),
            pltpu.VMEM((model_width, units), low_type),
            pltpu.VMEM((model_width, units), low_type),
            pltpu.VMEM((units, model_width), low_type),
            pltpu.VMEM((size, CHUNKS, chunk_rows, model_width), low_type),
            pltpu.VMEM((CHUNKS, all_rows, units), low_type),
            pltpu.VMEM((CHUNKS, all_rows, units), low_type),
            pltpu.VMEM((all_rows, units), low_type),
            pltpu.VMEM(chunked, wide_type),
            pltpu.VMEM(chunked, wide_type),
            pltpu.VMEM((2, CHUNKS, size - 1, chunk_rows, model_width), low_type),
            pltpu.VMEM(lined, low_type),
            pltpu.VMEM((half_rows, model_width), wide_type),
            dma((6,)),
            dma((8, CHUNKS)),
            dma((2, CHUNKS, size - 1, HALVES)),
            dma((2, CHUNKS, size - 1, HALVES)),
            dma((2, CHUNKS, size - 1, HALVES)),
            dma((2, CHUNKS, size - 1, HALVES)),
            dma((2, 7, 2)),
            dma((2, 7, 2)),
            dma((2, 10)),
            dma((2, 10)),
            dma((CHUNKS, size)),
            dma((CHUNKS, 8)),
            pltpu.SemaphoreType.REGULAR((3,)),
        ],
        compiler_params=pltpu.CompilerParams(
            collective_id=1, has_side_effects=True, vmem_limit_bytes=VMEM_BYTES
        ),
        cost_estimate=pl.CostEstimate(
            flops=flops, bytes_accessed=64 << 20, transcendentals=0
        ),
        name="middle",
    )(
        attended.reshape(size, CHUNKS, chunk_rows, heads_width),
        rows_all.reshape(size, *chunked),
        cotangent_grouped,
        attention_scale,
        feedforward_scale,
        output_full,
        gate_full,
        up_shard,
        down_shard,
    )
    rows = CHUNKS * all_rows
    return (
        outs[1].reshape(rows, units),
        outs[2].reshape(rows, model_width),
        outs[3].reshape(rows, model_width),
        outs[4],
        outs[5].reshape(own_rows, model_width),
        *outs[6:],
    )


def turn_kernel(
    size,
    branch_cot_hbm,
    output_hbm,
    query_rot_hbm,
    key_rot_hbm,
    value_hbm,
    query_hat_hbm,
    key_hat_hbm,
    cosine_hbm,
    sine_hbm,
    stats,
    query_scale,
    key_scale,
    attention_gain,
    feedforward_gain,
    grad_out,
    gain_terms,
    branch_cot,
    output_weight,
    query_rot,
    key_rot,
    value,
    query_hat,
    key_hat,
    cosine,
    sine,
    grad_attended,
    grad_query,
    grad_key,
    grad_value,
    scaled_query,
    scaled_key,
    products,
    shared,
    grad,
    load_sem,
    store_sem,
    share_send,
    share_recv,
):
    me = lax.axis_index("tensor")
    group_rows, model_width = branch_cot.shape
    local_width = query_rot.shape[1]
    heads = local_width // 128
    own_rows = group_rows // size
    block = model_width // 8
    barrier = pltpu.get_barrier_semaphore()
    for offset in range(1, size):
        pl.semaphore_signal(
            barrier,
            inc=1,
            device_id={"tensor": lax.rem(me + offset, size)},
            device_id_type=pl.DeviceIdType.MESH,
        )
    loads = [
        pltpu.make_async_copy(source, target, load_sem.at[place])
        for place, (source, target) in enumerate(
            (
                (output_hbm, output_weight),
                (branch_cot_hbm, branch_cot),
                (key_rot_hbm, key_rot),
                (query_rot_hbm, query_rot),
                (value_hbm, value),
                (query_hat_hbm, query_hat),
                (key_hat_hbm, key_hat),
                (cosine_hbm, cosine),
                (sine_hbm, sine),
            )
        )
    ]
    for copy in loads:
        copy.start()
    gain_terms[...] = jnp.zeros_like(gain_terms)
    products[...] = jnp.zeros_like(products)
    for copy in loads[:2]:
        copy.wait()

    def step_attended(index):
        here = pl.ds(pl.multiple_of(index * own_rows, own_rows), own_rows)
        for first in range(0, local_width, TILE):
            columns = pl.ds(first, TILE)
            grad_attended[here, columns] = low(
                rows_product(branch_cot[here, :], output_weight[columns, :])
            )

    each(size, step_attended)
    for copy in loads[2:]:
        copy.wait()
    score_scale = 128**-0.5

    def queries_block(origin, span):
        count = (origin + 1) * own_rows
        here = pl.ds(origin * own_rows, own_rows)
        keys = key_rot[pl.ds(0, count), span]
        queries = query_rot[here, span]
        grad_rows = grad_attended[here, span]
        return count, here, keys, queries, grad_rows

    def step_head(head):
        span = head_span(head)
        for origin in reversed(range(size)):
            count, here, keys, queries, grad_rows = queries_block(origin, span)
            scores = rows_product(keys, queries) * score_scale
            probs = jnp.exp(scores - stats[pl.ds(head, 1), here])
            near = probs[origin * own_rows :]
            near = jnp.where(ahead_of(near, 0, 0), 0.0, near)
            probs = jnp.concatenate([probs[: origin * own_rows], near], 0) if origin else near
            grad_probs = rows_product(value[pl.ds(0, count), span], grad_rows)
            delta = jnp.sum(grad_probs * probs, 0, keepdims=True)
            grad_scores = low(probs * (grad_probs - delta))
            for_values = jnp.dot(low(probs), grad_rows, preferred_element_type=jnp.float32)
            for_keys = jnp.dot(grad_scores, queries, preferred_element_type=jnp.float32)
            for_queries = jnp.dot(keys.T, grad_scores, preferred_element_type=jnp.float32)
            grad_query[here, :] = (for_queries * score_scale).T
            if origin == size - 1:
                grad_value[...] = for_values
                grad_key[...] = for_keys
            else:
                grad_value[pl.ds(0, count), :] += for_values
                grad_key[pl.ds(0, count), :] += for_keys
        grad[:, head_span(head + 2 * heads)] = low(grad_value[...])
        for kind, (source, factor, hat, scale, scaled) in enumerate(
            (
                (grad_query, 1.0, query_hat, query_scale, scaled_query),
                (grad_key, score_scale, key_hat, key_scale, scaled_key),
            )
        ):
            rotated = wide(low(source[...] * factor))
            normal = rotated * cosine[...] - pltpu.roll(rotated, 64, 1) * sine[...]
            hats = wide(hat[:, span])
            gain_terms[pl.ds(kind * heads + head, 1), :] = jnp.sum(
                normal * hats, 0, keepdims=True
            )
            normal = normal * scale[pl.ds(head, 1), :]
            scaled[:, span] = normal
            products[kind] += normal * hats

    each(heads, step_head)
    values_store = pltpu.make_async_copy(
        grad.at[:, pl.ds(2 * local_width, local_width)],
        grad_out.at[:, pl.ds(2 * local_width, local_width)],
        store_sem.at[0],
    )
    values_store.start()
    lines = []
    for kind in range(2):
        lines.append(
            jnp.concatenate(
                [
                    column_sums(products[kind, pl.ds(origin * own_rows, own_rows), :])
                    for origin in range(size)
                ],
                1,
            )
        )
    for gain in (attention_gain, feedforward_gain):
        total = jnp.sum(gain[...], 0, keepdims=True)
        lines += [total[:, : model_width // 2], total[:, model_width // 2 :]]
    lines.append(jnp.zeros((2, model_width // 2), jnp.float32))
    shared[me] = jnp.concatenate(lines, 0)

    def share_copy(offset):
        return pltpu.make_async_remote_copy(
            src_ref=shared.at[me],
            dst_ref=shared.at[me],
            send_sem=share_send.at[offset - 1],
            recv_sem=share_recv.at[offset - 1],
            device_id={"tensor": lax.rem(me + offset, size)},
            device_id_type=pl.DeviceIdType.MESH,
        )

    pl.semaphore_wait(barrier, size - 1)
    for offset in range(1, size):
        share_copy(offset).start()
    for offset in range(1, size):
        share_copy(offset).wait_recv()
    total = shared[0]
    for device in range(1, size):
        total = total + shared[device]
    for kind, (scaled, hat) in enumerate(((scaled_query, query_hat), (scaled_key, key_hat))):
        for origin in range(size):
            here = pl.ds(origin * own_rows, own_rows)
            columns = slice(origin * own_rows, (origin + 1) * own_rows)
            inner = turned_rows(total[kind : kind + 1, columns] / model_width)
            inverse = turned_rows(stats[pl.ds(heads + kind, 1), here])
            for head in range(heads):
                span = pl.ds(head * 128, 128)
                grad[here, pl.ds((kind * heads + head) * 128, 128)] = low(
                    inverse * (scaled[here, span] - wide(hat[here, span]) * inner)
                )
    rest_store = pltpu.make_async_copy(
        grad.at[:, pl.ds(0, 2 * local_width)],
        grad_out.at[:, pl.ds(0, 2 * local_width)],
        store_sem.at[1],
    )
    rest_store.start()
    height = gain_terms.shape[0] // 8
    for place in range(8):
        if place:
            gain_terms[pl.ds(place * height, 8), :] = gain_terms[pl.ds(0, 8), :]
        for kind in range(2):
            for line in range(block // 128):
                first = place * block + line * 128
                row, first = divmod(first, model_width // 2)
                gain_terms[
                    pl.ds(place * height + 8 + kind * (block // 128) + line, 1), :
                ] = total[2 + 2 * kind + row : 3 + 2 * kind + row, first : first + 128]
    for offset in range(1, size):
        share_copy(offset).wait_send()
    values_store.wait()
    rest_store.wait()


def turn(
    branch_cot,
    output_full,
    query_rot,
    key_rot,
    value_rows,
    query_hat,
    key_hat,
    cosine,
    sine,
    stats,
    query_scale,
    key_scale,
    attention_gain,
    feedforward_gain,
):
    size = lax.axis_size("tensor")
    group_rows, model_width = branch_cot.shape
    local_width = query_rot.shape[1]
    low_type, wide_type = jnp.bfloat16, jnp.float32
    anywhere = pl.BlockSpec(memory_space=pl.ANY)
    inside = pl.BlockSpec(memory_space=pltpu.VMEM)
    dma = pltpu.SemaphoreType.DMA
    local_rows = (group_rows, local_width)
    table = (group_rows, 128)
    return pl.pallas_call(
        functools.partial(turn_kernel, size),
        out_shape=[
            jax.ShapeDtypeStruct((group_rows, 3 * local_width), low_type),
            jax.ShapeDtypeStruct((8 * 32, 128), wide_type),
        ],
        in_specs=[anywhere] * 9 + [inside] * 5,
        out_specs=[anywhere, inside],
        scratch_shapes=[
            pltpu.VMEM((group_rows, model_width), low_type),
            pltpu.VMEM((local_width, model_width), low_type),
            *[pltpu.VMEM(local_rows, low_type)] * 5,
            *[pltpu.VMEM(table, wide_type)] * 2,
            pltpu.VMEM(local_rows, low_type),
            *[pltpu.VMEM(table, wide_type)] * 3,
            *[pltpu.VMEM(local_rows, wide_type)] * 2,
            pltpu.VMEM((2, *table), wide_type),
            pltpu.VMEM((size, 8, model_width // 2), wide_type),
            pltpu.VMEM((group_rows, 3 * local_width), low_type),
            dma((9,)),
            dma((2,)),
            dma((size - 1,)),
            dma((size - 1,)),
        ],
        compiler_params=pltpu.CompilerParams(
            collective_id=3, has_side_effects=True, vmem_limit_bytes=VMEM_BYTES
        ),
        cost_estimate=pl.CostEstimate(
            flops=2 * group_rows * model_width * local_width + 10 * group_rows**2 * local_width,
            bytes_accessed=16 << 20,
            transcendentals=group_rows**2 * local_width // 128,
        ),
        name="turn",
    )(
        branch_cot,
        output_full,
        query_rot,
        key_rot,
        value_rows,
        query_hat,
        key_hat,
        cosine,
        sine,
        stats,
        query_scale,
        key_scale,
        attention_gain,
        feedforward_gain,
    )


def back_kernel(
    size,
    grad_hbm,
    weight_hbm,
    attended_hbm,
    branch_cot_hbm,
    mixed_cot_hbm,
    inner_hbm,
    rows_hbm,
    gain_hbm,
    hidden_hbm,
    tokens_out,
    down_out,
    output_out,
    query_out,
    key_out,
    value_out,
    gain_out,
    grad,
    weight,
    attended,
    branch_cot,
    mixed_cot,
    inner,
    rows,
    gain,
    hidden,
    partial,
    arrived,
    down_far,
    down_near,
    output_far,
    output_near,
    attention_far,
    attention_near,
    gain_far,
    gain_near,
    down_total,
    output_total,
    load_sem,
    store_sem,
    sum_send,
    sum_recv,
    shard_send,
    shard_recv,
):
    me = lax.axis_index("tensor")
    last = size - 1
    own_rows, model_width = partial.shape[1:]
    piece_rows = own_rows // PIECES
    height = model_width // 8
    greet(((me < last, me + 1), (me > 0, me - 1)))
    loads = [
        pltpu.make_async_copy(source, target, load_sem.at[place])
        for place, (source, target) in enumerate(
            (
                (grad_hbm, grad),
                (weight_hbm, weight),
                (attended_hbm, attended),
                (branch_cot_hbm, branch_cot),
                (mixed_cot_hbm, mixed_cot),
                (inner_hbm, inner),
                (rows_hbm, rows),
                (gain_hbm, gain),
                (hidden_hbm, hidden),
            )
        )
    ]
    for copy in loads:
        copy.start()

    def flow(kind, near, far, shard_height):
        return ShardSum(
            stacked(near, 0, shard_height),
            stacked(far, 0, shard_height),
            lambda half: stacked(near, 4 * shard_height, shard_height)(0, half),
            lambda way, half: stacked(near, 5 * shard_height, shard_height)(way, half),
            shard_send.at[kind],
            shard_recv.at[kind],
        )

    down_flow = flow(0, down_near, down_far, height)
    output_flow = flow(1, output_near, output_far, height)
    attention_flow = flow(2, attention_near, attention_far, height)
    gain_flow = flow(3, gain_near, gain_far, gain.shape[0] // 8)
    flows = (down_flow, output_flow, attention_flow, gain_flow)

    def columns_of(source):
        return lambda place, width: source[:, pl.ds(place * width, width)]

    down_term = product_term(columns_of(mixed_cot), lambda columns: inner[:, columns], 512)
    output_term = product_term(columns_of(branch_cot), lambda columns: attended[:, columns], 512)
    attention_term = product_term(columns_of(rows), lambda columns: grad[:, columns], 512)

    def gain_term(place, target, adds):
        value = gain[pl.ds(place * target.shape[0], target.shape[0]), :]
        target[...] = value + target[...] if adds else value

    def terms(dest):
        def step(index, carry):
            columns = pl.ds(pl.multiple_of(index * TILE, TILE), TILE)
            span = pl.ds(pl.multiple_of(dest * own_rows, own_rows), own_rows)
            partial[dest, :, columns] = low(rows_product(grad[span, :], weight[columns, :]))
            return carry

        lax.fori_loop(0, model_width // TILE, step, 0)

    def terms_at(distance):
        for way in range(2):

            @pl.when(away(1 - way) >= distance)
            def _():
                terms(me + distance if way == 0 else me - distance)

    def away(way):
        return me if way == 0 else last - me

    def span_of(piece):
        return pl.ds(piece * piece_rows, piece_rows)

    def sum_copy(step, piece, way, dest):
        return pltpu.make_async_remote_copy(
            src_ref=partial.at[dest, span_of(piece)],
            dst_ref=arrived.at[way, step - 1, span_of(piece)],
            send_sem=sum_send.at[way, step - 1, piece],
            recv_sem=sum_recv.at[way, step - 1, piece],
            device_id={"tensor": me + 1 - 2 * way},
            device_id_type=pl.DeviceIdType.MESH,
        )

    def sum_step(step, *pieces):
        for piece in pieces:
            for way in range(2):
                distance = away(way)

                @pl.when(distance <= step - 1)
                def _():
                    dest = me + size - step if way == 0 else me - size + step
                    if step > 1:

                        @pl.when(distance >= 1)
                        def _():
                            sum_copy(step - 1, piece, way, dest).wait_recv()
                            add_into(
                                partial.at[dest, span_of(piece)],
                                arrived.at[way, step - 2, span_of(piece)],
                            )

                    sum_copy(step, piece, way, dest).start()

    def sum_end(*pieces):
        for piece in pieces:
            add_into(hidden.at[span_of(piece)], partial.at[me, span_of(piece)])
            for way in range(2):

                @pl.when(away(way) >= 1)
                def _():
                    sum_copy(size - 1, piece, way, me).wait_recv()
                    add_into(
                        hidden.at[span_of(piece)], arrived.at[way, size - 2, span_of(piece)]
                    )

            for copy in token_stores(piece):
                copy.start()

    def token_stores(piece):
        return [
            pltpu.make_async_copy(
                hidden.at[span_of(piece), here],
                tokens_out.at[span_of(piece), natural],
                store_sem.at[1 + piece, place],
            )
            for place, (here, natural) in enumerate(column_blocks(height))
        ]

    def halves_of(total):
        rows_of_half = total.shape[0] // 2
        return lambda half: total.at[pl.ds(half * rows_of_half, rows_of_half), :]

    stores = [
        pltpu.make_async_copy(source, target, store_sem.at[0, place])
        for place, (source, target) in enumerate(((down_total, down_out), (output_total, output_out)))
    ]
    tiles = attended.shape[1] // TILE
    attention_stores = [
        pltpu.make_async_copy(
            down_total.at[pl.ds((kind * tiles + tile) * height, height), :],
            out.at[:, pl.ds(tile * TILE, TILE)],
            store_sem.at[0, 2 + kind * tiles + tile],
        )
        for kind, out in enumerate((query_out, key_out, value_out))
        for tile in range(tiles)
    ]

    pl.semaphore_wait(
        pltpu.get_barrier_semaphore(), 3 + jnp.minimum(me, 1) + jnp.minimum(last - me, 1)
    )
    loads[0].wait()
    loads[1].wait()
    terms_at(3)
    sum_step(1, *range(PIECES))
    loads[2].wait()
    loads[3].wait()
    output_flow.far_terms(output_term)
    loads[7].wait()
    gain_flow.far_terms(gain_term)
    loads[4].wait()
    loads[5].wait()
    down_flow.far_terms(down_term)
    output_flow.near_terms(output_term)
    gain_flow.near_terms(gain_term)
    terms_at(2)
    sum_step(2, 0)
    down_flow.near_terms(down_term)
    sum_step(2, 1)
    terms_at(1)
    loads[6].wait()
    sum_step(2, 2)
    attention_flow.far_terms(attention_term)
    output_flow.take_corner()
    gain_flow.take_corner()
    sum_step(2, 3)
    terms(me)
    sum_step(3, 0)
    attention_flow.near_terms(attention_term)
    sum_step(3, 1)
    down_flow.take_corner()
    sum_step(3, 2)
    sum_step(3, 3)
    loads[8].wait()
    output_flow.take_final_turned(output_total)
    stores[1].start()
    gain_flow.take_final(halves_of(gain_out))
    sum_end(0)
    attention_flow.take_corner()
    sum_end(1)
    down_flow.take_final_turned(down_total)
    stores[0].start()
    sum_end(2)
    sum_end(3)
    stores[0].wait()
    attention_flow.take_final_tiles(down_total)
    for copy in attention_stores:
        copy.start()
    for shard_flow in flows:
        shard_flow.sent()
    for step in range(1, size):
        for way in range(2):

            @pl.when(away(way) <= step - 1)
            def _():
                for piece in range(PIECES):
                    sum_copy(step, piece, way, 0).wait_send()

    for copy in stores[1:] + attention_stores:
        copy.wait()
    for piece in range(PIECES):
        for copy in token_stores(piece):
            copy.wait()


def back(
    grad_projected,
    attention_full,
    attended,
    branch_cot,
    mixed_cot,
    inner,
    rows_all,
    gain_terms,
    grad_hidden,
):
    size = lax.axis_size("tensor")
    own_rows, model_width = grad_hidden.shape
    height = model_width // 8
    operands = (
        grad_projected,
        attention_full,
        attended,
        branch_cot,
        mixed_cot,
        inner,
        rows_all,
        gain_terms,
        grad_hidden,
    )
    widths = (inner.shape[1], attended.shape[1], grad_projected.shape[1])
    gain_height, gain_width = gain_terms.shape[0] // 8, gain_terms.shape[1]
    low_type, wide_type = jnp.bfloat16, jnp.float32
    anywhere = pl.BlockSpec(memory_space=pl.ANY)
    dma = pltpu.SemaphoreType.DMA
    buffers = []
    for width in widths:
        buffers.append(pltpu.VMEM((4 * height, width), low_type))
        buffers.append(pltpu.VMEM((7 * height, width), low_type))
    return pl.pallas_call(
        functools.partial(back_kernel, size),
        out_shape=[
            jax.ShapeDtypeStruct((own_rows, model_width), wide_type),
            *(jax.ShapeDtypeStruct((width, height), wide_type) for width in widths[:2]),
            *[jax.ShapeDtypeStruct((height, attended.shape[1]), wide_type)] * 3,
            jax.ShapeDtypeStruct((gain_height, gain_width), wide_type),
        ],
        in_specs=[anywhere] * 9,
        out_specs=[anywhere] * 6 + [pl.BlockSpec(memory_space=pltpu.VMEM)],
        scratch_shapes=[
            *(pltpu.VMEM(operand.shape, operand.dtype) for operand in operands),
            pltpu.VMEM((size, own_rows, model_width), low_type),
            pltpu.VMEM((2, size - 1, own_rows, model_width), low_type),
            *buffers,
            pltpu.VMEM((4 * gain_height, gain_width), wide_type),
            pltpu.VMEM((7 * gain_height, gain_width), wide_type),
            *(pltpu.VMEM((width, height), wide_type) for width in widths[:2]),
            dma((9,)),
            dma((1 + PIECES, 8)),
            dma((2, size - 1, PIECES)),
            dma((2, size - 1, PIECES)),
            dma((4, 10)),
            dma((4, 10)),
        ],
        compiler_params=pltpu.CompilerParams(
            collective_id=2, has_side_effects=True, vmem_limit_bytes=VMEM_BYTES
        ),
        cost_estimate=pl.CostEstimate(
            flops=2 * size * own_rows * model_width * (sum(widths) + widths[2]),
            bytes_accessed=48 << 20,
            transcendentals=0,
        ),
        name="back",
    )(*operands)


def local(
    tokens,
    positions,
    cotangent,
    query_weight,
    key_weight,
    value_weight,
    output_weight,
    gate_weight,
    up_weight,
    down_weight,
    query_gain,
    key_gain,
    attention_gain,
    feedforward_gain,
):
    data_size = lax.axis_size("dp")
    data_index = lax.axis_index("dp")
    high_count = data_size // 8
    width = attention_gain.shape[0]
    channels, local_heads = query_gain.shape

    def high_block(low_bits, place):
        return low_bits + 8 * ((data_index // 8) ^ place)

    def grouped(array_in):
        if high_count == 1:
            return array_in
        return jnp.concatenate(
            [
                lax.dynamic_slice_in_dim(array_in, high_block(low_bits, place) * width, width, -1)
                for low_bits in range(8)
                for place in range(high_count)
            ],
            -1,
        )

    def ungrouped(array_in):
        if high_count == 1:
            return array_in
        return jnp.concatenate(
            [
                lax.dynamic_slice_in_dim(
                    array_in,
                    (low_bits * high_count + ((data_index // 8) ^ high_bits)) * width,
                    width,
                    -1,
                )
                for high_bits in range(high_count)
                for low_bits in range(8)
            ],
            -1,
        )

    head_gains = jnp.concatenate([query_gain.T, key_gain.T], 0)
    head_gains = lax.dynamic_update_slice_in_dim(
        jnp.zeros((2 * local_heads, channels * data_size), head_gains.dtype),
        head_gains,
        data_index * channels,
        1,
    )
    for bit in range(3, bits_of(data_size)):
        head_gains = head_gains + swap(head_gains, 1 << bit)
    gain_lines = [
        head_gains,
        gather_high(attention_gain[None], 1).reshape(-1, 128),
        gather_high(feedforward_gain[None], 1).reshape(-1, 128),
    ]
    line_count = sum(lines.shape[0] for lines in gain_lines)
    gain_shard = jnp.pad(jnp.concatenate(gain_lines, 0), ((0, 32 - line_count), (0, 0)))
    (
        rows_all,
        attention_full,
        output_full,
        gate_full,
        attended,
        query_rot,
        key_rot,
        value_rows,
        query_hat,
        key_hat,
        cosine,
        sine,
        stats,
        query_scale,
        key_scale,
        attention_scale,
        feedforward_scale,
    ) = front(
        grouped(tokens),
        gather_high(query_weight, 0),
        gather_high(key_weight, 0),
        gather_high(value_weight, 0),
        gather_high(output_weight, 1),
        gather_high(gate_weight, 0),
        gain_shard,
        positions,
    )
    (
        inner_act,
        mixed_cot,
        branch_cot,
        block_grouped,
        grad_hidden,
        grad_gate,
        grad_up,
        attention_gain_part,
        feedforward_gain_part,
    ) = middle(
        attended,
        rows_all,
        grouped(cotangent),
        attention_scale,
        feedforward_scale,
        output_full,
        gate_full,
        gather_high(up_weight, 0),
        gather_high(down_weight, 1),
    )
    grad_projected, gain_terms = turn(
        branch_cot,
        output_full,
        query_rot,
        key_rot,
        value_rows,
        query_hat,
        key_hat,
        cosine,
        sine,
        stats,
        query_scale,
        key_scale,
        attention_gain_part,
        feedforward_gain_part,
    )
    tokens_part, grad_down, grad_output, grad_query, grad_key, grad_value, gain_part = back(
        grad_projected,
        attention_full,
        attended,
        branch_cot,
        mixed_cot,
        inner_act,
        rows_all.reshape(-1, rows_all.shape[-1]),
        gain_terms,
        grad_hidden,
    )
    head_part = gain_part[: 2 * local_heads]
    for bit in range(3, bits_of(data_size)):
        head_part = head_part + swap(head_part, 1 << bit)
    head_part = lax.dynamic_slice_in_dim(head_part, data_index * channels, channels, 1)
    norm_part = gain_part[2 * local_heads : line_count].reshape(2, -1)

    def own_high(total, axis):
        return wide(scatter_high(total, axis))

    return (
        ungrouped(block_grouped),
        ungrouped(tokens_part),
        own_high(grad_query, 0),
        own_high(grad_key, 0),
        own_high(grad_value, 0),
        own_high(grad_output, 1),
        own_high(grad_gate, 0),
        own_high(grad_up, 0),
        own_high(grad_down, 1),
        head_part[:local_heads].T,
        head_part[local_heads:].T,
        own_high(norm_part[0], 0),
        own_high(norm_part[1], 0),
    )


def solution(mesh):
    return jax.shard_map(
        local,
        mesh=mesh,
        in_specs=(
            P(("dp", "tensor"), None),
            P("dp"),
            P(("dp", "tensor"), None),
            P("dp", "tensor"),
            P("dp", "tensor"),
            P("dp", "tensor"),
            P("tensor", "dp"),
            P("dp", "tensor"),
            P("dp", "tensor"),
            P("tensor", "dp"),
            P("dp", "tensor"),
            P("dp", "tensor"),
            P("dp"),
            P("dp"),
        ),
        out_specs=(
            P(("dp", "tensor"), None),
            P(("dp", "tensor"), None),
            P("dp", "tensor"),
            P("dp", "tensor"),
            P("dp", "tensor"),
            P("tensor", "dp"),
            P("dp", "tensor"),
            P("dp", "tensor"),
            P("tensor", "dp"),
            P("dp", "tensor"),
            P("dp", "tensor"),
            P("dp"),
            P("dp"),
        ),
        check_vma=False,
    )
```

```python
import functools

import jax
import jax.numpy as jnp
import numpy as np
from jax import lax
from jax.experimental import pallas as pl
from jax.experimental.pallas import tpu as pltpu
from jax.sharding import PartitionSpec as P

EPS = 1e-06
THETA = 500000.0
MASKED = -1e30
VMEM_BYTES = 64 * 1024 * 1024 - 128 * 1024


def norm_backward(grad_in, normalized, inverse_rms, gain_values):
    scaled = grad_in * gain_values
    return inverse_rms * (scaled - normalized * jnp.mean(scaled * normalized, -1, keepdims=True))


def bits_of(size):
    return size.bit_length() - 1


def swap(array_in, mask):
    size = lax.axis_size("dp")
    return lax.ppermute(array_in, "dp", [(index, index ^ mask) for index in range(size)])


def gather_high(shard, axis):
    for bit in range(3, bits_of(lax.axis_size("dp"))):
        shard = jnp.concatenate([shard, swap(shard, 1 << bit)], axis)
    return shard


def scatter_high(total, axis):
    for bit in reversed(range(3, bits_of(lax.axis_size("dp")))):
        kept, sent = jnp.split(total, 2, axis)
        total = low(wide(kept) + wide(swap(low(sent), 1 << bit)))
    return total


def low(array_in):
    return array_in.astype(jnp.bfloat16)


def wide(array_in):
    return array_in.astype(jnp.float32)


def rows_product(left, right):
    return lax.dot_general(
        left, right, (((1,), (1,)), ((), ())), preferred_element_type=jnp.float32
    )


TILE = 256
WIDE_TILE = 512
STRIP = 16
CHUNKS = 2
HALVES = 2
PIECES = 4


def shard_peer(mask):
    index = lax.axis_index("dp")
    return index + mask - 2 * mask * ((index // mask) % 2)


def low_place(mask):
    index = lax.axis_index("dp")
    total = 0
    for bit in (1, 2, 4):
        value = (index // bit) % 2
        total = total + bit * (1 - value if mask & bit else value)
    return total


ROUTE = {1: (1, 1), 2: (2, 2), 3: (1, 1), 4: (4, 4), 5: (1, 1), 6: (4, 2), 7: (1, 1)}
PLACES = {mask: place for place, mask in enumerate((0, 2, 4, 6, 1, 3, 5, 7))}


def column_blocks(width):
    return [
        (
            pl.ds(place * width, width),
            pl.ds(pl.multiple_of(low_place(mask) * width, width), width),
        )
        for mask, place in PLACES.items()
    ]


class ShardGather:
    def __init__(self, own, target, send_sem, recv_sem):
        self.own, self.target, self.send_sem, self.recv_sem = own, target, send_sem, recv_sem

    def copy(self, mask, half):
        route = ROUTE[mask][half]
        before = mask ^ route
        return pltpu.make_async_remote_copy(
            src_ref=self.target(PLACES[before], half) if before else self.own(half),
            dst_ref=self.target(PLACES[mask], half),
            send_sem=self.send_sem.at[mask - 1, half],
            recv_sem=self.recv_sem.at[mask - 1, half],
            device_id={"dp": shard_peer(route)},
            device_id_type=pl.DeviceIdType.MESH,
        )

    def start(self, *masks):
        for half in range(2):
            for mask in masks:
                self.copy(mask, half).start()

    def arrive(self, mask, halves=(0, 1)):
        for half in halves:
            self.copy(mask, half).wait_recv()
            for after, route in ROUTE.items():
                if after != mask and after ^ route[half] == mask:
                    self.copy(after, half).start()

    def sent(self):
        for mask in ROUTE:
            for half in range(2):
                self.copy(mask, half).wait_send()


def row_halves(buffer, height):
    def target(place, half):
        return buffer.at[pl.ds(place * height + half * (height // 2), height // 2), :]

    return target


def column_halves(buffer, width):
    height = buffer.shape[0] // 2

    def target(place, half):
        return buffer.at[pl.ds(half * height, height), pl.ds(place * width, width)]

    return target


def own_halves(shard):
    height = shard.shape[0] // 2
    return lambda half: shard.at[pl.ds(half * height, height), :]


def greet(line_devices):
    barrier = pltpu.get_barrier_semaphore()
    for mask in (1, 2, 4):
        pl.semaphore_signal(
            barrier,
            inc=1,
            device_id={"dp": shard_peer(mask)},
            device_id_type=pl.DeviceIdType.MESH,
        )
    for there, index in line_devices:

        @pl.when(there)
        def _():
            pl.semaphore_signal(
                barrier,
                inc=1,
                device_id={"tensor": index},
                device_id_type=pl.DeviceIdType.MESH,
            )


def turned_rows(row):
    return jnp.broadcast_to(row, (128, row.shape[1])).T


def column_sums(values):
    total = values[:, :128]
    for first in range(128, values.shape[1], 128):
        total = total + values[:, first : first + 128]
    return jnp.sum(total.T, 0, keepdims=True)


def ahead_of(values, first_key, first_query):
    key = first_key + lax.broadcasted_iota(jnp.int32, values.shape, 0)
    query = first_query + lax.broadcasted_iota(jnp.int32, values.shape, 1)
    return key > query


def head_span(head):
    return pl.ds(pl.multiple_of(head * 128, 128), 128)


def each(count, body):
    def step(index, carry):
        body(index)
        return carry

    lax.fori_loop(0, count, step, 0)


def front_kernel(
    size,
    tokens_hbm,
    query_hbm,
    key_hbm,
    value_hbm,
    output_hbm,
    gate_hbm,
    gain_hbm,
    positions,
    frequency,
    rows_out,
    attention_out,
    output_out,
    gate_out,
    attended_out,
    query_rot_out,
    key_rot_out,
    value_out,
    query_hat_out,
    key_hat_out,
    cosine_out,
    sine_out,
    stats,
    query_scale,
    key_scale,
    attention_scale,
    feedforward_scale,
    rows,
    weight,
    projected,
    gain,
    cosine,
    sine,
    squares,
    query_rot,
    key_rot,
    value,
    query_hat,
    key_hat,
    attended,
    load_sem,
    store_sem,
    hand_send,
    hand_recv,
    shard_send,
    shard_recv,
    square_send,
    square_recv,
):
    me = lax.axis_index("tensor")
    last = size - 1
    own_rows, model_width = rows.shape[1:]
    piece_rows = own_rows // PIECES
    local_width = query_hbm.shape[1]
    heads = local_width // 128
    everyone = True
    greet([(everyone, lax.rem(me + offset, size)) for offset in range(1, size)])
    block = model_width // 8
    token_loads = [
        pltpu.make_async_copy(
            tokens_hbm.at[:, natural], rows.at[me, :, here], load_sem.at[0, place]
        )
        for place, (here, natural) in enumerate(column_blocks(block))
    ]
    shard_rows = pl.ds(0, query_hbm.shape[0])
    loads = [
        pltpu.make_async_copy(source, target, load_sem.at[1, place])
        for place, (source, target) in enumerate(
            (
                (query_hbm, weight.at[shard_rows, pl.ds(0, local_width)]),
                (key_hbm, weight.at[shard_rows, pl.ds(local_width, local_width)]),
                (value_hbm, weight.at[shard_rows, pl.ds(2 * local_width, local_width)]),
                (gain_hbm, gain.at[pl.ds(0, gain_hbm.shape[0]), :]),
                (output_hbm, output_out.at[:, pl.ds(0, output_hbm.shape[1])]),
                (gate_hbm, gate_out.at[pl.ds(0, gate_hbm.shape[0]), :]),
            )
        )
    ]
    for copy in token_loads + loads:
        copy.start()
    attention_target = row_halves(weight, query_hbm.shape[0])
    attention_flow, output_flow, gate_flow, gain_flow = (
        ShardGather(own, target, shard_send.at[kind], shard_recv.at[kind])
        for kind, (own, target) in enumerate(
            (
                (functools.partial(attention_target, 0), attention_target),
                (own_halves(output_hbm), column_halves(output_out, output_hbm.shape[1])),
                (own_halves(gate_hbm), row_halves(gate_out, gate_hbm.shape[0])),
                (own_halves(gain_hbm), row_halves(gain, gain_hbm.shape[0])),
            )
        )
    )
    pl.semaphore_wait(pltpu.get_barrier_semaphore(), 3 + size - 1)

    def away(way):
        return me if way == 0 else last - me

    def hand_copy(hop, piece, way, origin):
        here = rows.at[origin, pl.ds(piece * piece_rows, piece_rows)]
        return pltpu.make_async_remote_copy(
            src_ref=here,
            dst_ref=here,
            send_sem=hand_send.at[way, hop - 1, piece],
            recv_sem=hand_recv.at[way, hop - 1, piece],
            device_id={"tensor": me + 1 - 2 * way},
            device_id_type=pl.DeviceIdType.MESH,
        )

    for copy in token_loads:
        copy.wait()
    for piece in range(PIECES):
        for way in range(2):

            @pl.when(away(1 - way) >= 1)
            def _():
                hand_copy(1, piece, way, me).start()

        if piece == 0:
            for copy in loads[:3]:
                copy.wait()
            attention_flow.start(2, 4, 1)
            gain_flow.start(2, 4, 1)

    def hand_on(hop, piece):
        for way in range(2):

            @pl.when(away(way) >= hop)
            def _():
                origin = me - hop if way == 0 else me + hop
                hand_copy(hop, piece, way, origin).wait_recv()
                if hop < size - 1:

                    @pl.when(away(1 - way) >= 1)
                    def _():
                        hand_copy(hop + 1, piece, way, origin).start()

    def row_store(origin):
        return pltpu.make_async_copy(rows.at[origin], rows_out.at[origin], store_sem.at[0, origin])

    whole_stores = [
        pltpu.make_async_copy(source, target, store_sem.at[1 + place // size, place % size])
        for place, (source, target) in enumerate(
            (
                (weight, attention_out),
                (cosine, cosine_out),
                (sine, sine_out),
                (query_hat, query_hat_out),
                (key_hat, key_hat_out),
                (query_rot, query_rot_out),
                (key_rot, key_rot_out),
                (value, value_out),
                (attended, attended_out),
            )
        )
    ]

    def span_of(origin):
        return pl.ds(pl.multiple_of(origin * own_rows, own_rows), own_rows)

    def square_copy(offset, origin):
        return pltpu.make_async_remote_copy(
            src_ref=squares.at[me, origin],
            dst_ref=squares.at[me, origin],
            send_sem=square_send.at[offset - 1, origin],
            recv_sem=square_recv.at[offset - 1, origin],
            device_id={"tensor": lax.rem(me + offset, size)},
            device_id_type=pl.DeviceIdType.MESH,
        )

    def project(origin):
        def step(index):
            columns = pl.ds(pl.multiple_of(index * WIDE_TILE, WIDE_TILE), WIDE_TILE)
            projected[origin, :, columns] = jnp.dot(
                rows[origin], weight[:, columns], preferred_element_type=jnp.float32
            )

        row_store(origin).start()
        each(weight.shape[1] // WIDE_TILE, step)
        queries = projected[origin, :, pl.ds(0, local_width)]
        keys = projected[origin, :, pl.ds(local_width, local_width)]
        squares[me, origin, pl.ds(0, 8), :] = jnp.concatenate(
            [
                column_sums(queries * queries),
                column_sums(keys * keys),
                jnp.zeros((6, own_rows), jnp.float32),
            ],
            0,
        )
        for offset in range(1, size):
            square_copy(offset, origin).start()

    def project_from(hop, way):
        @pl.when(away(way) >= hop)
        def _():
            project(me - hop if way == 0 else me + hop)

    def normalize(origin):
        for offset in range(1, size):
            square_copy(offset, origin).wait_recv()
        total = squares[0, origin]
        for device in range(1, size):
            total = total + squares[device, origin]
        inverse = lax.rsqrt(total / model_width + EPS)
        here = span_of(origin)
        stats[pl.ds(heads, 2), here] = inverse[:2]
        for kind, (hat, rot, scale) in enumerate(
            ((query_hat, query_rot, query_scale), (key_hat, key_rot, key_scale))
        ):
            column = turned_rows(inverse[kind : kind + 1])

            def step(head):
                span = head_span(head)
                source = head_span(head + kind * heads)
                normalized = projected[origin, :, source] * column
                hat[here, span] = low(normalized)
                scaled = normalized * scale[pl.ds(head, 1), :]
                rot[here, span] = low(
                    scaled * cosine[here, :] + pltpu.roll(scaled, 64, 1) * sine[here, :]
                )

            each(heads, step)
        value[here, :] = low(projected[origin, :, pl.ds(2 * local_width, local_width)])

    def tables():
        for origin in range(size):
            here = pl.ds(origin * own_rows, own_rows)
            angles = turned_rows(wide(positions[:, here])) * frequency[...]
            cosine[here, :] = jnp.cos(angles)
            lane = lax.broadcasted_iota(jnp.int32, angles.shape, 1)
            sine[here, :] = jnp.where(lane < 64, -1.0, 1.0) * jnp.sin(angles)

    def scales():
        for kind, scale in enumerate((query_scale, key_scale)):
            total = wide(gain[pl.ds(0, 16), :])
            for place in range(1, 8):
                total = total + wide(gain[pl.ds(place * gain_hbm.shape[0], 16), :])
            scale[...] = jnp.concatenate(
                [total[kind * heads : (kind + 1) * heads], jnp.zeros((8 - heads, 128), jnp.float32)],
                0,
            )
        for place in range(8):
            lines = wide(gain[pl.ds(place * gain_hbm.shape[0], 16), :])
            for kind, scale in enumerate((attention_scale, feedforward_scale)):
                for line in range(block // 128):
                    at = 2 * heads + kind * (block // 128) + line
                    scale[:, pl.ds(place * block + line * 128, 128)] = lines[at : at + 1]

    def attend(origin):
        count = (origin + 1) * own_rows
        here = pl.ds(origin * own_rows, own_rows)

        def step(head):
            span = head_span(head)
            scores = rows_product(key_rot[pl.ds(0, count), span], query_rot[here, span])
            scores = scores * (128**-0.5)
            near = scores[origin * own_rows :]
            near = jnp.where(ahead_of(near, 0, 0), MASKED, near)
            scores = jnp.concatenate([scores[: origin * own_rows], near], 0) if origin else near
            row_max = jnp.max(scores, 0, keepdims=True)
            exponent = jnp.exp(scores - row_max)
            row_total = jnp.sum(exponent, 0, keepdims=True)
            result = jnp.dot(
                value[pl.ds(0, count), span].T, low(exponent), preferred_element_type=jnp.float32
            )
            attended[here, span] = low((result * (1.0 / row_total)).T)
            stats[pl.ds(head, 1), here] = row_max + jnp.log(row_total)

        each(heads, step)

    def turns(beat):
        if beat == 1:
            tables()
            for copy in whole_stores[1:3]:
                copy.start()
        elif beat == 2:
            attention_flow.arrive(2, (0,))
            attention_flow.arrive(4, (0,))
        elif beat == 3:
            attention_flow.arrive(2, (1,))
            attention_flow.arrive(4, (1,))
            output_flow.start(2, 4, 1)
            gain_flow.arrive(2)
            gain_flow.arrive(4)
        elif beat == 5:
            attention_flow.arrive(6)
            gate_flow.start(2, 4, 1)
            gain_flow.arrive(6)
        elif beat == 6:
            output_flow.arrive(2)
            output_flow.arrive(4)
            for mask in (1, 3, 5, 7):
                attention_flow.arrive(mask)
            whole_stores[0].start()
            project(me)
        elif beat == 7:
            project_from(1, 0)
        elif beat == 8:
            project_from(1, 1)
            output_flow.arrive(6)
            loads[3].wait()
            for mask in (1, 3, 5, 7):
                gain_flow.arrive(mask)
            scales()
        elif beat == 9:
            gate_flow.arrive(2, (0,))
            gate_flow.arrive(4, (0,))
        elif beat == 10:
            project_from(2, 0)
        elif beat == 11:
            project_from(2, 1)
            gate_flow.arrive(2, (1,))
            gate_flow.arrive(4, (1,))

    for beat in range(1, (size - 1) * PIECES + 1):
        if beat == (size - 1) * PIECES:
            for origin in range(1, last):
                normalize(origin)
        hand_on((beat - 1) // PIECES + 1, (beat - 1) % PIECES)
        turns(beat)
    project_from(3, 0)
    project_from(3, 1)
    gate_flow.arrive(6)
    for origin in (0, last):
        normalize(origin)
    for copy in whole_stores[3:8]:
        copy.start()
    for origin in range(size):
        attend(origin)
    whole_stores[8].start()
    for flow in (output_flow, gate_flow):
        for mask in (1, 3, 5, 7):
            flow.arrive(mask)
    for hop in range(1, size):
        for way in range(2):

            @pl.when(jnp.logical_and(away(way) >= hop - 1, away(1 - way) >= 1))
            def _():
                for piece in range(PIECES):
                    hand_copy(hop, piece, way, 0).wait_send()

    for flow in (attention_flow, output_flow, gate_flow, gain_flow):
        flow.sent()
    for offset in range(1, size):
        for origin in range(size):
            square_copy(offset, origin).wait_send()
    for copy in loads[4:]:
        copy.wait()
    for origin in range(size):
        row_store(origin).wait()
    for copy in whole_stores:
        copy.wait()


def front(
    tokens_grouped,
    query_shard,
    key_shard,
    value_shard,
    output_shard,
    gate_shard,
    gain_shard,
    positions,
):
    size = lax.axis_size("tensor")
    own_rows, model_width = tokens_grouped.shape
    local_width = query_shard.shape[1]
    group_rows = size * own_rows
    low_type, wide_type = jnp.bfloat16, jnp.float32
    anywhere = pl.BlockSpec(memory_space=pl.ANY)
    inside = pl.BlockSpec(memory_space=pltpu.VMEM)
    dma = pltpu.SemaphoreType.DMA
    hands = (2, size - 1, PIECES)
    half_head = np.arange(128, dtype=np.float32) % 64
    frequency = (np.float32(THETA) ** (-(half_head * np.float32(2.0 / 128))))[None]

    def shape(dims, kind=low_type):
        return jax.ShapeDtypeStruct(dims, kind)

    local_rows = (group_rows, local_width)
    tables = (group_rows, 128)
    return pl.pallas_call(
        functools.partial(front_kernel, size),
        out_shape=[
            shape((size, own_rows, model_width)),
            shape((model_width, 3 * local_width)),
            shape((output_shard.shape[0], model_width)),
            shape((model_width, gate_shard.shape[1])),
            *[shape(local_rows)] * 6,
            *[shape(tables, wide_type)] * 2,
            shape((8, group_rows), wide_type),
            *[shape((8, 128), wide_type)] * 2,
            *[shape((1, model_width), wide_type)] * 2,
        ],
        in_specs=[anywhere] * 7 + [inside] * 2,
        out_specs=[anywhere] * 12 + [inside] * 5,
        scratch_shapes=[
            pltpu.VMEM((size, own_rows, model_width), low_type),
            pltpu.VMEM((model_width, 3 * local_width), low_type),
            pltpu.VMEM((size, own_rows, 3 * local_width), wide_type),
            pltpu.VMEM((8 * gain_shard.shape[0], gain_shard.shape[1]), low_type),
            pltpu.VMEM(tables, wide_type),
            pltpu.VMEM(tables, wide_type),
            pltpu.VMEM((size, size, 8, own_rows), wide_type),
            *[pltpu.VMEM(local_rows, low_type)] * 6,
            dma((2, 8)),
            dma((4, size)),
            dma(hands),
            dma(hands),
            dma((4, 7, 2)),
            dma((4, 7, 2)),
            dma((size - 1, size)),
            dma((size - 1, size)),
        ],
        compiler_params=pltpu.CompilerParams(
            collective_id=0, has_side_effects=True, vmem_limit_bytes=VMEM_BYTES
        ),
        cost_estimate=pl.CostEstimate(
            flops=6 * group_rows * model_width * local_width,
            bytes_accessed=32 << 20,
            transcendentals=0,
        ),
        name="front",
    )(
        tokens_grouped,
        query_shard,
        key_shard,
        value_shard,
        output_shard,
        gate_shard,
        gain_shard,
        positions.reshape(1, group_rows),
        frequency,
    )


class ShardSum:
    def __init__(self, near, far, corner, final, send_sem, recv_sem, deferred=False, own=None):
        self.near, self.far, self.corner, self.final = near, far, corner, final
        self.deferred = deferred
        self.own = own or functools.partial(near, 0)
        self.send_sem, self.recv_sem = send_sem, recv_sem

    def remote(self, source, target, place, route):
        return pltpu.make_async_remote_copy(
            src_ref=source,
            dst_ref=target,
            send_sem=self.send_sem.at[place],
            recv_sem=self.recv_sem.at[place],
            device_id={"dp": shard_peer(route)},
            device_id_type=pl.DeviceIdType.MESH,
        )

    def core_copy(self, place):
        return self.remote(self.far(place), self.near(place), place, 1)

    def corner_copy(self, half):
        return self.remote(self.near(3, half), self.corner(half), 4 + half, (4, 2)[half])

    def final_copy(self, way, half):
        return self.remote(
            self.near(1 + way, half), self.final(way, half), 6 + 2 * way + half, (2, 4)[way]
        )

    def far_term(self, term, place):
        term(4 + place, self.far(place), False)
        self.core_copy(place).start()

    def near_term(self, term, place):
        self.core_copy(place).wait_recv()
        term(place, self.near(place), True)
        if place == 3:
            for half in range(2):
                self.corner_copy(half).start()
        elif place and not self.deferred:
            self.final_copy(place - 1, 2 - place).start()

    def first_terms(self, term):
        self.far_term(term, 3)
        self.far_term(term, 1)
        self.near_term(term, 3)
        self.far_term(term, 2)

    def other_terms(self, term):
        self.near_term(term, 1)
        self.far_term(term, 0)
        self.near_term(term, 2)
        self.near_term(term, 0)

    def take_corner(self):
        for half in range(2):
            self.corner_copy(half).wait_recv()
            add_into(self.near(1 + half, half), self.corner(half))
            if not self.deferred:
                self.final_copy(half, half).start()

    def take_final(self, target):
        for half in range(2):
            for way in range(2):
                self.final_copy(way, half).wait_recv()
            own, first, second = self.own(half), self.final(0, half), self.final(1, half)
            out = target(half)
            rows = own.shape[0]

            def step(index):
                span = pl.ds(pl.multiple_of(index * STRIP, STRIP), STRIP)
                out[span, :] = wide(own[span, :]) + wide(first[span, :]) + wide(second[span, :])

            each(rows // STRIP, step)

    def take_final_tiles(self, out):
        for half in range(2):
            for way in range(2):
                self.final_copy(way, half).wait_recv()
            own, first, second = self.own(half), self.final(0, half), self.final(1, half)
            rows = own.shape[0]

            def step(index):
                span = pl.ds(pl.multiple_of(index * TILE, TILE), TILE)
                value = wide(own[:, span]) + wide(first[:, span]) + wide(second[:, span])
                out[pl.ds(pl.multiple_of(index * 2 * rows + half * rows, STRIP), rows), :] = value

            each(own.shape[1] // TILE, step)

    def take_final_turned(self, out):
        for half in range(2):
            for way in range(2):
                self.final_copy(way, half).wait_recv()
            own, first, second = self.own(half), self.final(0, half), self.final(1, half)
            rows = own.shape[0]

            def step(index):
                span = pl.ds(pl.multiple_of(index * TILE, TILE), TILE)
                value = wide(own[:, span]) + wide(first[:, span]) + wide(second[:, span])
                out[span, pl.ds(half * rows, rows)] = value.T

            each(own.shape[1] // TILE, step)

    def sent(self, core=True):
        for place in range(4) if core else ():
            self.core_copy(place).wait_send()
        for half in range(2):
            self.corner_copy(half).wait_send()
            for way in range(2) if not self.deferred else ():
                self.final_copy(way, half).wait_send()


def add_into(target, source):
    def step(index, carry):
        span = pl.ds(pl.multiple_of(index * STRIP, STRIP), STRIP)
        target[span, :] = (wide(target[span, :]) + wide(source[span, :])).astype(target.dtype)
        return carry

    lax.fori_loop(0, target.shape[0] // STRIP, step, 0)


def product_term(left, right):
    def term(place, target, adds):
        height, width = target.shape
        tile = 1024 if width % 1024 == 0 else 512
        turned = left(place, height).T

        def step(index, carry):
            columns = pl.ds(pl.multiple_of(index * tile, tile), tile)
            value = jnp.dot(turned, right(columns, tile), preferred_element_type=jnp.float32)
            if adds:
                value = value + wide(target[:, columns])
            target[:, columns] = value.astype(target.dtype)
            return carry

        lax.fori_loop(0, target.shape[1] // tile, step, 0)

    return term


def stacked(buffer, first, height):
    def view(place, half=None):
        at = first + place * height
        if half is None:
            return buffer.at[pl.ds(at, height), :]
        return buffer.at[pl.ds(at + half * (height // 2), height // 2), :]

    return view


def middle_kernel(size, *refs):
    (
        attended_hbm,
        rows_hbm,
        cotangent_hbm,
        attention_scale,
        feedforward_scale,
        output_hbm,
        gate_hbm,
        up_hbm,
        down_hbm,
        mlp_out,
        inner_out,
        mixed_cot_out,
        branch_cot_out,
        block_out,
        grad_hidden_out,
        gate_grad_out,
        up_near_out,
        attention_gain_out,
        feedforward_gain_out,
        attended,
        tokens,
        cotangent,
        output_weight,
        gate_weight,
        up_weight,
        down_weight,
        everyone,
        gate_act,
        up_act,
        inner,
        hidden,
        branch,
        arrived,
        partial,
        total,
        load_sem,
        store_sem,
        sum_send,
        sum_recv,
        hand_send,
        hand_recv,
        shard_send,
        shard_recv,
        grad_send,
        grad_recv,
        again_sem,
        shuffle_sem,
        free_sem,
    ) = refs
    me = lax.axis_index("tensor")
    last = size - 1
    chunk_rows, model_width = tokens.shape[1], tokens.shape[2]
    units = gate_weight.shape[1]
    half_rows = chunk_rows // HALVES
    all_rows = size * chunk_rows

    greet(((me < last, me + 1), (me > 0, me - 1)))
    first_loads = [
        pltpu.make_async_copy(source, target, load_sem.at[place])
        for place, (source, target) in enumerate(
            (
                (attended_hbm, attended),
                (output_hbm, output_weight),
                (rows_hbm.at[me], tokens),
                (gate_hbm, gate_weight),
                (up_hbm, up_weight.at[pl.ds(0, up_hbm.shape[0]), :]),
                (down_hbm, down_weight.at[:, pl.ds(0, down_hbm.shape[1])]),
            )
        )
    ]
    first_loads += [
        pltpu.make_async_copy(
            cotangent_hbm.at[pl.ds(chunk * chunk_rows, chunk_rows), natural],
            cotangent.at[chunk, :, here],
            shuffle_sem.at[chunk, place],
        )
        for chunk in range(CHUNKS)
        for place, (here, natural) in enumerate(column_blocks(model_width // 8))
    ]
    for copy in first_loads[:2]:
        copy.start()
    up_flow = ShardGather(
        own_halves(up_hbm),
        row_halves(up_weight, up_hbm.shape[0]),
        shard_send.at[0],
        shard_recv.at[0],
    )
    down_flow = ShardGather(
        own_halves(down_hbm),
        column_halves(down_weight, down_hbm.shape[1]),
        shard_send.at[1],
        shard_recv.at[1],
    )
    pl.semaphore_wait(
        pltpu.get_barrier_semaphore(), 3 + jnp.minimum(me, 1) + jnp.minimum(last - me, 1)
    )
    up_flow.start(2, 4, 1)
    down_flow.start(1)

    height = model_width // 8
    again = [
        pltpu.make_async_copy(
            mlp_out.at[chunk, origin],
            down_weight.at[pl.ds((chunk * size + origin) * chunk_rows, chunk_rows), :],
            again_sem.at[chunk, origin],
        )
        for chunk in range(CHUNKS)
        for origin in range(size)
    ]
    gate_grads, up_grads = (
        ShardSum(
            stacked(buffer, 0, height),
            stacked(down_weight, 4 * height, height),
            functools.partial(stacked(buffer, 4 * height, height), 0),
            stacked(buffer, 5 * height, height),
            grad_send.at[kind],
            grad_recv.at[kind],
            deferred=kind == 1,
        )
        for kind, buffer in enumerate((gate_weight, up_weight))
    )

    def rows_again(place, shard_width):
        return down_weight[pl.ds(0, CHUNKS * all_rows), pl.ds(place * shard_width, shard_width)]

    def grad_term(act):
        def columns_of(columns, tile):
            return act[:, :, columns].reshape(CHUNKS * all_rows, tile)

        return product_term(rows_again, columns_of)

    def weights_free():
        for place, mask in enumerate((1, 2, 4)):
            pl.semaphore_signal(
                free_sem.at[place],
                inc=1,
                device_id={"dp": shard_peer(mask)},
                device_id_type=pl.DeviceIdType.MESH,
            )
        for copy in again:
            copy.start()

    up_store = pltpu.make_async_copy(
        up_weight.at[pl.ds(0, 3 * height), :], up_near_out, again_sem.at[0, 0]
    )

    def grad_turns(tick, half):
        gate_term, up_term = grad_term(gate_act), grad_term(up_act)
        if (tick, half) == (21, 0):
            for copy in again:
                copy.wait()
            for place in range(3):
                pl.semaphore_wait(free_sem.at[place], 1)
            gate_grads.far_term(gate_term, 3)
            gate_grads.far_term(gate_term, 1)
        elif (tick, half) == (21, 1):
            gate_grads.near_term(gate_term, 3)
            gate_grads.far_term(gate_term, 2)
        elif (tick, half) == (22, 0):
            gate_grads.near_term(gate_term, 1)
            gate_grads.far_term(gate_term, 0)
        elif (tick, half) == (22, 1):
            gate_grads.near_term(gate_term, 2)
            gate_grads.near_term(gate_term, 0)
        elif (tick, half) == (23, 0):
            for place in range(4):
                gate_grads.core_copy(place).wait_send()
            up_grads.far_term(up_term, 3)
            up_grads.far_term(up_term, 1)
        elif (tick, half) == (23, 1):
            gate_grads.take_corner()
            up_grads.near_term(up_term, 3)
            up_grads.far_term(up_term, 2)
        elif (tick, half) == (24, 0):
            up_grads.near_term(up_term, 1)
            up_grads.far_term(up_term, 0)
        elif (tick, half) == (24, 1):
            up_grads.near_term(up_term, 2)
            up_grads.near_term(up_term, 0)
        elif (tick, half) == (26, 0):
            gate_grads.take_final(lambda half: hidden.at[half])
            for half in range(HALVES):
                store(6, half).start()
        elif (tick, half) == (26, 1):
            up_grads.take_corner()
            up_store.start()

    def turns(tick, half):
        if (tick, half) == (2, 1):
            up_flow.arrive(2, (0,))
            up_flow.arrive(4, (0,))
        elif (tick, half) == (3, 0):
            up_flow.arrive(2, (1,))
            up_flow.arrive(4, (1,))
            down_flow.start(2, 4)
        elif (tick, half) == (4, 1):
            up_flow.arrive(6)
        elif (tick, half) == (5, 0):
            down_flow.arrive(2, (0,))
            down_flow.arrive(4, (0,))
        elif (tick, half) == (6, 0):
            down_flow.arrive(2, (1,))
            down_flow.arrive(4, (1,))
        elif (tick, half) == (7, 0):
            down_flow.arrive(6)

    attention_gain_out[...] = jnp.zeros_like(attention_gain_out)
    feedforward_gain_out[...] = jnp.zeros_like(feedforward_gain_out)

    def half_span(half):
        return pl.ds(half * half_rows, half_rows)

    def strips(half, body):
        def step(index, carry):
            body(
                pl.ds(pl.multiple_of(half * half_rows + index * STRIP, STRIP), STRIP),
                pl.ds(pl.multiple_of(index * STRIP, STRIP), STRIP),
            )
            return carry

        lax.fori_loop(0, half_rows // STRIP, step, 0)

    def sum_copy(chunk, step, half, way, dest):
        return pltpu.make_async_remote_copy(
            src_ref=partial.at[chunk, dest, half_span(half)],
            dst_ref=arrived.at[way, chunk, step - 1, half_span(half)],
            send_sem=sum_send.at[way, chunk, step - 1, half],
            recv_sem=sum_recv.at[way, chunk, step - 1, half],
            device_id={"tensor": me + 1 - 2 * way},
            device_id_type=pl.DeviceIdType.MESH,
        )

    def hand_copy(chunk, hop, half, way, origin):
        rows = everyone.at[origin, chunk, half_span(half)]
        return pltpu.make_async_remote_copy(
            src_ref=rows,
            dst_ref=rows,
            send_sem=hand_send.at[way, chunk, hop - 1, half],
            recv_sem=hand_recv.at[way, chunk, hop - 1, half],
            device_id={"tensor": me + 1 - 2 * way},
            device_id_type=pl.DeviceIdType.MESH,
        )

    def away(way):
        return me if way == 0 else last - me

    def sum_step(chunk, step, half):
        for way in range(2):
            distance = away(way)

            @pl.when(distance <= step - 1)
            def _():
                dest = me + size - step if way == 0 else me - size + step
                if step > 1:

                    @pl.when(distance >= 1)
                    def _():
                        sum_copy(chunk, step - 1, half, way, dest).wait_recv()

                        def add(rows, _):
                            partial[chunk, dest, rows] = low(
                                wide(partial[chunk, dest, rows])
                                + wide(arrived[way, chunk, step - 2, rows])
                            )

                        strips(half, add)

                sum_copy(chunk, step, half, way, dest).start()

    def sum_end(chunk, half):
        def begin(rows, here):
            total[here] = wide(partial[chunk, me, rows])

        strips(half, begin)
        for way in range(2):

            @pl.when(away(way) >= 1)
            def _():
                sum_copy(chunk, size - 1, half, way, me).wait_recv()

                def add(rows, here):
                    total[here] = total[here] + wide(arrived[way, chunk, size - 2, rows])

                strips(half, add)

    def sum_sent(chunk):
        for step in range(1, size):
            for way in range(2):

                @pl.when(away(way) <= step - 1)
                def _():
                    for half in range(HALVES):
                        sum_copy(chunk, step, half, way, 0).wait_send()

    def hand_first(chunk, half):
        for way in range(2):

            @pl.when(away(1 - way) >= 1)
            def _():
                hand_copy(chunk, 1, half, way, me).start()

    def hand_on(chunk, hop, half):
        for way in range(2):

            @pl.when(away(way) >= hop)
            def _():
                origin = me - hop if way == 0 else me + hop
                hand_copy(chunk, hop, half, way, origin).wait_recv()
                if hop < size - 1:

                    @pl.when(away(1 - way) >= 1)
                    def _():
                        hand_copy(chunk, hop + 1, half, way, origin).start()

    def hand_sent(chunk):
        for hop in range(1, size):
            for way in range(2):

                @pl.when(jnp.logical_and(away(way) >= hop - 1, away(1 - way) >= 1))
                def _():
                    for half in range(HALVES):
                        hand_copy(chunk, hop, half, way, 0).wait_send()

    def inverse_rms(values):
        return lax.rsqrt(jnp.mean(values * values, -1, keepdims=True) + EPS)

    def fold(values):
        return values[:8] + values[8:]

    def own_rows(chunk, stage, half):
        def after_branch(rows, here):
            value = total[here]
            branch[chunk, rows] = value
            state = wide(tokens[chunk, rows]) + value * inverse_rms(value) * attention_scale[...]
            hidden[chunk, rows] = state
            everyone[me, chunk, rows] = low(state)

        def after_mixed(rows, here):
            value = total[here]
            inverse = inverse_rms(value)
            normalized = value * inverse
            hidden[chunk, rows] = hidden[chunk, rows] + normalized * feedforward_scale[...]
            grad = wide(cotangent[chunk, rows])
            feedforward_gain_out[...] += fold(grad * normalized)
            everyone[me, chunk, rows] = low(
                norm_backward(grad, normalized, inverse, feedforward_scale[...])
            )

        def after_gradient(rows, here):
            grad = total[here] + wide(cotangent[chunk, rows])
            value = branch[chunk, rows]
            inverse = inverse_rms(value)
            normalized = value * inverse
            branch[chunk, rows] = grad
            attention_gain_out[...] += fold(grad * normalized)
            everyone[me, chunk, rows] = low(
                norm_backward(grad, normalized, inverse, attention_scale[...])
            )

        strips(half, (after_branch, after_mixed, after_gradient)[stage])

    def gathered(chunk):
        return everyone[:, chunk].reshape(all_rows, model_width)

    def tiles(first, end, body):
        def step(index, carry):
            body(pl.ds(pl.multiple_of(index * WIDE_TILE, WIDE_TILE), WIDE_TILE))
            return carry

        lax.fori_loop(first, end, step, 0)

    def store(kind, chunk):
        source, target = (
            (everyone.at[:, chunk], mlp_out.at[chunk]),
            (inner, inner_out.at[chunk]),
            (everyone.at[:, chunk], mixed_cot_out.at[chunk]),
            (everyone.at[:, chunk], branch_cot_out.at[:, chunk]),
            None,
            (branch.at[chunk], grad_hidden_out.at[chunk]),
            (hidden.at[chunk], gate_grad_out.at[pl.ds(chunk * chunk_rows, chunk_rows), :]),
        )[kind]
        return pltpu.make_async_copy(source, target, store_sem.at[kind, chunk])

    def block_stores(chunk):
        return [
            pltpu.make_async_copy(
                hidden.at[chunk, :, here],
                block_out.at[pl.ds(chunk * chunk_rows, chunk_rows), natural],
                shuffle_sem.at[chunk, place],
            )
            for place, (here, natural) in enumerate(column_blocks(model_width // 8))
        ]

    def put_partial(chunk, columns, values):
        partial[chunk, :, :, columns] = low(values).reshape(size, chunk_rows, WIDE_TILE)

    def branch_terms(chunk):
        def tile(columns):
            rows = attended[:, chunk].reshape(all_rows, attended.shape[-1])
            put_partial(
                chunk,
                columns,
                jnp.dot(rows, output_weight[:, columns], preferred_element_type=jnp.float32),
            )

        tiles(0, model_width // WIDE_TILE, tile)

    def gate_tile(chunk):
        def tile(columns):
            rows = gathered(chunk)
            gate = jnp.dot(rows, gate_weight[:, columns], preferred_element_type=jnp.float32)
            up = jnp.dot(rows, up_weight[:, columns], preferred_element_type=jnp.float32)
            gate_act[chunk, :, columns] = low(gate)
            up_act[chunk, :, columns] = low(up)
            inner[:, columns] = low(gate * jax.nn.sigmoid(gate) * up)

        return tile

    def down_tile(chunk):
        def tile(columns):
            put_partial(
                chunk,
                columns,
                jnp.dot(inner[...], down_weight[:, columns], preferred_element_type=jnp.float32),
            )

        return tile

    def grad_inner_tile(chunk):
        def tile(columns):
            grad = rows_product(gathered(chunk), down_weight[columns, :])
            gate = wide(gate_act[chunk, :, columns])
            up = wide(up_act[chunk, :, columns])
            sigmoid = jax.nn.sigmoid(gate)
            gate_act[chunk, :, columns] = low(
                grad * up * sigmoid * (1.0 + gate * (1.0 - sigmoid))
            )
            up_act[chunk, :, columns] = low(grad * gate * sigmoid)

        return tile

    def grad_inner_half_tile(chunk, half):
        spans = [
            pl.ds(origin * chunk_rows + half * half_rows, half_rows) for origin in range(size)
        ]

        def tile(columns):
            rows = everyone[:, chunk, half_span(half)].reshape(size * half_rows, model_width)
            grad = rows_product(rows, down_weight[columns, :])
            gate = wide(jnp.concatenate([gate_act[chunk, span, columns] for span in spans], 0))
            up = wide(jnp.concatenate([up_act[chunk, span, columns] for span in spans], 0))
            sigmoid = jax.nn.sigmoid(gate)
            for_gate = low(grad * up * sigmoid * (1.0 + gate * (1.0 - sigmoid)))
            for_up = low(grad * gate * sigmoid)
            for origin, span in enumerate(spans):
                here = slice(origin * half_rows, (origin + 1) * half_rows)
                gate_act[chunk, span, columns] = for_gate[here]
                up_act[chunk, span, columns] = for_up[here]

        return tile

    def grad_input_tile(chunk):
        def tile(columns):
            put_partial(
                chunk,
                columns,
                rows_product(gate_act[chunk], gate_weight[columns, :])
                + rows_product(up_act[chunk], up_weight[columns, :]),
            )

        return tile

    unit_tiles, width_tiles = units // WIDE_TILE, model_width // WIDE_TILE

    def forward_piece(chunk, piece):
        if piece == 0:
            if chunk == 0:
                for mask in (1, 3, 5, 7):
                    up_flow.arrive(mask)
                for copy in first_loads[3:6]:
                    copy.wait()
            store(0, chunk).start()
            tiles(0, unit_tiles // 2, gate_tile(chunk))
        elif piece == 1:
            tiles(unit_tiles // 2, unit_tiles, gate_tile(chunk))
            store(1, chunk).start()
            sum_sent(chunk)
            hand_sent(chunk)
        else:
            if chunk == 0:
                for mask in (1, 3, 5, 7):
                    down_flow.arrive(mask)
            tiles(0, width_tiles, down_tile(chunk))
            store(0, chunk).wait()
            store(1, chunk).wait()

    def backward_piece(chunk, piece):
        if piece == 0:
            store(2, chunk).start()
            for copy in block_stores(chunk):
                copy.start()
            tiles(0, unit_tiles // 2, grad_inner_half_tile(chunk, 1))
            tiles(unit_tiles // 2, unit_tiles, grad_inner_tile(chunk))
        elif piece == 1:
            sum_sent(chunk)
            hand_sent(chunk)
            tiles(0, width_tiles // 2, grad_input_tile(chunk))
        else:
            tiles(width_tiles // 2, width_tiles, grad_input_tile(chunk))
            store(2, chunk).wait()
            for copy in block_stores(chunk):
                copy.wait()
            if chunk == CHUNKS - 1:
                up_flow.sent()
                down_flow.sent()
                weights_free()

    def end_piece(chunk, piece):
        if piece == 0:
            store(3, chunk).start()
            store(5, chunk).start()

    first_loads[0].wait()
    first_loads[1].wait()
    for copy in first_loads[2:]:
        copy.start()
    branch_terms(0)
    first_loads[2].wait()
    for copy in first_loads[6:]:
        copy.wait()
    bases = {
        (chunk, stage): (CHUNKS * stage + chunk) * size
        for stage in range(3)
        for chunk in range(CHUNKS)
    }
    ticks = max(bases.values()) + 2 * size
    for tick in range(1, ticks + 1):
        for half in range(HALVES):
            for (chunk, stage), base in bases.items():
                at = tick - base
                if size < at < 2 * size:
                    hand_on(chunk, at - size, half)
            for (chunk, stage), base in bases.items():
                at = tick - base
                if 1 <= at < size:
                    sum_step(chunk, at, half)
                elif at == size:
                    sum_end(chunk, half)
                    own_rows(chunk, stage, half)
                    hand_first(chunk, half)
            turns(tick, half)
            if tick == 1 and half == 1:
                branch_terms(1)
            for (chunk, stage), base in bases.items():
                piece = (tick - base - 2 * size + 1) * HALVES + half - 1
                if piece == -1 and stage == 1:
                    tiles(0, unit_tiles // 2, grad_inner_half_tile(chunk, 0))
                elif 0 <= piece < 3:
                    (forward_piece, backward_piece, end_piece)[stage](chunk, piece)
            grad_turns(tick, half)
    gate_grads.sent(False)
    up_grads.sent()
    for chunk in range(CHUNKS):
        sum_sent(chunk)
        hand_sent(chunk)
        store(3, chunk).wait()
        store(5, chunk).wait()
        store(6, chunk).wait()
    up_store.wait()


def middle(
    attended,
    rows_all,
    cotangent_grouped,
    attention_scale,
    feedforward_scale,
    output_full,
    gate_full,
    up_shard,
    down_shard,
):
    size = lax.axis_size("tensor")
    own_rows, model_width = cotangent_grouped.shape
    chunk_rows = own_rows // CHUNKS
    all_rows = size * chunk_rows
    half_rows = chunk_rows // HALVES
    heads_width = attended.shape[1]
    units = gate_full.shape[1]
    chunked = (CHUNKS, chunk_rows, model_width)
    lined = (CHUNKS, size, chunk_rows, model_width)
    low_type, wide_type = jnp.bfloat16, jnp.float32

    def shape(dims, kind=low_type):
        return jax.ShapeDtypeStruct(dims, kind)

    anywhere = pl.BlockSpec(memory_space=pl.ANY)
    inside = pl.BlockSpec(memory_space=pltpu.VMEM)
    dma = pltpu.SemaphoreType.DMA
    flops = 2 * CHUNKS * all_rows * model_width * (2 * heads_width + 6 * units)
    outs = pl.pallas_call(
        functools.partial(middle_kernel, size),
        out_shape=[
            shape(lined),
            shape((CHUNKS, all_rows, units)),
            shape(lined),
            shape((size, CHUNKS, chunk_rows, model_width)),
            shape((own_rows, model_width), wide_type),
            shape(chunked, wide_type),
            shape((model_width // 8, units), wide_type),
            shape((3 * model_width // 8, units)),
            shape((8, model_width), wide_type),
            shape((8, model_width), wide_type),
        ],
        in_specs=[anywhere] * 3 + [inside] * 2 + [anywhere] * 4,
        out_specs=[anywhere] * 8 + [inside] * 2,
        scratch_shapes=[
            pltpu.VMEM((size, CHUNKS, chunk_rows, heads_width), low_type),
            pltpu.VMEM(chunked, low_type),
            pltpu.VMEM(chunked, low_type),
            pltpu.VMEM((heads_width, model_width), low_type),
            pltpu.VMEM((model_width, units), low_type),
            pltpu.VMEM((model_width, units), low_type),
            pltpu.VMEM((units, model_width), low_type),
            pltpu.VMEM((size, CHUNKS, chunk_rows, model_width), low_type),
            pltpu.VMEM((CHUNKS, all_rows, units), low_type),
            pltpu.VMEM((CHUNKS, all_rows, units), low_type),
            pltpu.VMEM((all_rows, units), low_type),
            pltpu.VMEM(chunked, wide_type),
            pltpu.VMEM(chunked, wide_type),
            pltpu.VMEM((2, CHUNKS, size - 1, chunk_rows, model_width), low_type),
            pltpu.VMEM(lined, low_type),
            pltpu.VMEM((half_rows, model_width), wide_type),
            dma((6,)),
            dma((8, CHUNKS)),
            dma((2, CHUNKS, size - 1, HALVES)),
            dma((2, CHUNKS, size - 1, HALVES)),
            dma((2, CHUNKS, size - 1, HALVES)),
            dma((2, CHUNKS, size - 1, HALVES)),
            dma((2, 7, 2)),
            dma((2, 7, 2)),
            dma((2, 10)),
            dma((2, 10)),
            dma((CHUNKS, size)),
            dma((CHUNKS, 8)),
            pltpu.SemaphoreType.REGULAR((3,)),
        ],
        compiler_params=pltpu.CompilerParams(
            collective_id=1, has_side_effects=True, vmem_limit_bytes=VMEM_BYTES
        ),
        cost_estimate=pl.CostEstimate(
            flops=flops, bytes_accessed=64 << 20, transcendentals=0
        ),
        name="middle",
    )(
        attended.reshape(size, CHUNKS, chunk_rows, heads_width),
        rows_all.reshape(size, *chunked),
        cotangent_grouped,
        attention_scale,
        feedforward_scale,
        output_full,
        gate_full,
        up_shard,
        down_shard,
    )
    rows = CHUNKS * all_rows
    return (
        outs[1].reshape(rows, units),
        outs[2].reshape(rows, model_width),
        outs[3].reshape(rows, model_width),
        outs[4],
        outs[5].reshape(own_rows, model_width),
        *outs[6:],
    )


def turn_kernel(
    size,
    branch_cot_hbm,
    output_hbm,
    query_rot_hbm,
    key_rot_hbm,
    value_hbm,
    query_hat_hbm,
    key_hat_hbm,
    cosine_hbm,
    sine_hbm,
    up_near,
    stats,
    query_scale,
    key_scale,
    attention_gain,
    feedforward_gain,
    grad_out,
    up_out,
    gain_terms,
    branch_cot,
    output_weight,
    query_rot,
    key_rot,
    value,
    query_hat,
    key_hat,
    cosine,
    sine,
    grad_attended,
    grad_query,
    grad_key,
    grad_value,
    scaled_query,
    scaled_key,
    products,
    shared,
    grad,
    up_own,
    up_final,
    up_total,
    load_sem,
    store_sem,
    share_send,
    share_recv,
    shard_send,
    shard_recv,
):
    me = lax.axis_index("tensor")
    group_rows, model_width = branch_cot.shape
    local_width = query_rot.shape[1]
    heads = local_width // 128
    own_rows = group_rows // size
    block = model_width // 8
    greet([(True, lax.rem(me + offset, size)) for offset in range(1, size)])
    loads = [
        pltpu.make_async_copy(source, target, load_sem.at[place])
        for place, (source, target) in enumerate(
            (
                (output_hbm, output_weight),
                (branch_cot_hbm, branch_cot),
                (key_rot_hbm, key_rot),
                (query_rot_hbm, query_rot),
                (value_hbm, value),
                (query_hat_hbm, query_hat),
                (key_hat_hbm, key_hat),
                (cosine_hbm, cosine),
                (sine_hbm, sine),
                (up_near.at[pl.ds(0, block), :], up_own),
            )
        )
    ]
    for copy in loads[:2]:
        copy.start()
    gain_terms[...] = jnp.zeros_like(gain_terms)
    products[...] = jnp.zeros_like(products)
    up_flow = ShardSum(
        stacked(up_near, 0, block),
        None,
        None,
        stacked(up_final, 0, block),
        shard_send,
        shard_recv,
        own=functools.partial(stacked(up_own, 0, block), 0),
    )
    pl.semaphore_wait(pltpu.get_barrier_semaphore(), 3 + size - 1)
    for half in range(2):
        for way in range(2):
            up_flow.final_copy(way, half).start()
    for copy in loads[:2]:
        copy.wait()
    for copy in loads[2:]:
        copy.start()

    def step_attended(index):
        here = pl.ds(pl.multiple_of(index * own_rows, own_rows), own_rows)
        for first in range(0, local_width, TILE):
            columns = pl.ds(first, TILE)
            grad_attended[here, columns] = low(
                rows_product(branch_cot[here, :], output_weight[columns, :])
            )

    each(size, step_attended)
    for copy in loads[2:]:
        copy.wait()
    score_scale = 128**-0.5

    def queries_block(origin, span):
        count = (origin + 1) * own_rows
        here = pl.ds(origin * own_rows, own_rows)
        keys = key_rot[pl.ds(0, count), span]
        queries = query_rot[here, span]
        grad_rows = grad_attended[here, span]
        return count, here, keys, queries, grad_rows

    def step_head(head):
        span = head_span(head)
        for origin in reversed(range(size)):
            count, here, keys, queries, grad_rows = queries_block(origin, span)
            scores = rows_product(keys, queries) * score_scale
            probs = jnp.exp(scores - stats[pl.ds(head, 1), here])
            near = probs[origin * own_rows :]
            near = jnp.where(ahead_of(near, 0, 0), 0.0, near)
            probs = jnp.concatenate([probs[: origin * own_rows], near], 0) if origin else near
            grad_probs = rows_product(value[pl.ds(0, count), span], grad_rows)
            delta = jnp.sum(grad_probs * probs, 0, keepdims=True)
            grad_scores = low(probs * (grad_probs - delta))
            for_values = jnp.dot(low(probs), grad_rows, preferred_element_type=jnp.float32)
            for_keys = jnp.dot(grad_scores, queries, preferred_element_type=jnp.float32)
            for_queries = jnp.dot(keys.T, grad_scores, preferred_element_type=jnp.float32)
            grad_query[here, :] = (for_queries * score_scale).T
            if origin == size - 1:
                grad_value[...] = for_values
                grad_key[...] = for_keys
            else:
                grad_value[pl.ds(0, count), :] += for_values
                grad_key[pl.ds(0, count), :] += for_keys
        grad[:, head_span(head + 2 * heads)] = low(grad_value[...])
        for kind, (source, factor, hat, scale, scaled) in enumerate(
            (
                (grad_query, 1.0, query_hat, query_scale, scaled_query),
                (grad_key, score_scale, key_hat, key_scale, scaled_key),
            )
        ):
            rotated = wide(low(source[...] * factor))
            normal = rotated * cosine[...] - pltpu.roll(rotated, 64, 1) * sine[...]
            hats = wide(hat[:, span])
            gain_terms[pl.ds(kind * heads + head, 1), :] = jnp.sum(
                normal * hats, 0, keepdims=True
            )
            normal = normal * scale[pl.ds(head, 1), :]
            scaled[:, span] = normal
            products[kind] += normal * hats

    each(heads, step_head)
    values_store = pltpu.make_async_copy(
        grad.at[:, pl.ds(2 * local_width, local_width)],
        grad_out.at[:, pl.ds(2 * local_width, local_width)],
        store_sem.at[0],
    )
    values_store.start()
    lines = []
    for kind in range(2):
        lines.append(
            jnp.concatenate(
                [
                    column_sums(products[kind, pl.ds(origin * own_rows, own_rows), :])
                    for origin in range(size)
                ],
                1,
            )
        )
    for gain in (attention_gain, feedforward_gain):
        total = jnp.sum(gain[...], 0, keepdims=True)
        lines += [total[:, : model_width // 2], total[:, model_width // 2 :]]
    lines.append(jnp.zeros((2, model_width // 2), jnp.float32))
    shared[me] = jnp.concatenate(lines, 0)

    def share_copy(offset):
        return pltpu.make_async_remote_copy(
            src_ref=shared.at[me],
            dst_ref=shared.at[me],
            send_sem=share_send.at[offset - 1],
            recv_sem=share_recv.at[offset - 1],
            device_id={"tensor": lax.rem(me + offset, size)},
            device_id_type=pl.DeviceIdType.MESH,
        )

    for offset in range(1, size):
        share_copy(offset).start()
    for offset in range(1, size):
        share_copy(offset).wait_recv()
    total = shared[0]
    for device in range(1, size):
        total = total + shared[device]
    for kind, (scaled, hat) in enumerate(((scaled_query, query_hat), (scaled_key, key_hat))):
        for origin in range(size):
            here = pl.ds(origin * own_rows, own_rows)
            columns = slice(origin * own_rows, (origin + 1) * own_rows)
            inner = turned_rows(total[kind : kind + 1, columns] / model_width)
            inverse = turned_rows(stats[pl.ds(heads + kind, 1), here])
            for head in range(heads):
                span = pl.ds(head * 128, 128)
                grad[here, pl.ds((kind * heads + head) * 128, 128)] = low(
                    inverse * (scaled[here, span] - wide(hat[here, span]) * inner)
                )
    rest_store = pltpu.make_async_copy(
        grad.at[:, pl.ds(0, 2 * local_width)],
        grad_out.at[:, pl.ds(0, 2 * local_width)],
        store_sem.at[1],
    )
    rest_store.start()
    height = gain_terms.shape[0] // 8
    for place in range(8):
        if place:
            gain_terms[pl.ds(place * height, 8), :] = gain_terms[pl.ds(0, 8), :]
        for kind in range(2):
            for line in range(block // 128):
                first = place * block + line * 128
                row, first = divmod(first, model_width // 2)
                gain_terms[
                    pl.ds(place * height + 8 + kind * (block // 128) + line, 1), :
                ] = total[2 + 2 * kind + row : 3 + 2 * kind + row, first : first + 128]
    up_flow.take_final(stacked(up_total, 0, block // 2))
    up_store = pltpu.make_async_copy(up_total, up_out, store_sem.at[2])
    up_store.start()
    for half in range(2):
        for way in range(2):
            up_flow.final_copy(way, half).wait_send()
    for offset in range(1, size):
        share_copy(offset).wait_send()
    up_store.wait()
    values_store.wait()
    rest_store.wait()


def turn(
    branch_cot,
    output_full,
    query_rot,
    key_rot,
    value_rows,
    query_hat,
    key_hat,
    cosine,
    sine,
    up_near,
    stats,
    query_scale,
    key_scale,
    attention_gain,
    feedforward_gain,
):
    size = lax.axis_size("tensor")
    group_rows, model_width = branch_cot.shape
    local_width = query_rot.shape[1]
    units = up_near.shape[1]
    low_type, wide_type = jnp.bfloat16, jnp.float32
    anywhere = pl.BlockSpec(memory_space=pl.ANY)
    inside = pl.BlockSpec(memory_space=pltpu.VMEM)
    dma = pltpu.SemaphoreType.DMA
    local_rows = (group_rows, local_width)
    table = (group_rows, 128)
    return pl.pallas_call(
        functools.partial(turn_kernel, size),
        out_shape=[
            jax.ShapeDtypeStruct((group_rows, 3 * local_width), low_type),
            jax.ShapeDtypeStruct((model_width // 8, units), wide_type),
            jax.ShapeDtypeStruct((8 * 32, 128), wide_type),
        ],
        in_specs=[anywhere] * 10 + [inside] * 5,
        out_specs=[anywhere, anywhere, inside],
        scratch_shapes=[
            pltpu.VMEM((group_rows, model_width), low_type),
            pltpu.VMEM((local_width, model_width), low_type),
            *[pltpu.VMEM(local_rows, low_type)] * 5,
            *[pltpu.VMEM(table, wide_type)] * 2,
            pltpu.VMEM(local_rows, low_type),
            *[pltpu.VMEM(table, wide_type)] * 3,
            *[pltpu.VMEM(local_rows, wide_type)] * 2,
            pltpu.VMEM((2, *table), wide_type),
            pltpu.VMEM((size, 8, model_width // 2), wide_type),
            pltpu.VMEM((group_rows, 3 * local_width), low_type),
            pltpu.VMEM((model_width // 8, units), low_type),
            pltpu.VMEM((2 * model_width // 8, units), low_type),
            pltpu.VMEM((model_width // 8, units), wide_type),
            dma((10,)),
            dma((3,)),
            dma((size - 1,)),
            dma((size - 1,)),
            dma((10,)),
            dma((10,)),
        ],
        compiler_params=pltpu.CompilerParams(
            collective_id=3, has_side_effects=True, vmem_limit_bytes=VMEM_BYTES
        ),
        cost_estimate=pl.CostEstimate(
            flops=2 * group_rows * model_width * local_width + 10 * group_rows**2 * local_width,
            bytes_accessed=16 << 20,
            transcendentals=group_rows**2 * local_width // 128,
        ),
        name="turn",
    )(
        branch_cot,
        output_full,
        query_rot,
        key_rot,
        value_rows,
        query_hat,
        key_hat,
        cosine,
        sine,
        up_near,
        stats,
        query_scale,
        key_scale,
        attention_gain,
        feedforward_gain,
    )


def back_kernel(
    size,
    grad_hbm,
    weight_hbm,
    attended_hbm,
    branch_cot_hbm,
    mixed_cot_hbm,
    inner_hbm,
    rows_hbm,
    gain_hbm,
    hidden_hbm,
    tokens_out,
    down_out,
    output_out,
    query_out,
    key_out,
    value_out,
    gain_out,
    grad,
    weight,
    attended,
    branch_cot,
    mixed_cot,
    inner,
    rows,
    gain,
    hidden,
    partial,
    arrived,
    down_far,
    down_near,
    output_far,
    output_near,
    attention_far,
    attention_near,
    gain_far,
    gain_near,
    down_total,
    output_total,
    load_sem,
    store_sem,
    sum_send,
    sum_recv,
    shard_send,
    shard_recv,
):
    me = lax.axis_index("tensor")
    last = size - 1
    own_rows, model_width = partial.shape[1:]
    piece_rows = own_rows // PIECES
    height = model_width // 8
    greet(((me < last, me + 1), (me > 0, me - 1)))
    loads = [
        pltpu.make_async_copy(source, target, load_sem.at[place])
        for place, (source, target) in enumerate(
            (
                (grad_hbm, grad),
                (weight_hbm, weight),
                (attended_hbm, attended),
                (branch_cot_hbm, branch_cot),
                (mixed_cot_hbm, mixed_cot),
                (inner_hbm, inner),
                (rows_hbm, rows),
                (gain_hbm, gain),
                (hidden_hbm, hidden),
            )
        )
    ]
    for place in (0, 1):
        loads[place].start()

    def flow(kind, near, far, shard_height):
        return ShardSum(
            stacked(near, 0, shard_height),
            stacked(far, 0, shard_height),
            lambda half: stacked(near, 4 * shard_height, shard_height)(0, half),
            lambda way, half: stacked(near, 5 * shard_height, shard_height)(way, half),
            shard_send.at[kind],
            shard_recv.at[kind],
        )

    down_flow = flow(0, down_near, down_far, height)
    output_flow = flow(1, output_near, output_far, height)
    attention_flow = flow(2, attention_near, attention_far, height)
    gain_flow = flow(3, gain_near, gain_far, gain.shape[0] // 8)
    flows = (down_flow, output_flow, attention_flow, gain_flow)

    def columns_of(source):
        return lambda place, width: source[:, pl.ds(place * width, width)]

    down_term = product_term(columns_of(mixed_cot), lambda columns, _: inner[:, columns])
    output_term = product_term(columns_of(branch_cot), lambda columns, _: attended[:, columns])
    attention_term = product_term(columns_of(rows), lambda columns, _: grad[:, columns])

    def gain_term(place, target, adds):
        value = gain[pl.ds(place * target.shape[0], target.shape[0]), :]
        target[...] = value + target[...] if adds else value

    def terms(dest):
        def step(index, carry):
            columns = pl.ds(pl.multiple_of(index * WIDE_TILE, WIDE_TILE), WIDE_TILE)
            span = pl.ds(pl.multiple_of(dest * own_rows, own_rows), own_rows)
            partial[dest, :, columns] = low(rows_product(grad[span, :], weight[columns, :]))
            return carry

        lax.fori_loop(0, model_width // WIDE_TILE, step, 0)

    def terms_at(distance):
        for way in range(2):

            @pl.when(away(1 - way) >= distance)
            def _():
                terms(me + distance if way == 0 else me - distance)

    def away(way):
        return me if way == 0 else last - me

    def span_of(piece):
        return pl.ds(piece * piece_rows, piece_rows)

    def sum_copy(step, piece, way, dest):
        return pltpu.make_async_remote_copy(
            src_ref=partial.at[dest, span_of(piece)],
            dst_ref=arrived.at[way, step - 1, span_of(piece)],
            send_sem=sum_send.at[way, step - 1, piece],
            recv_sem=sum_recv.at[way, step - 1, piece],
            device_id={"tensor": me + 1 - 2 * way},
            device_id_type=pl.DeviceIdType.MESH,
        )

    def sum_step(step, *pieces):
        for piece in pieces:
            for way in range(2):
                distance = away(way)

                @pl.when(distance <= step - 1)
                def _():
                    dest = me + size - step if way == 0 else me - size + step
                    if step > 1:

                        @pl.when(distance >= 1)
                        def _():
                            sum_copy(step - 1, piece, way, dest).wait_recv()
                            add_into(
                                partial.at[dest, span_of(piece)],
                                arrived.at[way, step - 2, span_of(piece)],
                            )

                    sum_copy(step, piece, way, dest).start()

    def sum_end(*pieces):
        for piece in pieces:
            add_into(hidden.at[span_of(piece)], partial.at[me, span_of(piece)])
            for way in range(2):

                @pl.when(away(way) >= 1)
                def _():
                    sum_copy(size - 1, piece, way, me).wait_recv()
                    add_into(
                        hidden.at[span_of(piece)], arrived.at[way, size - 2, span_of(piece)]
                    )

            for copy in token_stores(piece):
                copy.start()

    def token_stores(piece):
        return [
            pltpu.make_async_copy(
                hidden.at[span_of(piece), here],
                tokens_out.at[span_of(piece), natural],
                store_sem.at[1 + piece, place],
            )
            for place, (here, natural) in enumerate(column_blocks(height))
        ]

    def halves_of(total):
        rows_of_half = total.shape[0] // 2
        return lambda half: total.at[pl.ds(half * rows_of_half, rows_of_half), :]

    stores = [
        pltpu.make_async_copy(source, target, store_sem.at[0, place])
        for place, (source, target) in enumerate(((down_total, down_out), (output_total, output_out)))
    ]
    tiles = attended.shape[1] // TILE
    attention_stores = [
        pltpu.make_async_copy(
            down_total.at[pl.ds((kind * tiles + tile) * height, height), :],
            out.at[:, pl.ds(tile * TILE, TILE)],
            store_sem.at[0, 2 + kind * tiles + tile],
        )
        for kind, out in enumerate((query_out, key_out, value_out))
        for tile in range(tiles)
    ]

    pl.semaphore_wait(
        pltpu.get_barrier_semaphore(), 3 + jnp.minimum(me, 1) + jnp.minimum(last - me, 1)
    )
    loads[0].wait()
    loads[1].wait()
    for place in (3, 2, 4, 5, 7, 6, 8):
        loads[place].start()
    terms_at(3)
    sum_step(1, *range(PIECES))
    loads[2].wait()
    loads[3].wait()
    output_flow.first_terms(output_term)
    output_flow.other_terms(output_term)
    loads[4].wait()
    loads[5].wait()
    down_flow.first_terms(down_term)
    terms_at(2)
    sum_step(2, 0)
    down_flow.other_terms(down_term)
    loads[7].wait()
    gain_flow.first_terms(gain_term)
    gain_flow.other_terms(gain_term)
    sum_step(2, 1)
    output_flow.take_corner()
    sum_step(2, 2)
    terms_at(1)
    loads[6].wait()
    attention_flow.first_terms(attention_term)
    sum_step(2, 3)
    attention_flow.other_terms(attention_term)
    sum_step(3, 0)
    down_flow.take_corner()
    gain_flow.take_corner()
    sum_step(3, 1)
    terms(me)
    sum_step(3, 2)
    sum_step(3, 3)
    loads[8].wait()
    attention_flow.take_corner()
    output_flow.take_final_turned(output_total)
    stores[1].start()
    gain_flow.take_final(halves_of(gain_out))
    sum_end(0)
    sum_end(1)
    down_flow.take_final_turned(down_total)
    stores[0].start()
    sum_end(2)
    sum_end(3)
    stores[0].wait()
    attention_flow.take_final_tiles(down_total)
    for copy in attention_stores:
        copy.start()
    for shard_flow in flows:
        shard_flow.sent()
    for step in range(1, size):
        for way in range(2):

            @pl.when(away(way) <= step - 1)
            def _():
                for piece in range(PIECES):
                    sum_copy(step, piece, way, 0).wait_send()

    for copy in stores[1:] + attention_stores:
        copy.wait()
    for piece in range(PIECES):
        for copy in token_stores(piece):
            copy.wait()


def back(
    grad_projected,
    attention_full,
    attended,
    branch_cot,
    mixed_cot,
    inner,
    rows_all,
    gain_terms,
    grad_hidden,
):
    size = lax.axis_size("tensor")
    own_rows, model_width = grad_hidden.shape
    height = model_width // 8
    operands = (
        grad_projected,
        attention_full,
        attended,
        branch_cot,
        mixed_cot,
        inner,
        rows_all,
        gain_terms,
        grad_hidden,
    )
    widths = (inner.shape[1], attended.shape[1], grad_projected.shape[1])
    gain_height, gain_width = gain_terms.shape[0] // 8, gain_terms.shape[1]
    low_type, wide_type = jnp.bfloat16, jnp.float32
    anywhere = pl.BlockSpec(memory_space=pl.ANY)
    dma = pltpu.SemaphoreType.DMA
    buffers = []
    for width in widths:
        buffers.append(pltpu.VMEM((4 * height, width), low_type))
        buffers.append(pltpu.VMEM((7 * height, width), low_type))
    return pl.pallas_call(
        functools.partial(back_kernel, size),
        out_shape=[
            jax.ShapeDtypeStruct((own_rows, model_width), wide_type),
            *(jax.ShapeDtypeStruct((width, height), wide_type) for width in widths[:2]),
            *[jax.ShapeDtypeStruct((height, attended.shape[1]), wide_type)] * 3,
            jax.ShapeDtypeStruct((gain_height, gain_width), wide_type),
        ],
        in_specs=[anywhere] * 9,
        out_specs=[anywhere] * 6 + [pl.BlockSpec(memory_space=pltpu.VMEM)],
        scratch_shapes=[
            *(pltpu.VMEM(operand.shape, operand.dtype) for operand in operands),
            pltpu.VMEM((size, own_rows, model_width), low_type),
            pltpu.VMEM((2, size - 1, own_rows, model_width), low_type),
            *buffers,
            pltpu.VMEM((4 * gain_height, gain_width), wide_type),
            pltpu.VMEM((7 * gain_height, gain_width), wide_type),
            *(pltpu.VMEM((width, height), wide_type) for width in widths[:2]),
            dma((9,)),
            dma((1 + PIECES, 8)),
            dma((2, size - 1, PIECES)),
            dma((2, size - 1, PIECES)),
            dma((4, 10)),
            dma((4, 10)),
        ],
        compiler_params=pltpu.CompilerParams(
            collective_id=2, has_side_effects=True, vmem_limit_bytes=VMEM_BYTES
        ),
        cost_estimate=pl.CostEstimate(
            flops=2 * size * own_rows * model_width * (sum(widths) + widths[2]),
            bytes_accessed=48 << 20,
            transcendentals=0,
        ),
        name="back",
    )(*operands)


def finish_kernel(count, *refs):
    sources, targets, buffers = refs[:count], refs[count : 2 * count], refs[2 * count : -1]
    sem = refs[-1]
    loads, stores = (
        [
            pltpu.make_async_copy(source, target, sem.at[way, place])
            for place, (source, target) in enumerate(pairs)
        ]
        for way, pairs in enumerate((zip(sources, buffers), zip(buffers, targets)))
    )
    for copy in loads:
        copy.start()
    for load, store in zip(loads, stores):
        load.wait()
        store.start()
    for copy in stores:
        copy.wait()


def finish(*arrays):
    anywhere = pl.BlockSpec(memory_space=pl.ANY)
    count = len(arrays)
    return pl.pallas_call(
        functools.partial(finish_kernel, count),
        out_shape=[jax.ShapeDtypeStruct(array.shape, array.dtype) for array in arrays],
        in_specs=[anywhere] * count,
        out_specs=[anywhere] * count,
        scratch_shapes=[
            *(pltpu.VMEM(array.shape, array.dtype) for array in arrays),
            pltpu.SemaphoreType.DMA((2, count)),
        ],
        compiler_params=pltpu.CompilerParams(vmem_limit_bytes=VMEM_BYTES),
        name="finish",
    )(*arrays)


def local(
    tokens,
    positions,
    cotangent,
    query_weight,
    key_weight,
    value_weight,
    output_weight,
    gate_weight,
    up_weight,
    down_weight,
    query_gain,
    key_gain,
    attention_gain,
    feedforward_gain,
):
    data_size = lax.axis_size("dp")
    data_index = lax.axis_index("dp")
    high_count = data_size // 8
    width = attention_gain.shape[0]
    channels, local_heads = query_gain.shape

    def high_block(low_bits, place):
        return low_bits + 8 * ((data_index // 8) ^ place)

    def grouped(array_in):
        if high_count == 1:
            return array_in
        return jnp.concatenate(
            [
                lax.dynamic_slice_in_dim(array_in, high_block(low_bits, place) * width, width, -1)
                for low_bits in range(8)
                for place in range(high_count)
            ],
            -1,
        )

    def ungrouped(array_in):
        if high_count == 1:
            return array_in
        return jnp.concatenate(
            [
                lax.dynamic_slice_in_dim(
                    array_in,
                    (low_bits * high_count + ((data_index // 8) ^ high_bits)) * width,
                    width,
                    -1,
                )
                for high_bits in range(high_count)
                for low_bits in range(8)
            ],
            -1,
        )

    head_gains = jnp.concatenate([query_gain.T, key_gain.T], 0)
    head_gains = lax.dynamic_update_slice_in_dim(
        jnp.zeros((2 * local_heads, channels * data_size), head_gains.dtype),
        head_gains,
        data_index * channels,
        1,
    )
    for bit in range(3, bits_of(data_size)):
        head_gains = head_gains + swap(head_gains, 1 << bit)
    gain_lines = [
        head_gains,
        gather_high(attention_gain[None], 1).reshape(-1, 128),
        gather_high(feedforward_gain[None], 1).reshape(-1, 128),
    ]
    line_count = sum(lines.shape[0] for lines in gain_lines)
    gain_shard = jnp.pad(jnp.concatenate(gain_lines, 0), ((0, 32 - line_count), (0, 0)))
    (
        rows_all,
        attention_full,
        output_full,
        gate_full,
        attended,
        query_rot,
        key_rot,
        value_rows,
        query_hat,
        key_hat,
        cosine,
        sine,
        stats,
        query_scale,
        key_scale,
        attention_scale,
        feedforward_scale,
    ) = front(
        grouped(tokens),
        gather_high(query_weight, 0),
        gather_high(key_weight, 0),
        gather_high(value_weight, 0),
        gather_high(output_weight, 1),
        gather_high(gate_weight, 0),
        gain_shard,
        positions,
    )
    (
        inner_act,
        mixed_cot,
        branch_cot,
        block_grouped,
        grad_hidden,
        grad_gate,
        up_near,
        attention_gain_part,
        feedforward_gain_part,
    ) = middle(
        attended,
        rows_all,
        grouped(cotangent),
        attention_scale,
        feedforward_scale,
        output_full,
        gate_full,
        gather_high(up_weight, 0),
        gather_high(down_weight, 1),
    )
    grad_projected, grad_up, gain_terms = turn(
        branch_cot,
        output_full,
        query_rot,
        key_rot,
        value_rows,
        query_hat,
        key_hat,
        cosine,
        sine,
        up_near,
        stats,
        query_scale,
        key_scale,
        attention_gain_part,
        feedforward_gain_part,
    )
    tokens_part, grad_down, grad_output, grad_query, grad_key, grad_value, gain_part = back(
        grad_projected,
        attention_full,
        attended,
        branch_cot,
        mixed_cot,
        inner_act,
        rows_all.reshape(-1, rows_all.shape[-1]),
        gain_terms,
        grad_hidden,
    )
    head_part = gain_part[: 2 * local_heads]
    for bit in range(3, bits_of(data_size)):
        head_part = head_part + swap(head_part, 1 << bit)
    head_part = lax.dynamic_slice_in_dim(head_part, data_index * channels, channels, 1)
    norm_part = gain_part[2 * local_heads : line_count].reshape(2, -1)

    def own_high(total, axis):
        return wide(scatter_high(total, axis))

    large = (
        ungrouped(block_grouped),
        ungrouped(tokens_part),
        own_high(grad_query, 0),
        own_high(grad_key, 0),
        own_high(grad_value, 0),
        own_high(grad_output, 1),
        own_high(grad_gate, 0),
        own_high(grad_up, 0),
        own_high(grad_down, 1),
    )
    if high_count == 1:
        large = finish(*large)
    return (
        *large,
        head_part[:local_heads].T,
        head_part[local_heads:].T,
        own_high(norm_part[0], 0),
        own_high(norm_part[1], 0),
    )


def solution(mesh):
    return jax.shard_map(
        local,
        mesh=mesh,
        in_specs=(
            P(("dp", "tensor"), None),
            P("dp"),
            P(("dp", "tensor"), None),
            P("dp", "tensor"),
            P("dp", "tensor"),
            P("dp", "tensor"),
            P("tensor", "dp"),
            P("dp", "tensor"),
            P("dp", "tensor"),
            P("tensor", "dp"),
            P("dp", "tensor"),
            P("dp", "tensor"),
            P("dp"),
            P("dp"),
        ),
        out_specs=(
            P(("dp", "tensor"), None),
            P(("dp", "tensor"), None),
            P("dp", "tensor"),
            P("dp", "tensor"),
            P("dp", "tensor"),
            P("tensor", "dp"),
            P("dp", "tensor"),
            P("dp", "tensor"),
            P("tensor", "dp"),
            P("dp", "tensor"),
            P("dp", "tensor"),
            P("dp"),
            P("dp"),
        ),
        check_vma=False,
    )
```

```python
import functools

import jax
import jax.numpy as jnp
import numpy as np
from jax import lax
from jax.experimental import pallas as pl
from jax.experimental.pallas import tpu as pltpu
from jax.sharding import PartitionSpec as P

EPS = 1e-06
THETA = 500000.0
MASKED = -1e30
VMEM_BYTES = 64 * 1024 * 1024 - 128 * 1024


def norm_backward(grad_in, normalized, inverse_rms, gain_values):
    scaled = grad_in * gain_values
    return inverse_rms * (scaled - normalized * jnp.mean(scaled * normalized, -1, keepdims=True))


def bits_of(size):
    return size.bit_length() - 1


def swap(array_in, mask):
    size = lax.axis_size("dp")
    return lax.ppermute(array_in, "dp", [(index, index ^ mask) for index in range(size)])


def gather_high(shard, axis):
    for bit in range(3, bits_of(lax.axis_size("dp"))):
        shard = jnp.concatenate([shard, swap(shard, 1 << bit)], axis)
    return shard


def scatter_high(total, axis):
    for bit in reversed(range(3, bits_of(lax.axis_size("dp")))):
        kept, sent = jnp.split(total, 2, axis)
        total = low(wide(kept) + wide(swap(low(sent), 1 << bit)))
    return total


def low(array_in):
    return array_in.astype(jnp.bfloat16)


def wide(array_in):
    return array_in.astype(jnp.float32)


def rows_product(left, right):
    return lax.dot_general(
        left, right, (((1,), (1,)), ((), ())), preferred_element_type=jnp.float32
    )


TILE = 256
WIDE_TILE = 512
STRIP = 16
CHUNKS = 2
HALVES = 2
PIECES = 4


def shard_peer(mask):
    index = lax.axis_index("dp")
    return index + mask - 2 * mask * ((index // mask) % 2)


def low_place(mask):
    index = lax.axis_index("dp")
    total = 0
    for bit in (1, 2, 4):
        value = (index // bit) % 2
        total = total + bit * (1 - value if mask & bit else value)
    return total


ROUTE = {1: (1, 1), 2: (2, 2), 3: (1, 1), 4: (4, 4), 5: (1, 1), 6: (4, 2), 7: (1, 1)}
PLACES = {mask: place for place, mask in enumerate((0, 2, 4, 6, 1, 3, 5, 7))}


def column_blocks(width):
    return [
        (
            pl.ds(place * width, width),
            pl.ds(pl.multiple_of(low_place(mask) * width, width), width),
        )
        for mask, place in PLACES.items()
    ]


class ShardGather:
    def __init__(self, own, target, send_sem, recv_sem):
        self.own, self.target, self.send_sem, self.recv_sem = own, target, send_sem, recv_sem

    def copy(self, mask, half):
        route = ROUTE[mask][half]
        before = mask ^ route
        return pltpu.make_async_remote_copy(
            src_ref=self.target(PLACES[before], half) if before else self.own(half),
            dst_ref=self.target(PLACES[mask], half),
            send_sem=self.send_sem.at[mask - 1, half],
            recv_sem=self.recv_sem.at[mask - 1, half],
            device_id={"dp": shard_peer(route)},
            device_id_type=pl.DeviceIdType.MESH,
        )

    def start(self, *masks):
        for half in range(2):
            for mask in masks:
                self.copy(mask, half).start()

    def arrive(self, mask, halves=(0, 1)):
        for half in halves:
            self.copy(mask, half).wait_recv()
            for after, route in ROUTE.items():
                if after != mask and after ^ route[half] == mask:
                    self.copy(after, half).start()

    def sent(self):
        for mask in ROUTE:
            for half in range(2):
                self.copy(mask, half).wait_send()


def row_halves(buffer, height):
    def target(place, half):
        return buffer.at[pl.ds(place * height + half * (height // 2), height // 2), :]

    return target


def column_halves(buffer, width):
    height = buffer.shape[0] // 2

    def target(place, half):
        return buffer.at[pl.ds(half * height, height), pl.ds(place * width, width)]

    return target


def own_halves(shard):
    height = shard.shape[0] // 2
    return lambda half: shard.at[pl.ds(half * height, height), :]


def greet(line_devices):
    barrier = pltpu.get_barrier_semaphore()
    for mask in (1, 2, 4):
        pl.semaphore_signal(
            barrier,
            inc=1,
            device_id={"dp": shard_peer(mask)},
            device_id_type=pl.DeviceIdType.MESH,
        )
    for there, index in line_devices:

        @pl.when(there)
        def _():
            pl.semaphore_signal(
                barrier,
                inc=1,
                device_id={"tensor": index},
                device_id_type=pl.DeviceIdType.MESH,
            )


def turned_rows(row):
    return jnp.broadcast_to(row, (128, row.shape[1])).T


def column_sums(values):
    total = values[:, :128]
    for first in range(128, values.shape[1], 128):
        total = total + values[:, first : first + 128]
    return jnp.sum(total.T, 0, keepdims=True)


def ahead_of(values, first_key, first_query):
    key = first_key + lax.broadcasted_iota(jnp.int32, values.shape, 0)
    query = first_query + lax.broadcasted_iota(jnp.int32, values.shape, 1)
    return key > query


def head_span(head):
    return pl.ds(pl.multiple_of(head * 128, 128), 128)


def each(count, body):
    def step(index, carry):
        body(index)
        return carry

    lax.fori_loop(0, count, step, 0)


def front_kernel(
    size,
    tokens_hbm,
    query_hbm,
    key_hbm,
    value_hbm,
    output_hbm,
    gate_hbm,
    gain_hbm,
    positions,
    frequency,
    rows_out,
    attention_out,
    output_out,
    gate_out,
    attended_out,
    query_rot_out,
    key_rot_out,
    value_out,
    query_hat_out,
    key_hat_out,
    cosine_out,
    sine_out,
    stats,
    query_scale,
    key_scale,
    attention_scale,
    feedforward_scale,
    rows,
    weight,
    projected,
    gain,
    cosine,
    sine,
    squares,
    query_rot,
    key_rot,
    value,
    query_hat,
    key_hat,
    attended,
    load_sem,
    store_sem,
    hand_send,
    hand_recv,
    shard_send,
    shard_recv,
    square_send,
    square_recv,
):
    me = lax.axis_index("tensor")
    last = size - 1
    own_rows, model_width = rows.shape[1:]
    piece_rows = own_rows // PIECES
    local_width = query_hbm.shape[1]
    heads = local_width // 128
    everyone = True
    greet([(everyone, lax.rem(me + offset, size)) for offset in range(1, size)])
    block = model_width // 8
    token_loads = [
        pltpu.make_async_copy(
            tokens_hbm.at[:, natural], rows.at[me, :, here], load_sem.at[0, place]
        )
        for place, (here, natural) in enumerate(column_blocks(block))
    ]
    shard_rows = pl.ds(0, query_hbm.shape[0])
    loads = [
        pltpu.make_async_copy(source, target, load_sem.at[1, place])
        for place, (source, target) in enumerate(
            (
                (query_hbm, weight.at[shard_rows, pl.ds(0, local_width)]),
                (key_hbm, weight.at[shard_rows, pl.ds(local_width, local_width)]),
                (value_hbm, weight.at[shard_rows, pl.ds(2 * local_width, local_width)]),
                (gain_hbm, gain.at[pl.ds(0, gain_hbm.shape[0]), :]),
                (output_hbm, output_out.at[:, pl.ds(0, output_hbm.shape[1])]),
                (gate_hbm, gate_out.at[pl.ds(0, gate_hbm.shape[0]), :]),
            )
        )
    ]
    for copy in token_loads + loads:
        copy.start()
    attention_target = row_halves(weight, query_hbm.shape[0])
    attention_flow, output_flow, gate_flow, gain_flow = (
        ShardGather(own, target, shard_send.at[kind], shard_recv.at[kind])
        for kind, (own, target) in enumerate(
            (
                (functools.partial(attention_target, 0), attention_target),
                (own_halves(output_hbm), column_halves(output_out, output_hbm.shape[1])),
                (own_halves(gate_hbm), row_halves(gate_out, gate_hbm.shape[0])),
                (own_halves(gain_hbm), row_halves(gain, gain_hbm.shape[0])),
            )
        )
    )
    pl.semaphore_wait(pltpu.get_barrier_semaphore(), 3 + size - 1)

    def away(way):
        return me if way == 0 else last - me

    def hand_copy(hop, piece, way, origin):
        here = rows.at[origin, pl.ds(piece * piece_rows, piece_rows)]
        return pltpu.make_async_remote_copy(
            src_ref=here,
            dst_ref=here,
            send_sem=hand_send.at[way, hop - 1, piece],
            recv_sem=hand_recv.at[way, hop - 1, piece],
            device_id={"tensor": me + 1 - 2 * way},
            device_id_type=pl.DeviceIdType.MESH,
        )

    for copy in token_loads:
        copy.wait()
    for piece in range(PIECES):
        for way in range(2):

            @pl.when(away(1 - way) >= 1)
            def _():
                hand_copy(1, piece, way, me).start()

        if piece == 0:
            for copy in loads[:3]:
                copy.wait()
            attention_flow.start(2, 4, 1)
            gain_flow.start(2, 4, 1)

    def hand_on(hop, piece):
        for way in range(2):

            @pl.when(away(way) >= hop)
            def _():
                origin = me - hop if way == 0 else me + hop
                hand_copy(hop, piece, way, origin).wait_recv()
                if hop < size - 1:

                    @pl.when(away(1 - way) >= 1)
                    def _():
                        hand_copy(hop + 1, piece, way, origin).start()

    def row_store(origin):
        return pltpu.make_async_copy(rows.at[origin], rows_out.at[origin], store_sem.at[0, origin])

    whole_stores = [
        pltpu.make_async_copy(source, target, store_sem.at[1 + place // size, place % size])
        for place, (source, target) in enumerate(
            (
                (weight, attention_out),
                (cosine, cosine_out),
                (sine, sine_out),
                (query_hat, query_hat_out),
                (key_hat, key_hat_out),
                (query_rot, query_rot_out),
                (key_rot, key_rot_out),
                (value, value_out),
                (attended, attended_out),
            )
        )
    ]

    def span_of(origin):
        return pl.ds(pl.multiple_of(origin * own_rows, own_rows), own_rows)

    def square_copy(offset, origin):
        return pltpu.make_async_remote_copy(
            src_ref=squares.at[me, origin],
            dst_ref=squares.at[me, origin],
            send_sem=square_send.at[offset - 1, origin],
            recv_sem=square_recv.at[offset - 1, origin],
            device_id={"tensor": lax.rem(me + offset, size)},
            device_id_type=pl.DeviceIdType.MESH,
        )

    def project(origin):
        def step(index):
            columns = pl.ds(pl.multiple_of(index * WIDE_TILE, WIDE_TILE), WIDE_TILE)
            projected[origin, :, columns] = jnp.dot(
                rows[origin], weight[:, columns], preferred_element_type=jnp.float32
            )

        row_store(origin).start()
        each(weight.shape[1] // WIDE_TILE, step)
        queries = projected[origin, :, pl.ds(0, local_width)]
        keys = projected[origin, :, pl.ds(local_width, local_width)]
        squares[me, origin, pl.ds(0, 8), :] = jnp.concatenate(
            [
                column_sums(queries * queries),
                column_sums(keys * keys),
                jnp.zeros((6, own_rows), jnp.float32),
            ],
            0,
        )
        for offset in range(1, size):
            square_copy(offset, origin).start()

    def project_from(hop, way):
        @pl.when(away(way) >= hop)
        def _():
            project(me - hop if way == 0 else me + hop)

    def normalize(origin):
        for offset in range(1, size):
            square_copy(offset, origin).wait_recv()
        total = squares[0, origin]
        for device in range(1, size):
            total = total + squares[device, origin]
        inverse = lax.rsqrt(total / model_width + EPS)
        here = span_of(origin)
        stats[pl.ds(heads, 2), here] = inverse[:2]
        for kind, (hat, rot, scale) in enumerate(
            ((query_hat, query_rot, query_scale), (key_hat, key_rot, key_scale))
        ):
            column = turned_rows(inverse[kind : kind + 1])

            def step(head):
                span = head_span(head)
                source = head_span(head + kind * heads)
                normalized = projected[origin, :, source] * column
                hat[here, span] = low(normalized)
                scaled = normalized * scale[pl.ds(head, 1), :]
                rot[here, span] = low(
                    scaled * cosine[here, :] + pltpu.roll(scaled, 64, 1) * sine[here, :]
                )

            each(heads, step)
        value[here, :] = low(projected[origin, :, pl.ds(2 * local_width, local_width)])

    def tables():
        for origin in range(size):
            here = pl.ds(origin * own_rows, own_rows)
            angles = turned_rows(wide(positions[:, here])) * frequency[...]
            cosine[here, :] = jnp.cos(angles)
            lane = lax.broadcasted_iota(jnp.int32, angles.shape, 1)
            sine[here, :] = jnp.where(lane < 64, -1.0, 1.0) * jnp.sin(angles)

    def scales():
        for kind, scale in enumerate((query_scale, key_scale)):
            total = wide(gain[pl.ds(0, 16), :])
            for place in range(1, 8):
                total = total + wide(gain[pl.ds(place * gain_hbm.shape[0], 16), :])
            scale[...] = jnp.concatenate(
                [total[kind * heads : (kind + 1) * heads], jnp.zeros((8 - heads, 128), jnp.float32)],
                0,
            )
        for place in range(8):
            lines = wide(gain[pl.ds(place * gain_hbm.shape[0], 16), :])
            for kind, scale in enumerate((attention_scale, feedforward_scale)):
                for line in range(block // 128):
                    at = 2 * heads + kind * (block // 128) + line
                    scale[:, pl.ds(place * block + line * 128, 128)] = lines[at : at + 1]

    def attend(head):
        span = head_span(head)
        for origin in range(size):
            count = (origin + 1) * own_rows
            here = pl.ds(origin * own_rows, own_rows)
            scores = rows_product(key_rot[pl.ds(0, count), span], query_rot[here, span])
            scores = scores * (128**-0.5)
            near = scores[origin * own_rows :]
            near = jnp.where(ahead_of(near, 0, 0), MASKED, near)
            scores = jnp.concatenate([scores[: origin * own_rows], near], 0) if origin else near
            row_max = jnp.max(scores, 0, keepdims=True)
            exponent = jnp.exp(scores - row_max)
            row_total = jnp.sum(exponent, 0, keepdims=True)
            result = jnp.dot(
                value[pl.ds(0, count), span].T, low(exponent), preferred_element_type=jnp.float32
            )
            attended[here, span] = low((result * (1.0 / row_total)).T)
            stats[pl.ds(head, 1), here] = row_max + jnp.log(row_total)

    def turns(beat):
        if beat == 1:
            tables()
            for copy in whole_stores[1:3]:
                copy.start()
        elif beat == 2:
            attention_flow.arrive(2, (0,))
            attention_flow.arrive(4, (0,))
        elif beat == 3:
            attention_flow.arrive(2, (1,))
            attention_flow.arrive(4, (1,))
            output_flow.start(2, 4, 1)
            gain_flow.arrive(2)
            gain_flow.arrive(4)
        elif beat == 5:
            attention_flow.arrive(6)
            gate_flow.start(2, 4, 1)
            gain_flow.arrive(6)
        elif beat == 6:
            output_flow.arrive(2)
            output_flow.arrive(4)
            for mask in (1, 3, 5, 7):
                attention_flow.arrive(mask)
            whole_stores[0].start()
            project(me)
        elif beat == 7:
            project_from(1, 0)
        elif beat == 8:
            project_from(1, 1)
            output_flow.arrive(6)
            loads[3].wait()
            for mask in (1, 3, 5, 7):
                gain_flow.arrive(mask)
            scales()
        elif beat == 9:
            gate_flow.arrive(2, (0,))
            gate_flow.arrive(4, (0,))
        elif beat == 10:
            project_from(2, 0)
        elif beat == 11:
            project_from(2, 1)
            gate_flow.arrive(2, (1,))
            gate_flow.arrive(4, (1,))

    for beat in range(1, (size - 1) * PIECES + 1):
        if beat == (size - 1) * PIECES:
            for origin in range(1, last):
                normalize(origin)
        hand_on((beat - 1) // PIECES + 1, (beat - 1) % PIECES)
        turns(beat)
    project_from(3, 0)
    project_from(3, 1)
    gate_flow.arrive(6)
    for origin in (0, last):
        normalize(origin)
    for copy in whole_stores[3:8]:
        copy.start()
    each(heads, attend)
    whole_stores[8].start()
    for flow in (output_flow, gate_flow):
        for mask in (1, 3, 5, 7):
            flow.arrive(mask)
    for hop in range(1, size):
        for way in range(2):

            @pl.when(jnp.logical_and(away(way) >= hop - 1, away(1 - way) >= 1))
            def _():
                for piece in range(PIECES):
                    hand_copy(hop, piece, way, 0).wait_send()

    for flow in (attention_flow, output_flow, gate_flow, gain_flow):
        flow.sent()
    for offset in range(1, size):
        for origin in range(size):
            square_copy(offset, origin).wait_send()
    for copy in loads[4:]:
        copy.wait()
    for origin in range(size):
        row_store(origin).wait()
    for copy in whole_stores:
        copy.wait()


def front(
    tokens_grouped,
    query_shard,
    key_shard,
    value_shard,
    output_shard,
    gate_shard,
    gain_shard,
    positions,
):
    size = lax.axis_size("tensor")
    own_rows, model_width = tokens_grouped.shape
    local_width = query_shard.shape[1]
    group_rows = size * own_rows
    low_type, wide_type = jnp.bfloat16, jnp.float32
    anywhere = pl.BlockSpec(memory_space=pl.ANY)
    inside = pl.BlockSpec(memory_space=pltpu.VMEM)
    dma = pltpu.SemaphoreType.DMA
    hands = (2, size - 1, PIECES)
    half_head = np.arange(128, dtype=np.float32) % 64
    frequency = (np.float32(THETA) ** (-(half_head * np.float32(2.0 / 128))))[None]

    def shape(dims, kind=low_type):
        return jax.ShapeDtypeStruct(dims, kind)

    local_rows = (group_rows, local_width)
    tables = (group_rows, 128)
    return pl.pallas_call(
        functools.partial(front_kernel, size),
        out_shape=[
            shape((size, own_rows, model_width)),
            shape((model_width, 3 * local_width)),
            shape((output_shard.shape[0], model_width)),
            shape((model_width, gate_shard.shape[1])),
            *[shape(local_rows)] * 6,
            *[shape(tables, wide_type)] * 2,
            shape((8, group_rows), wide_type),
            *[shape((8, 128), wide_type)] * 2,
            *[shape((1, model_width), wide_type)] * 2,
        ],
        in_specs=[anywhere] * 7 + [inside] * 2,
        out_specs=[anywhere] * 12 + [inside] * 5,
        scratch_shapes=[
            pltpu.VMEM((size, own_rows, model_width), low_type),
            pltpu.VMEM((model_width, 3 * local_width), low_type),
            pltpu.VMEM((size, own_rows, 3 * local_width), wide_type),
            pltpu.VMEM((8 * gain_shard.shape[0], gain_shard.shape[1]), low_type),
            pltpu.VMEM(tables, wide_type),
            pltpu.VMEM(tables, wide_type),
            pltpu.VMEM((size, size, 8, own_rows), wide_type),
            *[pltpu.VMEM(local_rows, low_type)] * 6,
            dma((2, 8)),
            dma((4, size)),
            dma(hands),
            dma(hands),
            dma((4, 7, 2)),
            dma((4, 7, 2)),
            dma((size - 1, size)),
            dma((size - 1, size)),
        ],
        compiler_params=pltpu.CompilerParams(
            collective_id=0, has_side_effects=True, vmem_limit_bytes=VMEM_BYTES
        ),
        cost_estimate=pl.CostEstimate(
            flops=6 * group_rows * model_width * local_width,
            bytes_accessed=32 << 20,
            transcendentals=0,
        ),
        name="front",
    )(
        tokens_grouped,
        query_shard,
        key_shard,
        value_shard,
        output_shard,
        gate_shard,
        gain_shard,
        positions.reshape(1, group_rows),
        frequency,
    )


class ShardSum:
    def __init__(self, near, far, corner, final, send_sem, recv_sem, deferred=False, own=None):
        self.near, self.far, self.corner, self.final = near, far, corner, final
        self.deferred = deferred
        self.own = own or functools.partial(near, 0)
        self.send_sem, self.recv_sem = send_sem, recv_sem

    def remote(self, source, target, place, route):
        return pltpu.make_async_remote_copy(
            src_ref=source,
            dst_ref=target,
            send_sem=self.send_sem.at[place],
            recv_sem=self.recv_sem.at[place],
            device_id={"dp": shard_peer(route)},
            device_id_type=pl.DeviceIdType.MESH,
        )

    def core_copy(self, place):
        return self.remote(self.far(place), self.near(place), place, 1)

    def corner_copy(self, half):
        return self.remote(self.near(3, half), self.corner(half), 4 + half, (4, 2)[half])

    def final_copy(self, way, half):
        return self.remote(
            self.near(1 + way, half), self.final(way, half), 6 + 2 * way + half, (2, 4)[way]
        )

    def far_term(self, term, place):
        term(4 + place, self.far(place), False)
        self.core_copy(place).start()

    def near_term(self, term, place):
        self.core_copy(place).wait_recv()
        term(place, self.near(place), True)
        if place == 3:
            for half in range(2):
                self.corner_copy(half).start()
        elif place and not self.deferred:
            self.final_copy(place - 1, 2 - place).start()

    def first_terms(self, term):
        self.far_term(term, 3)
        self.far_term(term, 1)
        self.near_term(term, 3)
        self.far_term(term, 2)

    def other_terms(self, term):
        self.near_term(term, 1)
        self.far_term(term, 0)
        self.near_term(term, 2)
        self.near_term(term, 0)

    def take_corner(self):
        for half in range(2):
            self.corner_copy(half).wait_recv()
            add_into(self.near(1 + half, half), self.corner(half))
            if not self.deferred:
                self.final_copy(half, half).start()

    def take_final(self, target):
        for half in range(2):
            for way in range(2):
                self.final_copy(way, half).wait_recv()
            own, first, second = self.own(half), self.final(0, half), self.final(1, half)
            out = target(half)
            rows = own.shape[0]

            def step(index):
                span = pl.ds(pl.multiple_of(index * STRIP, STRIP), STRIP)
                out[span, :] = wide(own[span, :]) + wide(first[span, :]) + wide(second[span, :])

            each(rows // STRIP, step)

    def take_final_tiles(self, out):
        for half in range(2):
            for way in range(2):
                self.final_copy(way, half).wait_recv()
            own, first, second = self.own(half), self.final(0, half), self.final(1, half)
            rows = own.shape[0]

            def step(index):
                span = pl.ds(pl.multiple_of(index * TILE, TILE), TILE)
                value = wide(own[:, span]) + wide(first[:, span]) + wide(second[:, span])
                out[pl.ds(pl.multiple_of(index * 2 * rows + half * rows, STRIP), rows), :] = value

            each(own.shape[1] // TILE, step)

    def take_final_turned(self, out):
        for half in range(2):
            for way in range(2):
                self.final_copy(way, half).wait_recv()
            own, first, second = self.own(half), self.final(0, half), self.final(1, half)
            rows = own.shape[0]

            def step(index):
                span = pl.ds(pl.multiple_of(index * TILE, TILE), TILE)
                value = wide(own[:, span]) + wide(first[:, span]) + wide(second[:, span])
                out[span, pl.ds(half * rows, rows)] = value.T

            each(own.shape[1] // TILE, step)

    def sent(self, core=True):
        for place in range(4) if core else ():
            self.core_copy(place).wait_send()
        for half in range(2):
            self.corner_copy(half).wait_send()
            for way in range(2) if not self.deferred else ():
                self.final_copy(way, half).wait_send()


def add_into(target, source):
    def step(index, carry):
        span = pl.ds(pl.multiple_of(index * STRIP, STRIP), STRIP)
        target[span, :] = (wide(target[span, :]) + wide(source[span, :])).astype(target.dtype)
        return carry

    lax.fori_loop(0, target.shape[0] // STRIP, step, 0)


def product_term(left, right):
    def term(place, target, adds):
        height, width = target.shape
        tile = 1024 if width % 1024 == 0 else 512
        turned = left(place, height).T

        def step(index, carry):
            columns = pl.ds(pl.multiple_of(index * tile, tile), tile)
            value = jnp.dot(turned, right(columns, tile), preferred_element_type=jnp.float32)
            if adds:
                value = value + wide(target[:, columns])
            target[:, columns] = value.astype(target.dtype)
            return carry

        lax.fori_loop(0, target.shape[1] // tile, step, 0)

    return term


def stacked(buffer, first, height):
    def view(place, half=None):
        at = first + place * height
        if half is None:
            return buffer.at[pl.ds(at, height), :]
        return buffer.at[pl.ds(at + half * (height // 2), height // 2), :]

    return view


def middle_kernel(size, *refs):
    (
        attended_hbm,
        rows_hbm,
        cotangent_hbm,
        attention_scale,
        feedforward_scale,
        output_hbm,
        gate_hbm,
        up_hbm,
        down_hbm,
        mlp_out,
        inner_out,
        mixed_cot_out,
        branch_cot_out,
        block_out,
        grad_hidden_out,
        gate_grad_out,
        up_near_out,
        attention_gain_out,
        feedforward_gain_out,
        attended,
        tokens,
        cotangent,
        output_weight,
        gate_weight,
        up_weight,
        down_weight,
        everyone,
        gate_act,
        up_act,
        inner,
        hidden,
        branch,
        arrived,
        partial,
        total,
        load_sem,
        store_sem,
        sum_send,
        sum_recv,
        hand_send,
        hand_recv,
        shard_send,
        shard_recv,
        grad_send,
        grad_recv,
        again_sem,
        shuffle_sem,
        free_sem,
    ) = refs
    me = lax.axis_index("tensor")
    last = size - 1
    chunk_rows, model_width = tokens.shape[1], tokens.shape[2]
    units = gate_weight.shape[1]
    half_rows = chunk_rows // HALVES
    all_rows = size * chunk_rows

    greet(((me < last, me + 1), (me > 0, me - 1)))
    first_loads = [
        pltpu.make_async_copy(source, target, load_sem.at[place])
        for place, (source, target) in enumerate(
            (
                (attended_hbm, attended),
                (output_hbm, output_weight),
                (rows_hbm.at[me], tokens),
                (gate_hbm, gate_weight),
                (up_hbm, up_weight.at[pl.ds(0, up_hbm.shape[0]), :]),
                (down_hbm, down_weight.at[:, pl.ds(0, down_hbm.shape[1])]),
            )
        )
    ]
    first_loads += [
        pltpu.make_async_copy(
            cotangent_hbm.at[pl.ds(chunk * chunk_rows, chunk_rows), natural],
            cotangent.at[chunk, :, here],
            shuffle_sem.at[chunk, place],
        )
        for chunk in range(CHUNKS)
        for place, (here, natural) in enumerate(column_blocks(model_width // 8))
    ]
    for copy in first_loads[:2]:
        copy.start()
    up_flow = ShardGather(
        own_halves(up_hbm),
        row_halves(up_weight, up_hbm.shape[0]),
        shard_send.at[0],
        shard_recv.at[0],
    )
    down_flow = ShardGather(
        own_halves(down_hbm),
        column_halves(down_weight, down_hbm.shape[1]),
        shard_send.at[1],
        shard_recv.at[1],
    )
    pl.semaphore_wait(
        pltpu.get_barrier_semaphore(), 3 + jnp.minimum(me, 1) + jnp.minimum(last - me, 1)
    )
    up_flow.start(2, 4, 1)
    down_flow.start(1)

    height = model_width // 8
    again = [
        pltpu.make_async_copy(
            mlp_out.at[chunk, origin],
            down_weight.at[pl.ds((chunk * size + origin) * chunk_rows, chunk_rows), :],
            again_sem.at[chunk, origin],
        )
        for chunk in range(CHUNKS)
        for origin in range(size)
    ]
    gate_grads, up_grads = (
        ShardSum(
            stacked(buffer, 0, height),
            stacked(down_weight, 4 * height, height),
            functools.partial(stacked(buffer, 4 * height, height), 0),
            stacked(buffer, 5 * height, height),
            grad_send.at[kind],
            grad_recv.at[kind],
            deferred=kind == 1,
        )
        for kind, buffer in enumerate((gate_weight, up_weight))
    )

    def rows_again(place, shard_width):
        return down_weight[pl.ds(0, CHUNKS * all_rows), pl.ds(place * shard_width, shard_width)]

    def grad_term(act):
        def columns_of(columns, tile):
            return act[:, :, columns].reshape(CHUNKS * all_rows, tile)

        return product_term(rows_again, columns_of)

    def weights_free():
        for place, mask in enumerate((1, 2, 4)):
            pl.semaphore_signal(
                free_sem.at[place],
                inc=1,
                device_id={"dp": shard_peer(mask)},
                device_id_type=pl.DeviceIdType.MESH,
            )
        for copy in again:
            copy.start()

    up_store = pltpu.make_async_copy(
        up_weight.at[pl.ds(0, 3 * height), :], up_near_out, again_sem.at[0, 0]
    )

    def grad_turns(tick, half):
        gate_term, up_term = grad_term(gate_act), grad_term(up_act)
        if (tick, half) == (21, 0):
            for copy in again:
                copy.wait()
            for place in range(3):
                pl.semaphore_wait(free_sem.at[place], 1)
            gate_grads.far_term(gate_term, 3)
            gate_grads.far_term(gate_term, 1)
        elif (tick, half) == (21, 1):
            gate_grads.near_term(gate_term, 3)
            gate_grads.far_term(gate_term, 2)
        elif (tick, half) == (22, 0):
            gate_grads.near_term(gate_term, 1)
            gate_grads.far_term(gate_term, 0)
        elif (tick, half) == (22, 1):
            gate_grads.near_term(gate_term, 2)
            gate_grads.near_term(gate_term, 0)
        elif (tick, half) == (23, 0):
            for place in range(4):
                gate_grads.core_copy(place).wait_send()
            up_grads.far_term(up_term, 3)
            up_grads.far_term(up_term, 1)
        elif (tick, half) == (23, 1):
            gate_grads.take_corner()
            up_grads.near_term(up_term, 3)
            up_grads.far_term(up_term, 2)
        elif (tick, half) == (24, 0):
            up_grads.near_term(up_term, 1)
            up_grads.far_term(up_term, 0)
        elif (tick, half) == (24, 1):
            up_grads.near_term(up_term, 2)
            up_grads.near_term(up_term, 0)
        elif (tick, half) == (26, 0):
            gate_grads.take_final(lambda half: hidden.at[half])
            for half in range(HALVES):
                store(6, half).start()
        elif (tick, half) == (26, 1):
            up_grads.take_corner()
            up_store.start()

    def turns(tick, half):
        if (tick, half) == (2, 1):
            up_flow.arrive(2, (0,))
            up_flow.arrive(4, (0,))
        elif (tick, half) == (3, 0):
            up_flow.arrive(2, (1,))
            up_flow.arrive(4, (1,))
            down_flow.start(2, 4)
        elif (tick, half) == (4, 1):
            up_flow.arrive(6)
        elif (tick, half) == (5, 0):
            down_flow.arrive(2, (0,))
            down_flow.arrive(4, (0,))
        elif (tick, half) == (6, 0):
            down_flow.arrive(2, (1,))
            down_flow.arrive(4, (1,))
        elif (tick, half) == (7, 0):
            down_flow.arrive(6)

    attention_gain_out[...] = jnp.zeros_like(attention_gain_out)
    feedforward_gain_out[...] = jnp.zeros_like(feedforward_gain_out)

    def half_span(half):
        return pl.ds(half * half_rows, half_rows)

    def strips(half, body):
        def step(index, carry):
            body(
                pl.ds(pl.multiple_of(half * half_rows + index * STRIP, STRIP), STRIP),
                pl.ds(pl.multiple_of(index * STRIP, STRIP), STRIP),
            )
            return carry

        lax.fori_loop(0, half_rows // STRIP, step, 0)

    def sum_copy(chunk, step, half, way, dest):
        return pltpu.make_async_remote_copy(
            src_ref=partial.at[chunk, dest, half_span(half)],
            dst_ref=arrived.at[way, chunk, step - 1, half_span(half)],
            send_sem=sum_send.at[way, chunk, step - 1, half],
            recv_sem=sum_recv.at[way, chunk, step - 1, half],
            device_id={"tensor": me + 1 - 2 * way},
            device_id_type=pl.DeviceIdType.MESH,
        )

    def hand_copy(chunk, hop, half, way, origin):
        rows = everyone.at[origin, chunk, half_span(half)]
        return pltpu.make_async_remote_copy(
            src_ref=rows,
            dst_ref=rows,
            send_sem=hand_send.at[way, chunk, hop - 1, half],
            recv_sem=hand_recv.at[way, chunk, hop - 1, half],
            device_id={"tensor": me + 1 - 2 * way},
            device_id_type=pl.DeviceIdType.MESH,
        )

    def away(way):
        return me if way == 0 else last - me

    def sum_step(chunk, step, half):
        for way in range(2):
            distance = away(way)

            @pl.when(distance <= step - 1)
            def _():
                dest = me + size - step if way == 0 else me - size + step
                if step > 1:

                    @pl.when(distance >= 1)
                    def _():
                        sum_copy(chunk, step - 1, half, way, dest).wait_recv()

                        def add(rows, _):
                            partial[chunk, dest, rows] = low(
                                wide(partial[chunk, dest, rows])
                                + wide(arrived[way, chunk, step - 2, rows])
                            )

                        strips(half, add)

                sum_copy(chunk, step, half, way, dest).start()

    def sum_end(chunk, half):
        def begin(rows, here):
            total[here] = wide(partial[chunk, me, rows])

        strips(half, begin)
        for way in range(2):

            @pl.when(away(way) >= 1)
            def _():
                sum_copy(chunk, size - 1, half, way, me).wait_recv()

                def add(rows, here):
                    total[here] = total[here] + wide(arrived[way, chunk, size - 2, rows])

                strips(half, add)

    def sum_sent(chunk):
        for step in range(1, size):
            for way in range(2):

                @pl.when(away(way) <= step - 1)
                def _():
                    for half in range(HALVES):
                        sum_copy(chunk, step, half, way, 0).wait_send()

    def hand_first(chunk, half):
        for way in range(2):

            @pl.when(away(1 - way) >= 1)
            def _():
                hand_copy(chunk, 1, half, way, me).start()

    def hand_on(chunk, hop, half):
        for way in range(2):

            @pl.when(away(way) >= hop)
            def _():
                origin = me - hop if way == 0 else me + hop
                hand_copy(chunk, hop, half, way, origin).wait_recv()
                if hop < size - 1:

                    @pl.when(away(1 - way) >= 1)
                    def _():
                        hand_copy(chunk, hop + 1, half, way, origin).start()

    def hand_sent(chunk):
        for hop in range(1, size):
            for way in range(2):

                @pl.when(jnp.logical_and(away(way) >= hop - 1, away(1 - way) >= 1))
                def _():
                    for half in range(HALVES):
                        hand_copy(chunk, hop, half, way, 0).wait_send()

    def inverse_rms(values):
        return lax.rsqrt(jnp.mean(values * values, -1, keepdims=True) + EPS)

    def fold(values):
        return values[:8] + values[8:]

    def own_rows(chunk, stage, half):
        def after_branch(rows, here):
            value = total[here]
            branch[chunk, rows] = value
            state = wide(tokens[chunk, rows]) + value * inverse_rms(value) * attention_scale[...]
            hidden[chunk, rows] = state
            everyone[me, chunk, rows] = low(state)

        def after_mixed(rows, here):
            value = total[here]
            inverse = inverse_rms(value)
            normalized = value * inverse
            hidden[chunk, rows] = hidden[chunk, rows] + normalized * feedforward_scale[...]
            grad = wide(cotangent[chunk, rows])
            feedforward_gain_out[...] += fold(grad * normalized)
            everyone[me, chunk, rows] = low(
                norm_backward(grad, normalized, inverse, feedforward_scale[...])
            )

        def after_gradient(rows, here):
            grad = total[here] + wide(cotangent[chunk, rows])
            value = branch[chunk, rows]
            inverse = inverse_rms(value)
            normalized = value * inverse
            branch[chunk, rows] = grad
            attention_gain_out[...] += fold(grad * normalized)
            everyone[me, chunk, rows] = low(
                norm_backward(grad, normalized, inverse, attention_scale[...])
            )

        strips(half, (after_branch, after_mixed, after_gradient)[stage])

    def gathered(chunk):
        return everyone[:, chunk].reshape(all_rows, model_width)

    def tiles(first, end, body):
        def step(index, carry):
            body(pl.ds(pl.multiple_of(index * WIDE_TILE, WIDE_TILE), WIDE_TILE))
            return carry

        lax.fori_loop(first, end, step, 0)

    def store(kind, chunk):
        source, target = (
            (everyone.at[:, chunk], mlp_out.at[chunk]),
            (inner, inner_out.at[chunk]),
            (everyone.at[:, chunk], mixed_cot_out.at[chunk]),
            (everyone.at[:, chunk], branch_cot_out.at[:, chunk]),
            None,
            (branch.at[chunk], grad_hidden_out.at[chunk]),
            (hidden.at[chunk], gate_grad_out.at[pl.ds(chunk * chunk_rows, chunk_rows), :]),
        )[kind]
        return pltpu.make_async_copy(source, target, store_sem.at[kind, chunk])

    def block_stores(chunk):
        return [
            pltpu.make_async_copy(
                hidden.at[chunk, :, here],
                block_out.at[pl.ds(chunk * chunk_rows, chunk_rows), natural],
                shuffle_sem.at[chunk, place],
            )
            for place, (here, natural) in enumerate(column_blocks(model_width // 8))
        ]

    def put_partial(chunk, columns, values):
        partial[chunk, :, :, columns] = low(values).reshape(size, chunk_rows, WIDE_TILE)

    def branch_terms(chunk):
        def tile(columns):
            rows = attended[:, chunk].reshape(all_rows, attended.shape[-1])
            put_partial(
                chunk,
                columns,
                jnp.dot(rows, output_weight[:, columns], preferred_element_type=jnp.float32),
            )

        tiles(0, model_width // WIDE_TILE, tile)

    def gate_tile(chunk):
        def tile(columns):
            rows = gathered(chunk)
            gate = jnp.dot(rows, gate_weight[:, columns], preferred_element_type=jnp.float32)
            up = jnp.dot(rows, up_weight[:, columns], preferred_element_type=jnp.float32)
            gate_act[chunk, :, columns] = low(gate)
            up_act[chunk, :, columns] = low(up)
            inner[:, columns] = low(gate * jax.nn.sigmoid(gate) * up)

        return tile

    def down_tile(chunk):
        def tile(columns):
            put_partial(
                chunk,
                columns,
                jnp.dot(inner[...], down_weight[:, columns], preferred_element_type=jnp.float32),
            )

        return tile

    def grad_inner_tile(chunk):
        def tile(columns):
            grad = rows_product(gathered(chunk), down_weight[columns, :])
            gate = wide(gate_act[chunk, :, columns])
            up = wide(up_act[chunk, :, columns])
            sigmoid = jax.nn.sigmoid(gate)
            gate_act[chunk, :, columns] = low(
                grad * up * sigmoid * (1.0 + gate * (1.0 - sigmoid))
            )
            up_act[chunk, :, columns] = low(grad * gate * sigmoid)

        return tile

    def grad_inner_half_tile(chunk, half):
        spans = [
            pl.ds(origin * chunk_rows + half * half_rows, half_rows) for origin in range(size)
        ]

        def tile(columns):
            rows = everyone[:, chunk, half_span(half)].reshape(size * half_rows, model_width)
            grad = rows_product(rows, down_weight[columns, :])
            gate = wide(jnp.concatenate([gate_act[chunk, span, columns] for span in spans], 0))
            up = wide(jnp.concatenate([up_act[chunk, span, columns] for span in spans], 0))
            sigmoid = jax.nn.sigmoid(gate)
            for_gate = low(grad * up * sigmoid * (1.0 + gate * (1.0 - sigmoid)))
            for_up = low(grad * gate * sigmoid)
            for origin, span in enumerate(spans):
                here = slice(origin * half_rows, (origin + 1) * half_rows)
                gate_act[chunk, span, columns] = for_gate[here]
                up_act[chunk, span, columns] = for_up[here]

        return tile

    def grad_input_tile(chunk):
        def tile(columns):
            put_partial(
                chunk,
                columns,
                rows_product(gate_act[chunk], gate_weight[columns, :])
                + rows_product(up_act[chunk], up_weight[columns, :]),
            )

        return tile

    unit_tiles, width_tiles = units // WIDE_TILE, model_width // WIDE_TILE

    def forward_piece(chunk, piece):
        if piece == 0:
            if chunk == 0:
                for mask in (1, 3, 5, 7):
                    up_flow.arrive(mask)
                for copy in first_loads[3:6]:
                    copy.wait()
            store(0, chunk).start()
            tiles(0, unit_tiles // 2, gate_tile(chunk))
        elif piece == 1:
            tiles(unit_tiles // 2, unit_tiles, gate_tile(chunk))
            store(1, chunk).start()
            sum_sent(chunk)
            hand_sent(chunk)
        else:
            if chunk == 0:
                for mask in (1, 3, 5, 7):
                    down_flow.arrive(mask)
            tiles(0, width_tiles, down_tile(chunk))
            store(0, chunk).wait()
            store(1, chunk).wait()

    def backward_piece(chunk, piece):
        if piece == 0:
            store(2, chunk).start()
            for copy in block_stores(chunk):
                copy.start()
            tiles(0, unit_tiles // 2, grad_inner_half_tile(chunk, 1))
            tiles(unit_tiles // 2, unit_tiles, grad_inner_tile(chunk))
        elif piece == 1:
            sum_sent(chunk)
            hand_sent(chunk)
            tiles(0, width_tiles // 2, grad_input_tile(chunk))
        else:
            tiles(width_tiles // 2, width_tiles, grad_input_tile(chunk))
            store(2, chunk).wait()
            for copy in block_stores(chunk):
                copy.wait()
            if chunk == CHUNKS - 1:
                up_flow.sent()
                down_flow.sent()
                weights_free()

    def end_piece(chunk, piece):
        if piece == 0:
            store(3, chunk).start()
            store(5, chunk).start()

    first_loads[0].wait()
    first_loads[1].wait()
    for copy in first_loads[2:]:
        copy.start()
    branch_terms(0)
    first_loads[2].wait()
    for copy in first_loads[6:]:
        copy.wait()
    bases = {
        (chunk, stage): (CHUNKS * stage + chunk) * size
        for stage in range(3)
        for chunk in range(CHUNKS)
    }
    ticks = max(bases.values()) + 2 * size
    for tick in range(1, ticks + 1):
        for half in range(HALVES):
            for (chunk, stage), base in bases.items():
                at = tick - base
                if size < at < 2 * size:
                    hand_on(chunk, at - size, half)
            for (chunk, stage), base in bases.items():
                at = tick - base
                if 1 <= at < size:
                    sum_step(chunk, at, half)
                elif at == size:
                    sum_end(chunk, half)
                    own_rows(chunk, stage, half)
                    hand_first(chunk, half)
            turns(tick, half)
            if tick == 1 and half == 1:
                branch_terms(1)
            for (chunk, stage), base in bases.items():
                piece = (tick - base - 2 * size + 1) * HALVES + half - 1
                if piece == -1 and stage == 1:
                    tiles(0, unit_tiles // 2, grad_inner_half_tile(chunk, 0))
                elif 0 <= piece < 3:
                    (forward_piece, backward_piece, end_piece)[stage](chunk, piece)
            grad_turns(tick, half)
    gate_grads.sent(False)
    up_grads.sent()
    for chunk in range(CHUNKS):
        sum_sent(chunk)
        hand_sent(chunk)
        store(3, chunk).wait()
        store(5, chunk).wait()
        store(6, chunk).wait()
    up_store.wait()


def middle(
    attended,
    rows_all,
    cotangent_grouped,
    attention_scale,
    feedforward_scale,
    output_full,
    gate_full,
    up_shard,
    down_shard,
):
    size = lax.axis_size("tensor")
    own_rows, model_width = cotangent_grouped.shape
    chunk_rows = own_rows // CHUNKS
    all_rows = size * chunk_rows
    half_rows = chunk_rows // HALVES
    heads_width = attended.shape[1]
    units = gate_full.shape[1]
    chunked = (CHUNKS, chunk_rows, model_width)
    lined = (CHUNKS, size, chunk_rows, model_width)
    low_type, wide_type = jnp.bfloat16, jnp.float32

    def shape(dims, kind=low_type):
        return jax.ShapeDtypeStruct(dims, kind)

    anywhere = pl.BlockSpec(memory_space=pl.ANY)
    inside = pl.BlockSpec(memory_space=pltpu.VMEM)
    dma = pltpu.SemaphoreType.DMA
    flops = 2 * CHUNKS * all_rows * model_width * (2 * heads_width + 6 * units)
    outs = pl.pallas_call(
        functools.partial(middle_kernel, size),
        out_shape=[
            shape(lined),
            shape((CHUNKS, all_rows, units)),
            shape(lined),
            shape((size, CHUNKS, chunk_rows, model_width)),
            shape((own_rows, model_width), wide_type),
            shape(chunked, wide_type),
            shape((model_width // 8, units), wide_type),
            shape((3 * model_width // 8, units)),
            shape((8, model_width), wide_type),
            shape((8, model_width), wide_type),
        ],
        in_specs=[anywhere] * 3 + [inside] * 2 + [anywhere] * 4,
        out_specs=[anywhere] * 8 + [inside] * 2,
        scratch_shapes=[
            pltpu.VMEM((size, CHUNKS, chunk_rows, heads_width), low_type),
            pltpu.VMEM(chunked, low_type),
            pltpu.VMEM(chunked, low_type),
            pltpu.VMEM((heads_width, model_width), low_type),
            pltpu.VMEM((model_width, units), low_type),
            pltpu.VMEM((model_width, units), low_type),
            pltpu.VMEM((units, model_width), low_type),
            pltpu.VMEM((size, CHUNKS, chunk_rows, model_width), low_type),
            pltpu.VMEM((CHUNKS, all_rows, units), low_type),
            pltpu.VMEM((CHUNKS, all_rows, units), low_type),
            pltpu.VMEM((all_rows, units), low_type),
            pltpu.VMEM(chunked, wide_type),
            pltpu.VMEM(chunked, wide_type),
            pltpu.VMEM((2, CHUNKS, size - 1, chunk_rows, model_width), low_type),
            pltpu.VMEM(lined, low_type),
            pltpu.VMEM((half_rows, model_width), wide_type),
            dma((6,)),
            dma((8, CHUNKS)),
            dma((2, CHUNKS, size - 1, HALVES)),
            dma((2, CHUNKS, size - 1, HALVES)),
            dma((2, CHUNKS, size - 1, HALVES)),
            dma((2, CHUNKS, size - 1, HALVES)),
            dma((2, 7, 2)),
            dma((2, 7, 2)),
            dma((2, 10)),
            dma((2, 10)),
            dma((CHUNKS, size)),
            dma((CHUNKS, 8)),
            pltpu.SemaphoreType.REGULAR((3,)),
        ],
        compiler_params=pltpu.CompilerParams(
            collective_id=1, has_side_effects=True, vmem_limit_bytes=VMEM_BYTES
        ),
        cost_estimate=pl.CostEstimate(
            flops=flops, bytes_accessed=64 << 20, transcendentals=0
        ),
        name="middle",
    )(
        attended.reshape(size, CHUNKS, chunk_rows, heads_width),
        rows_all.reshape(size, *chunked),
        cotangent_grouped,
        attention_scale,
        feedforward_scale,
        output_full,
        gate_full,
        up_shard,
        down_shard,
    )
    rows = CHUNKS * all_rows
    return (
        outs[1].reshape(rows, units),
        outs[2].reshape(rows, model_width),
        outs[3].reshape(rows, model_width),
        outs[4],
        outs[5].reshape(own_rows, model_width),
        *outs[6:],
    )


def back_kernel(
    size,
    branch_cot_hbm,
    output_hbm,
    query_rot_hbm,
    key_rot_hbm,
    value_hbm,
    query_hat_hbm,
    key_hat_hbm,
    cosine_hbm,
    sine_hbm,
    up_near,
    attended_hbm,
    weight_hbm,
    mixed_cot_hbm,
    inner_hbm,
    rows_hbm,
    hidden_hbm,
    stats,
    query_scale,
    key_scale,
    attention_gain,
    feedforward_gain,
    tokens_out,
    up_out,
    down_out,
    output_out,
    query_out,
    key_out,
    value_out,
    gain_out,
    left,
    attended,
    weight,
    mixed_cot,
    inner,
    grad,
    gain,
    shared,
    hidden,
    partial,
    arrived,
    far,
    down_near,
    output_far,
    output_near,
    attention_near,
    gain_far,
    gain_near,
    up_final,
    wide_total,
    output_total,
    load_sem,
    store_sem,
    share_send,
    share_recv,
    sum_send,
    sum_recv,
    shard_send,
    shard_recv,
):
    me = lax.axis_index("tensor")
    last = size - 1
    own_rows, model_width = partial.shape[1:]
    group_rows = size * own_rows
    local_width = attended.shape[1]
    heads = local_width // 128
    piece_rows = own_rows // PIECES
    height = model_width // 8
    greet([(True, lax.rem(me + offset, size)) for offset in range(1, size)])

    def beside(index):
        return pl.ds(index * local_width, local_width)

    pairs = [
        (output_hbm, far.at[pl.ds(0, local_width), :]),
        (branch_cot_hbm, left),
        (key_rot_hbm, partial.at[:, :, beside(1)]),
        (query_rot_hbm, partial.at[:, :, beside(0)]),
        (value_hbm, partial.at[:, :, beside(2)]),
        (attended_hbm, attended),
        (query_hat_hbm, partial.at[:, :, beside(3)]),
        (cosine_hbm, wide_total.at[pl.ds(0, group_rows), pl.ds(0, 128)]),
        (sine_hbm, wide_total.at[pl.ds(0, group_rows), pl.ds(128, 128)]),
        (up_near.at[pl.ds(0, height), :], far.at[pl.ds(2 * height, height), :]),
    ]
    pairs += [
        (key_hat_hbm.at[origin], far.at[pl.ds(3 * height, own_rows), beside(origin)])
        for origin in range(size)
    ]
    pairs += [
        (weight_hbm, weight),
        (mixed_cot_hbm, mixed_cot),
        (inner_hbm, inner),
        (rows_hbm, left),
        (hidden_hbm, hidden),
    ]
    loads = [
        pltpu.make_async_copy(source, target, load_sem.at[place])
        for place, (source, target) in enumerate(pairs)
    ]
    weight_load, mixed_load, inner_load, rows_load, hidden_load = loads[-5:]
    for copy in loads[:2]:
        copy.start()

    def flow(kind, near, far_view, shard_height):
        return ShardSum(
            stacked(near, 0, shard_height),
            far_view,
            lambda half: stacked(near, 4 * shard_height, shard_height)(0, half),
            lambda way, half: stacked(near, 5 * shard_height, shard_height)(way, half),
            shard_send.at[kind],
            shard_recv.at[kind],
        )

    down_flow = flow(0, down_near, stacked(far, 0, height), height)
    output_flow = flow(1, output_near, stacked(output_far, 0, height), height)
    attention_flow = flow(
        2,
        attention_near,
        lambda place: far.at[pl.ds(place * height, height), pl.ds(0, 3 * local_width)],
        height,
    )
    gain_height = gain.shape[0] // 8
    gain_flow = flow(3, gain_near, stacked(gain_far, 0, gain_height), gain_height)
    up_flow = ShardSum(
        stacked(up_near, 0, height),
        None,
        None,
        stacked(up_final, 0, height),
        shard_send.at[4],
        shard_recv.at[4],
        own=functools.partial(stacked(far, 2 * height, height), 0),
    )

    def columns_of(source):
        return lambda place, width: source[:, pl.ds(place * width, width)]

    down_term = product_term(columns_of(mixed_cot), lambda columns, _: inner[:, columns])
    output_term = product_term(columns_of(left), lambda columns, _: attended[:, columns])
    attention_term = product_term(columns_of(left), lambda columns, _: grad[:, columns])

    def gain_term(place, target, adds):
        value = gain[pl.ds(place * target.shape[0], target.shape[0]), :]
        target[...] = value + target[...] if adds else value

    def away(way):
        return me if way == 0 else last - me

    def step_attended(index):
        here = pl.ds(pl.multiple_of(index * own_rows, own_rows), own_rows)
        for first in range(0, local_width, TILE):
            columns = pl.ds(first, TILE)
            output_far[here, columns] = low(rows_product(left[here, :], far[columns, :]))

    def held(kind, head):
        return pl.ds(pl.multiple_of(kind * local_width + head * 128, 128), 128)

    score_scale = 128**-0.5
    query_grad, key_grad = pl.ds(0, 128), pl.ds(128, 128)

    def product_columns(kind, origin):
        return pl.ds((kind * size + origin) * 128, 128)

    def step_head(head):
        span = head_span(head)
        for origin in reversed(range(size)):
            count = (origin + 1) * own_rows
            here = pl.ds(origin * own_rows, own_rows)
            seen = pl.ds(0, origin + 1)
            keys = partial[seen, :, held(1, head)].reshape(count, 128)
            values = partial[seen, :, held(2, head)].reshape(count, 128)
            queries = partial[origin, :, held(0, head)]
            grad_rows = output_far[here, span]
            delta = column_sums(wide(grad_rows) * wide(attended[here, span]))
            probs = jnp.exp(
                rows_product(keys, queries) * score_scale - stats[pl.ds(head, 1), here]
            )
            near = probs[origin * own_rows :]
            near = jnp.where(ahead_of(near, 0, 0), 0.0, near)
            probs = jnp.concatenate([probs[: origin * own_rows], near], 0) if origin else near
            grad_scores = low(probs * (rows_product(values, grad_rows) - delta))
            for_values = jnp.dot(low(probs), grad_rows, preferred_element_type=jnp.float32)
            for_keys = jnp.dot(grad_scores, queries, preferred_element_type=jnp.float32)
            for_queries = jnp.dot(keys.T, grad_scores, preferred_element_type=jnp.float32)
            wide_total[pl.ds(group_rows + origin * own_rows, own_rows), query_grad] = (
                for_queries * score_scale
            ).T
            first = origin == size - 1
            at = pl.ds(group_rows, count)
            wide_total[at, key_grad] = for_keys if first else wide_total[at, key_grad] + for_keys
            for block in range(origin + 1):
                term = for_values[block * own_rows : (block + 1) * own_rows]
                columns = product_columns(2, block)
                hidden[:, columns] = term if first else hidden[:, columns] + term
        for kind, (factor, scale) in enumerate(((1.0, query_scale), (score_scale, key_scale))):
            gain_total = jnp.zeros((1, 128), jnp.float32)
            for origin in range(size):
                here = pl.ds(origin * own_rows, own_rows)
                source = wide_total[
                    pl.ds(group_rows + origin * own_rows, own_rows), (query_grad, key_grad)[kind]
                ]
                rotated = wide(low(source * factor))
                normal = rotated * wide_total[here, pl.ds(0, 128)]
                normal = normal - pltpu.roll(rotated, 64, 1) * wide_total[here, pl.ds(128, 128)]
                hats = hat_of(kind, origin, head)
                gain_total = gain_total + jnp.sum(normal * hats, 0, keepdims=True)
                normal = normal * scale[pl.ds(head, 1), :]
                grad[here, held(kind, head)] = low(normal)
                hidden[:, product_columns(kind, origin)] += normal * hats
            gain[pl.ds(kind * heads + head, 1), :] = gain_total
        for origin in range(size):
            grad[pl.ds(origin * own_rows, own_rows), held(2, head)] = low(
                hidden[:, product_columns(2, origin)]
            )

    def hat_of(kind, origin, head):
        if kind == 0:
            return wide(partial[origin, :, held(3, head)])
        return wide(far[pl.ds(3 * height, own_rows), held(origin, head)])

    def share_copy(offset):
        return pltpu.make_async_remote_copy(
            src_ref=shared.at[me],
            dst_ref=shared.at[me],
            send_sem=share_send.at[offset - 1],
            recv_sem=share_recv.at[offset - 1],
            device_id={"tensor": lax.rem(me + offset, size)},
            device_id_type=pl.DeviceIdType.MESH,
        )

    def share():
        half_width = model_width // 2
        lines = [
            jnp.concatenate(
                [column_sums(hidden[:, product_columns(kind, origin)]) for origin in range(size)],
                1,
            )
            for kind in range(2)
        ]
        for part in (attention_gain, feedforward_gain):
            total = jnp.sum(part[...], 0, keepdims=True)
            lines += [total[:, :half_width], total[:, half_width:]]
        lines.append(jnp.zeros((2, half_width), jnp.float32))
        shared[me] = jnp.concatenate(lines, 0)
        for offset in range(1, size):
            share_copy(offset).start()

    def take_shares():
        for offset in range(1, size):
            share_copy(offset).wait_recv()
        total = shared[0]
        for device in range(1, size):
            total = total + shared[device]
        for kind in range(2):
            for origin in range(size):
                here = pl.ds(origin * own_rows, own_rows)
                columns = slice(origin * own_rows, (origin + 1) * own_rows)
                inner_column = turned_rows(total[kind : kind + 1, columns] / model_width)
                inverse = turned_rows(stats[pl.ds(heads + kind, 1), here])
                for head in range(heads):
                    span = pl.ds((kind * heads + head) * 128, 128)
                    hats = hat_of(kind, origin, head)
                    grad[here, span] = low(inverse * (wide(grad[here, span]) - hats * inner_column))
        for place in range(8):
            if place:
                gain[pl.ds(place * gain_height, 8), :] = gain[pl.ds(0, 8), :]
            for kind in range(2):
                for line in range(height // 128):
                    row, first = divmod(place * height + line * 128, model_width // 2)
                    gain[
                        pl.ds(place * gain_height + 8 + kind * (height // 128) + line, 1), :
                    ] = total[2 + 2 * kind + row : 3 + 2 * kind + row, first : first + 128]

    def terms(dest):
        span = pl.ds(pl.multiple_of(dest * own_rows, own_rows), own_rows)

        def step(index):
            columns = pl.ds(pl.multiple_of(index * WIDE_TILE, WIDE_TILE), WIDE_TILE)
            partial[dest, :, columns] = low(rows_product(grad[span, :], weight[columns, :]))

        each(model_width // WIDE_TILE, step)

    def terms_at(distance):
        for way in range(2):

            @pl.when(away(1 - way) >= distance)
            def _():
                terms(me + distance if way == 0 else me - distance)

    def span_of(piece):
        return pl.ds(piece * piece_rows, piece_rows)

    def sum_copy(step, piece, way, dest):
        return pltpu.make_async_remote_copy(
            src_ref=partial.at[dest, span_of(piece)],
            dst_ref=arrived.at[way, step - 1, span_of(piece)],
            send_sem=sum_send.at[way, step - 1, piece],
            recv_sem=sum_recv.at[way, step - 1, piece],
            device_id={"tensor": me + 1 - 2 * way},
            device_id_type=pl.DeviceIdType.MESH,
        )

    def sum_step(step, *pieces):
        for piece in pieces:
            for way in range(2):
                distance = away(way)

                @pl.when(distance <= step - 1)
                def _():
                    dest = me + size - step if way == 0 else me - size + step
                    if step > 1:

                        @pl.when(distance >= 1)
                        def _():
                            sum_copy(step - 1, piece, way, dest).wait_recv()
                            add_into(
                                partial.at[dest, span_of(piece)],
                                arrived.at[way, step - 2, span_of(piece)],
                            )

                    sum_copy(step, piece, way, dest).start()

    def token_stores(piece):
        return [
            pltpu.make_async_copy(
                hidden.at[span_of(piece), here],
                tokens_out.at[span_of(piece), natural],
                store_sem.at[1 + piece, place],
            )
            for place, (here, natural) in enumerate(column_blocks(height))
        ]

    def sum_end(*pieces):
        for piece in pieces:
            add_into(hidden.at[span_of(piece)], partial.at[me, span_of(piece)])
            for way in range(2):

                @pl.when(away(way) >= 1)
                def _():
                    sum_copy(size - 1, piece, way, me).wait_recv()
                    add_into(
                        hidden.at[span_of(piece)], arrived.at[way, size - 2, span_of(piece)]
                    )

            for copy in token_stores(piece):
                copy.start()

    def tile_stores(outs, sems):
        tiles = [
            out.at[:, pl.ds(first, TILE)] for out in outs for first in range(0, out.shape[1], TILE)
        ]
        return [
            pltpu.make_async_copy(
                wide_total.at[pl.ds(place * height, height), :], target, sems.at[place]
            )
            for place, target in enumerate(tiles)
        ]

    up_stores = tile_stores((up_out,), store_sem.at[0])
    attention_stores = tile_stores((query_out, key_out, value_out), store_sem.at[0])
    down_store = pltpu.make_async_copy(wide_total, down_out, store_sem.at[1 + PIECES, 0])
    output_store = pltpu.make_async_copy(output_total, output_out, store_sem.at[1 + PIECES, 1])

    gain[...] = jnp.zeros_like(gain)
    hidden[...] = jnp.zeros_like(hidden)
    pl.semaphore_wait(pltpu.get_barrier_semaphore(), 3 + size - 1)
    for half in range(2):
        for way in range(2):
            up_flow.final_copy(way, half).start()
    for copy in loads[:2]:
        copy.wait()
    for copy in loads[2:-5]:
        copy.start()
    each(size, step_attended)
    for copy in loads[2:-5]:
        copy.wait()
    for copy in (weight_load, mixed_load, inner_load):
        copy.start()
    each(heads, step_head)
    share()
    hidden_load.start()
    output_flow.first_terms(output_term)
    output_flow.other_terms(output_term)
    rows_load.start()
    up_flow.take_final_tiles(wide_total)
    for copy in up_stores:
        copy.start()
    take_shares()
    weight_load.wait()
    terms_at(3)
    sum_step(1, *range(PIECES))
    mixed_load.wait()
    inner_load.wait()
    down_flow.first_terms(down_term)
    terms_at(2)
    sum_step(2, 0)
    down_flow.other_terms(down_term)
    gain_flow.first_terms(gain_term)
    gain_flow.other_terms(gain_term)
    sum_step(2, 1)
    output_flow.take_corner()
    sum_step(2, 2)
    terms_at(1)
    rows_load.wait()
    for place in range(4):
        down_flow.core_copy(place).wait_send()
    attention_flow.first_terms(attention_term)
    sum_step(2, 3)
    attention_flow.other_terms(attention_term)
    sum_step(3, 0)
    down_flow.take_corner()
    gain_flow.take_corner()
    sum_step(3, 1)
    terms(me)
    sum_step(3, 2)
    sum_step(3, 3)
    hidden_load.wait()
    attention_flow.take_corner()
    output_flow.take_final_turned(output_total)
    output_store.start()
    gain_flow.take_final(stacked(gain_out, 0, gain_height // 2))
    for copy in up_stores:
        copy.wait()
    sum_end(0)
    sum_end(1)
    down_flow.take_final_turned(wide_total)
    down_store.start()
    sum_end(2)
    sum_end(3)
    down_store.wait()
    attention_flow.take_final_tiles(wide_total)
    for copy in attention_stores:
        copy.start()
    down_flow.sent(False)
    for shard_flow in (output_flow, attention_flow, gain_flow):
        shard_flow.sent()
    for half in range(2):
        for way in range(2):
            up_flow.final_copy(way, half).wait_send()
    for offset in range(1, size):
        share_copy(offset).wait_send()
    for step in range(1, size):
        for way in range(2):

            @pl.when(away(way) <= step - 1)
            def _():
                for piece in range(PIECES):
                    sum_copy(step, piece, way, 0).wait_send()

    for copy in [output_store] + attention_stores:
        copy.wait()
    for piece in range(PIECES):
        for copy in token_stores(piece):
            copy.wait()


def back(
    branch_cot,
    output_full,
    query_rot,
    key_rot,
    value_rows,
    query_hat,
    key_hat,
    cosine,
    sine,
    up_near,
    attended,
    attention_full,
    mixed_cot,
    inner,
    rows_all,
    grad_hidden,
    *small,
):
    size = lax.axis_size("tensor")
    own_rows, model_width = grad_hidden.shape
    group_rows = size * own_rows
    height = model_width // 8
    local_width, units = attended.shape[1], inner.shape[1]
    low_type, wide_type = jnp.bfloat16, jnp.float32
    anywhere = pl.BlockSpec(memory_space=pl.ANY)
    inside = pl.BlockSpec(memory_space=pltpu.VMEM)
    dma = pltpu.SemaphoreType.DMA
    by_device = (size, own_rows, local_width)

    def shape(*dims):
        return jax.ShapeDtypeStruct(dims, wide_type)

    return pl.pallas_call(
        functools.partial(back_kernel, size),
        out_shape=[
            shape(own_rows, model_width),
            shape(height, units),
            shape(units, height),
            shape(local_width, height),
            *[shape(height, local_width)] * 3,
            shape(32, 128),
        ],
        in_specs=[anywhere] * 16 + [inside] * len(small),
        out_specs=[anywhere] * 7 + [inside],
        scratch_shapes=[
            pltpu.VMEM((group_rows, model_width), low_type),
            pltpu.VMEM((group_rows, local_width), low_type),
            pltpu.VMEM((model_width, 3 * local_width), low_type),
            pltpu.VMEM((group_rows, model_width), low_type),
            pltpu.VMEM((group_rows, units), low_type),
            pltpu.VMEM((group_rows, 3 * local_width), low_type),
            pltpu.VMEM((8 * 32, 128), wide_type),
            pltpu.VMEM((size, 8, model_width // 2), wide_type),
            pltpu.VMEM((own_rows, model_width), wide_type),
            pltpu.VMEM((size, own_rows, model_width), low_type),
            pltpu.VMEM((2, size - 1, own_rows, model_width), low_type),
            pltpu.VMEM((4 * height, units), low_type),
            pltpu.VMEM((7 * height, units), low_type),
            pltpu.VMEM((4 * height, local_width), low_type),
            pltpu.VMEM((7 * height, local_width), low_type),
            pltpu.VMEM((7 * height, 3 * local_width), low_type),
            pltpu.VMEM((4 * 32, 128), wide_type),
            pltpu.VMEM((7 * 32, 128), wide_type),
            pltpu.VMEM((2 * height, units), low_type),
            pltpu.VMEM((units, height), wide_type),
            pltpu.VMEM((local_width, height), wide_type),
            dma((15 + size,)),
            dma((2 + PIECES, 8)),
            dma((size - 1,)),
            dma((size - 1,)),
            dma((2, size - 1, PIECES)),
            dma((2, size - 1, PIECES)),
            dma((5, 10)),
            dma((5, 10)),
        ],
        compiler_params=pltpu.CompilerParams(
            collective_id=2, has_side_effects=True, vmem_limit_bytes=VMEM_BYTES
        ),
        cost_estimate=pl.CostEstimate(
            flops=2 * group_rows * model_width * (units + 8 * local_width),
            bytes_accessed=48 << 20,
            transcendentals=group_rows**2 * local_width // 128,
        ),
        name="back",
    )(
        branch_cot,
        output_full,
        query_rot.reshape(by_device),
        key_rot.reshape(by_device),
        value_rows.reshape(by_device),
        query_hat.reshape(by_device),
        key_hat.reshape(by_device),
        cosine,
        sine,
        up_near,
        attended,
        attention_full,
        mixed_cot,
        inner,
        rows_all,
        grad_hidden,
        *small,
    )


def finish_kernel(count, *refs):
    sources, gain, refs = refs[:count], refs[count], refs[count + 1 :]
    targets, head_outs, norm_outs = refs[:count], refs[count : count + 2], refs[count + 2 : count + 4]
    buffers, sem = refs[count + 4 : -1], refs[-1]
    loads, stores = (
        [
            pltpu.make_async_copy(source, target, sem.at[way, place])
            for place, (source, target) in enumerate(pairs)
        ]
        for way, pairs in enumerate((zip(sources, buffers), zip(buffers, targets)))
    )
    for copy in loads:
        copy.start()
    heads, channels = head_outs[0].shape
    shift = lax.rem(128 - lax.axis_index("dp") * channels, 128)
    own = pltpu.roll(gain[pl.ds(0, 2 * heads), :], shift, 1)
    lines = norm_outs[0].shape[0]
    for kind in range(2):
        head_outs[kind][...] = own[kind * heads : (kind + 1) * heads, :channels]
        at = 2 * heads + kind * lines
        norm_outs[kind][...] = gain[pl.ds(at, lines), :]
    for load, store in zip(loads, stores):
        load.wait()
        store.start()
    for copy in stores:
        copy.wait()


def finish(gain_part, head_shape, lines, *arrays):
    anywhere = pl.BlockSpec(memory_space=pl.ANY)
    inside = pl.BlockSpec(memory_space=pltpu.VMEM)
    count = len(arrays)
    return pl.pallas_call(
        functools.partial(finish_kernel, count),
        out_shape=[
            *(jax.ShapeDtypeStruct(array.shape, array.dtype) for array in arrays),
            *[jax.ShapeDtypeStruct(head_shape, jnp.float32)] * 2,
            *[jax.ShapeDtypeStruct((lines, 128), jnp.float32)] * 2,
        ],
        in_specs=[anywhere] * count + [inside],
        out_specs=[anywhere] * count + [inside] * 4,
        scratch_shapes=[
            *(pltpu.VMEM(array.shape, array.dtype) for array in arrays),
            pltpu.SemaphoreType.DMA((2, count)),
        ],
        compiler_params=pltpu.CompilerParams(vmem_limit_bytes=VMEM_BYTES),
        name="finish",
    )(*arrays, gain_part)


def local(
    tokens,
    positions,
    cotangent,
    query_weight,
    key_weight,
    value_weight,
    output_weight,
    gate_weight,
    up_weight,
    down_weight,
    query_gain,
    key_gain,
    attention_gain,
    feedforward_gain,
):
    data_size = lax.axis_size("dp")
    data_index = lax.axis_index("dp")
    high_count = data_size // 8
    width = attention_gain.shape[0]
    channels, local_heads = query_gain.shape

    def high_block(low_bits, place):
        return low_bits + 8 * ((data_index // 8) ^ place)

    def grouped(array_in):
        if high_count == 1:
            return array_in
        return jnp.concatenate(
            [
                lax.dynamic_slice_in_dim(array_in, high_block(low_bits, place) * width, width, -1)
                for low_bits in range(8)
                for place in range(high_count)
            ],
            -1,
        )

    def ungrouped(array_in):
        if high_count == 1:
            return array_in
        return jnp.concatenate(
            [
                lax.dynamic_slice_in_dim(
                    array_in,
                    (low_bits * high_count + ((data_index // 8) ^ high_bits)) * width,
                    width,
                    -1,
                )
                for high_bits in range(high_count)
                for low_bits in range(8)
            ],
            -1,
        )

    head_gains = jnp.concatenate([query_gain.T, key_gain.T], 0)
    head_gains = lax.dynamic_update_slice_in_dim(
        jnp.zeros((2 * local_heads, channels * data_size), head_gains.dtype),
        head_gains,
        data_index * channels,
        1,
    )
    for bit in range(3, bits_of(data_size)):
        head_gains = head_gains + swap(head_gains, 1 << bit)
    gain_lines = [
        head_gains,
        gather_high(attention_gain[None], 1).reshape(-1, 128),
        gather_high(feedforward_gain[None], 1).reshape(-1, 128),
    ]
    line_count = sum(lines.shape[0] for lines in gain_lines)
    gain_shard = jnp.pad(jnp.concatenate(gain_lines, 0), ((0, 32 - line_count), (0, 0)))
    (
        rows_all,
        attention_full,
        output_full,
        gate_full,
        attended,
        query_rot,
        key_rot,
        value_rows,
        query_hat,
        key_hat,
        cosine,
        sine,
        stats,
        query_scale,
        key_scale,
        attention_scale,
        feedforward_scale,
    ) = front(
        grouped(tokens),
        gather_high(query_weight, 0),
        gather_high(key_weight, 0),
        gather_high(value_weight, 0),
        gather_high(output_weight, 1),
        gather_high(gate_weight, 0),
        gain_shard,
        positions,
    )
    (
        inner_act,
        mixed_cot,
        branch_cot,
        block_grouped,
        grad_hidden,
        grad_gate,
        up_near,
        attention_gain_part,
        feedforward_gain_part,
    ) = middle(
        attended,
        rows_all,
        grouped(cotangent),
        attention_scale,
        feedforward_scale,
        output_full,
        gate_full,
        gather_high(up_weight, 0),
        gather_high(down_weight, 1),
    )
    (
        tokens_part,
        grad_up,
        grad_down,
        grad_output,
        grad_query,
        grad_key,
        grad_value,
        gain_part,
    ) = back(
        branch_cot,
        output_full,
        query_rot,
        key_rot,
        value_rows,
        query_hat,
        key_hat,
        cosine,
        sine,
        up_near,
        attended,
        attention_full,
        mixed_cot,
        inner_act,
        rows_all.reshape(-1, rows_all.shape[-1]),
        grad_hidden,
        stats,
        query_scale,
        key_scale,
        attention_gain_part,
        feedforward_gain_part,
    )
    def own_high(total, axis):
        return wide(scatter_high(total, axis))

    large = (
        ungrouped(block_grouped),
        ungrouped(tokens_part),
        own_high(grad_query, 0),
        own_high(grad_key, 0),
        own_high(grad_value, 0),
        own_high(grad_output, 1),
        own_high(grad_gate, 0),
        own_high(grad_up, 0),
        own_high(grad_down, 1),
    )
    if high_count == 1:
        *large, query_part, key_part, attention_part, feedforward_part = finish(
            gain_part, query_gain.shape[::-1], width // 128, *large
        )
        return (
            *large,
            query_part.T,
            key_part.T,
            attention_part.reshape(width),
            feedforward_part.reshape(width),
        )
    head_part = gain_part[: 2 * local_heads]
    for bit in range(3, bits_of(data_size)):
        head_part = head_part + swap(head_part, 1 << bit)
    head_part = lax.dynamic_slice_in_dim(head_part, data_index * channels, channels, 1)
    norm_part = gain_part[2 * local_heads : line_count].reshape(2, -1)

    return (
        *large,
        head_part[:local_heads].T,
        head_part[local_heads:].T,
        own_high(norm_part[0], 0),
        own_high(norm_part[1], 0),
    )


def solution(mesh):
    return jax.shard_map(
        local,
        mesh=mesh,
        in_specs=(
            P(("dp", "tensor"), None),
            P("dp"),
            P(("dp", "tensor"), None),
            P("dp", "tensor"),
            P("dp", "tensor"),
            P("dp", "tensor"),
            P("tensor", "dp"),
            P("dp", "tensor"),
            P("dp", "tensor"),
            P("tensor", "dp"),
            P("dp", "tensor"),
            P("dp", "tensor"),
            P("dp"),
            P("dp"),
        ),
        out_specs=(
            P(("dp", "tensor"), None),
            P(("dp", "tensor"), None),
            P("dp", "tensor"),
            P("dp", "tensor"),
            P("dp", "tensor"),
            P("tensor", "dp"),
            P("dp", "tensor"),
            P("dp", "tensor"),
            P("tensor", "dp"),
            P("dp", "tensor"),
            P("dp", "tensor"),
            P("dp"),
            P("dp"),
        ),
        check_vma=False,
    )
```

```python
import functools

import jax
import jax.numpy as jnp
import numpy as np
from jax import lax
from jax.experimental import pallas as pl
from jax.experimental.pallas import tpu as pltpu
from jax.sharding import PartitionSpec as P

EPS = 1e-06
THETA = 500000.0
MASKED = -1e30
VMEM_BYTES = 64 * 1024 * 1024 - 128 * 1024


def norm_backward(grad_in, normalized, inverse_rms, gain_values):
    scaled = grad_in * gain_values
    return inverse_rms * (scaled - normalized * jnp.mean(scaled * normalized, -1, keepdims=True))


def bits_of(size):
    return size.bit_length() - 1


def swap(array_in, mask):
    size = lax.axis_size("dp")
    return lax.ppermute(array_in, "dp", [(index, index ^ mask) for index in range(size)])


def gather_high(shard, axis):
    for bit in range(3, bits_of(lax.axis_size("dp"))):
        shard = jnp.concatenate([shard, swap(shard, 1 << bit)], axis)
    return shard


def scatter_high(total, axis):
    for bit in reversed(range(3, bits_of(lax.axis_size("dp")))):
        kept, sent = jnp.split(total, 2, axis)
        total = low(wide(kept) + wide(swap(low(sent), 1 << bit)))
    return total


def low(array_in):
    return array_in.astype(jnp.bfloat16)


def wide(array_in):
    return array_in.astype(jnp.float32)


def rows_product(left, right):
    return lax.dot_general(
        left, right, (((1,), (1,)), ((), ())), preferred_element_type=jnp.float32
    )


TILE = 256
WIDE_TILE = 512
STRIP = 16
CHUNKS = 2
HALVES = 2
PIECES = 4


def shard_peer(mask):
    index = lax.axis_index("dp")
    return index + mask - 2 * mask * ((index // mask) % 2)


def low_place(mask):
    index = lax.axis_index("dp")
    total = 0
    for bit in (1, 2, 4):
        value = (index // bit) % 2
        total = total + bit * (1 - value if mask & bit else value)
    return total


ROUTE = {1: (1, 1), 2: (2, 2), 3: (1, 1), 4: (4, 4), 5: (1, 1), 6: (4, 2), 7: (1, 1)}
PLACES = {mask: place for place, mask in enumerate((0, 2, 4, 6, 1, 3, 5, 7))}


def column_blocks(width):
    return [
        (
            pl.ds(place * width, width),
            pl.ds(pl.multiple_of(low_place(mask) * width, width), width),
        )
        for mask, place in PLACES.items()
    ]


class ShardGather:
    def __init__(self, own, target, send_sem, recv_sem):
        self.own, self.target, self.send_sem, self.recv_sem = own, target, send_sem, recv_sem

    def copy(self, mask, half):
        route = ROUTE[mask][half]
        before = mask ^ route
        return pltpu.make_async_remote_copy(
            src_ref=self.target(PLACES[before], half) if before else self.own(half),
            dst_ref=self.target(PLACES[mask], half),
            send_sem=self.send_sem.at[mask - 1, half],
            recv_sem=self.recv_sem.at[mask - 1, half],
            device_id={"dp": shard_peer(route)},
            device_id_type=pl.DeviceIdType.MESH,
        )

    def start(self, *masks):
        for half in range(2):
            for mask in masks:
                self.copy(mask, half).start()

    def arrive(self, mask, halves=(0, 1)):
        for half in halves:
            self.copy(mask, half).wait_recv()
            for after, route in ROUTE.items():
                if after != mask and after ^ route[half] == mask:
                    self.copy(after, half).start()

    def sent(self):
        for mask in ROUTE:
            for half in range(2):
                self.copy(mask, half).wait_send()


def row_halves(buffer, height):
    def target(place, half):
        return buffer.at[pl.ds(place * height + half * (height // 2), height // 2), :]

    return target


def column_halves(buffer, width):
    height = buffer.shape[0] // 2

    def target(place, half):
        return buffer.at[pl.ds(half * height, height), pl.ds(place * width, width)]

    return target


def own_halves(shard):
    height = shard.shape[0] // 2
    return lambda half: shard.at[pl.ds(half * height, height), :]


def greet(line_devices):
    barrier = pltpu.get_barrier_semaphore()
    for mask in (1, 2, 4):
        pl.semaphore_signal(
            barrier,
            inc=1,
            device_id={"dp": shard_peer(mask)},
            device_id_type=pl.DeviceIdType.MESH,
        )
    for there, index in line_devices:

        @pl.when(there)
        def _():
            pl.semaphore_signal(
                barrier,
                inc=1,
                device_id={"tensor": index},
                device_id_type=pl.DeviceIdType.MESH,
            )


def turned_rows(row):
    return jnp.broadcast_to(row, (128, row.shape[1])).T


def column_sums(values):
    total = values[:, :128]
    for first in range(128, values.shape[1], 128):
        total = total + values[:, first : first + 128]
    return jnp.sum(total.T, 0, keepdims=True)


def ahead_of(values, first_key, first_query):
    key = first_key + lax.broadcasted_iota(jnp.int32, values.shape, 0)
    query = first_query + lax.broadcasted_iota(jnp.int32, values.shape, 1)
    return key > query


def head_span(head):
    return pl.ds(pl.multiple_of(head * 128, 128), 128)


def each(count, body):
    def step(index, carry):
        body(index)
        return carry

    lax.fori_loop(0, count, step, 0)


def front_kernel(
    size,
    tokens_hbm,
    query_hbm,
    key_hbm,
    value_hbm,
    output_hbm,
    gate_hbm,
    gain_hbm,
    positions,
    frequency,
    rows_out,
    attention_out,
    output_out,
    gate_out,
    attended_out,
    query_rot_out,
    key_rot_out,
    value_out,
    query_hat_out,
    key_hat_out,
    cosine_out,
    sine_out,
    stats,
    query_scale,
    key_scale,
    attention_scale,
    feedforward_scale,
    rows,
    weight,
    projected,
    gain,
    cosine,
    sine,
    squares,
    query_rot,
    key_rot,
    value,
    query_hat,
    key_hat,
    attended,
    load_sem,
    store_sem,
    hand_send,
    hand_recv,
    shard_send,
    shard_recv,
    square_send,
    square_recv,
):
    me = lax.axis_index("tensor")
    last = size - 1
    own_rows, model_width = rows.shape[1:]
    piece_rows = own_rows // PIECES
    local_width = query_hbm.shape[1]
    heads = local_width // 128
    everyone = True
    greet([(everyone, lax.rem(me + offset, size)) for offset in range(1, size)])
    block = model_width // 8
    token_loads = [
        pltpu.make_async_copy(
            tokens_hbm.at[:, natural], rows.at[me, :, here], load_sem.at[0, place]
        )
        for place, (here, natural) in enumerate(column_blocks(block))
    ]
    shard_rows = pl.ds(0, query_hbm.shape[0])
    loads = [
        pltpu.make_async_copy(source, target, load_sem.at[1, place])
        for place, (source, target) in enumerate(
            (
                (query_hbm, weight.at[shard_rows, pl.ds(0, local_width)]),
                (key_hbm, weight.at[shard_rows, pl.ds(local_width, local_width)]),
                (value_hbm, weight.at[shard_rows, pl.ds(2 * local_width, local_width)]),
                (gain_hbm, gain.at[pl.ds(0, gain_hbm.shape[0]), :]),
                (output_hbm, output_out.at[:, pl.ds(0, output_hbm.shape[1])]),
                (gate_hbm, gate_out.at[pl.ds(0, gate_hbm.shape[0]), :]),
            )
        )
    ]
    for copy in token_loads + loads:
        copy.start()
    attention_target = row_halves(weight, query_hbm.shape[0])
    attention_flow, output_flow, gate_flow, gain_flow = (
        ShardGather(own, target, shard_send.at[kind], shard_recv.at[kind])
        for kind, (own, target) in enumerate(
            (
                (functools.partial(attention_target, 0), attention_target),
                (own_halves(output_hbm), column_halves(output_out, output_hbm.shape[1])),
                (own_halves(gate_hbm), row_halves(gate_out, gate_hbm.shape[0])),
                (own_halves(gain_hbm), row_halves(gain, gain_hbm.shape[0])),
            )
        )
    )
    pl.semaphore_wait(pltpu.get_barrier_semaphore(), 3 + size - 1)

    def away(way):
        return me if way == 0 else last - me

    def hand_copy(hop, piece, way, origin):
        here = rows.at[origin, pl.ds(piece * piece_rows, piece_rows)]
        return pltpu.make_async_remote_copy(
            src_ref=here,
            dst_ref=here,
            send_sem=hand_send.at[way, hop - 1, piece],
            recv_sem=hand_recv.at[way, hop - 1, piece],
            device_id={"tensor": me + 1 - 2 * way},
            device_id_type=pl.DeviceIdType.MESH,
        )

    for copy in token_loads:
        copy.wait()
    for piece in range(PIECES):
        for way in range(2):

            @pl.when(away(1 - way) >= 1)
            def _():
                hand_copy(1, piece, way, me).start()

        if piece == 0:
            for copy in loads[:3]:
                copy.wait()
            attention_flow.start(2, 4, 1)
            gain_flow.start(2, 4, 1)

    def hand_on(hop, piece):
        for way in range(2):

            @pl.when(away(way) >= hop)
            def _():
                origin = me - hop if way == 0 else me + hop
                hand_copy(hop, piece, way, origin).wait_recv()
                if hop < size - 1:

                    @pl.when(away(1 - way) >= 1)
                    def _():
                        hand_copy(hop + 1, piece, way, origin).start()

    def row_store(origin):
        return pltpu.make_async_copy(rows.at[origin], rows_out.at[origin], store_sem.at[0, origin])

    whole_stores = [
        pltpu.make_async_copy(source, target, store_sem.at[1 + place // size, place % size])
        for place, (source, target) in enumerate(
            (
                (weight, attention_out),
                (cosine, cosine_out),
                (sine, sine_out),
                (query_hat, query_hat_out),
                (key_hat, key_hat_out),
                (query_rot, query_rot_out),
                (key_rot, key_rot_out),
                (value, value_out),
                (attended, attended_out),
            )
        )
    ]

    def span_of(origin):
        return pl.ds(pl.multiple_of(origin * own_rows, own_rows), own_rows)

    def square_copy(offset, origin):
        return pltpu.make_async_remote_copy(
            src_ref=squares.at[me, origin],
            dst_ref=squares.at[me, origin],
            send_sem=square_send.at[offset - 1, origin],
            recv_sem=square_recv.at[offset - 1, origin],
            device_id={"tensor": lax.rem(me + offset, size)},
            device_id_type=pl.DeviceIdType.MESH,
        )

    def project(origin):
        def step(index):
            columns = pl.ds(pl.multiple_of(index * WIDE_TILE, WIDE_TILE), WIDE_TILE)
            projected[origin, :, columns] = jnp.dot(
                rows[origin], weight[:, columns], preferred_element_type=jnp.float32
            )

        row_store(origin).start()
        each(weight.shape[1] // WIDE_TILE, step)
        queries = projected[origin, :, pl.ds(0, local_width)]
        keys = projected[origin, :, pl.ds(local_width, local_width)]
        squares[me, origin, pl.ds(0, 8), :] = jnp.concatenate(
            [
                column_sums(queries * queries),
                column_sums(keys * keys),
                jnp.zeros((6, own_rows), jnp.float32),
            ],
            0,
        )
        for offset in range(1, size):
            square_copy(offset, origin).start()

    def project_from(hop, way):
        @pl.when(away(way) >= hop)
        def _():
            project(me - hop if way == 0 else me + hop)

    def normalize(origin):
        for offset in range(1, size):
            square_copy(offset, origin).wait_recv()
        total = squares[0, origin]
        for device in range(1, size):
            total = total + squares[device, origin]
        inverse = lax.rsqrt(total / model_width + EPS)
        here = span_of(origin)
        stats[pl.ds(heads, 2), here] = inverse[:2]
        for kind, (hat, rot, scale) in enumerate(
            ((query_hat, query_rot, query_scale), (key_hat, key_rot, key_scale))
        ):
            column = turned_rows(inverse[kind : kind + 1])

            def step(head):
                span = head_span(head)
                source = head_span(head + kind * heads)
                normalized = projected[origin, :, source] * column
                hat[here, span] = low(normalized)
                scaled = normalized * scale[pl.ds(head, 1), :]
                rot[here, span] = low(
                    scaled * cosine[here, :] + pltpu.roll(scaled, 64, 1) * sine[here, :]
                )

            each(heads, step)
        value[here, :] = low(projected[origin, :, pl.ds(2 * local_width, local_width)])

    def tables():
        for origin in range(size):
            here = pl.ds(origin * own_rows, own_rows)
            angles = turned_rows(wide(positions[:, here])) * frequency[...]
            cosine[here, :] = jnp.cos(angles)
            lane = lax.broadcasted_iota(jnp.int32, angles.shape, 1)
            sine[here, :] = jnp.where(lane < 64, -1.0, 1.0) * jnp.sin(angles)

    def scales():
        for kind, scale in enumerate((query_scale, key_scale)):
            total = wide(gain[pl.ds(0, 16), :])
            for place in range(1, 8):
                total = total + wide(gain[pl.ds(place * gain_hbm.shape[0], 16), :])
            scale[...] = jnp.concatenate(
                [total[kind * heads : (kind + 1) * heads], jnp.zeros((8 - heads, 128), jnp.float32)],
                0,
            )
        for place in range(8):
            lines = wide(gain[pl.ds(place * gain_hbm.shape[0], 16), :])
            for kind, scale in enumerate((attention_scale, feedforward_scale)):
                for line in range(block // 128):
                    at = 2 * heads + kind * (block // 128) + line
                    scale[:, pl.ds(place * block + line * 128, 128)] = lines[at : at + 1]

    def attend(head):
        span = head_span(head)
        for origin in range(size):
            count = (origin + 1) * own_rows
            here = pl.ds(origin * own_rows, own_rows)
            scores = rows_product(key_rot[pl.ds(0, count), span], query_rot[here, span])
            scores = scores * (128**-0.5)
            near = scores[origin * own_rows :]
            near = jnp.where(ahead_of(near, 0, 0), MASKED, near)
            scores = jnp.concatenate([scores[: origin * own_rows], near], 0) if origin else near
            row_max = jnp.max(scores, 0, keepdims=True)
            exponent = jnp.exp(scores - row_max)
            row_total = jnp.sum(exponent, 0, keepdims=True)
            result = jnp.dot(
                value[pl.ds(0, count), span].T, low(exponent), preferred_element_type=jnp.float32
            )
            attended[here, span] = low((result * (1.0 / row_total)).T)
            stats[pl.ds(head, 1), here] = row_max + jnp.log(row_total)

    def turns(beat):
        if beat == 1:
            tables()
            for copy in whole_stores[1:3]:
                copy.start()
        elif beat == 2:
            attention_flow.arrive(2, (0,))
            attention_flow.arrive(4, (0,))
        elif beat == 3:
            attention_flow.arrive(2, (1,))
            attention_flow.arrive(4, (1,))
            output_flow.start(2, 4, 1)
            gain_flow.arrive(2)
            gain_flow.arrive(4)
        elif beat == 5:
            attention_flow.arrive(6)
            gate_flow.start(2, 4, 1)
            gain_flow.arrive(6)
        elif beat == 6:
            output_flow.arrive(2)
            output_flow.arrive(4)
            for mask in (1, 3, 5, 7):
                attention_flow.arrive(mask)
            whole_stores[0].start()
            project(me)
        elif beat == 7:
            project_from(1, 0)
        elif beat == 8:
            project_from(1, 1)
            output_flow.arrive(6)
            loads[3].wait()
            for mask in (1, 3, 5, 7):
                gain_flow.arrive(mask)
            scales()
        elif beat == 9:
            gate_flow.arrive(2, (0,))
            gate_flow.arrive(4, (0,))
        elif beat == 10:
            project_from(2, 0)
        elif beat == 11:
            project_from(2, 1)
            gate_flow.arrive(2, (1,))
            gate_flow.arrive(4, (1,))

    for beat in range(1, (size - 1) * PIECES + 1):
        if beat == (size - 1) * PIECES:
            for origin in range(1, last):
                normalize(origin)
        hand_on((beat - 1) // PIECES + 1, (beat - 1) % PIECES)
        turns(beat)
    project_from(3, 0)
    project_from(3, 1)
    gate_flow.arrive(6)
    for origin in (0, last):
        normalize(origin)
    for copy in whole_stores[3:8]:
        copy.start()
    each(heads, attend)
    whole_stores[8].start()
    for flow in (output_flow, gate_flow):
        for mask in (1, 3, 5, 7):
            flow.arrive(mask)
    for hop in range(1, size):
        for way in range(2):

            @pl.when(jnp.logical_and(away(way) >= hop - 1, away(1 - way) >= 1))
            def _():
                for piece in range(PIECES):
                    hand_copy(hop, piece, way, 0).wait_send()

    for flow in (attention_flow, output_flow, gate_flow, gain_flow):
        flow.sent()
    for offset in range(1, size):
        for origin in range(size):
            square_copy(offset, origin).wait_send()
    for copy in loads[4:]:
        copy.wait()
    for origin in range(size):
        row_store(origin).wait()
    for copy in whole_stores:
        copy.wait()


def front(
    tokens_grouped,
    query_shard,
    key_shard,
    value_shard,
    output_shard,
    gate_shard,
    gain_shard,
    positions,
):
    size = lax.axis_size("tensor")
    own_rows, model_width = tokens_grouped.shape
    local_width = query_shard.shape[1]
    group_rows = size * own_rows
    low_type, wide_type = jnp.bfloat16, jnp.float32
    anywhere = pl.BlockSpec(memory_space=pl.ANY)
    inside = pl.BlockSpec(memory_space=pltpu.VMEM)
    dma = pltpu.SemaphoreType.DMA
    hands = (2, size - 1, PIECES)
    half_head = np.arange(128, dtype=np.float32) % 64
    frequency = (np.float32(THETA) ** (-(half_head * np.float32(2.0 / 128))))[None]

    def shape(dims, kind=low_type):
        return jax.ShapeDtypeStruct(dims, kind)

    local_rows = (group_rows, local_width)
    tables = (group_rows, 128)
    return pl.pallas_call(
        functools.partial(front_kernel, size),
        out_shape=[
            shape((size, own_rows, model_width)),
            shape((model_width, 3 * local_width)),
            shape((output_shard.shape[0], model_width)),
            shape((model_width, gate_shard.shape[1])),
            *[shape(local_rows)] * 6,
            *[shape(tables, wide_type)] * 2,
            shape((8, group_rows), wide_type),
            *[shape((8, 128), wide_type)] * 2,
            *[shape((1, model_width), wide_type)] * 2,
        ],
        in_specs=[anywhere] * 7 + [inside] * 2,
        out_specs=[anywhere] * 12 + [inside] * 5,
        scratch_shapes=[
            pltpu.VMEM((size, own_rows, model_width), low_type),
            pltpu.VMEM((model_width, 3 * local_width), low_type),
            pltpu.VMEM((size, own_rows, 3 * local_width), wide_type),
            pltpu.VMEM((8 * gain_shard.shape[0], gain_shard.shape[1]), low_type),
            pltpu.VMEM(tables, wide_type),
            pltpu.VMEM(tables, wide_type),
            pltpu.VMEM((size, size, 8, own_rows), wide_type),
            *[pltpu.VMEM(local_rows, low_type)] * 6,
            dma((2, 8)),
            dma((4, size)),
            dma(hands),
            dma(hands),
            dma((4, 7, 2)),
            dma((4, 7, 2)),
            dma((size - 1, size)),
            dma((size - 1, size)),
        ],
        compiler_params=pltpu.CompilerParams(
            collective_id=0, has_side_effects=True, vmem_limit_bytes=VMEM_BYTES
        ),
        cost_estimate=pl.CostEstimate(
            flops=6 * group_rows * model_width * local_width,
            bytes_accessed=32 << 20,
            transcendentals=0,
        ),
        name="front",
    )(
        tokens_grouped,
        query_shard,
        key_shard,
        value_shard,
        output_shard,
        gate_shard,
        gain_shard,
        positions.reshape(1, group_rows),
        frequency,
    )


class ShardSum:
    def __init__(self, near, far, corner, final, send_sem, recv_sem, core_only=False, deferred=False, own=None, awaited=None):
        self.near, self.far, self.corner, self.final = near, far, corner, final
        self.core_only, self.deferred = core_only, deferred
        self.own = own or functools.partial(near, 0)
        self.awaited = awaited or ((0, 0), (0, 1), (1, 0), (1, 1))
        self.send_sem, self.recv_sem = send_sem, recv_sem

    def remote(self, source, target, place, route):
        return pltpu.make_async_remote_copy(
            src_ref=source,
            dst_ref=target,
            send_sem=self.send_sem.at[place],
            recv_sem=self.recv_sem.at[place],
            device_id={"dp": shard_peer(route)},
            device_id_type=pl.DeviceIdType.MESH,
        )

    def core_copy(self, place):
        return self.remote(self.far(place), self.near(place), place, 1)

    def corner_copy(self, half):
        return self.remote(self.near(3, half), self.corner(half), 4 + half, (4, 2)[half])

    def final_copy(self, way, half):
        return self.remote(
            self.near(1 + way, half), self.final(way, half), 6 + 2 * way + half, (2, 4)[way]
        )

    def far_term(self, term, place):
        term(4 + place, self.far(place), False)
        self.core_copy(place).start()

    def near_term(self, term, place):
        self.core_copy(place).wait_recv()
        term(place, self.near(place), True)
        if not self.core_only:
            self.near_ready(place)

    def near_ready(self, place):
        if place == 3:
            for half in range(2):
                self.corner_copy(half).start()
        elif place:
            self.final_copy(place - 1, 2 - place).start()

    def first_terms(self, term):
        self.far_term(term, 3)
        self.far_term(term, 1)
        self.near_term(term, 3)
        self.far_term(term, 2)

    def other_terms(self, term):
        self.near_term(term, 1)
        self.far_term(term, 0)
        self.near_term(term, 2)
        self.near_term(term, 0)

    def take_corner(self):
        for half in range(2):
            self.corner_copy(half).wait_recv()
            add_into(self.near(1 + half, half), self.corner(half))
            if not self.deferred:
                self.final_copy(half, half).start()

    def final_arrived(self, half):
        for way in range(2):
            if (way, half) in self.awaited:
                self.final_copy(way, half).wait_recv()

    def take_final(self, target):
        for half in range(2):
            self.final_arrived(half)
            own, first, second = self.own(half), self.final(0, half), self.final(1, half)
            out = target(half)
            rows = own.shape[0]

            def step(index):
                span = pl.ds(pl.multiple_of(index * STRIP, STRIP), STRIP)
                out[span, :] = wide(own[span, :]) + wide(first[span, :]) + wide(second[span, :])

            each(rows // STRIP, step)

    def take_final_tiles(self, out):
        for half in range(2):
            self.final_arrived(half)
            own, first, second = self.own(half), self.final(0, half), self.final(1, half)
            rows = own.shape[0]

            def step(index):
                span = pl.ds(pl.multiple_of(index * TILE, TILE), TILE)
                value = wide(own[:, span]) + wide(first[:, span]) + wide(second[:, span])
                out[pl.ds(pl.multiple_of(index * 2 * rows + half * rows, STRIP), rows), :] = value

            each(own.shape[1] // TILE, step)

    def take_final_turned(self, out):
        for half in range(2):
            self.final_arrived(half)
            own, first, second = self.own(half), self.final(0, half), self.final(1, half)
            rows = own.shape[0]

            def step(index):
                span = pl.ds(pl.multiple_of(index * TILE, TILE), TILE)
                value = wide(own[:, span]) + wide(first[:, span]) + wide(second[:, span])
                out[span, pl.ds(half * rows, rows)] = value.T

            each(own.shape[1] // TILE, step)

    def sent(self, core=True):
        for place in range(4) if core else ():
            self.core_copy(place).wait_send()
        for half in range(2):
            self.corner_copy(half).wait_send()
            for way in range(2):
                if way != half or not self.deferred:
                    self.final_copy(way, half).wait_send()


def add_into(target, source):
    def step(index, carry):
        span = pl.ds(pl.multiple_of(index * STRIP, STRIP), STRIP)
        target[span, :] = (wide(target[span, :]) + wide(source[span, :])).astype(target.dtype)
        return carry

    lax.fori_loop(0, target.shape[0] // STRIP, step, 0)


def product_term(left, right):
    def term(place, target, adds):
        height, width = target.shape
        tile = 1024 if width % 1024 == 0 else 512
        turned = left(place, height).T

        def step(index, carry):
            columns = pl.ds(pl.multiple_of(index * tile, tile), tile)
            value = jnp.dot(turned, right(columns, tile), preferred_element_type=jnp.float32)
            if adds:
                value = value + wide(target[:, columns])
            target[:, columns] = value.astype(target.dtype)
            return carry

        lax.fori_loop(0, target.shape[1] // tile, step, 0)

    return term


def stacked(buffer, first, height):
    def view(place, half=None):
        at = first + place * height
        if half is None:
            return buffer.at[pl.ds(at, height), :]
        return buffer.at[pl.ds(at + half * (height // 2), height // 2), :]

    return view


def middle_kernel(size, *refs):
    (
        attended_hbm,
        rows_hbm,
        cotangent_hbm,
        attention_scale,
        feedforward_scale,
        output_hbm,
        gate_hbm,
        up_hbm,
        down_hbm,
        mlp_out,
        inner_out,
        mixed_cot_out,
        branch_cot_out,
        block_out,
        grad_hidden_out,
        gate_grad_out,
        up_near_out,
        up_early_out,
        down_near_out,
        attention_gain_out,
        feedforward_gain_out,
        attended,
        tokens,
        cotangent,
        output_weight,
        gate_weight,
        up_weight,
        down_weight,
        everyone,
        gate_act,
        up_act,
        inner,
        hidden,
        branch,
        arrived,
        partial,
        total,
        load_sem,
        store_sem,
        sum_send,
        sum_recv,
        hand_send,
        hand_recv,
        shard_send,
        shard_recv,
        grad_send,
        grad_recv,
        again_sem,
        shuffle_sem,
        free_sem,
    ) = refs
    me = lax.axis_index("tensor")
    last = size - 1
    chunk_rows, model_width = tokens.shape[1], tokens.shape[2]
    units = gate_weight.shape[1]
    half_rows = chunk_rows // HALVES
    all_rows = size * chunk_rows

    greet(((me < last, me + 1), (me > 0, me - 1)))
    first_loads = [
        pltpu.make_async_copy(source, target, load_sem.at[place])
        for place, (source, target) in enumerate(
            (
                (attended_hbm, attended),
                (output_hbm, output_weight),
                (rows_hbm.at[me], tokens),
                (gate_hbm, gate_weight),
                (up_hbm, up_weight.at[pl.ds(0, up_hbm.shape[0]), :]),
                (down_hbm, down_weight.at[:, pl.ds(0, down_hbm.shape[1])]),
            )
        )
    ]
    first_loads += [
        pltpu.make_async_copy(
            cotangent_hbm.at[pl.ds(chunk * chunk_rows, chunk_rows), natural],
            cotangent.at[chunk, :, here],
            shuffle_sem.at[chunk, place],
        )
        for chunk in range(CHUNKS)
        for place, (here, natural) in enumerate(column_blocks(model_width // 8))
    ]
    for copy in first_loads[:2]:
        copy.start()
    up_flow = ShardGather(
        own_halves(up_hbm),
        row_halves(up_weight, up_hbm.shape[0]),
        shard_send.at[0],
        shard_recv.at[0],
    )
    down_flow = ShardGather(
        own_halves(down_hbm),
        column_halves(down_weight, down_hbm.shape[1]),
        shard_send.at[1],
        shard_recv.at[1],
    )
    pl.semaphore_wait(
        pltpu.get_barrier_semaphore(), 3 + jnp.minimum(me, 1) + jnp.minimum(last - me, 1)
    )
    up_flow.start(2, 4, 1)
    down_flow.start(1)

    height = model_width // 8
    again = [
        pltpu.make_async_copy(
            mlp_out.at[chunk, origin],
            down_weight.at[pl.ds((chunk * size + origin) * chunk_rows, chunk_rows), :],
            again_sem.at[chunk, origin],
        )
        for chunk in range(CHUNKS)
        for origin in range(size)
    ]
    gate_grads, up_grads = (
        ShardSum(
            stacked(buffer, 0, height),
            stacked(down_weight, 4 * height, height),
            functools.partial(stacked(buffer, 4 * height, height), 0),
            stacked(buffer, 5 * height, height),
            grad_send.at[kind],
            grad_recv.at[kind],
            deferred=kind == 1,
        )
        for kind, buffer in enumerate((gate_weight, up_weight))
    )

    down_grads = ShardSum(
        lambda place: up_act.at[place // 2, pl.ds(place % 2 * height, height), :],
        stacked(down_weight, 4 * height, height),
        None,
        None,
        grad_send.at[2],
        grad_recv.at[2],
        core_only=True,
    )
    down_again = [
        pltpu.make_async_copy(
            mixed_cot_out.at[chunk, origin],
            down_weight.at[pl.ds((chunk * size + origin) * chunk_rows, chunk_rows), :],
            again_sem.at[chunk, origin],
        )
        for chunk in range(CHUNKS)
        for origin in range(size)
    ] + [
        pltpu.make_async_copy(inner_out.at[chunk], gate_act.at[chunk], again_sem.at[chunk, size])
        for chunk in range(CHUNKS)
    ]

    def signal_free(place, mask):
        pl.semaphore_signal(
            free_sem.at[place],
            inc=1,
            device_id={"dp": shard_peer(mask)},
            device_id_type=pl.DeviceIdType.MESH,
        )

    def rows_again(place, shard_width):
        return down_weight[pl.ds(0, CHUNKS * all_rows), pl.ds(place * shard_width, shard_width)]

    def grad_term(act):
        def columns_of(columns, tile):
            return act[:, :, columns].reshape(CHUNKS * all_rows, tile)

        return product_term(rows_again, columns_of)

    def weights_free():
        for place, mask in enumerate((1, 2, 4)):
            signal_free(place, mask)

    def near_store(chunk):
        return pltpu.make_async_copy(
            up_act.at[chunk],
            down_near_out.at[pl.ds(chunk * all_rows, all_rows), :],
            again_sem.at[chunk, 0],
        )

    gate_stores = [
        pltpu.make_async_copy(
            hidden.at[half],
            gate_grad_out.at[pl.ds(half * chunk_rows, chunk_rows), :],
            store_sem.at[6, half],
        )
        for half in range(HALVES)
    ]
    up_stores = [
        pltpu.make_async_copy(up_weight.at[pl.ds(first, count), :], target, store_sem.at[7, place])
        for place, (first, count, target) in enumerate(
            (
                (0, 3 * height, up_near_out),
                (5 * height + height // 2, height, up_early_out),
            )
        )
    ]

    def grad_turns(tick, half):
        gate_term, up_term = grad_term(gate_act), grad_term(up_act)
        if (tick, half) == (21, 0):
            for copy in again:
                copy.wait()
            for place in range(3):
                pl.semaphore_wait(free_sem.at[place], 1)
            gate_grads.far_term(gate_term, 3)
            gate_grads.far_term(gate_term, 1)
            gate_grads.near_term(gate_term, 3)
        elif (tick, half) == (21, 1):
            gate_grads.far_term(gate_term, 2)
            gate_grads.near_term(gate_term, 1)
            gate_grads.far_term(gate_term, 0)
        elif (tick, half) == (22, 0):
            gate_grads.near_term(gate_term, 2)
            gate_grads.near_term(gate_term, 0)
        elif (tick, half) == (22, 1):
            for place in range(4):
                gate_grads.core_copy(place).wait_send()
            up_grads.far_term(up_term, 3)
            up_grads.far_term(up_term, 1)
        elif (tick, half) == (23, 0):
            gate_grads.take_corner()
            up_grads.near_term(up_term, 3)
            up_grads.far_term(up_term, 2)
        elif (tick, half) == (23, 1):
            up_grads.near_term(up_term, 1)
            up_grads.far_term(up_term, 0)
        elif (tick, half) == (24, 0):
            up_grads.near_term(up_term, 2)
            up_grads.near_term(up_term, 0)
            signal_free(3, 1)
            for copy in down_again:
                copy.start()
        elif (tick, half) == (25, 0):
            for copy in down_again:
                copy.wait()
            for place in range(4):
                up_grads.core_copy(place).wait_send()
            pl.semaphore_wait(free_sem.at[3], 1)
            down_grads.far_term(gate_term, 3)
            down_grads.far_term(gate_term, 1)
        elif (tick, half) == (25, 1):
            down_grads.far_term(gate_term, 2)
            down_grads.far_term(gate_term, 0)
        elif (tick, half) == (26, 0):
            up_grads.take_corner()
            up_stores[0].start()
            down_grads.near_term(gate_term, 3)
            down_grads.near_term(gate_term, 2)
            near_store(1).start()
        elif (tick, half) == (26, 1):
            down_grads.near_term(gate_term, 1)
            down_grads.near_term(gate_term, 0)
            near_store(0).start()
            gate_grads.take_final(lambda half: hidden.at[half])
            for copy in gate_stores:
                copy.start()

    def turns(tick, half):
        if (tick, half) == (2, 1):
            up_flow.arrive(2, (0,))
            up_flow.arrive(4, (0,))
        elif (tick, half) == (3, 0):
            up_flow.arrive(2, (1,))
            up_flow.arrive(4, (1,))
            down_flow.start(2, 4)
        elif (tick, half) == (4, 1):
            up_flow.arrive(6)
        elif (tick, half) == (5, 0):
            down_flow.arrive(2, (0,))
            down_flow.arrive(4, (0,))
        elif (tick, half) == (6, 0):
            down_flow.arrive(2, (1,))
            down_flow.arrive(4, (1,))
        elif (tick, half) == (7, 0):
            down_flow.arrive(6)

    attention_gain_out[...] = jnp.zeros_like(attention_gain_out)
    feedforward_gain_out[...] = jnp.zeros_like(feedforward_gain_out)

    def half_span(half):
        return pl.ds(half * half_rows, half_rows)

    def strips(half, body):
        def step(index, carry):
            body(
                pl.ds(pl.multiple_of(half * half_rows + index * STRIP, STRIP), STRIP),
                pl.ds(pl.multiple_of(index * STRIP, STRIP), STRIP),
            )
            return carry

        lax.fori_loop(0, half_rows // STRIP, step, 0)

    def sum_copy(chunk, step, half, way, dest):
        return pltpu.make_async_remote_copy(
            src_ref=partial.at[chunk, dest, half_span(half)],
            dst_ref=arrived.at[way, chunk, step - 1, half_span(half)],
            send_sem=sum_send.at[way, chunk, step - 1, half],
            recv_sem=sum_recv.at[way, chunk, step - 1, half],
            device_id={"tensor": me + 1 - 2 * way},
            device_id_type=pl.DeviceIdType.MESH,
        )

    def hand_copy(chunk, hop, half, way, origin):
        rows = everyone.at[origin, chunk, half_span(half)]
        return pltpu.make_async_remote_copy(
            src_ref=rows,
            dst_ref=rows,
            send_sem=hand_send.at[way, chunk, hop - 1, half],
            recv_sem=hand_recv.at[way, chunk, hop - 1, half],
            device_id={"tensor": me + 1 - 2 * way},
            device_id_type=pl.DeviceIdType.MESH,
        )

    def away(way):
        return me if way == 0 else last - me

    def sum_step(chunk, step, half):
        for way in range(2):
            distance = away(way)

            @pl.when(distance <= step - 1)
            def _():
                dest = me + size - step if way == 0 else me - size + step
                if step > 1:

                    @pl.when(distance >= 1)
                    def _():
                        sum_copy(chunk, step - 1, half, way, dest).wait_recv()

                        def add(rows, _):
                            partial[chunk, dest, rows] = low(
                                wide(partial[chunk, dest, rows])
                                + wide(arrived[way, chunk, step - 2, rows])
                            )

                        strips(half, add)

                sum_copy(chunk, step, half, way, dest).start()

    def sum_end(chunk, half):
        def begin(rows, here):
            total[here] = wide(partial[chunk, me, rows])

        strips(half, begin)
        for way in range(2):

            @pl.when(away(way) >= 1)
            def _():
                sum_copy(chunk, size - 1, half, way, me).wait_recv()

                def add(rows, here):
                    total[here] = total[here] + wide(arrived[way, chunk, size - 2, rows])

                strips(half, add)

    def sum_sent(chunk):
        for step in range(1, size):
            for way in range(2):

                @pl.when(away(way) <= step - 1)
                def _():
                    for half in range(HALVES):
                        sum_copy(chunk, step, half, way, 0).wait_send()

    def hand_first(chunk, half):
        for way in range(2):

            @pl.when(away(1 - way) >= 1)
            def _():
                hand_copy(chunk, 1, half, way, me).start()

    def hand_on(chunk, hop, half):
        for way in range(2):

            @pl.when(away(way) >= hop)
            def _():
                origin = me - hop if way == 0 else me + hop
                hand_copy(chunk, hop, half, way, origin).wait_recv()
                if hop < size - 1:

                    @pl.when(away(1 - way) >= 1)
                    def _():
                        hand_copy(chunk, hop + 1, half, way, origin).start()

    def hand_sent(chunk):
        for hop in range(1, size):
            for way in range(2):

                @pl.when(jnp.logical_and(away(way) >= hop - 1, away(1 - way) >= 1))
                def _():
                    for half in range(HALVES):
                        hand_copy(chunk, hop, half, way, 0).wait_send()

    def inverse_rms(values):
        return lax.rsqrt(jnp.mean(values * values, -1, keepdims=True) + EPS)

    def fold(values):
        return values[:8] + values[8:]

    def own_rows(chunk, stage, half):
        def after_branch(rows, here):
            value = total[here]
            branch[chunk, rows] = value
            state = wide(tokens[chunk, rows]) + value * inverse_rms(value) * attention_scale[...]
            hidden[chunk, rows] = state
            everyone[me, chunk, rows] = low(state)

        def after_mixed(rows, here):
            value = total[here]
            inverse = inverse_rms(value)
            normalized = value * inverse
            hidden[chunk, rows] = hidden[chunk, rows] + normalized * feedforward_scale[...]
            grad = wide(cotangent[chunk, rows])
            feedforward_gain_out[...] += fold(grad * normalized)
            everyone[me, chunk, rows] = low(
                norm_backward(grad, normalized, inverse, feedforward_scale[...])
            )

        def after_gradient(rows, here):
            grad = total[here] + wide(cotangent[chunk, rows])
            value = branch[chunk, rows]
            inverse = inverse_rms(value)
            normalized = value * inverse
            branch[chunk, rows] = grad
            attention_gain_out[...] += fold(grad * normalized)
            everyone[me, chunk, rows] = low(
                norm_backward(grad, normalized, inverse, attention_scale[...])
            )

        strips(half, (after_branch, after_mixed, after_gradient)[stage])

    def gathered(chunk):
        return everyone[:, chunk].reshape(all_rows, model_width)

    def tiles(first, end, body):
        def step(index, carry):
            body(pl.ds(pl.multiple_of(index * WIDE_TILE, WIDE_TILE), WIDE_TILE))
            return carry

        lax.fori_loop(first, end, step, 0)

    def store(kind, chunk):
        source, target = (
            (everyone.at[:, chunk], mlp_out.at[chunk]),
            (inner, inner_out.at[chunk]),
            (everyone.at[:, chunk], mixed_cot_out.at[chunk]),
            (everyone.at[:, chunk], branch_cot_out.at[:, chunk]),
            None,
            (branch.at[chunk], grad_hidden_out.at[chunk]),
        )[kind]
        return pltpu.make_async_copy(source, target, store_sem.at[kind, chunk])

    def block_stores(chunk):
        return [
            pltpu.make_async_copy(
                hidden.at[chunk, :, here],
                block_out.at[pl.ds(chunk * chunk_rows, chunk_rows), natural],
                shuffle_sem.at[chunk, place],
            )
            for place, (here, natural) in enumerate(column_blocks(model_width // 8))
        ]

    def put_partial(chunk, columns, values):
        partial[chunk, :, :, columns] = low(values).reshape(size, chunk_rows, WIDE_TILE)

    def branch_terms(chunk):
        def tile(columns):
            rows = attended[:, chunk].reshape(all_rows, attended.shape[-1])
            put_partial(
                chunk,
                columns,
                jnp.dot(rows, output_weight[:, columns], preferred_element_type=jnp.float32),
            )

        tiles(0, model_width // WIDE_TILE, tile)

    def gate_tile(chunk):
        def tile(columns):
            rows = gathered(chunk)
            gate = jnp.dot(rows, gate_weight[:, columns], preferred_element_type=jnp.float32)
            up = jnp.dot(rows, up_weight[:, columns], preferred_element_type=jnp.float32)
            gate_act[chunk, :, columns] = low(gate)
            up_act[chunk, :, columns] = low(up)
            inner[:, columns] = low(gate * jax.nn.sigmoid(gate) * up)

        return tile

    def down_tile(chunk):
        def tile(columns):
            put_partial(
                chunk,
                columns,
                jnp.dot(inner[...], down_weight[:, columns], preferred_element_type=jnp.float32),
            )

        return tile

    def grad_inner_tile(chunk):
        def tile(columns):
            grad = rows_product(gathered(chunk), down_weight[columns, :])
            gate = wide(gate_act[chunk, :, columns])
            up = wide(up_act[chunk, :, columns])
            sigmoid = jax.nn.sigmoid(gate)
            gate_act[chunk, :, columns] = low(
                grad * up * sigmoid * (1.0 + gate * (1.0 - sigmoid))
            )
            up_act[chunk, :, columns] = low(grad * gate * sigmoid)

        return tile

    def grad_inner_half_tile(chunk, half):
        spans = [
            pl.ds(origin * chunk_rows + half * half_rows, half_rows) for origin in range(size)
        ]

        def tile(columns):
            rows = everyone[:, chunk, half_span(half)].reshape(size * half_rows, model_width)
            grad = rows_product(rows, down_weight[columns, :])
            gate = wide(jnp.concatenate([gate_act[chunk, span, columns] for span in spans], 0))
            up = wide(jnp.concatenate([up_act[chunk, span, columns] for span in spans], 0))
            sigmoid = jax.nn.sigmoid(gate)
            for_gate = low(grad * up * sigmoid * (1.0 + gate * (1.0 - sigmoid)))
            for_up = low(grad * gate * sigmoid)
            for origin, span in enumerate(spans):
                here = slice(origin * half_rows, (origin + 1) * half_rows)
                gate_act[chunk, span, columns] = for_gate[here]
                up_act[chunk, span, columns] = for_up[here]

        return tile

    def grad_input_tile(chunk):
        def tile(columns):
            put_partial(
                chunk,
                columns,
                rows_product(gate_act[chunk], gate_weight[columns, :])
                + rows_product(up_act[chunk], up_weight[columns, :]),
            )

        return tile

    unit_tiles, width_tiles = units // WIDE_TILE, model_width // WIDE_TILE

    def forward_piece(chunk, piece):
        if piece == 0:
            if chunk == 0:
                for mask in (1, 3, 5, 7):
                    up_flow.arrive(mask)
                for copy in first_loads[3:6]:
                    copy.wait()
            store(0, chunk).start()
            tiles(0, unit_tiles // 2, gate_tile(chunk))
        elif piece == 1:
            tiles(unit_tiles // 2, unit_tiles, gate_tile(chunk))
            store(1, chunk).start()
            sum_sent(chunk)
            hand_sent(chunk)
        else:
            if chunk == 0:
                for mask in (1, 3, 5, 7):
                    down_flow.arrive(mask)
            tiles(0, width_tiles, down_tile(chunk))
            store(0, chunk).wait()
            store(1, chunk).wait()

    def backward_piece(chunk, piece):
        if piece == 0:
            store(2, chunk).start()
            for copy in block_stores(chunk):
                copy.start()
            tiles(0, unit_tiles // 2, grad_inner_half_tile(chunk, 1))
            tiles(unit_tiles // 2, unit_tiles, grad_inner_tile(chunk))
            if chunk == CHUNKS - 1:
                down_flow.sent()
                for copy in again:
                    copy.start()
        elif piece == 1:
            sum_sent(chunk)
            hand_sent(chunk)
            tiles(0, width_tiles // 2, grad_input_tile(chunk))
        else:
            tiles(width_tiles // 2, width_tiles, grad_input_tile(chunk))
            store(2, chunk).wait()
            for copy in block_stores(chunk):
                copy.wait()
            if chunk == CHUNKS - 1:
                up_flow.sent()
                weights_free()

    def end_piece(chunk, piece):
        if piece == 0:
            store(3, chunk).start()
            store(5, chunk).start()

    first_loads[0].wait()
    first_loads[1].wait()
    for copy in first_loads[2:]:
        copy.start()
    branch_terms(0)
    first_loads[2].wait()
    for copy in first_loads[6:]:
        copy.wait()
    bases = {
        (chunk, stage): (CHUNKS * stage + chunk) * size
        for stage in range(3)
        for chunk in range(CHUNKS)
    }
    ticks = max(bases.values()) + 2 * size
    for tick in range(1, ticks + 1):
        for half in range(HALVES):
            for (chunk, stage), base in bases.items():
                at = tick - base
                if size < at < 2 * size:
                    hand_on(chunk, at - size, half)
            for (chunk, stage), base in bases.items():
                at = tick - base
                if 1 <= at < size:
                    sum_step(chunk, at, half)
                elif at == size:
                    sum_end(chunk, half)
                    own_rows(chunk, stage, half)
                    hand_first(chunk, half)
            turns(tick, half)
            if tick == 1 and half == 1:
                branch_terms(1)
            for (chunk, stage), base in bases.items():
                piece = (tick - base - 2 * size + 1) * HALVES + half - 1
                if piece == -1 and stage == 1:
                    tiles(0, unit_tiles // 2, grad_inner_half_tile(chunk, 0))
                elif 0 <= piece < 3:
                    (forward_piece, backward_piece, end_piece)[stage](chunk, piece)
            grad_turns(tick, half)
    for half in range(2):
        up_grads.final_copy(1 - half, half).wait_recv()
    up_stores[1].start()
    gate_grads.sent(False)
    up_grads.sent(False)
    for place in range(4):
        down_grads.core_copy(place).wait_send()
    for chunk in range(CHUNKS):
        sum_sent(chunk)
        hand_sent(chunk)
        store(3, chunk).wait()
        store(5, chunk).wait()
        near_store(chunk).wait()
    for copy in gate_stores + up_stores:
        copy.wait()


def middle(
    attended,
    rows_all,
    cotangent_grouped,
    attention_scale,
    feedforward_scale,
    output_full,
    gate_full,
    up_shard,
    down_shard,
):
    size = lax.axis_size("tensor")
    own_rows, model_width = cotangent_grouped.shape
    chunk_rows = own_rows // CHUNKS
    all_rows = size * chunk_rows
    half_rows = chunk_rows // HALVES
    heads_width = attended.shape[1]
    units = gate_full.shape[1]
    chunked = (CHUNKS, chunk_rows, model_width)
    lined = (CHUNKS, size, chunk_rows, model_width)
    low_type, wide_type = jnp.bfloat16, jnp.float32

    def shape(dims, kind=low_type):
        return jax.ShapeDtypeStruct(dims, kind)

    anywhere = pl.BlockSpec(memory_space=pl.ANY)
    inside = pl.BlockSpec(memory_space=pltpu.VMEM)
    dma = pltpu.SemaphoreType.DMA
    flops = 2 * CHUNKS * all_rows * model_width * (2 * heads_width + 6 * units)
    outs = pl.pallas_call(
        functools.partial(middle_kernel, size),
        out_shape=[
            shape(lined),
            shape((CHUNKS, all_rows, units)),
            shape(lined),
            shape((size, CHUNKS, chunk_rows, model_width)),
            shape((own_rows, model_width), wide_type),
            shape(chunked, wide_type),
            shape((model_width // 8, units), wide_type),
            shape((3 * model_width // 8, units)),
            shape((model_width // 8, units)),
            shape((model_width // 2, units)),
            shape((8, model_width), wide_type),
            shape((8, model_width), wide_type),
        ],
        in_specs=[anywhere] * 3 + [inside] * 2 + [anywhere] * 4,
        out_specs=[anywhere] * 10 + [inside] * 2,
        scratch_shapes=[
            pltpu.VMEM((size, CHUNKS, chunk_rows, heads_width), low_type),
            pltpu.VMEM(chunked, low_type),
            pltpu.VMEM(chunked, low_type),
            pltpu.VMEM((heads_width, model_width), low_type),
            pltpu.VMEM((model_width, units), low_type),
            pltpu.VMEM((model_width, units), low_type),
            pltpu.VMEM((units, model_width), low_type),
            pltpu.VMEM((size, CHUNKS, chunk_rows, model_width), low_type),
            pltpu.VMEM((CHUNKS, all_rows, units), low_type),
            pltpu.VMEM((CHUNKS, all_rows, units), low_type),
            pltpu.VMEM((all_rows, units), low_type),
            pltpu.VMEM(chunked, wide_type),
            pltpu.VMEM(chunked, wide_type),
            pltpu.VMEM((2, CHUNKS, size - 1, chunk_rows, model_width), low_type),
            pltpu.VMEM(lined, low_type),
            pltpu.VMEM((half_rows, model_width), wide_type),
            dma((6,)),
            dma((8, CHUNKS)),
            dma((2, CHUNKS, size - 1, HALVES)),
            dma((2, CHUNKS, size - 1, HALVES)),
            dma((2, CHUNKS, size - 1, HALVES)),
            dma((2, CHUNKS, size - 1, HALVES)),
            dma((2, 7, 2)),
            dma((2, 7, 2)),
            dma((3, 10)),
            dma((3, 10)),
            dma((CHUNKS, size + 1)),
            dma((CHUNKS, 8)),
            pltpu.SemaphoreType.REGULAR((4,)),
        ],
        compiler_params=pltpu.CompilerParams(
            collective_id=1, has_side_effects=True, vmem_limit_bytes=VMEM_BYTES
        ),
        cost_estimate=pl.CostEstimate(
            flops=flops, bytes_accessed=64 << 20, transcendentals=0
        ),
        name="middle",
    )(
        attended.reshape(size, CHUNKS, chunk_rows, heads_width),
        rows_all.reshape(size, *chunked),
        cotangent_grouped,
        attention_scale,
        feedforward_scale,
        output_full,
        gate_full,
        up_shard,
        down_shard,
    )
    rows = CHUNKS * all_rows
    return (
        outs[3].reshape(rows, model_width),
        outs[4],
        outs[5].reshape(own_rows, model_width),
        *outs[6:],
    )


def back_kernel(
    size,
    branch_cot_hbm,
    output_hbm,
    query_rot_hbm,
    key_rot_hbm,
    value_hbm,
    query_hat_hbm,
    key_hat_hbm,
    cosine_hbm,
    sine_hbm,
    down_near_hbm,
    up_near,
    up_early,
    attended_hbm,
    weight_hbm,
    rows_hbm,
    hidden_hbm,
    stats,
    query_scale,
    key_scale,
    attention_gain,
    feedforward_gain,
    tokens_out,
    up_out,
    down_out,
    output_out,
    query_out,
    key_out,
    value_out,
    gain_out,
    left,
    attended,
    weight,
    grad,
    gain,
    shared,
    hidden,
    partial,
    arrived,
    far,
    down_near,
    output_far,
    output_near,
    attention_near,
    gain_far,
    gain_near,
    up_final,
    wide_total,
    output_total,
    load_sem,
    store_sem,
    share_send,
    share_recv,
    sum_send,
    sum_recv,
    shard_send,
    shard_recv,
):
    me = lax.axis_index("tensor")
    last = size - 1
    own_rows, model_width = partial.shape[1:]
    group_rows = size * own_rows
    local_width = attended.shape[1]
    heads = local_width // 128
    piece_rows = own_rows // PIECES
    height = model_width // 8
    greet([(True, lax.rem(me + offset, size)) for offset in range(1, size)])

    def beside(index):
        return pl.ds(index * local_width, local_width)

    pairs = [
        (output_hbm, far.at[pl.ds(0, local_width), :]),
        (branch_cot_hbm, left),
        (down_near_hbm, down_near.at[pl.ds(0, 4 * height), :]),
        (up_near.at[pl.ds(0, height), :], up_final.at[pl.ds(2 * height, height), :]),
        (up_early, up_final.at[pl.ds(height // 2, height), :]),
        (key_rot_hbm, partial.at[:, :, beside(1)]),
        (query_rot_hbm, partial.at[:, :, beside(0)]),
        (value_hbm, partial.at[:, :, beside(2)]),
        (attended_hbm, attended),
        (query_hat_hbm, partial.at[:, :, beside(3)]),
        (cosine_hbm, wide_total.at[pl.ds(0, group_rows), pl.ds(0, 128)]),
        (sine_hbm, wide_total.at[pl.ds(0, group_rows), pl.ds(128, 128)]),
    ]
    pairs += [
        (key_hat_hbm.at[origin], far.at[pl.ds(3 * height, own_rows), beside(origin)])
        for origin in range(size)
    ]
    pairs += [
        (weight_hbm, weight),
        (rows_hbm, left),
        (hidden_hbm, hidden),
    ]
    loads = [
        pltpu.make_async_copy(source, target, load_sem.at[place])
        for place, (source, target) in enumerate(pairs)
    ]
    weight_load, rows_load, hidden_load = loads[-3:]
    for copy in loads[:-3]:
        copy.start()

    def flow(kind, near, far_view, shard_height):
        return ShardSum(
            stacked(near, 0, shard_height),
            far_view,
            lambda half: stacked(near, 4 * shard_height, shard_height)(0, half),
            lambda way, half: stacked(near, 5 * shard_height, shard_height)(way, half),
            shard_send.at[kind],
            shard_recv.at[kind],
        )

    down_flow = flow(0, down_near, None, height)
    output_flow = flow(1, output_near, stacked(output_far, 0, height), height)
    attention_flow = flow(
        2,
        attention_near,
        lambda place: far.at[pl.ds(place * height, height), pl.ds(0, 3 * local_width)],
        height,
    )
    gain_height = gain.shape[0] // 8
    gain_flow = flow(3, gain_near, stacked(gain_far, 0, gain_height), gain_height)
    up_flow = ShardSum(
        stacked(up_near, 0, height),
        None,
        None,
        stacked(up_final, 0, height),
        shard_send.at[4],
        shard_recv.at[4],
        own=functools.partial(stacked(up_final, 2 * height, height), 0),
        awaited=((0, 0), (1, 1)),
    )

    def columns_of(source):
        return lambda place, width: source[:, pl.ds(place * width, width)]

    output_term = product_term(columns_of(left), lambda columns, _: attended[:, columns])
    attention_term = product_term(columns_of(left), lambda columns, _: grad[:, columns])

    def gain_term(place, target, adds):
        value = gain[pl.ds(place * target.shape[0], target.shape[0]), :]
        target[...] = value + target[...] if adds else value

    def away(way):
        return me if way == 0 else last - me

    def step_attended(index):
        here = pl.ds(pl.multiple_of(index * own_rows, own_rows), own_rows)
        for first in range(0, local_width, TILE):
            columns = pl.ds(first, TILE)
            output_far[here, columns] = low(rows_product(left[here, :], far[columns, :]))

    def held(kind, head):
        return pl.ds(pl.multiple_of(kind * local_width + head * 128, 128), 128)

    score_scale = 128**-0.5
    query_grad, key_grad = pl.ds(0, 128), pl.ds(128, 128)

    def product_columns(kind, origin):
        return pl.ds((kind * size + origin) * 128, 128)

    def step_head(head):
        span = head_span(head)
        for origin in reversed(range(size)):
            count = (origin + 1) * own_rows
            here = pl.ds(origin * own_rows, own_rows)
            seen = pl.ds(0, origin + 1)
            keys = partial[seen, :, held(1, head)].reshape(count, 128)
            values = partial[seen, :, held(2, head)].reshape(count, 128)
            queries = partial[origin, :, held(0, head)]
            grad_rows = output_far[here, span]
            delta = column_sums(wide(grad_rows) * wide(attended[here, span]))
            probs = jnp.exp(
                rows_product(keys, queries) * score_scale - stats[pl.ds(head, 1), here]
            )
            near = probs[origin * own_rows :]
            near = jnp.where(ahead_of(near, 0, 0), 0.0, near)
            probs = jnp.concatenate([probs[: origin * own_rows], near], 0) if origin else near
            grad_scores = low(probs * (rows_product(values, grad_rows) - delta))
            for_values = jnp.dot(low(probs), grad_rows, preferred_element_type=jnp.float32)
            for_keys = jnp.dot(grad_scores, queries, preferred_element_type=jnp.float32)
            for_queries = jnp.dot(keys.T, grad_scores, preferred_element_type=jnp.float32)
            wide_total[pl.ds(group_rows + origin * own_rows, own_rows), query_grad] = (
                for_queries * score_scale
            ).T
            first = origin == size - 1
            at = pl.ds(group_rows, count)
            wide_total[at, key_grad] = for_keys if first else wide_total[at, key_grad] + for_keys
            for block in range(origin + 1):
                term = for_values[block * own_rows : (block + 1) * own_rows]
                columns = product_columns(2, block)
                hidden[:, columns] = term if first else hidden[:, columns] + term
        for kind, (factor, scale) in enumerate(((1.0, query_scale), (score_scale, key_scale))):
            gain_total = jnp.zeros((1, 128), jnp.float32)
            for origin in range(size):
                here = pl.ds(origin * own_rows, own_rows)
                source = wide_total[
                    pl.ds(group_rows + origin * own_rows, own_rows), (query_grad, key_grad)[kind]
                ]
                rotated = wide(low(source * factor))
                normal = rotated * wide_total[here, pl.ds(0, 128)]
                normal = normal - pltpu.roll(rotated, 64, 1) * wide_total[here, pl.ds(128, 128)]
                hats = hat_of(kind, origin, head)
                gain_total = gain_total + jnp.sum(normal * hats, 0, keepdims=True)
                normal = normal * scale[pl.ds(head, 1), :]
                grad[here, held(kind, head)] = low(normal)
                hidden[:, product_columns(kind, origin)] += normal * hats
            gain[pl.ds(kind * heads + head, 1), :] = gain_total
        for origin in range(size):
            grad[pl.ds(origin * own_rows, own_rows), held(2, head)] = low(
                hidden[:, product_columns(2, origin)]
            )

    def hat_of(kind, origin, head):
        if kind == 0:
            return wide(partial[origin, :, held(3, head)])
        return wide(far[pl.ds(3 * height, own_rows), held(origin, head)])

    def share_copy(offset):
        return pltpu.make_async_remote_copy(
            src_ref=shared.at[me],
            dst_ref=shared.at[me],
            send_sem=share_send.at[offset - 1],
            recv_sem=share_recv.at[offset - 1],
            device_id={"tensor": lax.rem(me + offset, size)},
            device_id_type=pl.DeviceIdType.MESH,
        )

    def share():
        half_width = model_width // 2
        lines = [
            jnp.concatenate(
                [column_sums(hidden[:, product_columns(kind, origin)]) for origin in range(size)],
                1,
            )
            for kind in range(2)
        ]
        for part in (attention_gain, feedforward_gain):
            total = jnp.sum(part[...], 0, keepdims=True)
            lines += [total[:, :half_width], total[:, half_width:]]
        lines.append(jnp.zeros((2, half_width), jnp.float32))
        shared[me] = jnp.concatenate(lines, 0)
        for offset in range(1, size):
            share_copy(offset).start()

    def take_shares():
        for offset in range(1, size):
            share_copy(offset).wait_recv()
        total = shared[0]
        for device in range(1, size):
            total = total + shared[device]
        for kind in range(2):
            for origin in range(size):
                here = pl.ds(origin * own_rows, own_rows)
                columns = slice(origin * own_rows, (origin + 1) * own_rows)
                inner_column = turned_rows(total[kind : kind + 1, columns] / model_width)
                inverse = turned_rows(stats[pl.ds(heads + kind, 1), here])
                for head in range(heads):
                    span = pl.ds((kind * heads + head) * 128, 128)
                    hats = hat_of(kind, origin, head)
                    grad[here, span] = low(inverse * (wide(grad[here, span]) - hats * inner_column))
        for place in range(8):
            if place:
                gain[pl.ds(place * gain_height, 8), :] = gain[pl.ds(0, 8), :]
            for kind in range(2):
                for line in range(height // 128):
                    row, first = divmod(place * height + line * 128, model_width // 2)
                    gain[
                        pl.ds(place * gain_height + 8 + kind * (height // 128) + line, 1), :
                    ] = total[2 + 2 * kind + row : 3 + 2 * kind + row, first : first + 128]

    def terms(dest):
        span = pl.ds(pl.multiple_of(dest * own_rows, own_rows), own_rows)

        def step(index):
            columns = pl.ds(pl.multiple_of(index * WIDE_TILE, WIDE_TILE), WIDE_TILE)
            partial[dest, :, columns] = low(rows_product(grad[span, :], weight[columns, :]))

        each(model_width // WIDE_TILE, step)

    def terms_at(distance):
        for way in range(2):

            @pl.when(away(1 - way) >= distance)
            def _():
                terms(me + distance if way == 0 else me - distance)

    def span_of(piece):
        return pl.ds(piece * piece_rows, piece_rows)

    def sum_copy(step, piece, way, dest):
        return pltpu.make_async_remote_copy(
            src_ref=partial.at[dest, span_of(piece)],
            dst_ref=arrived.at[way, step - 1, span_of(piece)],
            send_sem=sum_send.at[way, step - 1, piece],
            recv_sem=sum_recv.at[way, step - 1, piece],
            device_id={"tensor": me + 1 - 2 * way},
            device_id_type=pl.DeviceIdType.MESH,
        )

    def sum_step(step, *pieces):
        for piece in pieces:
            for way in range(2):
                distance = away(way)

                @pl.when(distance <= step - 1)
                def _():
                    dest = me + size - step if way == 0 else me - size + step
                    if step > 1:

                        @pl.when(distance >= 1)
                        def _():
                            sum_copy(step - 1, piece, way, dest).wait_recv()
                            add_into(
                                partial.at[dest, span_of(piece)],
                                arrived.at[way, step - 2, span_of(piece)],
                            )

                    sum_copy(step, piece, way, dest).start()

    def token_stores(piece):
        return [
            pltpu.make_async_copy(
                hidden.at[span_of(piece), here],
                tokens_out.at[span_of(piece), natural],
                store_sem.at[1 + piece, place],
            )
            for place, (here, natural) in enumerate(column_blocks(height))
        ]

    def sum_end(*pieces):
        for piece in pieces:
            add_into(hidden.at[span_of(piece)], partial.at[me, span_of(piece)])
            for way in range(2):

                @pl.when(away(way) >= 1)
                def _():
                    sum_copy(size - 1, piece, way, me).wait_recv()
                    add_into(
                        hidden.at[span_of(piece)], arrived.at[way, size - 2, span_of(piece)]
                    )

            for copy in token_stores(piece):
                copy.start()

    def tile_stores(outs, sems):
        tiles = [
            out.at[:, pl.ds(first, TILE)] for out in outs for first in range(0, out.shape[1], TILE)
        ]
        return [
            pltpu.make_async_copy(
                wide_total.at[pl.ds(place * height, height), :], target, sems.at[place]
            )
            for place, target in enumerate(tiles)
        ]

    up_stores = tile_stores((up_out,), store_sem.at[0])
    attention_stores = tile_stores((query_out, key_out, value_out), store_sem.at[0])
    down_store = pltpu.make_async_copy(wide_total, down_out, store_sem.at[1 + PIECES, 0])
    output_store = pltpu.make_async_copy(output_total, output_out, store_sem.at[1 + PIECES, 1])

    gain[...] = jnp.zeros_like(gain)
    hidden[...] = jnp.zeros_like(hidden)
    pl.semaphore_wait(pltpu.get_barrier_semaphore(), 3 + size - 1)
    for half in range(2):
        up_flow.final_copy(half, half).start()
    for copy in loads[:3]:
        copy.wait()
    for place in (3, 1, 2):
        down_flow.near_ready(place)
    each(size, step_attended)
    for copy in loads[3:-3]:
        copy.wait()
    weight_load.start()
    each(heads, step_head)
    share()
    hidden_load.start()
    output_flow.first_terms(output_term)
    take_shares()
    weight_load.wait()
    terms_at(3)
    sum_step(1, *range(PIECES))
    output_flow.other_terms(output_term)
    rows_load.start()
    down_flow.take_corner()
    terms_at(2)
    sum_step(2, 0)
    up_flow.take_final_tiles(wide_total)
    for copy in up_stores:
        copy.start()
    gain_flow.first_terms(gain_term)
    gain_flow.other_terms(gain_term)
    rows_load.wait()
    attention_flow.first_terms(attention_term)
    sum_step(2, 1)
    output_flow.take_corner()
    sum_step(2, 2)
    attention_flow.other_terms(attention_term)
    sum_step(2, 3)
    terms_at(1)
    sum_step(3, 0)
    gain_flow.take_corner()
    sum_step(3, 1)
    terms(me)
    sum_step(3, 2)
    sum_step(3, 3)
    hidden_load.wait()
    attention_flow.take_corner()
    output_flow.take_final_turned(output_total)
    output_store.start()
    gain_flow.take_final(stacked(gain_out, 0, gain_height // 2))
    for copy in up_stores:
        copy.wait()
    sum_end(0)
    sum_end(1)
    down_flow.take_final_turned(wide_total)
    down_store.start()
    sum_end(2)
    sum_end(3)
    down_store.wait()
    attention_flow.take_final_tiles(wide_total)
    for copy in attention_stores:
        copy.start()
    down_flow.sent(False)
    for shard_flow in (output_flow, attention_flow, gain_flow):
        shard_flow.sent()
    for half in range(2):
        up_flow.final_copy(half, half).wait_send()
    for offset in range(1, size):
        share_copy(offset).wait_send()
    for step in range(1, size):
        for way in range(2):

            @pl.when(away(way) <= step - 1)
            def _():
                for piece in range(PIECES):
                    sum_copy(step, piece, way, 0).wait_send()

    for copy in [output_store] + attention_stores:
        copy.wait()
    for piece in range(PIECES):
        for copy in token_stores(piece):
            copy.wait()


def back(
    branch_cot,
    output_full,
    query_rot,
    key_rot,
    value_rows,
    query_hat,
    key_hat,
    cosine,
    sine,
    down_near,
    up_near,
    up_early,
    attended,
    attention_full,
    rows_all,
    grad_hidden,
    *small,
):
    size = lax.axis_size("tensor")
    own_rows, model_width = grad_hidden.shape
    group_rows = size * own_rows
    height = model_width // 8
    local_width, units = attended.shape[1], down_near.shape[1]
    low_type, wide_type = jnp.bfloat16, jnp.float32
    anywhere = pl.BlockSpec(memory_space=pl.ANY)
    inside = pl.BlockSpec(memory_space=pltpu.VMEM)
    dma = pltpu.SemaphoreType.DMA
    by_device = (size, own_rows, local_width)

    def shape(*dims):
        return jax.ShapeDtypeStruct(dims, wide_type)

    return pl.pallas_call(
        functools.partial(back_kernel, size),
        out_shape=[
            shape(own_rows, model_width),
            shape(height, units),
            shape(units, height),
            shape(local_width, height),
            *[shape(height, local_width)] * 3,
            shape(32, 128),
        ],
        in_specs=[anywhere] * 16 + [inside] * len(small),
        out_specs=[anywhere] * 7 + [inside],
        scratch_shapes=[
            pltpu.VMEM((group_rows, model_width), low_type),
            pltpu.VMEM((group_rows, local_width), low_type),
            pltpu.VMEM((model_width, 3 * local_width), low_type),
            pltpu.VMEM((group_rows, 3 * local_width), low_type),
            pltpu.VMEM((8 * 32, 128), wide_type),
            pltpu.VMEM((size, 8, model_width // 2), wide_type),
            pltpu.VMEM((own_rows, model_width), wide_type),
            pltpu.VMEM((size, own_rows, model_width), low_type),
            pltpu.VMEM((2, size - 1, own_rows, model_width), low_type),
            pltpu.VMEM((4 * height, units), low_type),
            pltpu.VMEM((7 * height, units), low_type),
            pltpu.VMEM((4 * height, local_width), low_type),
            pltpu.VMEM((7 * height, local_width), low_type),
            pltpu.VMEM((7 * height, 3 * local_width), low_type),
            pltpu.VMEM((4 * 32, 128), wide_type),
            pltpu.VMEM((7 * 32, 128), wide_type),
            pltpu.VMEM((3 * height, units), low_type),
            pltpu.VMEM((units, height), wide_type),
            pltpu.VMEM((local_width, height), wide_type),
            dma((15 + size,)),
            dma((2 + PIECES, 8)),
            dma((size - 1,)),
            dma((size - 1,)),
            dma((2, size - 1, PIECES)),
            dma((2, size - 1, PIECES)),
            dma((5, 10)),
            dma((5, 10)),
        ],
        compiler_params=pltpu.CompilerParams(
            collective_id=2, has_side_effects=True, vmem_limit_bytes=VMEM_BYTES
        ),
        cost_estimate=pl.CostEstimate(
            flops=2 * group_rows * model_width * (units + 8 * local_width),
            bytes_accessed=48 << 20,
            transcendentals=group_rows**2 * local_width // 128,
        ),
        name="back",
    )(
        branch_cot,
        output_full,
        query_rot.reshape(by_device),
        key_rot.reshape(by_device),
        value_rows.reshape(by_device),
        query_hat.reshape(by_device),
        key_hat.reshape(by_device),
        cosine,
        sine,
        down_near,
        up_near,
        up_early,
        attended,
        attention_full,
        rows_all,
        grad_hidden,
        *small,
    )


def finish_kernel(count, *refs):
    sources, gain, refs = refs[:count], refs[count], refs[count + 1 :]
    targets, head_outs, norm_outs = refs[:count], refs[count : count + 2], refs[count + 2 : count + 4]
    buffers, sem = refs[count + 4 : -1], refs[-1]
    loads, stores = (
        [
            pltpu.make_async_copy(source, target, sem.at[way, place])
            for place, (source, target) in enumerate(pairs)
        ]
        for way, pairs in enumerate((zip(sources, buffers), zip(buffers, targets)))
    )
    for copy in loads:
        copy.start()
    heads, channels = head_outs[0].shape
    shift = lax.rem(128 - lax.axis_index("dp") * channels, 128)
    own = pltpu.roll(gain[pl.ds(0, 2 * heads), :], shift, 1)
    lines = norm_outs[0].shape[0]
    for kind in range(2):
        head_outs[kind][...] = own[kind * heads : (kind + 1) * heads, :channels]
        at = 2 * heads + kind * lines
        norm_outs[kind][...] = gain[pl.ds(at, lines), :]
    for load, store in zip(loads, stores):
        load.wait()
        store.start()
    for copy in stores:
        copy.wait()


def finish(gain_part, head_shape, lines, *arrays):
    anywhere = pl.BlockSpec(memory_space=pl.ANY)
    inside = pl.BlockSpec(memory_space=pltpu.VMEM)
    count = len(arrays)
    return pl.pallas_call(
        functools.partial(finish_kernel, count),
        out_shape=[
            *(jax.ShapeDtypeStruct(array.shape, array.dtype) for array in arrays),
            *[jax.ShapeDtypeStruct(head_shape, jnp.float32)] * 2,
            *[jax.ShapeDtypeStruct((lines, 128), jnp.float32)] * 2,
        ],
        in_specs=[anywhere] * count + [inside],
        out_specs=[anywhere] * count + [inside] * 4,
        scratch_shapes=[
            *(pltpu.VMEM(array.shape, array.dtype) for array in arrays),
            pltpu.SemaphoreType.DMA((2, count)),
        ],
        compiler_params=pltpu.CompilerParams(vmem_limit_bytes=VMEM_BYTES),
        name="finish",
    )(*arrays, gain_part)


def local(
    tokens,
    positions,
    cotangent,
    query_weight,
    key_weight,
    value_weight,
    output_weight,
    gate_weight,
    up_weight,
    down_weight,
    query_gain,
    key_gain,
    attention_gain,
    feedforward_gain,
):
    data_size = lax.axis_size("dp")
    data_index = lax.axis_index("dp")
    high_count = data_size // 8
    width = attention_gain.shape[0]
    channels, local_heads = query_gain.shape

    def high_block(low_bits, place):
        return low_bits + 8 * ((data_index // 8) ^ place)

    def grouped(array_in):
        if high_count == 1:
            return array_in
        return jnp.concatenate(
            [
                lax.dynamic_slice_in_dim(array_in, high_block(low_bits, place) * width, width, -1)
                for low_bits in range(8)
                for place in range(high_count)
            ],
            -1,
        )

    def ungrouped(array_in):
        if high_count == 1:
            return array_in
        return jnp.concatenate(
            [
                lax.dynamic_slice_in_dim(
                    array_in,
                    (low_bits * high_count + ((data_index // 8) ^ high_bits)) * width,
                    width,
                    -1,
                )
                for high_bits in range(high_count)
                for low_bits in range(8)
            ],
            -1,
        )

    head_gains = jnp.concatenate([query_gain.T, key_gain.T], 0)
    head_gains = lax.dynamic_update_slice_in_dim(
        jnp.zeros((2 * local_heads, channels * data_size), head_gains.dtype),
        head_gains,
        data_index * channels,
        1,
    )
    for bit in range(3, bits_of(data_size)):
        head_gains = head_gains + swap(head_gains, 1 << bit)
    gain_lines = [
        head_gains,
        gather_high(attention_gain[None], 1).reshape(-1, 128),
        gather_high(feedforward_gain[None], 1).reshape(-1, 128),
    ]
    line_count = sum(lines.shape[0] for lines in gain_lines)
    gain_shard = jnp.pad(jnp.concatenate(gain_lines, 0), ((0, 32 - line_count), (0, 0)))
    (
        rows_all,
        attention_full,
        output_full,
        gate_full,
        attended,
        query_rot,
        key_rot,
        value_rows,
        query_hat,
        key_hat,
        cosine,
        sine,
        stats,
        query_scale,
        key_scale,
        attention_scale,
        feedforward_scale,
    ) = front(
        grouped(tokens),
        gather_high(query_weight, 0),
        gather_high(key_weight, 0),
        gather_high(value_weight, 0),
        gather_high(output_weight, 1),
        gather_high(gate_weight, 0),
        gain_shard,
        positions,
    )
    (
        branch_cot,
        block_grouped,
        grad_hidden,
        grad_gate,
        up_near,
        up_early,
        down_near,
        attention_gain_part,
        feedforward_gain_part,
    ) = middle(
        attended,
        rows_all,
        grouped(cotangent),
        attention_scale,
        feedforward_scale,
        output_full,
        gate_full,
        gather_high(up_weight, 0),
        gather_high(down_weight, 1),
    )
    (
        tokens_part,
        grad_up,
        grad_down,
        grad_output,
        grad_query,
        grad_key,
        grad_value,
        gain_part,
    ) = back(
        branch_cot,
        output_full,
        query_rot,
        key_rot,
        value_rows,
        query_hat,
        key_hat,
        cosine,
        sine,
        down_near,
        up_near,
        up_early,
        attended,
        attention_full,
        rows_all.reshape(-1, rows_all.shape[-1]),
        grad_hidden,
        stats,
        query_scale,
        key_scale,
        attention_gain_part,
        feedforward_gain_part,
    )
    def own_high(total, axis):
        return wide(scatter_high(total, axis))

    large = (
        ungrouped(block_grouped),
        ungrouped(tokens_part),
        own_high(grad_query, 0),
        own_high(grad_key, 0),
        own_high(grad_value, 0),
        own_high(grad_output, 1),
        own_high(grad_gate, 0),
        own_high(grad_up, 0),
        own_high(grad_down, 1),
    )
    if high_count == 1:
        *large, query_part, key_part, attention_part, feedforward_part = finish(
            gain_part, query_gain.shape[::-1], width // 128, *large
        )
        return (
            *large,
            query_part.T,
            key_part.T,
            attention_part.reshape(width),
            feedforward_part.reshape(width),
        )
    head_part = gain_part[: 2 * local_heads]
    for bit in range(3, bits_of(data_size)):
        head_part = head_part + swap(head_part, 1 << bit)
    head_part = lax.dynamic_slice_in_dim(head_part, data_index * channels, channels, 1)
    norm_part = gain_part[2 * local_heads : line_count].reshape(2, -1)

    return (
        *large,
        head_part[:local_heads].T,
        head_part[local_heads:].T,
        own_high(norm_part[0], 0),
        own_high(norm_part[1], 0),
    )


def solution(mesh):
    return jax.shard_map(
        local,
        mesh=mesh,
        in_specs=(
            P(("dp", "tensor"), None),
            P("dp"),
            P(("dp", "tensor"), None),
            P("dp", "tensor"),
            P("dp", "tensor"),
            P("dp", "tensor"),
            P("tensor", "dp"),
            P("dp", "tensor"),
            P("dp", "tensor"),
            P("tensor", "dp"),
            P("dp", "tensor"),
            P("dp", "tensor"),
            P("dp"),
            P("dp"),
        ),
        out_specs=(
            P(("dp", "tensor"), None),
            P(("dp", "tensor"), None),
            P("dp", "tensor"),
            P("dp", "tensor"),
            P("dp", "tensor"),
            P("tensor", "dp"),
            P("dp", "tensor"),
            P("dp", "tensor"),
            P("tensor", "dp"),
            P("dp", "tensor"),
            P("dp", "tensor"),
            P("dp"),
            P("dp"),
        ),
        check_vma=False,
    )
```

```python
import functools

import jax
import jax.numpy as jnp
import numpy as np
from jax import lax
from jax.experimental import pallas as pl
from jax.experimental.pallas import tpu as pltpu
from jax.sharding import PartitionSpec as P

EPS = 1e-06
THETA = 500000.0
MASKED = -1e30
VMEM_BYTES = 64 * 1024 * 1024 - 128 * 1024


def norm_backward(grad_in, normalized, inverse_rms, gain_values):
    scaled = grad_in * gain_values
    return inverse_rms * (scaled - normalized * jnp.mean(scaled * normalized, -1, keepdims=True))


def bits_of(size):
    return size.bit_length() - 1


def swap(array_in, mask):
    size = lax.axis_size("dp")
    return lax.ppermute(array_in, "dp", [(index, index ^ mask) for index in range(size)])


def gather_high(shard, axis):
    for bit in range(3, bits_of(lax.axis_size("dp"))):
        shard = jnp.concatenate([shard, swap(shard, 1 << bit)], axis)
    return shard


def scatter_high(total, axis):
    for bit in reversed(range(3, bits_of(lax.axis_size("dp")))):
        kept, sent = jnp.split(total, 2, axis)
        total = low(wide(kept) + wide(swap(low(sent), 1 << bit)))
    return total


def low(array_in):
    return array_in.astype(jnp.bfloat16)


def wide(array_in):
    return array_in.astype(jnp.float32)


def rows_product(left, right):
    return lax.dot_general(
        left, right, (((1,), (1,)), ((), ())), preferred_element_type=jnp.float32
    )


TILE = 256
WIDE_TILE = 512
STRIP = 16
CHUNKS = 2
HALVES = 2
PIECES = 4
WINDOW = 6


def shard_peer(mask):
    index = lax.axis_index("dp")
    return index + mask - 2 * mask * ((index // mask) % 2)


def low_place(mask):
    index = lax.axis_index("dp")
    total = 0
    for bit in (1, 2, 4):
        value = (index // bit) % 2
        total = total + bit * (1 - value if mask & bit else value)
    return total


ROUTE = {1: (1, 1), 2: (2, 2), 3: (1, 1), 4: (4, 4), 5: (1, 1), 6: (4, 2), 7: (1, 1)}
PLACES = {mask: place for place, mask in enumerate((0, 2, 4, 6, 1, 3, 5, 7))}


def column_blocks(width):
    return [
        (
            pl.ds(place * width, width),
            pl.ds(pl.multiple_of(low_place(mask) * width, width), width),
        )
        for mask, place in PLACES.items()
    ]


class ShardGather:
    def __init__(self, own, target, send_sem, recv_sem):
        self.own, self.target, self.send_sem, self.recv_sem = own, target, send_sem, recv_sem

    def copy(self, mask, half):
        route = ROUTE[mask][half]
        before = mask ^ route
        return pltpu.make_async_remote_copy(
            src_ref=self.target(PLACES[before], half) if before else self.own(half),
            dst_ref=self.target(PLACES[mask], half),
            send_sem=self.send_sem.at[mask - 1, half],
            recv_sem=self.recv_sem.at[mask - 1, half],
            device_id={"dp": shard_peer(route)},
            device_id_type=pl.DeviceIdType.MESH,
        )

    def start(self, *masks):
        for half in range(2):
            for mask in masks:
                self.copy(mask, half).start()

    def arrive(self, mask, halves=(0, 1)):
        for half in halves:
            self.copy(mask, half).wait_recv()
            for after, route in ROUTE.items():
                if after != mask and after ^ route[half] == mask:
                    self.copy(after, half).start()

    def sent(self):
        for mask in ROUTE:
            for half in range(2):
                self.copy(mask, half).wait_send()


def row_halves(buffer, height):
    def target(place, half):
        return buffer.at[pl.ds(place * height + half * (height // 2), height // 2), :]

    return target


def column_halves(buffer, width):
    height = buffer.shape[0] // 2

    def target(place, half):
        return buffer.at[pl.ds(half * height, height), pl.ds(place * width, width)]

    return target


def own_halves(shard):
    height = shard.shape[0] // 2
    return lambda half: shard.at[pl.ds(half * height, height), :]


def greet(line_devices):
    barrier = pltpu.get_barrier_semaphore()
    for mask in (1, 2, 4):
        pl.semaphore_signal(
            barrier,
            inc=1,
            device_id={"dp": shard_peer(mask)},
            device_id_type=pl.DeviceIdType.MESH,
        )
    for there, index in line_devices:

        @pl.when(there)
        def _():
            pl.semaphore_signal(
                barrier,
                inc=1,
                device_id={"tensor": index},
                device_id_type=pl.DeviceIdType.MESH,
            )


def turned_rows(row):
    return jnp.broadcast_to(row, (128, row.shape[1])).T


def column_sums(values):
    total = values[:, :128]
    for first in range(128, values.shape[1], 128):
        total = total + values[:, first : first + 128]
    return jnp.sum(total.T, 0, keepdims=True)


def ahead_of(values, first_key, first_query):
    key = first_key + lax.broadcasted_iota(jnp.int32, values.shape, 0)
    query = first_query + lax.broadcasted_iota(jnp.int32, values.shape, 1)
    return key > query


def head_span(head):
    return pl.ds(pl.multiple_of(head * 128, 128), 128)


def each(count, body):
    def step(index, carry):
        body(index)
        return carry

    lax.fori_loop(0, count, step, 0)


def front_kernel(
    size,
    tokens_hbm,
    query_hbm,
    key_hbm,
    value_hbm,
    output_hbm,
    gate_hbm,
    gain_hbm,
    positions,
    frequency,
    rows_out,
    attention_out,
    output_out,
    gate_out,
    attended_out,
    query_rot_out,
    key_rot_out,
    value_out,
    query_hat_out,
    key_hat_out,
    cosine_out,
    sine_out,
    stats,
    query_scale,
    key_scale,
    attention_scale,
    feedforward_scale,
    rows,
    weight,
    projected,
    gain,
    cosine,
    sine,
    squares,
    query_rot,
    key_rot,
    value,
    query_hat,
    key_hat,
    attended,
    load_sem,
    store_sem,
    hand_send,
    hand_recv,
    shard_send,
    shard_recv,
    square_send,
    square_recv,
):
    me = lax.axis_index("tensor")
    last = size - 1
    own_rows, model_width = rows.shape[1:]
    piece_rows = own_rows // PIECES
    local_width = query_hbm.shape[1]
    heads = local_width // 128
    everyone = True
    greet([(everyone, lax.rem(me + offset, size)) for offset in range(1, size)])
    block = model_width // 8
    token_loads = [
        pltpu.make_async_copy(
            tokens_hbm.at[:, natural], rows.at[me, :, here], load_sem.at[0, place]
        )
        for place, (here, natural) in enumerate(column_blocks(block))
    ]
    shard_rows = pl.ds(0, query_hbm.shape[0])
    loads = [
        pltpu.make_async_copy(source, target, load_sem.at[1, place])
        for place, (source, target) in enumerate(
            (
                (query_hbm, weight.at[shard_rows, pl.ds(0, local_width)]),
                (key_hbm, weight.at[shard_rows, pl.ds(local_width, local_width)]),
                (value_hbm, weight.at[shard_rows, pl.ds(2 * local_width, local_width)]),
                (gain_hbm, gain.at[pl.ds(0, gain_hbm.shape[0]), :]),
                (output_hbm, output_out.at[:, pl.ds(0, output_hbm.shape[1])]),
                (gate_hbm, gate_out.at[pl.ds(0, gate_hbm.shape[0]), :]),
            )
        )
    ]
    for copy in token_loads + loads:
        copy.start()
    attention_target = row_halves(weight, query_hbm.shape[0])
    attention_flow, output_flow, gate_flow, gain_flow = (
        ShardGather(own, target, shard_send.at[kind], shard_recv.at[kind])
        for kind, (own, target) in enumerate(
            (
                (functools.partial(attention_target, 0), attention_target),
                (own_halves(output_hbm), column_halves(output_out, output_hbm.shape[1])),
                (own_halves(gate_hbm), row_halves(gate_out, gate_hbm.shape[0])),
                (own_halves(gain_hbm), row_halves(gain, gain_hbm.shape[0])),
            )
        )
    )
    pl.semaphore_wait(pltpu.get_barrier_semaphore(), 3 + size - 1)

    def away(way):
        return me if way == 0 else last - me

    def hand_copy(hop, piece, way, origin):
        here = rows.at[origin, pl.ds(piece * piece_rows, piece_rows)]
        return pltpu.make_async_remote_copy(
            src_ref=here,
            dst_ref=here,
            send_sem=hand_send.at[way, hop - 1, piece],
            recv_sem=hand_recv.at[way, hop - 1, piece],
            device_id={"tensor": me + 1 - 2 * way},
            device_id_type=pl.DeviceIdType.MESH,
        )

    for copy in token_loads:
        copy.wait()
    for piece in range(PIECES):
        for way in range(2):

            @pl.when(away(1 - way) >= 1)
            def _():
                hand_copy(1, piece, way, me).start()

        if piece == 0:
            for copy in loads[:3]:
                copy.wait()
            attention_flow.start(2, 4, 1)
            gain_flow.start(2, 4, 1)

    def hand_on(hop, piece):
        for way in range(2):

            @pl.when(away(way) >= hop)
            def _():
                origin = me - hop if way == 0 else me + hop
                hand_copy(hop, piece, way, origin).wait_recv()
                if hop < size - 1:

                    @pl.when(away(1 - way) >= 1)
                    def _():
                        hand_copy(hop + 1, piece, way, origin).start()

    def row_store(origin):
        return pltpu.make_async_copy(rows.at[origin], rows_out.at[origin], store_sem.at[0, origin])

    whole_stores = [
        pltpu.make_async_copy(source, target, store_sem.at[1 + place // size, place % size])
        for place, (source, target) in enumerate(
            (
                (weight, attention_out),
                (cosine, cosine_out),
                (sine, sine_out),
                (query_hat, query_hat_out),
                (key_hat, key_hat_out),
                (query_rot, query_rot_out),
                (key_rot, key_rot_out),
                (value, value_out),
                (attended, attended_out),
            )
        )
    ]

    def span_of(origin):
        return pl.ds(pl.multiple_of(origin * own_rows, own_rows), own_rows)

    def square_copy(offset, origin):
        return pltpu.make_async_remote_copy(
            src_ref=squares.at[me, origin],
            dst_ref=squares.at[me, origin],
            send_sem=square_send.at[offset - 1, origin],
            recv_sem=square_recv.at[offset - 1, origin],
            device_id={"tensor": lax.rem(me + offset, size)},
            device_id_type=pl.DeviceIdType.MESH,
        )

    def project(origin):
        def step(index):
            columns = pl.ds(pl.multiple_of(index * WIDE_TILE, WIDE_TILE), WIDE_TILE)
            projected[origin, :, columns] = jnp.dot(
                rows[origin], weight[:, columns], preferred_element_type=jnp.float32
            )

        row_store(origin).start()
        each(weight.shape[1] // WIDE_TILE, step)
        queries = projected[origin, :, pl.ds(0, local_width)]
        keys = projected[origin, :, pl.ds(local_width, local_width)]
        squares[me, origin, pl.ds(0, 8), :] = jnp.concatenate(
            [
                column_sums(queries * queries),
                column_sums(keys * keys),
                jnp.zeros((6, own_rows), jnp.float32),
            ],
            0,
        )
        for offset in range(1, size):
            square_copy(offset, origin).start()

    def project_from(hop, way):
        @pl.when(away(way) >= hop)
        def _():
            project(me - hop if way == 0 else me + hop)

    def normalize(origin):
        for offset in range(1, size):
            square_copy(offset, origin).wait_recv()
        total = squares[0, origin]
        for device in range(1, size):
            total = total + squares[device, origin]
        inverse = lax.rsqrt(total / model_width + EPS)
        here = span_of(origin)
        stats[pl.ds(heads, 2), here] = inverse[:2]
        for kind, (hat, rot, scale) in enumerate(
            ((query_hat, query_rot, query_scale), (key_hat, key_rot, key_scale))
        ):
            column = turned_rows(inverse[kind : kind + 1])

            def step(head):
                span = head_span(head)
                source = head_span(head + kind * heads)
                normalized = projected[origin, :, source] * column
                hat[here, span] = low(normalized)
                scaled = normalized * scale[pl.ds(head, 1), :]
                rot[here, span] = low(
                    scaled * cosine[here, :] + pltpu.roll(scaled, 64, 1) * sine[here, :]
                )

            each(heads, step)
        value[here, :] = low(projected[origin, :, pl.ds(2 * local_width, local_width)])

    def tables():
        for origin in range(size):
            here = pl.ds(origin * own_rows, own_rows)
            angles = turned_rows(wide(positions[:, here])) * frequency[...]
            cosine[here, :] = jnp.cos(angles)
            lane = lax.broadcasted_iota(jnp.int32, angles.shape, 1)
            sine[here, :] = jnp.where(lane < 64, -1.0, 1.0) * jnp.sin(angles)

    def scales():
        for kind, scale in enumerate((query_scale, key_scale)):
            total = wide(gain[pl.ds(0, 16), :])
            for place in range(1, 8):
                total = total + wide(gain[pl.ds(place * gain_hbm.shape[0], 16), :])
            scale[...] = jnp.concatenate(
                [total[kind * heads : (kind + 1) * heads], jnp.zeros((8 - heads, 128), jnp.float32)],
                0,
            )
        for place in range(8):
            lines = wide(gain[pl.ds(place * gain_hbm.shape[0], 16), :])
            for kind, scale in enumerate((attention_scale, feedforward_scale)):
                for line in range(block // 128):
                    at = 2 * heads + kind * (block // 128) + line
                    scale[:, pl.ds(place * block + line * 128, 128)] = lines[at : at + 1]

    def attend(head):
        span = head_span(head)
        for origin in range(size):
            count = (origin + 1) * own_rows
            here = pl.ds(origin * own_rows, own_rows)
            scores = rows_product(key_rot[pl.ds(0, count), span], query_rot[here, span])
            scores = scores * (128**-0.5)
            near = scores[origin * own_rows :]
            near = jnp.where(ahead_of(near, 0, 0), MASKED, near)
            scores = jnp.concatenate([scores[: origin * own_rows], near], 0) if origin else near
            row_max = jnp.max(scores, 0, keepdims=True)
            exponent = jnp.exp(scores - row_max)
            row_total = jnp.sum(exponent, 0, keepdims=True)
            result = jnp.dot(
                value[pl.ds(0, count), span].T, low(exponent), preferred_element_type=jnp.float32
            )
            attended[here, span] = low((result * (1.0 / row_total)).T)
            stats[pl.ds(head, 1), here] = row_max + jnp.log(row_total)

    def turns(beat):
        if beat == 1:
            tables()
            for copy in whole_stores[1:3]:
                copy.start()
        elif beat == 2:
            attention_flow.arrive(2, (0,))
            attention_flow.arrive(4, (0,))
        elif beat == 3:
            attention_flow.arrive(2, (1,))
            attention_flow.arrive(4, (1,))
            output_flow.start(2, 4, 1)
            gain_flow.arrive(2)
            gain_flow.arrive(4)
        elif beat == 5:
            attention_flow.arrive(6)
            gate_flow.start(2, 4, 1)
            gain_flow.arrive(6)
        elif beat == 6:
            output_flow.arrive(2)
            output_flow.arrive(4)
            for mask in (1, 3, 5, 7):
                attention_flow.arrive(mask)
            whole_stores[0].start()
            project(me)
        elif beat == 7:
            project_from(1, 0)
        elif beat == 8:
            project_from(1, 1)
            output_flow.arrive(6)
            loads[3].wait()
            for mask in (1, 3, 5, 7):
                gain_flow.arrive(mask)
            scales()
        elif beat == 9:
            gate_flow.arrive(2, (0,))
            gate_flow.arrive(4, (0,))
        elif beat == 10:
            project_from(2, 0)
        elif beat == 11:
            project_from(2, 1)
            gate_flow.arrive(2, (1,))
            gate_flow.arrive(4, (1,))

    for beat in range(1, (size - 1) * PIECES + 1):
        if beat == (size - 1) * PIECES:
            for origin in range(1, last):
                normalize(origin)
        hand_on((beat - 1) // PIECES + 1, (beat - 1) % PIECES)
        turns(beat)
    project_from(3, 0)
    project_from(3, 1)
    gate_flow.arrive(6)
    for origin in (0, last):
        normalize(origin)
    for copy in whole_stores[3:8]:
        copy.start()
    each(heads, attend)
    whole_stores[8].start()
    for flow in (output_flow, gate_flow):
        for mask in (1, 3, 5, 7):
            flow.arrive(mask)
    for hop in range(1, size):
        for way in range(2):

            @pl.when(jnp.logical_and(away(way) >= hop - 1, away(1 - way) >= 1))
            def _():
                for piece in range(PIECES):
                    hand_copy(hop, piece, way, 0).wait_send()

    for flow in (attention_flow, output_flow, gate_flow, gain_flow):
        flow.sent()
    for offset in range(1, size):
        for origin in range(size):
            square_copy(offset, origin).wait_send()
    for copy in loads[4:]:
        copy.wait()
    for origin in range(size):
        row_store(origin).wait()
    for copy in whole_stores:
        copy.wait()


def front(
    tokens_grouped,
    query_shard,
    key_shard,
    value_shard,
    output_shard,
    gate_shard,
    gain_shard,
    positions,
):
    size = lax.axis_size("tensor")
    own_rows, model_width = tokens_grouped.shape
    local_width = query_shard.shape[1]
    group_rows = size * own_rows
    low_type, wide_type = jnp.bfloat16, jnp.float32
    anywhere = pl.BlockSpec(memory_space=pl.ANY)
    inside = pl.BlockSpec(memory_space=pltpu.VMEM)
    dma = pltpu.SemaphoreType.DMA
    hands = (2, size - 1, PIECES)
    half_head = np.arange(128, dtype=np.float32) % 64
    frequency = (np.float32(THETA) ** (-(half_head * np.float32(2.0 / 128))))[None]

    def shape(dims, kind=low_type):
        return jax.ShapeDtypeStruct(dims, kind)

    local_rows = (group_rows, local_width)
    tables = (group_rows, 128)
    return pl.pallas_call(
        functools.partial(front_kernel, size),
        out_shape=[
            shape((size, own_rows, model_width)),
            shape((model_width, 3 * local_width)),
            shape((output_shard.shape[0], model_width)),
            shape((model_width, gate_shard.shape[1])),
            *[shape(local_rows)] * 6,
            *[shape(tables, wide_type)] * 2,
            shape((8, group_rows), wide_type),
            *[shape((8, 128), wide_type)] * 2,
            *[shape((1, model_width), wide_type)] * 2,
        ],
        in_specs=[anywhere] * 7 + [inside] * 2,
        out_specs=[anywhere] * 12 + [inside] * 5,
        scratch_shapes=[
            pltpu.VMEM((size, own_rows, model_width), low_type),
            pltpu.VMEM((model_width, 3 * local_width), low_type),
            pltpu.VMEM((size, own_rows, 3 * local_width), wide_type),
            pltpu.VMEM((8 * gain_shard.shape[0], gain_shard.shape[1]), low_type),
            pltpu.VMEM(tables, wide_type),
            pltpu.VMEM(tables, wide_type),
            pltpu.VMEM((size, size, 8, own_rows), wide_type),
            *[pltpu.VMEM(local_rows, low_type)] * 6,
            dma((2, 8)),
            dma((4, size)),
            dma(hands),
            dma(hands),
            dma((4, 7, 2)),
            dma((4, 7, 2)),
            dma((size - 1, size)),
            dma((size - 1, size)),
        ],
        compiler_params=pltpu.CompilerParams(
            collective_id=0, has_side_effects=True, vmem_limit_bytes=VMEM_BYTES
        ),
        cost_estimate=pl.CostEstimate(
            flops=6 * group_rows * model_width * local_width,
            bytes_accessed=32 << 20,
            transcendentals=0,
        ),
        name="front",
    )(
        tokens_grouped,
        query_shard,
        key_shard,
        value_shard,
        output_shard,
        gate_shard,
        gain_shard,
        positions.reshape(1, group_rows),
        frequency,
    )


class ShardSum:
    def __init__(self, near, far, corner, final, send_sem, recv_sem, core_only=False, deferred=False, own=None, awaited=None):
        self.near, self.far, self.corner, self.final = near, far, corner, final
        self.core_only, self.deferred = core_only, deferred
        self.own = own or functools.partial(near, 0)
        self.awaited = awaited or ((0, 0), (0, 1), (1, 0), (1, 1))
        self.send_sem, self.recv_sem = send_sem, recv_sem

    def remote(self, source, target, place, route):
        return pltpu.make_async_remote_copy(
            src_ref=source,
            dst_ref=target,
            send_sem=self.send_sem.at[place],
            recv_sem=self.recv_sem.at[place],
            device_id={"dp": shard_peer(route)},
            device_id_type=pl.DeviceIdType.MESH,
        )

    def core_copy(self, place):
        return self.remote(self.far(place), self.near(place), place, 1)

    def corner_copy(self, half):
        return self.remote(self.near(3, half), self.corner(half), 4 + half, (4, 2)[half])

    def final_copy(self, way, half):
        return self.remote(
            self.near(1 + way, half), self.final(way, half), 6 + 2 * way + half, (2, 4)[way]
        )

    def far_terms(self, term, place, count=1):
        term(4 + place, self.far(place, None, count), False, count)
        for index in reversed(range(place, place + count)):
            self.core_copy(index).start()

    def near_terms(self, term, place, count=1):
        for index in range(place, place + count):
            self.core_copy(index).wait_recv()
        term(place, self.near(place, None, count), True, count)
        if not self.core_only:
            for index in range(place, place + count):
                self.near_ready(index)

    def near_ready(self, place):
        if place == 3:
            for half in range(2):
                self.corner_copy(half).start()
        elif place:
            self.final_copy(place - 1, 2 - place).start()

    def first_terms(self, term):
        self.far_terms(term, 3)
        self.far_terms(term, 2)
        self.near_terms(term, 3)

    def other_terms(self, term):
        self.far_terms(term, 0, 2)
        self.near_terms(term, 2)
        self.near_terms(term, 0, 2)

    def take_corner(self):
        for half in range(2):
            self.corner_copy(half).wait_recv()
            add_into(self.near(1 + half, half), self.corner(half))
            if not self.deferred:
                self.final_copy(half, half).start()

    def final_arrived(self, half):
        for way in range(2):
            if (way, half) in self.awaited:
                self.final_copy(way, half).wait_recv()

    def take_final(self):
        for half in range(2):
            self.final_arrived(half)
            add_into(self.own(half), self.final(0, half), self.final(1, half))

    def take_final_turned(self, out):
        for half in range(2):
            self.final_arrived(half)
            own, first, second = self.own(half), self.final(0, half), self.final(1, half)
            rows = own.shape[0]

            def step(index):
                span = pl.ds(pl.multiple_of(index * TILE, TILE), TILE)
                value = wide(own[:, span]) + wide(first[:, span]) + wide(second[:, span])
                out[span, pl.ds(half * rows, rows)] = low(value.T)

            each(own.shape[1] // TILE, step)

    def sent(self, core=True):
        for place in range(4) if core else ():
            self.core_copy(place).wait_send()
        for half in range(2):
            self.corner_copy(half).wait_send()
            for way in range(2):
                if way != half or not self.deferred:
                    self.final_copy(way, half).wait_send()


def add_into(target, *sources):
    def step(index):
        span = pl.ds(pl.multiple_of(index * STRIP, STRIP), STRIP)
        total = wide(target[span, :])
        for source in sources:
            total = total + wide(source[span, :])
        target[span, :] = total.astype(target.dtype)

    each(target.shape[0] // STRIP, step)


def product_term(left, right):
    def term(place, target, adds, count=1):
        height, width = target.shape
        tile = 1024 if width % 1024 == 0 and count == 1 else 512
        turned = left(place * (height // count), height).T

        def step(index, carry):
            columns = pl.ds(pl.multiple_of(index * tile, tile), tile)
            value = jnp.dot(turned, right(columns, tile), preferred_element_type=jnp.float32)
            if adds:
                value = value + wide(target[:, columns])
            target[:, columns] = value.astype(target.dtype)
            return carry

        lax.fori_loop(0, target.shape[1] // tile, step, 0)

    return term


def stacked(buffer, first, height):
    def view(place, half=None, count=1):
        at = first + place * height
        if half is None:
            return buffer.at[pl.ds(at, count * height), :]
        return buffer.at[pl.ds(at + half * (height // 2), height // 2), :]

    return view


def middle_kernel(size, *refs):
    (
        attended_hbm,
        rows_hbm,
        cotangent_hbm,
        attention_scale,
        feedforward_scale,
        output_hbm,
        gate_hbm,
        up_hbm,
        down_hbm,
        mlp_out,
        inner_out,
        mixed_cot_out,
        branch_cot_out,
        grad_attended_out,
        block_out,
        grad_hidden_out,
        gate_grad_out,
        up_near_out,
        up_early_out,
        down_near_out,
        attention_gain_out,
        feedforward_gain_out,
        attended,
        tokens,
        cotangent,
        output_weight,
        gate_weight,
        up_weight,
        down_weight,
        everyone,
        gate_act,
        up_act,
        inner,
        hidden,
        branch,
        arrived,
        partial,
        total,
        load_sem,
        store_sem,
        sum_send,
        sum_recv,
        hand_send,
        hand_recv,
        shard_send,
        shard_recv,
        grad_send,
        grad_recv,
        again_sem,
        shuffle_sem,
        free_sem,
    ) = refs
    me = lax.axis_index("tensor")
    last = size - 1
    chunk_rows, model_width = tokens.shape[1], tokens.shape[2]
    units = gate_weight.shape[1]
    half_rows = chunk_rows // HALVES
    all_rows = size * chunk_rows

    greet(((me < last, me + 1), (me > 0, me - 1)))
    first_loads = [
        pltpu.make_async_copy(source, target, load_sem.at[place])
        for place, (source, target) in enumerate(
            (
                (attended_hbm, attended),
                (output_hbm, output_weight),
                (rows_hbm.at[me], tokens),
                (gate_hbm, gate_weight),
                (up_hbm, up_weight.at[pl.ds(0, up_hbm.shape[0]), :]),
                (down_hbm, down_weight.at[:, pl.ds(0, down_hbm.shape[1])]),
            )
        )
    ]
    first_loads += [
        pltpu.make_async_copy(
            cotangent_hbm.at[pl.ds(chunk * chunk_rows, chunk_rows), natural],
            cotangent.at[chunk, :, here],
            shuffle_sem.at[chunk, place],
        )
        for chunk in range(CHUNKS)
        for place, (here, natural) in enumerate(column_blocks(model_width // 8))
    ]
    for copy in first_loads[:2]:
        copy.start()
    up_flow = ShardGather(
        own_halves(up_hbm),
        row_halves(up_weight, up_hbm.shape[0]),
        shard_send.at[0],
        shard_recv.at[0],
    )
    down_flow = ShardGather(
        own_halves(down_hbm),
        column_halves(down_weight, down_hbm.shape[1]),
        shard_send.at[1],
        shard_recv.at[1],
    )
    pl.semaphore_wait(
        pltpu.get_barrier_semaphore(), 3 + jnp.minimum(me, 1) + jnp.minimum(last - me, 1)
    )
    up_flow.start(2, 4, 1)
    down_flow.start(1)

    height = model_width // 8
    again = [
        pltpu.make_async_copy(
            mlp_out.at[chunk, origin],
            down_weight.at[pl.ds((chunk * size + origin) * chunk_rows, chunk_rows), :],
            again_sem.at[chunk, origin],
        )
        for chunk in range(CHUNKS)
        for origin in range(size)
    ]
    gate_grads, up_grads = (
        ShardSum(
            stacked(buffer, 0, height),
            stacked(down_weight, 4 * height, height),
            functools.partial(stacked(buffer, 4 * height, height), 0),
            stacked(buffer, 5 * height, height),
            grad_send.at[kind],
            grad_recv.at[kind],
            deferred=kind == 1,
        )
        for kind, buffer in enumerate((gate_weight, up_weight))
    )

    down_grads = ShardSum(
        lambda place, half=None, count=1: up_act.at[
            place // 2, pl.ds(place % 2 * height, count * height), :
        ],
        stacked(down_weight, 4 * height, height),
        None,
        None,
        grad_send.at[2],
        grad_recv.at[2],
        core_only=True,
    )
    down_again = [
        pltpu.make_async_copy(
            mixed_cot_out.at[chunk, origin],
            down_weight.at[pl.ds((chunk * size + origin) * chunk_rows, chunk_rows), :],
            again_sem.at[chunk, origin],
        )
        for chunk in range(CHUNKS)
        for origin in range(size)
    ] + [
        pltpu.make_async_copy(inner_out.at[chunk], gate_act.at[chunk], again_sem.at[chunk, size])
        for chunk in range(CHUNKS)
    ]

    def signal_free(place, mask):
        pl.semaphore_signal(
            free_sem.at[place],
            inc=1,
            device_id={"dp": shard_peer(mask)},
            device_id_type=pl.DeviceIdType.MESH,
        )

    def rows_again(first, shard_width):
        return down_weight[pl.ds(0, CHUNKS * all_rows), pl.ds(first, shard_width)]

    def grad_term(act):
        def columns_of(columns, tile):
            return act[:, :, columns].reshape(CHUNKS * all_rows, tile)

        return product_term(rows_again, columns_of)

    def weights_free():
        for place, mask in enumerate((1, 2, 4)):
            signal_free(place, mask)

    def near_store(chunk):
        return pltpu.make_async_copy(
            up_act.at[chunk],
            down_near_out.at[pl.ds(chunk * all_rows, all_rows), :],
            again_sem.at[chunk, 0],
        )

    gate_store = pltpu.make_async_copy(
        gate_weight.at[pl.ds(0, height), :], gate_grad_out, store_sem.at[6, 0]
    )
    up_stores = [
        pltpu.make_async_copy(up_weight.at[pl.ds(first, count), :], target, store_sem.at[7, place])
        for place, (first, count, target) in enumerate(
            (
                (0, 3 * height, up_near_out),
                (5 * height + height // 2, height, up_early_out),
            )
        )
    ]

    def grad_turns(tick, half):
        gate_term, up_term = grad_term(gate_act), grad_term(up_act)
        if (tick, half) == (21, 0):
            for copy in again:
                copy.wait()
            for place in range(3):
                pl.semaphore_wait(free_sem.at[place], 1)
            gate_grads.first_terms(gate_term)
        elif (tick, half) == (21, 1):
            gate_grads.far_terms(gate_term, 0, 2)
            gate_grads.near_terms(gate_term, 2)
        elif (tick, half) == (22, 0):
            gate_grads.near_terms(gate_term, 0, 2)
        elif (tick, half) == (22, 1):
            for place in range(4):
                gate_grads.core_copy(place).wait_send()
            up_grads.far_terms(up_term, 3)
            up_grads.far_terms(up_term, 2)
        elif (tick, half) == (23, 0):
            gate_grads.take_corner()
            up_grads.near_terms(up_term, 3)
            up_grads.far_terms(up_term, 0, 2)
        elif (tick, half) == (23, 1):
            up_grads.near_terms(up_term, 2)
            up_grads.near_terms(up_term, 0, 2)
            signal_free(3, 1)
            for copy in down_again:
                copy.start()
        elif (tick, half) == (24, 1):
            for copy in down_again:
                copy.wait()
            for place in range(4):
                up_grads.core_copy(place).wait_send()
            pl.semaphore_wait(free_sem.at[3], 1)
            down_grads.far_terms(gate_term, 2, 2)
        elif (tick, half) == (25, 0):
            down_grads.far_terms(gate_term, 0, 2)
        elif (tick, half) == (25, 1):
            down_grads.near_terms(gate_term, 2, 2)
            near_store(1).start()
        elif (tick, half) == (26, 0):
            up_grads.take_corner()
            up_stores[0].start()
        elif (tick, half) == (26, 1):
            down_grads.near_terms(gate_term, 0, 2)
            near_store(0).start()
            gate_grads.take_final()
            gate_store.start()

    def turns(tick, half):
        if (tick, half) == (2, 1):
            up_flow.arrive(2, (0,))
            up_flow.arrive(4, (0,))
        elif (tick, half) == (3, 0):
            up_flow.arrive(2, (1,))
            up_flow.arrive(4, (1,))
            down_flow.start(2, 4)
        elif (tick, half) == (4, 1):
            up_flow.arrive(6)
        elif (tick, half) == (5, 0):
            down_flow.arrive(2, (0,))
            down_flow.arrive(4, (0,))
        elif (tick, half) == (6, 0):
            down_flow.arrive(2, (1,))
            down_flow.arrive(4, (1,))
        elif (tick, half) == (7, 0):
            down_flow.arrive(6)

    attention_gain_out[...] = jnp.zeros_like(attention_gain_out)
    feedforward_gain_out[...] = jnp.zeros_like(feedforward_gain_out)

    def half_span(half):
        return pl.ds(half * half_rows, half_rows)

    def strips(half, body):
        def step(index, carry):
            body(
                pl.ds(pl.multiple_of(half * half_rows + index * STRIP, STRIP), STRIP),
                pl.ds(pl.multiple_of(index * STRIP, STRIP), STRIP),
            )
            return carry

        lax.fori_loop(0, half_rows // STRIP, step, 0)

    def sum_copy(chunk, step, half, way, dest):
        return pltpu.make_async_remote_copy(
            src_ref=partial.at[chunk, dest, half_span(half)],
            dst_ref=arrived.at[way, chunk, step - 1, half_span(half)],
            send_sem=sum_send.at[way, chunk, step - 1, half],
            recv_sem=sum_recv.at[way, chunk, step - 1, half],
            device_id={"tensor": me + 1 - 2 * way},
            device_id_type=pl.DeviceIdType.MESH,
        )

    def hand_copy(chunk, hop, half, way, origin):
        rows = everyone.at[origin, chunk, half_span(half)]
        return pltpu.make_async_remote_copy(
            src_ref=rows,
            dst_ref=rows,
            send_sem=hand_send.at[way, chunk, hop - 1, half],
            recv_sem=hand_recv.at[way, chunk, hop - 1, half],
            device_id={"tensor": me + 1 - 2 * way},
            device_id_type=pl.DeviceIdType.MESH,
        )

    def away(way):
        return me if way == 0 else last - me

    def sum_step(chunk, step, half):
        for way in range(2):
            distance = away(way)

            @pl.when(distance <= step - 1)
            def _():
                dest = me + size - step if way == 0 else me - size + step
                if step > 1:

                    @pl.when(distance >= 1)
                    def _():
                        sum_copy(chunk, step - 1, half, way, dest).wait_recv()

                        def add(rows, _):
                            partial[chunk, dest, rows] = low(
                                wide(partial[chunk, dest, rows])
                                + wide(arrived[way, chunk, step - 2, rows])
                            )

                        strips(half, add)

                sum_copy(chunk, step, half, way, dest).start()

    def sum_end(chunk, half):
        def begin(rows, here):
            total[here] = wide(partial[chunk, me, rows])

        strips(half, begin)
        for way in range(2):

            @pl.when(away(way) >= 1)
            def _():
                sum_copy(chunk, size - 1, half, way, me).wait_recv()

                def add(rows, here):
                    total[here] = total[here] + wide(arrived[way, chunk, size - 2, rows])

                strips(half, add)

    def sum_sent(chunk):
        for step in range(1, size):
            for way in range(2):

                @pl.when(away(way) <= step - 1)
                def _():
                    for half in range(HALVES):
                        sum_copy(chunk, step, half, way, 0).wait_send()

    def hand_first(chunk, half):
        for way in range(2):

            @pl.when(away(1 - way) >= 1)
            def _():
                hand_copy(chunk, 1, half, way, me).start()

    def hand_on(chunk, hop, half):
        for way in range(2):

            @pl.when(away(way) >= hop)
            def _():
                origin = me - hop if way == 0 else me + hop
                hand_copy(chunk, hop, half, way, origin).wait_recv()
                if hop < size - 1:

                    @pl.when(away(1 - way) >= 1)
                    def _():
                        hand_copy(chunk, hop + 1, half, way, origin).start()

    def hand_sent(chunk):
        for hop in range(1, size):
            for way in range(2):

                @pl.when(jnp.logical_and(away(way) >= hop - 1, away(1 - way) >= 1))
                def _():
                    for half in range(HALVES):
                        hand_copy(chunk, hop, half, way, 0).wait_send()

    def inverse_rms(values):
        return lax.rsqrt(jnp.mean(values * values, -1, keepdims=True) + EPS)

    def fold(values):
        return values[:8] + values[8:]

    def own_rows(chunk, stage, half):
        def after_branch(rows, here):
            value = total[here]
            branch[chunk, rows] = value
            state = wide(tokens[chunk, rows]) + value * inverse_rms(value) * attention_scale[...]
            hidden[chunk, rows] = state
            everyone[me, chunk, rows] = low(state)

        def after_mixed(rows, here):
            value = total[here]
            inverse = inverse_rms(value)
            normalized = value * inverse
            hidden[chunk, rows] = hidden[chunk, rows] + normalized * feedforward_scale[...]
            grad = wide(cotangent[chunk, rows])
            feedforward_gain_out[...] += fold(grad * normalized)
            everyone[me, chunk, rows] = low(
                norm_backward(grad, normalized, inverse, feedforward_scale[...])
            )

        def after_gradient(rows, here):
            grad = total[here] + wide(cotangent[chunk, rows])
            value = branch[chunk, rows]
            inverse = inverse_rms(value)
            normalized = value * inverse
            branch[chunk, rows] = grad
            attention_gain_out[...] += fold(grad * normalized)
            everyone[me, chunk, rows] = low(
                norm_backward(grad, normalized, inverse, attention_scale[...])
            )

        strips(half, (after_branch, after_mixed, after_gradient)[stage])

    def gathered(chunk):
        return everyone[:, chunk].reshape(all_rows, model_width)

    def tiles(first, end, body):
        def step(index, carry):
            body(pl.ds(pl.multiple_of(index * WIDE_TILE, WIDE_TILE), WIDE_TILE))
            return carry

        lax.fori_loop(first, end, step, 0)

    def store(kind, chunk):
        source, target = (
            (everyone.at[:, chunk], mlp_out.at[chunk]),
            (inner, inner_out.at[chunk]),
            (everyone.at[:, chunk], mixed_cot_out.at[chunk]),
            (everyone.at[:, chunk], branch_cot_out.at[:, chunk]),
            (attended.at[:, chunk], grad_attended_out.at[:, chunk]),
            (branch.at[chunk], grad_hidden_out.at[chunk]),
        )[kind]
        return pltpu.make_async_copy(source, target, store_sem.at[kind, chunk])

    def block_stores(chunk):
        return [
            pltpu.make_async_copy(
                hidden.at[chunk, :, here],
                block_out.at[pl.ds(chunk * chunk_rows, chunk_rows), natural],
                shuffle_sem.at[chunk, place],
            )
            for place, (here, natural) in enumerate(column_blocks(model_width // 8))
        ]

    def put_partial(chunk, columns, values):
        partial[chunk, :, :, columns] = low(values).reshape(size, chunk_rows, WIDE_TILE)

    def branch_terms(chunk):
        def tile(columns):
            rows = attended[:, chunk].reshape(all_rows, attended.shape[-1])
            put_partial(
                chunk,
                columns,
                jnp.dot(rows, output_weight[:, columns], preferred_element_type=jnp.float32),
            )

        tiles(0, model_width // WIDE_TILE, tile)

    def gate_tile(chunk):
        def tile(columns):
            rows = gathered(chunk)
            gate = jnp.dot(rows, gate_weight[:, columns], preferred_element_type=jnp.float32)
            up = jnp.dot(rows, up_weight[:, columns], preferred_element_type=jnp.float32)
            gate_act[chunk, :, columns] = low(gate)
            up_act[chunk, :, columns] = low(up)
            inner[:, columns] = low(gate * jax.nn.sigmoid(gate) * up)

        return tile

    def down_tile(chunk):
        def tile(columns):
            put_partial(
                chunk,
                columns,
                jnp.dot(inner[...], down_weight[:, columns], preferred_element_type=jnp.float32),
            )

        return tile

    def grad_inner_tile(chunk):
        def tile(columns):
            grad = rows_product(gathered(chunk), down_weight[columns, :])
            gate = wide(gate_act[chunk, :, columns])
            up = wide(up_act[chunk, :, columns])
            sigmoid = jax.nn.sigmoid(gate)
            gate_act[chunk, :, columns] = low(
                grad * up * sigmoid * (1.0 + gate * (1.0 - sigmoid))
            )
            up_act[chunk, :, columns] = low(grad * gate * sigmoid)

        return tile

    def grad_inner_half_tile(chunk, half):
        spans = [
            pl.ds(origin * chunk_rows + half * half_rows, half_rows) for origin in range(size)
        ]

        def tile(columns):
            rows = everyone[:, chunk, half_span(half)].reshape(size * half_rows, model_width)
            grad = rows_product(rows, down_weight[columns, :])
            gate = wide(jnp.concatenate([gate_act[chunk, span, columns] for span in spans], 0))
            up = wide(jnp.concatenate([up_act[chunk, span, columns] for span in spans], 0))
            sigmoid = jax.nn.sigmoid(gate)
            for_gate = low(grad * up * sigmoid * (1.0 + gate * (1.0 - sigmoid)))
            for_up = low(grad * gate * sigmoid)
            for origin, span in enumerate(spans):
                here = slice(origin * half_rows, (origin + 1) * half_rows)
                gate_act[chunk, span, columns] = for_gate[here]
                up_act[chunk, span, columns] = for_up[here]

        return tile

    def grad_input_tile(chunk):
        def tile(columns):
            put_partial(
                chunk,
                columns,
                rows_product(gate_act[chunk], gate_weight[columns, :])
                + rows_product(up_act[chunk], up_weight[columns, :]),
            )

        return tile

    unit_tiles, width_tiles = units // WIDE_TILE, model_width // WIDE_TILE

    def forward_piece(chunk, piece):
        if piece == 0:
            if chunk == 0:
                for mask in (1, 3, 5, 7):
                    up_flow.arrive(mask)
                for copy in first_loads[3:6]:
                    copy.wait()
            store(0, chunk).start()
            tiles(0, unit_tiles // 2, gate_tile(chunk))
        elif piece == 1:
            tiles(unit_tiles // 2, unit_tiles, gate_tile(chunk))
            store(1, chunk).start()
            sum_sent(chunk)
            hand_sent(chunk)
        else:
            if chunk == 0:
                for mask in (1, 3, 5, 7):
                    down_flow.arrive(mask)
            tiles(0, width_tiles, down_tile(chunk))
            store(0, chunk).wait()
            store(1, chunk).wait()

    def backward_piece(chunk, piece):
        if piece == 0:
            store(2, chunk).start()
            for copy in block_stores(chunk):
                copy.start()
            tiles(0, unit_tiles // 2, grad_inner_half_tile(chunk, 1))
            tiles(unit_tiles // 2, unit_tiles, grad_inner_tile(chunk))
            if chunk == CHUNKS - 1:
                down_flow.sent()
                for copy in again:
                    copy.start()
        elif piece == 1:
            sum_sent(chunk)
            hand_sent(chunk)
            tiles(0, width_tiles // 2, grad_input_tile(chunk))
        else:
            tiles(width_tiles // 2, width_tiles, grad_input_tile(chunk))
            store(2, chunk).wait()
            for copy in block_stores(chunk):
                copy.wait()
            if chunk == CHUNKS - 1:
                up_flow.sent()
                weights_free()

    def end_piece(chunk, piece):
        if piece == 0:
            store(3, chunk).start()
            store(5, chunk).start()
            for first in range(0, attended.shape[-1], TILE):
                columns = pl.ds(first, TILE)
                value = rows_product(gathered(chunk), output_weight[columns, :])
                attended[:, chunk, :, columns] = low(value).reshape(size, chunk_rows, TILE)
            store(4, chunk).start()

    first_loads[0].wait()
    first_loads[1].wait()
    for copy in first_loads[2:]:
        copy.start()
    branch_terms(0)
    first_loads[2].wait()
    for copy in first_loads[6:]:
        copy.wait()
    bases = {
        (chunk, stage): (CHUNKS * stage + chunk) * size
        for stage in range(3)
        for chunk in range(CHUNKS)
    }
    ticks = max(bases.values()) + 2 * size
    for tick in range(1, ticks + 1):
        for half in range(HALVES):
            for (chunk, stage), base in bases.items():
                at = tick - base
                if size < at < 2 * size:
                    hand_on(chunk, at - size, half)
            for (chunk, stage), base in bases.items():
                at = tick - base
                if 1 <= at < size:
                    sum_step(chunk, at, half)
                elif at == size:
                    sum_end(chunk, half)
                    own_rows(chunk, stage, half)
                    hand_first(chunk, half)
            turns(tick, half)
            if tick == 1 and half == 1:
                branch_terms(1)
            for (chunk, stage), base in bases.items():
                piece = (tick - base - 2 * size + 1) * HALVES + half - 1
                if piece == -1 and stage == 1:
                    tiles(0, unit_tiles // 2, grad_inner_half_tile(chunk, 0))
                elif 0 <= piece < 3:
                    (forward_piece, backward_piece, end_piece)[stage](chunk, piece)
            grad_turns(tick, half)
    for half in range(2):
        up_grads.final_copy(1 - half, half).wait_recv()
    up_stores[1].start()
    gate_grads.sent(False)
    up_grads.sent(False)
    for place in range(4):
        down_grads.core_copy(place).wait_send()
    for chunk in range(CHUNKS):
        sum_sent(chunk)
        hand_sent(chunk)
        store(3, chunk).wait()
        store(4, chunk).wait()
        store(5, chunk).wait()
        near_store(chunk).wait()
    for copy in [gate_store] + up_stores:
        copy.wait()


def middle(
    attended,
    rows_all,
    cotangent_grouped,
    attention_scale,
    feedforward_scale,
    output_full,
    gate_full,
    up_shard,
    down_shard,
):
    size = lax.axis_size("tensor")
    own_rows, model_width = cotangent_grouped.shape
    chunk_rows = own_rows // CHUNKS
    all_rows = size * chunk_rows
    half_rows = chunk_rows // HALVES
    heads_width = attended.shape[1]
    units = gate_full.shape[1]
    chunked = (CHUNKS, chunk_rows, model_width)
    lined = (CHUNKS, size, chunk_rows, model_width)
    low_type, wide_type = jnp.bfloat16, jnp.float32

    def shape(dims, kind=low_type):
        return jax.ShapeDtypeStruct(dims, kind)

    anywhere = pl.BlockSpec(memory_space=pl.ANY)
    inside = pl.BlockSpec(memory_space=pltpu.VMEM)
    dma = pltpu.SemaphoreType.DMA
    flops = 2 * CHUNKS * all_rows * model_width * (2 * heads_width + 6 * units)
    outs = pl.pallas_call(
        functools.partial(middle_kernel, size),
        out_shape=[
            shape(lined),
            shape((CHUNKS, all_rows, units)),
            shape(lined),
            shape((size, CHUNKS, chunk_rows, model_width)),
            shape((size, CHUNKS, chunk_rows, heads_width)),
            shape((own_rows, model_width), wide_type),
            shape(chunked, wide_type),
            shape((model_width // 8, units)),
            shape((3 * model_width // 8, units)),
            shape((model_width // 8, units)),
            shape((model_width // 2, units)),
            shape((8, model_width), wide_type),
            shape((8, model_width), wide_type),
        ],
        in_specs=[anywhere] * 3 + [inside] * 2 + [anywhere] * 4,
        out_specs=[anywhere] * 11 + [inside] * 2,
        scratch_shapes=[
            pltpu.VMEM((size, CHUNKS, chunk_rows, heads_width), low_type),
            pltpu.VMEM(chunked, low_type),
            pltpu.VMEM(chunked, low_type),
            pltpu.VMEM((heads_width, model_width), low_type),
            pltpu.VMEM((model_width, units), low_type),
            pltpu.VMEM((model_width, units), low_type),
            pltpu.VMEM((units, model_width), low_type),
            pltpu.VMEM((size, CHUNKS, chunk_rows, model_width), low_type),
            pltpu.VMEM((CHUNKS, all_rows, units), low_type),
            pltpu.VMEM((CHUNKS, all_rows, units), low_type),
            pltpu.VMEM((all_rows, units), low_type),
            pltpu.VMEM(chunked, wide_type),
            pltpu.VMEM(chunked, wide_type),
            pltpu.VMEM((2, CHUNKS, size - 1, chunk_rows, model_width), low_type),
            pltpu.VMEM(lined, low_type),
            pltpu.VMEM((half_rows, model_width), wide_type),
            dma((6,)),
            dma((8, CHUNKS)),
            dma((2, CHUNKS, size - 1, HALVES)),
            dma((2, CHUNKS, size - 1, HALVES)),
            dma((2, CHUNKS, size - 1, HALVES)),
            dma((2, CHUNKS, size - 1, HALVES)),
            dma((2, 7, 2)),
            dma((2, 7, 2)),
            dma((3, 10)),
            dma((3, 10)),
            dma((CHUNKS, size + 1)),
            dma((CHUNKS, 8)),
            pltpu.SemaphoreType.REGULAR((4,)),
        ],
        compiler_params=pltpu.CompilerParams(
            collective_id=1, has_side_effects=True, vmem_limit_bytes=VMEM_BYTES
        ),
        cost_estimate=pl.CostEstimate(
            flops=flops, bytes_accessed=64 << 20, transcendentals=0
        ),
        name="middle",
    )(
        attended.reshape(size, CHUNKS, chunk_rows, heads_width),
        rows_all.reshape(size, *chunked),
        cotangent_grouped,
        attention_scale,
        feedforward_scale,
        output_full,
        gate_full,
        up_shard,
        down_shard,
    )
    rows = CHUNKS * all_rows
    return (
        outs[3].reshape(rows, model_width),
        outs[4].reshape(rows, heads_width),
        outs[5],
        outs[6].reshape(own_rows, model_width),
        *outs[7:],
    )


def back_kernel(
    size,
    branch_cot_hbm,
    grad_attended_hbm,
    query_rot_hbm,
    key_rot_hbm,
    value_hbm,
    query_hat_hbm,
    key_hat_hbm,
    cosine_hbm,
    sine_hbm,
    down_near_hbm,
    up_near,
    up_early,
    attended_hbm,
    weight_hbm,
    rows_hbm,
    hidden_hbm,
    stats,
    query_scale,
    key_scale,
    attention_gain,
    feedforward_gain,
    tokens_out,
    up_out,
    down_out,
    output_out,
    query_out,
    key_out,
    value_out,
    gain_out,
    left,
    attended,
    weight,
    grad,
    gain,
    shared,
    hidden,
    partial,
    arrived,
    far,
    down_near,
    output_far,
    output_near,
    attention_near,
    gain_far,
    gain_near,
    up_final,
    wide_total,
    down_total,
    output_total,
    load_sem,
    store_sem,
    share_send,
    share_recv,
    sum_send,
    sum_recv,
    shard_send,
    shard_recv,
):
    me = lax.axis_index("tensor")
    last = size - 1
    own_rows, model_width = partial.shape[1:]
    group_rows = size * own_rows
    local_width = attended.shape[1]
    heads = local_width // 128
    piece_rows = own_rows // PIECES
    height = model_width // 8
    greet([(True, lax.rem(me + offset, size)) for offset in range(1, size)])

    def beside(index):
        return pl.ds(index * local_width, local_width)

    pairs = [
        (grad_attended_hbm, output_far),
        (key_rot_hbm, partial.at[:, :, beside(1)]),
        (query_rot_hbm, partial.at[:, :, beside(0)]),
        (value_hbm, partial.at[:, :, beside(2)]),
        (attended_hbm, attended),
        (query_hat_hbm, partial.at[:, :, beside(3)]),
        (cosine_hbm, wide_total.at[pl.ds(0, group_rows), pl.ds(0, 128)]),
        (sine_hbm, wide_total.at[pl.ds(0, group_rows), pl.ds(128, 128)]),
    ]
    pairs += [
        (key_hat_hbm.at[origin], far.at[pl.ds(3 * height, own_rows), beside(origin)])
        for origin in range(size)
    ]
    first_count = len(pairs)
    pairs += [
        (down_near_hbm, down_near.at[pl.ds(0, 4 * height), :]),
        (weight_hbm, weight),
        (branch_cot_hbm, left),
        (up_near.at[pl.ds(0, height), :], up_final.at[pl.ds(2 * height, height), :]),
        (up_early, up_final.at[pl.ds(height // 2, height), :]),
        (rows_hbm, left),
        (hidden_hbm, hidden),
    ]
    loads = [
        pltpu.make_async_copy(source, target, load_sem.at[place])
        for place, (source, target) in enumerate(pairs)
    ]
    near_load, weight_load, left_load, own_load, early_load, rows_load, hidden_load = loads[
        first_count:
    ]
    for copy in loads[:first_count]:
        copy.start()

    def flow(kind, near, far_view, shard_height):
        return ShardSum(
            stacked(near, 0, shard_height),
            far_view,
            lambda half: stacked(near, 4 * shard_height, shard_height)(0, half),
            lambda way, half: stacked(near, 5 * shard_height, shard_height)(way, half),
            shard_send.at[kind],
            shard_recv.at[kind],
        )

    down_flow = flow(0, down_near, None, height)
    output_flow = flow(1, output_near, stacked(output_far, 0, height), height)
    attention_flow = flow(
        2,
        attention_near,
        lambda place, half=None, count=1: far.at[
            pl.ds(place * height, count * height), pl.ds(0, 3 * local_width)
        ],
        height,
    )
    gain_height = gain.shape[0] // 8
    gain_flow = flow(3, gain_near, stacked(gain_far, 0, gain_height), gain_height)
    up_flow = ShardSum(
        stacked(up_near, 0, height),
        None,
        None,
        stacked(up_final, 0, height),
        shard_send.at[4],
        shard_recv.at[4],
        own=functools.partial(stacked(up_final, 2 * height, height), 0),
        awaited=((0, 0), (1, 1)),
    )

    def columns_of(source):
        return lambda first, width: source[:, pl.ds(first, width)]

    output_term = product_term(columns_of(left), lambda columns, _: attended[:, columns])
    attention_term = product_term(columns_of(left), lambda columns, _: grad[:, columns])

    def gain_term(place, target, adds, count):
        value = gain[pl.ds(place * gain_height, target.shape[0]), :]
        target[...] = value + target[...] if adds else value

    def away(way):
        return me if way == 0 else last - me

    def held(kind, head):
        return pl.ds(pl.multiple_of(kind * local_width + head * 128, 128), 128)

    score_scale = 128**-0.5
    query_grad, key_grad = pl.ds(0, 128), pl.ds(128, 128)

    def product_columns(kind, origin):
        return pl.ds((kind * size + origin) * 128, 128)

    def step_head(head):
        span = head_span(head)
        for origin in reversed(range(size)):
            count = (origin + 1) * own_rows
            here = pl.ds(origin * own_rows, own_rows)
            seen = pl.ds(0, origin + 1)
            keys = partial[seen, :, held(1, head)].reshape(count, 128)
            values = partial[seen, :, held(2, head)].reshape(count, 128)
            queries = partial[origin, :, held(0, head)]
            grad_rows = output_far[here, span]
            delta = column_sums(wide(grad_rows) * wide(attended[here, span]))
            probs = jnp.exp(
                rows_product(keys, queries) * score_scale - stats[pl.ds(head, 1), here]
            )
            near = probs[origin * own_rows :]
            near = jnp.where(ahead_of(near, 0, 0), 0.0, near)
            probs = jnp.concatenate([probs[: origin * own_rows], near], 0) if origin else near
            grad_scores = low(probs * (rows_product(values, grad_rows) - delta))
            for_values = jnp.dot(low(probs), grad_rows, preferred_element_type=jnp.float32)
            for_keys = jnp.dot(grad_scores, queries, preferred_element_type=jnp.float32)
            for_queries = jnp.dot(keys.T, grad_scores, preferred_element_type=jnp.float32)
            wide_total[pl.ds(group_rows + origin * own_rows, own_rows), query_grad] = (
                for_queries * score_scale
            ).T
            first = origin == size - 1
            at = pl.ds(group_rows, count)
            wide_total[at, key_grad] = for_keys if first else wide_total[at, key_grad] + for_keys
            for block in range(origin + 1):
                term = for_values[block * own_rows : (block + 1) * own_rows]
                columns = product_columns(2, block)
                hidden[:, columns] = term if first else hidden[:, columns] + term
        for kind, (factor, scale) in enumerate(((1.0, query_scale), (score_scale, key_scale))):
            gain_total = jnp.zeros((1, 128), jnp.float32)
            for origin in range(size):
                here = pl.ds(origin * own_rows, own_rows)
                source = wide_total[
                    pl.ds(group_rows + origin * own_rows, own_rows), (query_grad, key_grad)[kind]
                ]
                rotated = wide(low(source * factor))
                normal = rotated * wide_total[here, pl.ds(0, 128)]
                normal = normal - pltpu.roll(rotated, 64, 1) * wide_total[here, pl.ds(128, 128)]
                hats = hat_of(kind, origin, head)
                gain_total = gain_total + jnp.sum(normal * hats, 0, keepdims=True)
                normal = normal * scale[pl.ds(head, 1), :]
                grad[here, held(kind, head)] = low(normal)
                hidden[:, product_columns(kind, origin)] += normal * hats
            gain[pl.ds(kind * heads + head, 1), :] = gain_total
        for origin in range(size):
            grad[pl.ds(origin * own_rows, own_rows), held(2, head)] = low(
                hidden[:, product_columns(2, origin)]
            )

    def hat_of(kind, origin, head):
        if kind == 0:
            return wide(partial[origin, :, held(3, head)])
        return wide(far[pl.ds(3 * height, own_rows), held(origin, head)])

    def share_copy(offset):
        return pltpu.make_async_remote_copy(
            src_ref=shared.at[me],
            dst_ref=shared.at[me],
            send_sem=share_send.at[offset - 1],
            recv_sem=share_recv.at[offset - 1],
            device_id={"tensor": lax.rem(me + offset, size)},
            device_id_type=pl.DeviceIdType.MESH,
        )

    def share():
        half_width = model_width // 2
        lines = [
            jnp.concatenate(
                [column_sums(hidden[:, product_columns(kind, origin)]) for origin in range(size)],
                1,
            )
            for kind in range(2)
        ]
        for part in (attention_gain, feedforward_gain):
            total = jnp.sum(part[...], 0, keepdims=True)
            lines += [total[:, :half_width], total[:, half_width:]]
        lines.append(jnp.zeros((2, half_width), jnp.float32))
        shared[me] = jnp.concatenate(lines, 0)
        for offset in range(1, size):
            share_copy(offset).start()

    def take_shares():
        for offset in range(1, size):
            share_copy(offset).wait_recv()
        total = shared[0]
        for device in range(1, size):
            total = total + shared[device]
        for kind in range(2):
            for origin in range(size):
                here = pl.ds(origin * own_rows, own_rows)
                columns = slice(origin * own_rows, (origin + 1) * own_rows)
                inner_column = turned_rows(total[kind : kind + 1, columns] / model_width)
                inverse = turned_rows(stats[pl.ds(heads + kind, 1), here])
                for head in range(heads):
                    span = pl.ds((kind * heads + head) * 128, 128)
                    hats = hat_of(kind, origin, head)
                    grad[here, span] = low(inverse * (wide(grad[here, span]) - hats * inner_column))
        for place in range(8):
            if place:
                gain[pl.ds(place * gain_height, 8), :] = gain[pl.ds(0, 8), :]
            for kind in range(2):
                for line in range(height // 128):
                    row, first = divmod(place * height + line * 128, model_width // 2)
                    gain[
                        pl.ds(place * gain_height + 8 + kind * (height // 128) + line, 1), :
                    ] = total[2 + 2 * kind + row : 3 + 2 * kind + row, first : first + 128]

    def terms(dest, count):
        span = pl.ds(pl.multiple_of(dest * own_rows, own_rows), count * own_rows)

        def step(index):
            columns = pl.ds(pl.multiple_of(index * WIDE_TILE, WIDE_TILE), WIDE_TILE)
            value = low(rows_product(grad[span, :], weight[columns, :]))
            partial[pl.ds(dest, count), :, columns] = value.reshape(count, own_rows, WIDE_TILE)

        each(model_width // WIDE_TILE, step)

    low_side = 1 - 2 * me // size

    def first_terms():
        terms(last * low_side, 1)

    def other_terms():
        terms(1 - low_side, last)

    def span_of(piece):
        return pl.ds(piece * piece_rows, piece_rows)

    def sum_copy(step, piece, way, dest):
        return pltpu.make_async_remote_copy(
            src_ref=partial.at[dest, span_of(piece)],
            dst_ref=arrived.at[way, step - 1, span_of(piece)],
            send_sem=sum_send.at[way, step - 1, piece],
            recv_sem=sum_recv.at[way, step - 1, piece],
            device_id={"tensor": me + 1 - 2 * way},
            device_id_type=pl.DeviceIdType.MESH,
        )

    def sum_step(step, *pieces):
        for piece in pieces:
            for way in range(2):
                distance = away(way)

                @pl.when(distance <= step - 1)
                def _():
                    dest = me + size - step if way == 0 else me - size + step
                    if step > 1:

                        @pl.when(distance >= 1)
                        def _():
                            sum_copy(step - 1, piece, way, dest).wait_recv()
                            add_into(
                                partial.at[dest, span_of(piece)],
                                arrived.at[way, step - 2, span_of(piece)],
                            )

                    sum_copy(step, piece, way, dest).start()

    def token_stores(piece):
        return [
            pltpu.make_async_copy(
                hidden.at[span_of(piece), here],
                tokens_out.at[span_of(piece), natural],
                store_sem.at[1 + piece, place],
            )
            for place, (here, natural) in enumerate(column_blocks(height))
        ]

    def sum_end(*pieces):
        for piece in pieces:
            add_into(hidden.at[span_of(piece)], partial.at[me, span_of(piece)])
            for way in range(2):

                @pl.when(away(way) >= 1)
                def _():
                    sum_copy(size - 1, piece, way, me).wait_recv()
                    add_into(
                        hidden.at[span_of(piece)], arrived.at[way, size - 2, span_of(piece)]
                    )

            for copy in token_stores(piece):
                copy.start()

    up_store = pltpu.make_async_copy(
        up_final.at[pl.ds(2 * height, height), :], up_out, store_sem.at[0, 0]
    )
    down_store = pltpu.make_async_copy(down_total, down_out, store_sem.at[0, 1])
    output_store = pltpu.make_async_copy(output_total, output_out, store_sem.at[0, 2])
    attention_stores = [
        pltpu.make_async_copy(
            attention_near.at[pl.ds(0, height), beside(kind)], out, store_sem.at[0, 3 + kind]
        )
        for kind, out in enumerate((query_out, key_out, value_out))
    ]

    gain[...] = jnp.zeros_like(gain)
    hidden[...] = jnp.zeros_like(hidden)
    pl.semaphore_wait(pltpu.get_barrier_semaphore(), 3 + size - 1)
    for half in range(2):
        up_flow.final_copy(half, half).start()
    for copy in loads[:first_count]:
        copy.wait()
    for copy in (near_load, left_load, weight_load, own_load, early_load):
        copy.start()
    each(heads // 2, step_head)
    near_load.wait()
    for place in (3, 1, 2):
        down_flow.near_ready(place)
    each(heads - heads // 2, lambda index: step_head(heads // 2 + index))
    share()
    hidden_load.start()
    left_load.wait()
    output_flow.first_terms(output_term)
    take_shares()
    weight_load.wait()
    first_terms()
    sum_step(1, *range(PIECES))
    output_flow.other_terms(output_term)
    rows_load.start()
    down_flow.take_corner()
    other_terms()
    sum_step(2, 0)
    own_load.wait()
    early_load.wait()
    up_flow.take_final()
    up_store.start()
    gain_flow.first_terms(gain_term)
    gain_flow.other_terms(gain_term)
    rows_load.wait()
    attention_flow.first_terms(attention_term)
    sum_step(2, 1)
    output_flow.take_corner()
    sum_step(2, 2)
    attention_flow.other_terms(attention_term)
    sum_step(2, 3)
    sum_step(3, 0)
    gain_flow.take_corner()
    sum_step(3, 1)
    sum_step(3, 2)
    sum_step(3, 3)
    hidden_load.wait()
    attention_flow.take_corner()
    output_flow.take_final_turned(output_total)
    output_store.start()
    gain_flow.take_final()
    gain_out[...] = gain_near[pl.ds(0, gain_height), :]
    sum_end(0)
    sum_end(1)
    down_flow.take_final_turned(down_total)
    down_store.start()
    sum_end(2)
    sum_end(3)
    attention_flow.take_final()
    for copy in attention_stores:
        copy.start()
    down_flow.sent(False)
    for shard_flow in (output_flow, attention_flow, gain_flow):
        shard_flow.sent()
    for half in range(2):
        up_flow.final_copy(half, half).wait_send()
    for offset in range(1, size):
        share_copy(offset).wait_send()
    for step in range(1, size):
        for way in range(2):

            @pl.when(away(way) <= step - 1)
            def _():
                for piece in range(PIECES):
                    sum_copy(step, piece, way, 0).wait_send()

    for copy in [up_store, down_store, output_store] + attention_stores:
        copy.wait()
    for piece in range(PIECES):
        for copy in token_stores(piece):
            copy.wait()


def back(
    branch_cot,
    grad_attended,
    query_rot,
    key_rot,
    value_rows,
    query_hat,
    key_hat,
    cosine,
    sine,
    down_near,
    up_near,
    up_early,
    attended,
    attention_full,
    rows_all,
    grad_hidden,
    *small,
):
    size = lax.axis_size("tensor")
    own_rows, model_width = grad_hidden.shape
    group_rows = size * own_rows
    height = model_width // 8
    local_width, units = attended.shape[1], down_near.shape[1]
    low_type, wide_type = jnp.bfloat16, jnp.float32
    anywhere = pl.BlockSpec(memory_space=pl.ANY)
    inside = pl.BlockSpec(memory_space=pltpu.VMEM)
    dma = pltpu.SemaphoreType.DMA
    by_device = (size, own_rows, local_width)

    def shape(*dims):
        return jax.ShapeDtypeStruct(dims, wide_type)

    def low_shape(*dims):
        return jax.ShapeDtypeStruct(dims, low_type)

    return pl.pallas_call(
        functools.partial(back_kernel, size),
        out_shape=[
            shape(own_rows, model_width),
            low_shape(height, units),
            low_shape(units, height),
            low_shape(local_width, height),
            *[low_shape(height, local_width)] * 3,
            shape(32, 128),
        ],
        in_specs=[anywhere] * 16 + [inside] * len(small),
        out_specs=[anywhere] * 7 + [inside],
        scratch_shapes=[
            pltpu.VMEM((group_rows, model_width), low_type),
            pltpu.VMEM((group_rows, local_width), low_type),
            pltpu.VMEM((model_width, 3 * local_width), low_type),
            pltpu.VMEM((group_rows, 3 * local_width), low_type),
            pltpu.VMEM((8 * 32, 128), wide_type),
            pltpu.VMEM((size, 8, model_width // 2), wide_type),
            pltpu.VMEM((own_rows, model_width), wide_type),
            pltpu.VMEM((size, own_rows, model_width), low_type),
            pltpu.VMEM((2, size - 1, own_rows, model_width), low_type),
            pltpu.VMEM((4 * height, units), low_type),
            pltpu.VMEM((7 * height, units), low_type),
            pltpu.VMEM((4 * height, local_width), low_type),
            pltpu.VMEM((7 * height, local_width), low_type),
            pltpu.VMEM((7 * height, 3 * local_width), low_type),
            pltpu.VMEM((4 * 32, 128), wide_type),
            pltpu.VMEM((7 * 32, 128), wide_type),
            pltpu.VMEM((3 * height, units), low_type),
            pltpu.VMEM((2 * group_rows, 256), wide_type),
            pltpu.VMEM((units, height), low_type),
            pltpu.VMEM((local_width, height), low_type),
            dma((15 + size,)),
            dma((1 + PIECES, 8)),
            dma((size - 1,)),
            dma((size - 1,)),
            dma((2, size - 1, PIECES)),
            dma((2, size - 1, PIECES)),
            dma((5, 10)),
            dma((5, 10)),
        ],
        compiler_params=pltpu.CompilerParams(
            collective_id=2, has_side_effects=True, vmem_limit_bytes=VMEM_BYTES
        ),
        cost_estimate=pl.CostEstimate(
            flops=2 * group_rows * model_width * (units + 8 * local_width),
            bytes_accessed=48 << 20,
            transcendentals=group_rows**2 * local_width // 128,
        ),
        name="back",
    )(
        branch_cot,
        grad_attended,
        query_rot.reshape(by_device),
        key_rot.reshape(by_device),
        value_rows.reshape(by_device),
        query_hat.reshape(by_device),
        key_hat.reshape(by_device),
        cosine,
        sine,
        down_near,
        up_near,
        up_early,
        attended,
        attention_full,
        rows_all,
        grad_hidden,
        *small,
    )


def finish_kernel(count, *refs):
    sources, gain, refs = refs[:count], refs[count], refs[count + 1 :]
    targets, head_outs, norm_outs = refs[:count], refs[count : count + 2], refs[count + 2 : count + 4]
    buffers, sem = refs[count + 4 : 2 * count + 4], refs[-1]
    wides = list(refs[2 * count + 4 : -1])
    outgoing = [buffer if buffer.dtype == jnp.float32 else wides.pop(0) for buffer in buffers]
    loads, stores = [], []
    for place, (source, buffer, wider, target) in enumerate(
        zip(sources, buffers, outgoing, targets)
    ):
        rows = source.shape[0] // 2
        for half in range(2):
            span = pl.ds(half * rows, rows)
            here = buffer.at[span, :], wider.at[span, :]
            loads.append(
                pltpu.make_async_copy(source.at[span, :], here[0], sem.at[half, place])
            )
            stores.append(
                (here, pltpu.make_async_copy(here[1], target.at[span, :], sem.at[2 + half, place]))
            )
    for copy in loads[:WINDOW]:
        copy.start()
    heads, channels = head_outs[0].shape
    shift = lax.rem(128 - lax.axis_index("dp") * channels, 128)
    own = pltpu.roll(gain[pl.ds(0, 2 * heads), :], shift, 1)
    lines = norm_outs[0].shape[0]
    for kind in range(2):
        head_outs[kind][...] = own[kind * heads : (kind + 1) * heads, :channels]
        at = 2 * heads + kind * lines
        norm_outs[kind][...] = gain[pl.ds(at, lines), :]
    for place, (load, (here, store)) in enumerate(zip(loads, stores)):
        load.wait()
        if place + WINDOW < len(loads):
            loads[place + WINDOW].start()
        if here[0].dtype != here[1].dtype:
            widen(*here)
        store.start()
    for _, copy in stores:
        copy.wait()


def widen(source, target):
    def step(index):
        span = pl.ds(pl.multiple_of(index * STRIP, STRIP), STRIP)
        target[span, :] = wide(source[span, :])

    each(source.shape[0] // STRIP, step)


def finish(gain_part, head_shape, lines, *arrays):
    anywhere = pl.BlockSpec(memory_space=pl.ANY)
    inside = pl.BlockSpec(memory_space=pltpu.VMEM)
    count = len(arrays)
    return pl.pallas_call(
        functools.partial(finish_kernel, count),
        out_shape=[
            *(jax.ShapeDtypeStruct(array.shape, jnp.float32) for array in arrays),
            *[jax.ShapeDtypeStruct(head_shape, jnp.float32)] * 2,
            *[jax.ShapeDtypeStruct((lines, 128), jnp.float32)] * 2,
        ],
        in_specs=[anywhere] * count + [inside],
        out_specs=[anywhere] * count + [inside] * 4,
        scratch_shapes=[
            *(pltpu.VMEM(array.shape, array.dtype) for array in arrays),
            *(pltpu.VMEM(array.shape, jnp.float32) for array in arrays if array.dtype != jnp.float32),
            pltpu.SemaphoreType.DMA((4, count)),
        ],
        compiler_params=pltpu.CompilerParams(vmem_limit_bytes=VMEM_BYTES),
        name="finish",
    )(*arrays, gain_part)


def local(
    tokens,
    positions,
    cotangent,
    query_weight,
    key_weight,
    value_weight,
    output_weight,
    gate_weight,
    up_weight,
    down_weight,
    query_gain,
    key_gain,
    attention_gain,
    feedforward_gain,
):
    data_size = lax.axis_size("dp")
    data_index = lax.axis_index("dp")
    high_count = data_size // 8
    width = attention_gain.shape[0]
    channels, local_heads = query_gain.shape

    def high_block(low_bits, place):
        return low_bits + 8 * ((data_index // 8) ^ place)

    def grouped(array_in):
        if high_count == 1:
            return array_in
        return jnp.concatenate(
            [
                lax.dynamic_slice_in_dim(array_in, high_block(low_bits, place) * width, width, -1)
                for low_bits in range(8)
                for place in range(high_count)
            ],
            -1,
        )

    def ungrouped(array_in):
        if high_count == 1:
            return array_in
        return jnp.concatenate(
            [
                lax.dynamic_slice_in_dim(
                    array_in,
                    (low_bits * high_count + ((data_index // 8) ^ high_bits)) * width,
                    width,
                    -1,
                )
                for high_bits in range(high_count)
                for low_bits in range(8)
            ],
            -1,
        )

    head_gains = jnp.concatenate([query_gain.T, key_gain.T], 0)
    head_gains = lax.dynamic_update_slice_in_dim(
        jnp.zeros((2 * local_heads, channels * data_size), head_gains.dtype),
        head_gains,
        data_index * channels,
        1,
    )
    for bit in range(3, bits_of(data_size)):
        head_gains = head_gains + swap(head_gains, 1 << bit)
    gain_lines = [
        head_gains,
        gather_high(attention_gain[None], 1).reshape(-1, 128),
        gather_high(feedforward_gain[None], 1).reshape(-1, 128),
    ]
    line_count = sum(lines.shape[0] for lines in gain_lines)
    gain_shard = jnp.pad(jnp.concatenate(gain_lines, 0), ((0, 32 - line_count), (0, 0)))
    (
        rows_all,
        attention_full,
        output_full,
        gate_full,
        attended,
        query_rot,
        key_rot,
        value_rows,
        query_hat,
        key_hat,
        cosine,
        sine,
        stats,
        query_scale,
        key_scale,
        attention_scale,
        feedforward_scale,
    ) = front(
        grouped(tokens),
        gather_high(query_weight, 0),
        gather_high(key_weight, 0),
        gather_high(value_weight, 0),
        gather_high(output_weight, 1),
        gather_high(gate_weight, 0),
        gain_shard,
        positions,
    )
    (
        branch_cot,
        grad_attended,
        block_grouped,
        grad_hidden,
        grad_gate,
        up_near,
        up_early,
        down_near,
        attention_gain_part,
        feedforward_gain_part,
    ) = middle(
        attended,
        rows_all,
        grouped(cotangent),
        attention_scale,
        feedforward_scale,
        output_full,
        gate_full,
        gather_high(up_weight, 0),
        gather_high(down_weight, 1),
    )
    (
        tokens_part,
        grad_up,
        grad_down,
        grad_output,
        grad_query,
        grad_key,
        grad_value,
        gain_part,
    ) = back(
        branch_cot,
        grad_attended,
        query_rot,
        key_rot,
        value_rows,
        query_hat,
        key_hat,
        cosine,
        sine,
        down_near,
        up_near,
        up_early,
        attended,
        attention_full,
        rows_all.reshape(-1, rows_all.shape[-1]),
        grad_hidden,
        stats,
        query_scale,
        key_scale,
        attention_gain_part,
        feedforward_gain_part,
    )
    def own_high(total, axis):
        return total if high_count == 1 else wide(scatter_high(total, axis))

    large = (
        ungrouped(block_grouped),
        ungrouped(tokens_part),
        own_high(grad_query, 0),
        own_high(grad_key, 0),
        own_high(grad_value, 0),
        own_high(grad_output, 1),
        own_high(grad_gate, 0),
        own_high(grad_up, 0),
        own_high(grad_down, 1),
    )
    if high_count == 1:
        *large, query_part, key_part, attention_part, feedforward_part = finish(
            gain_part, query_gain.shape[::-1], width // 128, *large
        )
        return (
            *large,
            query_part.T,
            key_part.T,
            attention_part.reshape(width),
            feedforward_part.reshape(width),
        )
    head_part = gain_part[: 2 * local_heads]
    for bit in range(3, bits_of(data_size)):
        head_part = head_part + swap(head_part, 1 << bit)
    head_part = lax.dynamic_slice_in_dim(head_part, data_index * channels, channels, 1)
    norm_part = gain_part[2 * local_heads : line_count].reshape(2, -1)

    return (
        *large,
        head_part[:local_heads].T,
        head_part[local_heads:].T,
        own_high(norm_part[0], 0),
        own_high(norm_part[1], 0),
    )


def solution(mesh):
    return jax.shard_map(
        local,
        mesh=mesh,
        in_specs=(
            P(("dp", "tensor"), None),
            P("dp"),
            P(("dp", "tensor"), None),
            P("dp", "tensor"),
            P("dp", "tensor"),
            P("dp", "tensor"),
            P("tensor", "dp"),
            P("dp", "tensor"),
            P("dp", "tensor"),
            P("tensor", "dp"),
            P("dp", "tensor"),
            P("dp", "tensor"),
            P("dp"),
            P("dp"),
        ),
        out_specs=(
            P(("dp", "tensor"), None),
            P(("dp", "tensor"), None),
            P("dp", "tensor"),
            P("dp", "tensor"),
            P("dp", "tensor"),
            P("tensor", "dp"),
            P("dp", "tensor"),
            P("dp", "tensor"),
            P("tensor", "dp"),
            P("dp", "tensor"),
            P("dp", "tensor"),
            P("dp"),
            P("dp"),
        ),
        check_vma=False,
    )
```

```python
import functools

import jax
import jax.numpy as jnp
import numpy as np
from jax import lax
from jax.experimental import pallas as pl
from jax.experimental.pallas import tpu as pltpu
from jax.sharding import PartitionSpec as P

EPS = 1e-06
THETA = 500000.0
MASKED = -1e30
VMEM_BYTES = 64 * 1024 * 1024 - 128 * 1024


def norm_backward(grad_in, normalized, inverse_rms, gain_values):
    scaled = grad_in * gain_values
    return inverse_rms * (scaled - normalized * jnp.mean(scaled * normalized, -1, keepdims=True))


def bits_of(size):
    return size.bit_length() - 1


def swap(array_in, mask):
    size = lax.axis_size("dp")
    return lax.ppermute(array_in, "dp", [(index, index ^ mask) for index in range(size)])


def gather_high(shard, axis):
    for bit in range(3, bits_of(lax.axis_size("dp"))):
        shard = jnp.concatenate([shard, swap(shard, 1 << bit)], axis)
    return shard


def scatter_high(total, axis):
    for bit in reversed(range(3, bits_of(lax.axis_size("dp")))):
        kept, sent = jnp.split(total, 2, axis)
        total = low(wide(kept) + wide(swap(low(sent), 1 << bit)))
    return total


def low(array_in):
    return array_in.astype(jnp.bfloat16)


def wide(array_in):
    return array_in.astype(jnp.float32)


def rows_product(left, right):
    return lax.dot_general(
        left, right, (((1,), (1,)), ((), ())), preferred_element_type=jnp.float32
    )


TILE = 256
WIDE_TILE = 512
STRIP = 16
CHUNKS = 2
HALVES = 2
PIECES = 4
WINDOW = 6


def shard_peer(mask):
    index = lax.axis_index("dp")
    return index + mask - 2 * mask * ((index // mask) % 2)


def low_place(mask):
    index = lax.axis_index("dp")
    total = 0
    for bit in (1, 2, 4):
        value = (index // bit) % 2
        total = total + bit * (1 - value if mask & bit else value)
    return total


ROUTE = {1: (1, 1), 2: (2, 2), 3: (1, 1), 4: (4, 4), 5: (1, 1), 6: (4, 2), 7: (1, 1)}
PLACES = {mask: place for place, mask in enumerate((0, 2, 4, 6, 1, 3, 5, 7))}


def column_blocks(width):
    return [
        (
            pl.ds(place * width, width),
            pl.ds(pl.multiple_of(low_place(mask) * width, width), width),
        )
        for mask, place in PLACES.items()
    ]


class ShardGather:
    def __init__(self, own, target, send_sem, recv_sem):
        self.own, self.target, self.send_sem, self.recv_sem = own, target, send_sem, recv_sem

    def copy(self, mask, half):
        route = ROUTE[mask][half]
        before = mask ^ route
        return pltpu.make_async_remote_copy(
            src_ref=self.target(PLACES[before], half) if before else self.own(half),
            dst_ref=self.target(PLACES[mask], half),
            send_sem=self.send_sem.at[mask - 1, half],
            recv_sem=self.recv_sem.at[mask - 1, half],
            device_id={"dp": shard_peer(route)},
            device_id_type=pl.DeviceIdType.MESH,
        )

    def start(self, *masks):
        for half in range(2):
            for mask in masks:
                self.copy(mask, half).start()

    def arrive(self, mask, halves=(0, 1)):
        for half in halves:
            self.copy(mask, half).wait_recv()
            for after, route in ROUTE.items():
                if after != mask and after ^ route[half] == mask:
                    self.copy(after, half).start()

    def sent(self):
        for mask in ROUTE:
            for half in range(2):
                self.copy(mask, half).wait_send()


def row_halves(buffer, height):
    def target(place, half):
        return buffer.at[pl.ds(place * height + half * (height // 2), height // 2), :]

    return target


def column_halves(buffer, width):
    height = buffer.shape[0] // 2

    def target(place, half):
        return buffer.at[pl.ds(half * height, height), pl.ds(place * width, width)]

    return target


def own_halves(shard):
    height = shard.shape[0] // 2
    return lambda half: shard.at[pl.ds(half * height, height), :]


def greet(line_devices):
    barrier = pltpu.get_barrier_semaphore()
    for mask in (1, 2, 4):
        pl.semaphore_signal(
            barrier,
            inc=1,
            device_id={"dp": shard_peer(mask)},
            device_id_type=pl.DeviceIdType.MESH,
        )
    for there, index in line_devices:

        @pl.when(there)
        def _():
            pl.semaphore_signal(
                barrier,
                inc=1,
                device_id={"tensor": index},
                device_id_type=pl.DeviceIdType.MESH,
            )


def turned_rows(row):
    return jnp.broadcast_to(row, (128, row.shape[1])).T


def column_sums(values):
    total = values[:, :128]
    for first in range(128, values.shape[1], 128):
        total = total + values[:, first : first + 128]
    return jnp.sum(total.T, 0, keepdims=True)


def ahead_of(values, first_key, first_query):
    key = first_key + lax.broadcasted_iota(jnp.int32, values.shape, 0)
    query = first_query + lax.broadcasted_iota(jnp.int32, values.shape, 1)
    return key > query


def head_span(head):
    return pl.ds(pl.multiple_of(head * 128, 128), 128)


def each(count, body):
    def step(index, carry):
        body(index)
        return carry

    lax.fori_loop(0, count, step, 0)


def front_kernel(
    size,
    tokens_hbm,
    query_hbm,
    key_hbm,
    value_hbm,
    output_hbm,
    gate_hbm,
    gain_hbm,
    positions,
    frequency,
    rows_out,
    attention_out,
    output_out,
    gate_out,
    attended_out,
    query_rot_out,
    key_rot_out,
    value_out,
    query_hat_out,
    key_hat_out,
    cosine_out,
    sine_out,
    stats,
    query_scale,
    key_scale,
    attention_scale,
    feedforward_scale,
    rows,
    weight,
    projected,
    gain,
    cosine,
    sine,
    squares,
    query_rot,
    key_rot,
    value,
    query_hat,
    key_hat,
    attended,
    load_sem,
    store_sem,
    hand_send,
    hand_recv,
    shard_send,
    shard_recv,
    square_send,
    square_recv,
):
    me = lax.axis_index("tensor")
    last = size - 1
    own_rows, model_width = rows.shape[1:]
    piece_rows = own_rows // PIECES
    local_width = query_hbm.shape[1]
    heads = local_width // 128
    everyone = True
    greet([(everyone, lax.rem(me + offset, size)) for offset in range(1, size)])
    block = model_width // 8
    token_loads = [
        pltpu.make_async_copy(
            tokens_hbm.at[:, natural], rows.at[me, :, here], load_sem.at[0, place]
        )
        for place, (here, natural) in enumerate(column_blocks(block))
    ]
    shard_rows = pl.ds(0, query_hbm.shape[0])
    loads = [
        pltpu.make_async_copy(source, target, load_sem.at[1, place])
        for place, (source, target) in enumerate(
            (
                (query_hbm, weight.at[shard_rows, pl.ds(0, local_width)]),
                (key_hbm, weight.at[shard_rows, pl.ds(local_width, local_width)]),
                (value_hbm, weight.at[shard_rows, pl.ds(2 * local_width, local_width)]),
                (gain_hbm, gain.at[pl.ds(0, gain_hbm.shape[0]), :]),
                (output_hbm, output_out.at[:, pl.ds(0, output_hbm.shape[1])]),
                (gate_hbm, gate_out.at[pl.ds(0, gate_hbm.shape[0]), :]),
            )
        )
    ]
    for copy in token_loads + loads:
        copy.start()
    attention_target = row_halves(weight, query_hbm.shape[0])
    attention_flow, output_flow, gate_flow, gain_flow = (
        ShardGather(own, target, shard_send.at[kind], shard_recv.at[kind])
        for kind, (own, target) in enumerate(
            (
                (functools.partial(attention_target, 0), attention_target),
                (own_halves(output_hbm), column_halves(output_out, output_hbm.shape[1])),
                (own_halves(gate_hbm), row_halves(gate_out, gate_hbm.shape[0])),
                (own_halves(gain_hbm), row_halves(gain, gain_hbm.shape[0])),
            )
        )
    )
    pl.semaphore_wait(pltpu.get_barrier_semaphore(), 3 + size - 1)

    def away(way):
        return me if way == 0 else last - me

    def hand_copy(hop, piece, way, origin):
        here = rows.at[origin, pl.ds(piece * piece_rows, piece_rows)]
        return pltpu.make_async_remote_copy(
            src_ref=here,
            dst_ref=here,
            send_sem=hand_send.at[way, hop - 1, piece],
            recv_sem=hand_recv.at[way, hop - 1, piece],
            device_id={"tensor": me + 1 - 2 * way},
            device_id_type=pl.DeviceIdType.MESH,
        )

    for copy in token_loads:
        copy.wait()
    for piece in range(PIECES):
        for way in range(2):

            @pl.when(away(1 - way) >= 1)
            def _():
                hand_copy(1, piece, way, me).start()

        if piece == 0:
            for copy in loads[:3]:
                copy.wait()
            attention_flow.start(2, 4, 1)
            gain_flow.start(2, 4, 1)

    def hand_on(hop, piece):
        for way in range(2):

            @pl.when(away(way) >= hop)
            def _():
                origin = me - hop if way == 0 else me + hop
                hand_copy(hop, piece, way, origin).wait_recv()
                if hop < size - 1:

                    @pl.when(away(1 - way) >= 1)
                    def _():
                        hand_copy(hop + 1, piece, way, origin).start()

    def row_store(origin):
        return pltpu.make_async_copy(rows.at[origin], rows_out.at[origin], store_sem.at[0, origin])

    whole_stores = [
        pltpu.make_async_copy(source, target, store_sem.at[1 + place // size, place % size])
        for place, (source, target) in enumerate(
            (
                (weight, attention_out),
                (cosine, cosine_out),
                (sine, sine_out),
                (query_hat, query_hat_out),
                (key_hat, key_hat_out),
                (query_rot, query_rot_out),
                (key_rot, key_rot_out),
                (value, value_out),
                (attended, attended_out),
            )
        )
    ]

    def span_of(origin):
        return pl.ds(pl.multiple_of(origin * own_rows, own_rows), own_rows)

    def square_copy(offset, origin):
        return pltpu.make_async_remote_copy(
            src_ref=squares.at[me, origin],
            dst_ref=squares.at[me, origin],
            send_sem=square_send.at[offset - 1, origin],
            recv_sem=square_recv.at[offset - 1, origin],
            device_id={"tensor": lax.rem(me + offset, size)},
            device_id_type=pl.DeviceIdType.MESH,
        )

    def project(origin):
        def step(index):
            columns = pl.ds(pl.multiple_of(index * WIDE_TILE, WIDE_TILE), WIDE_TILE)
            projected[origin, :, columns] = jnp.dot(
                rows[origin], weight[:, columns], preferred_element_type=jnp.float32
            )

        row_store(origin).start()
        each(weight.shape[1] // WIDE_TILE, step)
        queries = projected[origin, :, pl.ds(0, local_width)]
        keys = projected[origin, :, pl.ds(local_width, local_width)]
        squares[me, origin, pl.ds(0, 8), :] = jnp.concatenate(
            [
                column_sums(queries * queries),
                column_sums(keys * keys),
                jnp.zeros((6, own_rows), jnp.float32),
            ],
            0,
        )
        for offset in range(1, size):
            square_copy(offset, origin).start()

    def project_from(hop, way):
        @pl.when(away(way) >= hop)
        def _():
            project(me - hop if way == 0 else me + hop)

    def normalize(origin):
        for offset in range(1, size):
            square_copy(offset, origin).wait_recv()
        total = squares[0, origin]
        for device in range(1, size):
            total = total + squares[device, origin]
        inverse = lax.rsqrt(total / model_width + EPS)
        here = span_of(origin)
        stats[pl.ds(heads, 2), here] = inverse[:2]
        for kind, (hat, rot, scale) in enumerate(
            ((query_hat, query_rot, query_scale), (key_hat, key_rot, key_scale))
        ):
            column = turned_rows(inverse[kind : kind + 1])

            def step(head):
                span = head_span(head)
                source = head_span(head + kind * heads)
                normalized = projected[origin, :, source] * column
                hat[here, span] = low(normalized)
                scaled = normalized * scale[pl.ds(head, 1), :]
                rot[here, span] = low(
                    scaled * cosine[here, :] + pltpu.roll(scaled, 64, 1) * sine[here, :]
                )

            each(heads, step)
        value[here, :] = low(projected[origin, :, pl.ds(2 * local_width, local_width)])

    def tables():
        for origin in range(size):
            here = pl.ds(origin * own_rows, own_rows)
            angles = turned_rows(wide(positions[:, here])) * frequency[...]
            cosine[here, :] = jnp.cos(angles)
            lane = lax.broadcasted_iota(jnp.int32, angles.shape, 1)
            sine[here, :] = jnp.where(lane < 64, -1.0, 1.0) * jnp.sin(angles)

    def scales():
        for kind, scale in enumerate((query_scale, key_scale)):
            total = wide(gain[pl.ds(0, 16), :])
            for place in range(1, 8):
                total = total + wide(gain[pl.ds(place * gain_hbm.shape[0], 16), :])
            scale[...] = jnp.concatenate(
                [total[kind * heads : (kind + 1) * heads], jnp.zeros((8 - heads, 128), jnp.float32)],
                0,
            )
        for place in range(8):
            lines = wide(gain[pl.ds(place * gain_hbm.shape[0], 16), :])
            for kind, scale in enumerate((attention_scale, feedforward_scale)):
                for line in range(block // 128):
                    at = 2 * heads + kind * (block // 128) + line
                    scale[:, pl.ds(place * block + line * 128, 128)] = lines[at : at + 1]

    def attend(head):
        span = head_span(head)
        for origin in range(size):
            count = (origin + 1) * own_rows
            here = pl.ds(origin * own_rows, own_rows)
            scores = rows_product(key_rot[pl.ds(0, count), span], query_rot[here, span])
            scores = scores * (128**-0.5)
            near = scores[origin * own_rows :]
            near = jnp.where(ahead_of(near, 0, 0), MASKED, near)
            scores = jnp.concatenate([scores[: origin * own_rows], near], 0) if origin else near
            row_max = jnp.max(scores, 0, keepdims=True)
            exponent = jnp.exp(scores - row_max)
            row_total = jnp.sum(exponent, 0, keepdims=True)
            result = jnp.dot(
                value[pl.ds(0, count), span].T, low(exponent), preferred_element_type=jnp.float32
            )
            attended[here, span] = low((result * (1.0 / row_total)).T)
            stats[pl.ds(head, 1), here] = row_max + jnp.log(row_total)

    def turns(beat):
        if beat == 1:
            tables()
            for copy in whole_stores[1:3]:
                copy.start()
        elif beat == 2:
            attention_flow.arrive(2, (0,))
            attention_flow.arrive(4, (0,))
        elif beat == 3:
            attention_flow.arrive(2, (1,))
            attention_flow.arrive(4, (1,))
            output_flow.start(2, 4, 1)
            gain_flow.arrive(2)
            gain_flow.arrive(4)
        elif beat == 5:
            attention_flow.arrive(6)
            gate_flow.start(2, 4, 1)
            gain_flow.arrive(6)
        elif beat == 6:
            output_flow.arrive(2)
            output_flow.arrive(4)
            for mask in (1, 3, 5, 7):
                attention_flow.arrive(mask)
            whole_stores[0].start()
            project(me)
        elif beat == 7:
            project_from(1, 0)
        elif beat == 8:
            project_from(1, 1)
            output_flow.arrive(6)
            loads[3].wait()
            for mask in (1, 3, 5, 7):
                gain_flow.arrive(mask)
            scales()
        elif beat == 9:
            gate_flow.arrive(2, (0,))
            gate_flow.arrive(4, (0,))
        elif beat == 10:
            project_from(2, 0)
        elif beat == 11:
            project_from(2, 1)
            gate_flow.arrive(2, (1,))
            gate_flow.arrive(4, (1,))

    for beat in range(1, (size - 1) * PIECES + 1):
        if beat == (size - 1) * PIECES:
            for origin in range(1, last):
                normalize(origin)
        hand_on((beat - 1) // PIECES + 1, (beat - 1) % PIECES)
        turns(beat)
    project_from(3, 0)
    project_from(3, 1)
    gate_flow.arrive(6)
    for origin in (0, last):
        normalize(origin)
    for copy in whole_stores[3:8]:
        copy.start()
    def attend_pair(index):
        attend(2 * index)
        attend(2 * index + 1)

    each(heads // 2, attend_pair)
    whole_stores[8].start()
    for flow in (output_flow, gate_flow):
        for mask in (1, 3, 5, 7):
            flow.arrive(mask)
    for hop in range(1, size):
        for way in range(2):

            @pl.when(jnp.logical_and(away(way) >= hop - 1, away(1 - way) >= 1))
            def _():
                for piece in range(PIECES):
                    hand_copy(hop, piece, way, 0).wait_send()

    for flow in (attention_flow, output_flow, gate_flow, gain_flow):
        flow.sent()
    for offset in range(1, size):
        for origin in range(size):
            square_copy(offset, origin).wait_send()
    for copy in loads[4:]:
        copy.wait()
    for origin in range(size):
        row_store(origin).wait()
    for copy in whole_stores:
        copy.wait()


def front(
    tokens_grouped,
    query_shard,
    key_shard,
    value_shard,
    output_shard,
    gate_shard,
    gain_shard,
    positions,
):
    size = lax.axis_size("tensor")
    own_rows, model_width = tokens_grouped.shape
    local_width = query_shard.shape[1]
    group_rows = size * own_rows
    low_type, wide_type = jnp.bfloat16, jnp.float32
    anywhere = pl.BlockSpec(memory_space=pl.ANY)
    inside = pl.BlockSpec(memory_space=pltpu.VMEM)
    dma = pltpu.SemaphoreType.DMA
    hands = (2, size - 1, PIECES)
    half_head = np.arange(128, dtype=np.float32) % 64
    frequency = (np.float32(THETA) ** (-(half_head * np.float32(2.0 / 128))))[None]

    def shape(dims, kind=low_type):
        return jax.ShapeDtypeStruct(dims, kind)

    local_rows = (group_rows, local_width)
    tables = (group_rows, 128)
    return pl.pallas_call(
        functools.partial(front_kernel, size),
        out_shape=[
            shape((size, own_rows, model_width)),
            shape((model_width, 3 * local_width)),
            shape((output_shard.shape[0], model_width)),
            shape((model_width, gate_shard.shape[1])),
            *[shape(local_rows)] * 6,
            *[shape(tables, wide_type)] * 2,
            shape((8, group_rows), wide_type),
            *[shape((8, 128), wide_type)] * 2,
            *[shape((1, model_width), wide_type)] * 2,
        ],
        in_specs=[anywhere] * 7 + [inside] * 2,
        out_specs=[anywhere] * 12 + [inside] * 5,
        scratch_shapes=[
            pltpu.VMEM((size, own_rows, model_width), low_type),
            pltpu.VMEM((model_width, 3 * local_width), low_type),
            pltpu.VMEM((size, own_rows, 3 * local_width), wide_type),
            pltpu.VMEM((8 * gain_shard.shape[0], gain_shard.shape[1]), low_type),
            pltpu.VMEM(tables, wide_type),
            pltpu.VMEM(tables, wide_type),
            pltpu.VMEM((size, size, 8, own_rows), wide_type),
            *[pltpu.VMEM(local_rows, low_type)] * 6,
            dma((2, 8)),
            dma((4, size)),
            dma(hands),
            dma(hands),
            dma((4, 7, 2)),
            dma((4, 7, 2)),
            dma((size - 1, size)),
            dma((size - 1, size)),
        ],
        compiler_params=pltpu.CompilerParams(
            collective_id=0, has_side_effects=True, vmem_limit_bytes=VMEM_BYTES
        ),
        cost_estimate=pl.CostEstimate(
            flops=6 * group_rows * model_width * local_width,
            bytes_accessed=32 << 20,
            transcendentals=0,
        ),
        name="front",
    )(
        tokens_grouped,
        query_shard,
        key_shard,
        value_shard,
        output_shard,
        gate_shard,
        gain_shard,
        positions.reshape(1, group_rows),
        frequency,
    )


class ShardSum:
    def __init__(self, near, far, corner, final, send_sem, recv_sem, core_only=False, deferred=False, own=None, awaited=None):
        self.near, self.far, self.corner, self.final = near, far, corner, final
        self.core_only, self.deferred = core_only, deferred
        self.own = own or functools.partial(near, 0)
        self.awaited = awaited or ((0, 0), (0, 1), (1, 0), (1, 1))
        self.send_sem, self.recv_sem = send_sem, recv_sem

    def remote(self, source, target, place, route):
        return pltpu.make_async_remote_copy(
            src_ref=source,
            dst_ref=target,
            send_sem=self.send_sem.at[place],
            recv_sem=self.recv_sem.at[place],
            device_id={"dp": shard_peer(route)},
            device_id_type=pl.DeviceIdType.MESH,
        )

    def core_copy(self, place):
        return self.remote(self.far(place), self.near(place), place, 1)

    def corner_copy(self, half):
        return self.remote(self.near(3, half), self.corner(half), 4 + half, (4, 2)[half])

    def final_copy(self, way, half):
        return self.remote(
            self.near(1 + way, half), self.final(way, half), 6 + 2 * way + half, (2, 4)[way]
        )

    def far_terms(self, term, place, count=1):
        term(4 + place, self.far(place, None, count), False, count)
        for index in reversed(range(place, place + count)):
            self.core_copy(index).start()

    def near_terms(self, term, place, count=1):
        for index in range(place, place + count):
            self.core_copy(index).wait_recv()
        term(place, self.near(place, None, count), True, count)
        if not self.core_only:
            for index in range(place, place + count):
                self.near_ready(index)

    def near_ready(self, place):
        if place == 3:
            for half in range(2):
                self.corner_copy(half).start()
        elif place:
            self.final_copy(place - 1, 2 - place).start()

    def first_terms(self, term):
        self.far_terms(term, 3)
        self.far_terms(term, 2)
        self.near_terms(term, 3)

    def other_terms(self, term):
        self.far_terms(term, 0, 2)
        self.near_terms(term, 2)
        self.near_terms(term, 0, 2)

    def take_corner(self):
        for half in range(2):
            self.corner_copy(half).wait_recv()
            add_into(self.near(1 + half, half), self.corner(half))
            if not self.deferred:
                self.final_copy(half, half).start()

    def final_arrived(self, half):
        for way in range(2):
            if (way, half) in self.awaited:
                self.final_copy(way, half).wait_recv()

    def take_final(self):
        for half in range(2):
            self.final_arrived(half)
            add_into(self.own(half), self.final(0, half), self.final(1, half))

    def take_final_turned(self, out):
        for half in range(2):
            self.final_arrived(half)
            own, first, second = self.own(half), self.final(0, half), self.final(1, half)
            rows = own.shape[0]

            def step(index):
                span = pl.ds(pl.multiple_of(index * TILE, TILE), TILE)
                value = wide(own[:, span]) + wide(first[:, span]) + wide(second[:, span])
                out[span, pl.ds(half * rows, rows)] = low(value.T)

            each(own.shape[1] // TILE, step)

    def sent(self, core=True):
        for place in range(4) if core else ():
            self.core_copy(place).wait_send()
        for half in range(2):
            self.corner_copy(half).wait_send()
            for way in range(2):
                if way != half or not self.deferred:
                    self.final_copy(way, half).wait_send()


def add_into(target, *sources):
    def step(index):
        span = pl.ds(pl.multiple_of(index * STRIP, STRIP), STRIP)
        total = wide(target[span, :])
        for source in sources:
            total = total + wide(source[span, :])
        target[span, :] = total.astype(target.dtype)

    each(target.shape[0] // STRIP, step)


def product_term(left, right):
    def term(place, target, adds, count=1):
        height, width = target.shape
        tile = 1024 if width % 1024 == 0 and count == 1 else 512
        turned = left(place * (height // count), height).T

        def step(index, carry):
            columns = pl.ds(pl.multiple_of(index * tile, tile), tile)
            value = jnp.dot(turned, right(columns, tile), preferred_element_type=jnp.float32)
            if adds:
                value = value + wide(target[:, columns])
            target[:, columns] = value.astype(target.dtype)
            return carry

        lax.fori_loop(0, target.shape[1] // tile, step, 0)

    return term


def stacked(buffer, first, height):
    def view(place, half=None, count=1):
        at = first + place * height
        if half is None:
            return buffer.at[pl.ds(at, count * height), :]
        return buffer.at[pl.ds(at + half * (height // 2), height // 2), :]

    return view


def middle_kernel(size, *refs):
    (
        attended_hbm,
        rows_hbm,
        cotangent_hbm,
        attention_scale,
        feedforward_scale,
        output_hbm,
        gate_hbm,
        up_hbm,
        down_hbm,
        mlp_out,
        inner_out,
        mixed_cot_out,
        branch_cot_out,
        grad_attended_out,
        block_out,
        grad_hidden_out,
        gate_grad_out,
        up_near_out,
        up_early_out,
        down_near_out,
        attention_gain_out,
        feedforward_gain_out,
        attended,
        tokens,
        cotangent,
        output_weight,
        gate_weight,
        up_weight,
        down_weight,
        everyone,
        gate_act,
        up_act,
        inner,
        hidden,
        branch,
        arrived,
        partial,
        total,
        load_sem,
        store_sem,
        sum_send,
        sum_recv,
        hand_send,
        hand_recv,
        shard_send,
        shard_recv,
        grad_send,
        grad_recv,
        again_sem,
        shuffle_sem,
        free_sem,
    ) = refs
    me = lax.axis_index("tensor")
    last = size - 1
    chunk_rows, model_width = tokens.shape[1], tokens.shape[2]
    units = gate_weight.shape[1]
    half_rows = chunk_rows // HALVES
    all_rows = size * chunk_rows

    greet(((me < last, me + 1), (me > 0, me - 1)))
    first_loads = [
        pltpu.make_async_copy(source, target, load_sem.at[place])
        for place, (source, target) in enumerate(
            (
                (attended_hbm, attended),
                (output_hbm, output_weight),
                (rows_hbm.at[me], tokens),
                (gate_hbm, gate_weight),
                (up_hbm, up_weight.at[pl.ds(0, up_hbm.shape[0]), :]),
                (down_hbm, down_weight.at[:, pl.ds(0, down_hbm.shape[1])]),
            )
        )
    ]
    first_loads += [
        pltpu.make_async_copy(
            cotangent_hbm.at[pl.ds(chunk * chunk_rows, chunk_rows), natural],
            cotangent.at[chunk, :, here],
            shuffle_sem.at[chunk, place],
        )
        for chunk in range(CHUNKS)
        for place, (here, natural) in enumerate(column_blocks(model_width // 8))
    ]
    for copy in first_loads[:2]:
        copy.start()
    up_flow = ShardGather(
        own_halves(up_hbm),
        row_halves(up_weight, up_hbm.shape[0]),
        shard_send.at[0],
        shard_recv.at[0],
    )
    down_flow = ShardGather(
        own_halves(down_hbm),
        column_halves(down_weight, down_hbm.shape[1]),
        shard_send.at[1],
        shard_recv.at[1],
    )
    pl.semaphore_wait(
        pltpu.get_barrier_semaphore(), 3 + jnp.minimum(me, 1) + jnp.minimum(last - me, 1)
    )
    up_flow.start(2, 4, 1)
    down_flow.start(1)

    height = model_width // 8
    again = [
        pltpu.make_async_copy(
            mlp_out.at[chunk, origin],
            down_weight.at[pl.ds((chunk * size + origin) * chunk_rows, chunk_rows), :],
            again_sem.at[chunk, origin],
        )
        for chunk in range(CHUNKS)
        for origin in range(size)
    ]
    gate_grads, up_grads = (
        ShardSum(
            stacked(buffer, 0, height),
            stacked(down_weight, 4 * height, height),
            functools.partial(stacked(buffer, 4 * height, height), 0),
            stacked(buffer, 5 * height, height),
            grad_send.at[kind],
            grad_recv.at[kind],
            deferred=kind == 1,
        )
        for kind, buffer in enumerate((gate_weight, up_weight))
    )

    down_grads = ShardSum(
        lambda place, half=None, count=1: up_act.at[
            place // 2, pl.ds(place % 2 * height, count * height), :
        ],
        stacked(down_weight, 4 * height, height),
        None,
        None,
        grad_send.at[2],
        grad_recv.at[2],
        core_only=True,
    )
    down_again = [
        pltpu.make_async_copy(
            mixed_cot_out.at[chunk, origin],
            down_weight.at[pl.ds((chunk * size + origin) * chunk_rows, chunk_rows), :],
            again_sem.at[chunk, origin],
        )
        for chunk in range(CHUNKS)
        for origin in range(size)
    ] + [
        pltpu.make_async_copy(inner_out.at[chunk], gate_act.at[chunk], again_sem.at[chunk, size])
        for chunk in range(CHUNKS)
    ]

    def signal_free(place, mask):
        pl.semaphore_signal(
            free_sem.at[place],
            inc=1,
            device_id={"dp": shard_peer(mask)},
            device_id_type=pl.DeviceIdType.MESH,
        )

    def rows_again(first, shard_width):
        return down_weight[pl.ds(0, CHUNKS * all_rows), pl.ds(first, shard_width)]

    def grad_term(act):
        def columns_of(columns, tile):
            return act[:, :, columns].reshape(CHUNKS * all_rows, tile)

        return product_term(rows_again, columns_of)

    def weights_free():
        for place, mask in enumerate((1, 2, 4)):
            signal_free(place, mask)

    def near_store(chunk):
        return pltpu.make_async_copy(
            up_act.at[chunk],
            down_near_out.at[pl.ds(chunk * all_rows, all_rows), :],
            again_sem.at[chunk, 0],
        )

    gate_store = pltpu.make_async_copy(
        gate_weight.at[pl.ds(0, height), :], gate_grad_out, store_sem.at[6, 0]
    )
    up_stores = [
        pltpu.make_async_copy(up_weight.at[pl.ds(first, count), :], target, store_sem.at[7, place])
        for place, (first, count, target) in enumerate(
            (
                (0, 3 * height, up_near_out),
                (5 * height + height // 2, height, up_early_out),
            )
        )
    ]

    def grad_turns(tick, half):
        gate_term, up_term = grad_term(gate_act), grad_term(up_act)
        if (tick, half) == (21, 0):
            for copy in again:
                copy.wait()
            for place in range(3):
                pl.semaphore_wait(free_sem.at[place], 1)
            gate_grads.first_terms(gate_term)
        elif (tick, half) == (21, 1):
            gate_grads.far_terms(gate_term, 0, 2)
            gate_grads.near_terms(gate_term, 2)
        elif (tick, half) == (22, 0):
            gate_grads.near_terms(gate_term, 0, 2)
        elif (tick, half) == (22, 1):
            for place in range(4):
                gate_grads.core_copy(place).wait_send()
            up_grads.far_terms(up_term, 3)
            up_grads.far_terms(up_term, 2)
        elif (tick, half) == (23, 0):
            gate_grads.take_corner()
            up_grads.near_terms(up_term, 3)
            up_grads.far_terms(up_term, 0, 2)
        elif (tick, half) == (23, 1):
            up_grads.near_terms(up_term, 2)
            up_grads.near_terms(up_term, 0, 2)
            signal_free(3, 1)
            for copy in down_again:
                copy.start()
        elif (tick, half) == (24, 1):
            for copy in down_again:
                copy.wait()
            for place in range(4):
                up_grads.core_copy(place).wait_send()
            pl.semaphore_wait(free_sem.at[3], 1)
            down_grads.far_terms(gate_term, 2, 2)
        elif (tick, half) == (25, 0):
            down_grads.far_terms(gate_term, 0, 2)
        elif (tick, half) == (25, 1):
            down_grads.near_terms(gate_term, 2, 2)
            near_store(1).start()
        elif (tick, half) == (26, 0):
            up_grads.take_corner()
            up_stores[0].start()
        elif (tick, half) == (26, 1):
            down_grads.near_terms(gate_term, 0, 2)
            near_store(0).start()
            gate_grads.take_final()
            gate_store.start()

    def turns(tick, half):
        if (tick, half) == (2, 1):
            up_flow.arrive(2, (0,))
            up_flow.arrive(4, (0,))
        elif (tick, half) == (3, 0):
            up_flow.arrive(2, (1,))
            up_flow.arrive(4, (1,))
            down_flow.start(2, 4)
        elif (tick, half) == (4, 1):
            up_flow.arrive(6)
        elif (tick, half) == (5, 0):
            down_flow.arrive(2, (0,))
            down_flow.arrive(4, (0,))
        elif (tick, half) == (6, 0):
            down_flow.arrive(2, (1,))
            down_flow.arrive(4, (1,))
        elif (tick, half) == (7, 0):
            down_flow.arrive(6)

    attention_gain_out[...] = jnp.zeros_like(attention_gain_out)
    feedforward_gain_out[...] = jnp.zeros_like(feedforward_gain_out)

    def half_span(half):
        return pl.ds(half * half_rows, half_rows)

    def strips(half, body):
        def step(index, carry):
            body(
                pl.ds(pl.multiple_of(half * half_rows + index * STRIP, STRIP), STRIP),
                pl.ds(pl.multiple_of(index * STRIP, STRIP), STRIP),
            )
            return carry

        lax.fori_loop(0, half_rows // STRIP, step, 0)

    def sum_copy(chunk, step, half, way, dest):
        return pltpu.make_async_remote_copy(
            src_ref=partial.at[chunk, dest, half_span(half)],
            dst_ref=arrived.at[way, chunk, step - 1, half_span(half)],
            send_sem=sum_send.at[way, chunk, step - 1, half],
            recv_sem=sum_recv.at[way, chunk, step - 1, half],
            device_id={"tensor": me + 1 - 2 * way},
            device_id_type=pl.DeviceIdType.MESH,
        )

    def hand_copy(chunk, hop, half, way, origin):
        rows = everyone.at[origin, chunk, half_span(half)]
        return pltpu.make_async_remote_copy(
            src_ref=rows,
            dst_ref=rows,
            send_sem=hand_send.at[way, chunk, hop - 1, half],
            recv_sem=hand_recv.at[way, chunk, hop - 1, half],
            device_id={"tensor": me + 1 - 2 * way},
            device_id_type=pl.DeviceIdType.MESH,
        )

    def away(way):
        return me if way == 0 else last - me

    def sum_step(chunk, step, half):
        for way in range(2):
            distance = away(way)

            @pl.when(distance <= step - 1)
            def _():
                dest = me + size - step if way == 0 else me - size + step
                if step > 1:

                    @pl.when(distance >= 1)
                    def _():
                        sum_copy(chunk, step - 1, half, way, dest).wait_recv()

                        def add(rows, _):
                            partial[chunk, dest, rows] = low(
                                wide(partial[chunk, dest, rows])
                                + wide(arrived[way, chunk, step - 2, rows])
                            )

                        strips(half, add)

                sum_copy(chunk, step, half, way, dest).start()

    def sum_end(chunk, half):
        def begin(rows, here):
            total[here] = wide(partial[chunk, me, rows])

        strips(half, begin)
        for way in range(2):

            @pl.when(away(way) >= 1)
            def _():
                sum_copy(chunk, size - 1, half, way, me).wait_recv()

                def add(rows, here):
                    total[here] = total[here] + wide(arrived[way, chunk, size - 2, rows])

                strips(half, add)

    def sum_sent(chunk):
        for step in range(1, size):
            for way in range(2):

                @pl.when(away(way) <= step - 1)
                def _():
                    for half in range(HALVES):
                        sum_copy(chunk, step, half, way, 0).wait_send()

    def hand_first(chunk, half):
        for way in range(2):

            @pl.when(away(1 - way) >= 1)
            def _():
                hand_copy(chunk, 1, half, way, me).start()

    def hand_on(chunk, hop, half):
        for way in range(2):

            @pl.when(away(way) >= hop)
            def _():
                origin = me - hop if way == 0 else me + hop
                hand_copy(chunk, hop, half, way, origin).wait_recv()
                if hop < size - 1:

                    @pl.when(away(1 - way) >= 1)
                    def _():
                        hand_copy(chunk, hop + 1, half, way, origin).start()

    def hand_sent(chunk):
        for hop in range(1, size):
            for way in range(2):

                @pl.when(jnp.logical_and(away(way) >= hop - 1, away(1 - way) >= 1))
                def _():
                    for half in range(HALVES):
                        hand_copy(chunk, hop, half, way, 0).wait_send()

    def inverse_rms(values):
        return lax.rsqrt(jnp.mean(values * values, -1, keepdims=True) + EPS)

    def fold(values):
        return values[:8] + values[8:]

    def own_rows(chunk, stage, half):
        def after_branch(rows, here):
            value = total[here]
            branch[chunk, rows] = value
            state = wide(tokens[chunk, rows]) + value * inverse_rms(value) * attention_scale[...]
            hidden[chunk, rows] = state
            everyone[me, chunk, rows] = low(state)

        def after_mixed(rows, here):
            value = total[here]
            inverse = inverse_rms(value)
            normalized = value * inverse
            hidden[chunk, rows] = hidden[chunk, rows] + normalized * feedforward_scale[...]
            grad = wide(cotangent[chunk, rows])
            feedforward_gain_out[...] += fold(grad * normalized)
            everyone[me, chunk, rows] = low(
                norm_backward(grad, normalized, inverse, feedforward_scale[...])
            )

        def after_gradient(rows, here):
            grad = total[here] + wide(cotangent[chunk, rows])
            value = branch[chunk, rows]
            inverse = inverse_rms(value)
            normalized = value * inverse
            branch[chunk, rows] = grad
            attention_gain_out[...] += fold(grad * normalized)
            everyone[me, chunk, rows] = low(
                norm_backward(grad, normalized, inverse, attention_scale[...])
            )

        strips(half, (after_branch, after_mixed, after_gradient)[stage])

    def gathered(chunk):
        return everyone[:, chunk].reshape(all_rows, model_width)

    def tiles(first, end, body):
        def step(index, carry):
            body(pl.ds(pl.multiple_of(index * WIDE_TILE, WIDE_TILE), WIDE_TILE))
            return carry

        lax.fori_loop(first, end, step, 0)

    def store(kind, chunk):
        source, target = (
            (everyone.at[:, chunk], mlp_out.at[chunk]),
            (inner, inner_out.at[chunk]),
            (everyone.at[:, chunk], mixed_cot_out.at[chunk]),
            (everyone.at[:, chunk], branch_cot_out.at[:, chunk]),
            (attended.at[:, chunk], grad_attended_out.at[:, chunk]),
            (branch.at[chunk], grad_hidden_out.at[chunk]),
        )[kind]
        return pltpu.make_async_copy(source, target, store_sem.at[kind, chunk])

    def block_stores(chunk):
        return [
            pltpu.make_async_copy(
                hidden.at[chunk, :, here],
                block_out.at[pl.ds(chunk * chunk_rows, chunk_rows), natural],
                shuffle_sem.at[chunk, place],
            )
            for place, (here, natural) in enumerate(column_blocks(model_width // 8))
        ]

    def put_partial(chunk, columns, values):
        partial[chunk, :, :, columns] = low(values).reshape(size, chunk_rows, WIDE_TILE)

    def branch_terms(chunk):
        def tile(columns):
            rows = attended[:, chunk].reshape(all_rows, attended.shape[-1])
            put_partial(
                chunk,
                columns,
                jnp.dot(rows, output_weight[:, columns], preferred_element_type=jnp.float32),
            )

        tiles(0, model_width // WIDE_TILE, tile)

    def gate_tile(chunk):
        def tile(columns):
            rows = gathered(chunk)
            gate = jnp.dot(rows, gate_weight[:, columns], preferred_element_type=jnp.float32)
            up = jnp.dot(rows, up_weight[:, columns], preferred_element_type=jnp.float32)
            gate_act[chunk, :, columns] = low(gate)
            up_act[chunk, :, columns] = low(up)
            inner[:, columns] = low(gate * jax.nn.sigmoid(gate) * up)

        return tile

    def down_tile(chunk):
        def tile(columns):
            put_partial(
                chunk,
                columns,
                jnp.dot(inner[...], down_weight[:, columns], preferred_element_type=jnp.float32),
            )

        return tile

    def grad_inner_tile(chunk):
        def tile(columns):
            grad = rows_product(gathered(chunk), down_weight[columns, :])
            gate = wide(gate_act[chunk, :, columns])
            up = wide(up_act[chunk, :, columns])
            sigmoid = jax.nn.sigmoid(gate)
            gate_act[chunk, :, columns] = low(
                grad * up * sigmoid * (1.0 + gate * (1.0 - sigmoid))
            )
            up_act[chunk, :, columns] = low(grad * gate * sigmoid)

        return tile

    def grad_inner_half_tile(chunk, half):
        spans = [
            pl.ds(origin * chunk_rows + half * half_rows, half_rows) for origin in range(size)
        ]

        def tile(columns):
            rows = everyone[:, chunk, half_span(half)].reshape(size * half_rows, model_width)
            grad = rows_product(rows, down_weight[columns, :])
            gate = wide(jnp.concatenate([gate_act[chunk, span, columns] for span in spans], 0))
            up = wide(jnp.concatenate([up_act[chunk, span, columns] for span in spans], 0))
            sigmoid = jax.nn.sigmoid(gate)
            for_gate = low(grad * up * sigmoid * (1.0 + gate * (1.0 - sigmoid)))
            for_up = low(grad * gate * sigmoid)
            for origin, span in enumerate(spans):
                here = slice(origin * half_rows, (origin + 1) * half_rows)
                gate_act[chunk, span, columns] = for_gate[here]
                up_act[chunk, span, columns] = for_up[here]

        return tile

    def grad_input_tile(chunk):
        def tile(columns):
            put_partial(
                chunk,
                columns,
                rows_product(gate_act[chunk], gate_weight[columns, :])
                + rows_product(up_act[chunk], up_weight[columns, :]),
            )

        return tile

    unit_tiles, width_tiles = units // WIDE_TILE, model_width // WIDE_TILE

    def forward_piece(chunk, piece):
        if piece == 0:
            if chunk == 0:
                for mask in (1, 3, 5, 7):
                    up_flow.arrive(mask)
                for copy in first_loads[3:6]:
                    copy.wait()
            store(0, chunk).start()
            tiles(0, unit_tiles // 2, gate_tile(chunk))
        elif piece == 1:
            tiles(unit_tiles // 2, unit_tiles, gate_tile(chunk))
            store(1, chunk).start()
            sum_sent(chunk)
            hand_sent(chunk)
        else:
            if chunk == 0:
                for mask in (1, 3, 5, 7):
                    down_flow.arrive(mask)
            tiles(0, width_tiles, down_tile(chunk))
            store(0, chunk).wait()
            store(1, chunk).wait()

    def backward_piece(chunk, piece):
        if piece == 0:
            store(2, chunk).start()
            for copy in block_stores(chunk):
                copy.start()
            tiles(0, unit_tiles // 2, grad_inner_half_tile(chunk, 1))
            tiles(unit_tiles // 2, unit_tiles, grad_inner_tile(chunk))
            if chunk == CHUNKS - 1:
                down_flow.sent()
                for copy in again:
                    copy.start()
        elif piece == 1:
            sum_sent(chunk)
            hand_sent(chunk)
            tiles(0, width_tiles // 2, grad_input_tile(chunk))
        else:
            tiles(width_tiles // 2, width_tiles, grad_input_tile(chunk))
            store(2, chunk).wait()
            for copy in block_stores(chunk):
                copy.wait()
            if chunk == CHUNKS - 1:
                up_flow.sent()
                weights_free()

    def end_piece(chunk, piece):
        if piece == 0:
            store(3, chunk).start()
            store(5, chunk).start()
            for first in range(0, attended.shape[-1], TILE):
                columns = pl.ds(first, TILE)
                value = rows_product(gathered(chunk), output_weight[columns, :])
                attended[:, chunk, :, columns] = low(value).reshape(size, chunk_rows, TILE)
            store(4, chunk).start()

    first_loads[0].wait()
    first_loads[1].wait()
    for copy in first_loads[2:]:
        copy.start()
    branch_terms(0)
    first_loads[2].wait()
    for copy in first_loads[6:]:
        copy.wait()
    bases = {
        (chunk, stage): (CHUNKS * stage + chunk) * size
        for stage in range(3)
        for chunk in range(CHUNKS)
    }
    ticks = max(bases.values()) + 2 * size
    for tick in range(1, ticks + 1):
        for half in range(HALVES):
            for (chunk, stage), base in bases.items():
                at = tick - base
                if size < at < 2 * size:
                    hand_on(chunk, at - size, half)
            for (chunk, stage), base in bases.items():
                at = tick - base
                if 1 <= at < size:
                    sum_step(chunk, at, half)
                elif at == size:
                    sum_end(chunk, half)
                    own_rows(chunk, stage, half)
                    hand_first(chunk, half)
            turns(tick, half)
            if tick == 1 and half == 1:
                branch_terms(1)
            for (chunk, stage), base in bases.items():
                piece = (tick - base - 2 * size + 1) * HALVES + half - 1
                if piece == -1 and stage == 1:
                    tiles(0, unit_tiles // 2, grad_inner_half_tile(chunk, 0))
                elif 0 <= piece < 3:
                    (forward_piece, backward_piece, end_piece)[stage](chunk, piece)
            grad_turns(tick, half)
    for half in range(2):
        up_grads.final_copy(1 - half, half).wait_recv()
    up_stores[1].start()
    gate_grads.sent(False)
    up_grads.sent(False)
    for place in range(4):
        down_grads.core_copy(place).wait_send()
    for chunk in range(CHUNKS):
        sum_sent(chunk)
        hand_sent(chunk)
        store(3, chunk).wait()
        store(4, chunk).wait()
        store(5, chunk).wait()
        near_store(chunk).wait()
    for copy in [gate_store] + up_stores:
        copy.wait()


def middle(
    attended,
    rows_all,
    cotangent_grouped,
    attention_scale,
    feedforward_scale,
    output_full,
    gate_full,
    up_shard,
    down_shard,
):
    size = lax.axis_size("tensor")
    own_rows, model_width = cotangent_grouped.shape
    chunk_rows = own_rows // CHUNKS
    all_rows = size * chunk_rows
    half_rows = chunk_rows // HALVES
    heads_width = attended.shape[1]
    units = gate_full.shape[1]
    chunked = (CHUNKS, chunk_rows, model_width)
    lined = (CHUNKS, size, chunk_rows, model_width)
    low_type, wide_type = jnp.bfloat16, jnp.float32

    def shape(dims, kind=low_type):
        return jax.ShapeDtypeStruct(dims, kind)

    anywhere = pl.BlockSpec(memory_space=pl.ANY)
    inside = pl.BlockSpec(memory_space=pltpu.VMEM)
    dma = pltpu.SemaphoreType.DMA
    flops = 2 * CHUNKS * all_rows * model_width * (2 * heads_width + 6 * units)
    outs = pl.pallas_call(
        functools.partial(middle_kernel, size),
        out_shape=[
            shape(lined),
            shape((CHUNKS, all_rows, units)),
            shape(lined),
            shape((size, CHUNKS, chunk_rows, model_width)),
            shape((size, CHUNKS, chunk_rows, heads_width)),
            shape((own_rows, model_width), wide_type),
            shape(chunked, wide_type),
            shape((model_width // 8, units)),
            shape((3 * model_width // 8, units)),
            shape((model_width // 8, units)),
            shape((model_width // 2, units)),
            shape((8, model_width), wide_type),
            shape((8, model_width), wide_type),
        ],
        in_specs=[anywhere] * 3 + [inside] * 2 + [anywhere] * 4,
        out_specs=[anywhere] * 11 + [inside] * 2,
        scratch_shapes=[
            pltpu.VMEM((size, CHUNKS, chunk_rows, heads_width), low_type),
            pltpu.VMEM(chunked, low_type),
            pltpu.VMEM(chunked, low_type),
            pltpu.VMEM((heads_width, model_width), low_type),
            pltpu.VMEM((model_width, units), low_type),
            pltpu.VMEM((model_width, units), low_type),
            pltpu.VMEM((units, model_width), low_type),
            pltpu.VMEM((size, CHUNKS, chunk_rows, model_width), low_type),
            pltpu.VMEM((CHUNKS, all_rows, units), low_type),
            pltpu.VMEM((CHUNKS, all_rows, units), low_type),
            pltpu.VMEM((all_rows, units), low_type),
            pltpu.VMEM(chunked, wide_type),
            pltpu.VMEM(chunked, wide_type),
            pltpu.VMEM((2, CHUNKS, size - 1, chunk_rows, model_width), low_type),
            pltpu.VMEM(lined, low_type),
            pltpu.VMEM((half_rows, model_width), wide_type),
            dma((6,)),
            dma((8, CHUNKS)),
            dma((2, CHUNKS, size - 1, HALVES)),
            dma((2, CHUNKS, size - 1, HALVES)),
            dma((2, CHUNKS, size - 1, HALVES)),
            dma((2, CHUNKS, size - 1, HALVES)),
            dma((2, 7, 2)),
            dma((2, 7, 2)),
            dma((3, 10)),
            dma((3, 10)),
            dma((CHUNKS, size + 1)),
            dma((CHUNKS, 8)),
            pltpu.SemaphoreType.REGULAR((4,)),
        ],
        compiler_params=pltpu.CompilerParams(
            collective_id=1, has_side_effects=True, vmem_limit_bytes=VMEM_BYTES
        ),
        cost_estimate=pl.CostEstimate(
            flops=flops, bytes_accessed=64 << 20, transcendentals=0
        ),
        name="middle",
    )(
        attended.reshape(size, CHUNKS, chunk_rows, heads_width),
        rows_all.reshape(size, *chunked),
        cotangent_grouped,
        attention_scale,
        feedforward_scale,
        output_full,
        gate_full,
        up_shard,
        down_shard,
    )
    rows = CHUNKS * all_rows
    return (
        outs[3].reshape(rows, model_width),
        outs[4].reshape(rows, heads_width),
        outs[5],
        outs[6].reshape(own_rows, model_width),
        *outs[7:],
    )


def back_kernel(
    size,
    branch_cot_hbm,
    grad_attended_hbm,
    query_rot_hbm,
    key_rot_hbm,
    value_hbm,
    query_hat_hbm,
    key_hat_hbm,
    cosine_hbm,
    sine_hbm,
    down_near_hbm,
    up_near,
    up_early,
    attended_hbm,
    weight_hbm,
    rows_hbm,
    hidden_hbm,
    stats,
    query_scale,
    key_scale,
    attention_gain,
    feedforward_gain,
    tokens_out,
    up_out,
    down_out,
    output_out,
    query_out,
    key_out,
    value_out,
    gain_out,
    left,
    attended,
    weight,
    grad,
    gain,
    shared,
    hidden,
    partial,
    arrived,
    far,
    down_near,
    output_far,
    output_near,
    attention_near,
    gain_far,
    gain_near,
    up_final,
    wide_total,
    down_total,
    output_total,
    load_sem,
    store_sem,
    share_send,
    share_recv,
    sum_send,
    sum_recv,
    shard_send,
    shard_recv,
):
    me = lax.axis_index("tensor")
    last = size - 1
    own_rows, model_width = partial.shape[1:]
    group_rows = size * own_rows
    local_width = attended.shape[1]
    heads = local_width // 128
    piece_rows = own_rows // PIECES
    height = model_width // 8
    greet([(True, lax.rem(me + offset, size)) for offset in range(1, size)])

    def beside(index):
        return pl.ds(index * local_width, local_width)

    pairs = [
        (grad_attended_hbm, output_far),
        (key_rot_hbm, partial.at[:, :, beside(1)]),
        (query_rot_hbm, partial.at[:, :, beside(0)]),
        (value_hbm, partial.at[:, :, beside(2)]),
        (attended_hbm, attended),
        (query_hat_hbm, partial.at[:, :, beside(3)]),
        (cosine_hbm, wide_total.at[pl.ds(0, group_rows), pl.ds(0, 128)]),
        (sine_hbm, wide_total.at[pl.ds(0, group_rows), pl.ds(128, 128)]),
    ]
    pairs += [
        (key_hat_hbm.at[origin], far.at[pl.ds(3 * height, own_rows), beside(origin)])
        for origin in range(size)
    ]
    first_count = len(pairs)
    pairs += [
        (down_near_hbm, down_near.at[pl.ds(0, 4 * height), :]),
        (weight_hbm, weight),
        (branch_cot_hbm, left),
        (up_near.at[pl.ds(0, height), :], up_final.at[pl.ds(2 * height, height), :]),
        (up_early, up_final.at[pl.ds(height // 2, height), :]),
        (rows_hbm, left),
        (hidden_hbm, hidden),
    ]
    loads = [
        pltpu.make_async_copy(source, target, load_sem.at[place])
        for place, (source, target) in enumerate(pairs)
    ]
    near_load, weight_load, left_load, own_load, early_load, rows_load, hidden_load = loads[
        first_count:
    ]
    for copy in loads[:first_count]:
        copy.start()

    def flow(kind, near, far_view, shard_height):
        return ShardSum(
            stacked(near, 0, shard_height),
            far_view,
            lambda half: stacked(near, 4 * shard_height, shard_height)(0, half),
            lambda way, half: stacked(near, 5 * shard_height, shard_height)(way, half),
            shard_send.at[kind],
            shard_recv.at[kind],
        )

    down_flow = flow(0, down_near, None, height)
    output_flow = flow(1, output_near, stacked(output_far, 0, height), height)
    attention_flow = flow(
        2,
        attention_near,
        lambda place, half=None, count=1: far.at[
            pl.ds(place * height, count * height), pl.ds(0, 3 * local_width)
        ],
        height,
    )
    gain_height = gain.shape[0] // 8
    gain_flow = flow(3, gain_near, stacked(gain_far, 0, gain_height), gain_height)
    up_flow = ShardSum(
        stacked(up_near, 0, height),
        None,
        None,
        stacked(up_final, 0, height),
        shard_send.at[4],
        shard_recv.at[4],
        own=functools.partial(stacked(up_final, 2 * height, height), 0),
        awaited=((0, 0), (1, 1)),
    )

    def columns_of(source):
        return lambda first, width: source[:, pl.ds(first, width)]

    output_term = product_term(columns_of(left), lambda columns, _: attended[:, columns])
    attention_term = product_term(columns_of(left), lambda columns, _: grad[:, columns])

    def gain_term(place, target, adds, count):
        value = gain[pl.ds(place * gain_height, target.shape[0]), :]
        target[...] = value + target[...] if adds else value

    def away(way):
        return me if way == 0 else last - me

    def held(kind, head):
        return pl.ds(pl.multiple_of(kind * local_width + head * 128, 128), 128)

    score_scale = 128**-0.5
    query_grad, key_grad = pl.ds(0, 128), pl.ds(128, 128)

    def product_columns(kind, origin):
        return pl.ds((kind * size + origin) * 128, 128)

    def step_head(head):
        span = head_span(head)
        for origin in reversed(range(size)):
            count = (origin + 1) * own_rows
            here = pl.ds(origin * own_rows, own_rows)
            seen = pl.ds(0, origin + 1)
            keys = partial[seen, :, held(1, head)].reshape(count, 128)
            values = partial[seen, :, held(2, head)].reshape(count, 128)
            queries = partial[origin, :, held(0, head)]
            grad_rows = output_far[here, span]
            delta = column_sums(wide(grad_rows) * wide(attended[here, span]))
            probs = jnp.exp(
                rows_product(keys, queries) * score_scale - stats[pl.ds(head, 1), here]
            )
            near = probs[origin * own_rows :]
            near = jnp.where(ahead_of(near, 0, 0), 0.0, near)
            probs = jnp.concatenate([probs[: origin * own_rows], near], 0) if origin else near
            grad_scores = low(probs * (rows_product(values, grad_rows) - delta))
            for_values = jnp.dot(low(probs), grad_rows, preferred_element_type=jnp.float32)
            for_keys = jnp.dot(grad_scores, queries, preferred_element_type=jnp.float32)
            for_queries = jnp.dot(keys.T, grad_scores, preferred_element_type=jnp.float32)
            wide_total[pl.ds(group_rows + origin * own_rows, own_rows), query_grad] = (
                for_queries * score_scale
            ).T
            first = origin == size - 1
            at = pl.ds(group_rows, count)
            wide_total[at, key_grad] = for_keys if first else wide_total[at, key_grad] + for_keys
            for block in range(origin + 1):
                term = for_values[block * own_rows : (block + 1) * own_rows]
                columns = product_columns(2, block)
                hidden[:, columns] = term if first else hidden[:, columns] + term
        for kind, (factor, scale) in enumerate(((1.0, query_scale), (score_scale, key_scale))):
            gain_total = jnp.zeros((1, 128), jnp.float32)
            for origin in range(size):
                here = pl.ds(origin * own_rows, own_rows)
                source = wide_total[
                    pl.ds(group_rows + origin * own_rows, own_rows), (query_grad, key_grad)[kind]
                ]
                rotated = wide(low(source * factor))
                normal = rotated * wide_total[here, pl.ds(0, 128)]
                normal = normal - pltpu.roll(rotated, 64, 1) * wide_total[here, pl.ds(128, 128)]
                hats = hat_of(kind, origin, head)
                gain_total = gain_total + jnp.sum(normal * hats, 0, keepdims=True)
                normal = normal * scale[pl.ds(head, 1), :]
                grad[here, held(kind, head)] = low(normal)
                hidden[:, product_columns(kind, origin)] += normal * hats
            gain[pl.ds(kind * heads + head, 1), :] = gain_total
        for origin in range(size):
            grad[pl.ds(origin * own_rows, own_rows), held(2, head)] = low(
                hidden[:, product_columns(2, origin)]
            )

    def hat_of(kind, origin, head):
        if kind == 0:
            return wide(partial[origin, :, held(3, head)])
        return wide(far[pl.ds(3 * height, own_rows), held(origin, head)])

    def share_copy(offset):
        return pltpu.make_async_remote_copy(
            src_ref=shared.at[me],
            dst_ref=shared.at[me],
            send_sem=share_send.at[offset - 1],
            recv_sem=share_recv.at[offset - 1],
            device_id={"tensor": lax.rem(me + offset, size)},
            device_id_type=pl.DeviceIdType.MESH,
        )

    def share():
        half_width = model_width // 2
        lines = [
            jnp.concatenate(
                [column_sums(hidden[:, product_columns(kind, origin)]) for origin in range(size)],
                1,
            )
            for kind in range(2)
        ]
        for part in (attention_gain, feedforward_gain):
            total = jnp.sum(part[...], 0, keepdims=True)
            lines += [total[:, :half_width], total[:, half_width:]]
        lines.append(jnp.zeros((2, half_width), jnp.float32))
        shared[me] = jnp.concatenate(lines, 0)
        for offset in range(1, size):
            share_copy(offset).start()

    def take_shares():
        for offset in range(1, size):
            share_copy(offset).wait_recv()
        total = shared[0]
        for device in range(1, size):
            total = total + shared[device]
        for kind in range(2):
            for origin in range(size):
                here = pl.ds(origin * own_rows, own_rows)
                columns = slice(origin * own_rows, (origin + 1) * own_rows)
                inner_column = turned_rows(total[kind : kind + 1, columns] / model_width)
                inverse = turned_rows(stats[pl.ds(heads + kind, 1), here])
                for head in range(heads):
                    span = pl.ds((kind * heads + head) * 128, 128)
                    hats = hat_of(kind, origin, head)
                    grad[here, span] = low(inverse * (wide(grad[here, span]) - hats * inner_column))
        for place in range(8):
            if place:
                gain[pl.ds(place * gain_height, 8), :] = gain[pl.ds(0, 8), :]
            for kind in range(2):
                for line in range(height // 128):
                    row, first = divmod(place * height + line * 128, model_width // 2)
                    gain[
                        pl.ds(place * gain_height + 8 + kind * (height // 128) + line, 1), :
                    ] = total[2 + 2 * kind + row : 3 + 2 * kind + row, first : first + 128]

    def terms(dest, count):
        span = pl.ds(pl.multiple_of(dest * own_rows, own_rows), count * own_rows)

        def step(index):
            columns = pl.ds(pl.multiple_of(index * WIDE_TILE, WIDE_TILE), WIDE_TILE)
            value = low(rows_product(grad[span, :], weight[columns, :]))
            partial[pl.ds(dest, count), :, columns] = value.reshape(count, own_rows, WIDE_TILE)

        each(model_width // WIDE_TILE, step)

    low_side = 1 - 2 * me // size

    def first_terms():
        terms(last * low_side, 1)

    def other_terms():
        terms(1 - low_side, last)

    def span_of(piece):
        return pl.ds(piece * piece_rows, piece_rows)

    def sum_copy(step, piece, way, dest):
        return pltpu.make_async_remote_copy(
            src_ref=partial.at[dest, span_of(piece)],
            dst_ref=arrived.at[way, step - 1, span_of(piece)],
            send_sem=sum_send.at[way, step - 1, piece],
            recv_sem=sum_recv.at[way, step - 1, piece],
            device_id={"tensor": me + 1 - 2 * way},
            device_id_type=pl.DeviceIdType.MESH,
        )

    def sum_step(step, *pieces):
        for piece in pieces:
            for way in range(2):
                distance = away(way)

                @pl.when(distance <= step - 1)
                def _():
                    dest = me + size - step if way == 0 else me - size + step
                    if step > 1:

                        @pl.when(distance >= 1)
                        def _():
                            sum_copy(step - 1, piece, way, dest).wait_recv()
                            add_into(
                                partial.at[dest, span_of(piece)],
                                arrived.at[way, step - 2, span_of(piece)],
                            )

                    sum_copy(step, piece, way, dest).start()

    def token_stores(piece):
        return [
            pltpu.make_async_copy(
                hidden.at[span_of(piece), here],
                tokens_out.at[span_of(piece), natural],
                store_sem.at[1 + piece, place],
            )
            for place, (here, natural) in enumerate(column_blocks(height))
        ]

    def sum_end(*pieces):
        for piece in pieces:
            add_into(hidden.at[span_of(piece)], partial.at[me, span_of(piece)])
            for way in range(2):

                @pl.when(away(way) >= 1)
                def _():
                    sum_copy(size - 1, piece, way, me).wait_recv()
                    add_into(
                        hidden.at[span_of(piece)], arrived.at[way, size - 2, span_of(piece)]
                    )

            for copy in token_stores(piece):
                copy.start()

    up_store = pltpu.make_async_copy(
        up_final.at[pl.ds(2 * height, height), :], up_out, store_sem.at[0, 0]
    )
    down_store = pltpu.make_async_copy(down_total, down_out, store_sem.at[0, 1])
    output_store = pltpu.make_async_copy(output_total, output_out, store_sem.at[0, 2])
    attention_stores = [
        pltpu.make_async_copy(
            attention_near.at[pl.ds(0, height), beside(kind)], out, store_sem.at[0, 3 + kind]
        )
        for kind, out in enumerate((query_out, key_out, value_out))
    ]

    gain[...] = jnp.zeros_like(gain)
    hidden[...] = jnp.zeros_like(hidden)
    pl.semaphore_wait(pltpu.get_barrier_semaphore(), 3 + size - 1)
    for half in range(2):
        up_flow.final_copy(half, half).start()
    for copy in loads[:first_count]:
        copy.wait()
    for copy in (near_load, left_load, weight_load, own_load, early_load):
        copy.start()
    def step_pair(index):
        step_head(2 * index)
        step_head(2 * index + 1)

    each(heads // 4, step_pair)
    near_load.wait()
    for place in (3, 1, 2):
        down_flow.near_ready(place)
    each(heads // 4, lambda index: step_pair(heads // 4 + index))
    share()
    hidden_load.start()
    left_load.wait()
    output_flow.first_terms(output_term)
    take_shares()
    weight_load.wait()
    first_terms()
    sum_step(1, *range(PIECES))
    output_flow.other_terms(output_term)
    rows_load.start()
    down_flow.take_corner()
    other_terms()
    sum_step(2, 0)
    own_load.wait()
    early_load.wait()
    up_flow.take_final()
    up_store.start()
    gain_flow.first_terms(gain_term)
    gain_flow.other_terms(gain_term)
    rows_load.wait()
    attention_flow.first_terms(attention_term)
    sum_step(2, 1)
    output_flow.take_corner()
    sum_step(2, 2)
    attention_flow.other_terms(attention_term)
    sum_step(2, 3)
    sum_step(3, 0)
    gain_flow.take_corner()
    sum_step(3, 1)
    sum_step(3, 2)
    sum_step(3, 3)
    hidden_load.wait()
    attention_flow.take_corner()
    output_flow.take_final_turned(output_total)
    output_store.start()
    gain_flow.take_final()
    gain_out[...] = gain_near[pl.ds(0, gain_height), :]
    sum_end(0)
    sum_end(1)
    down_flow.take_final_turned(down_total)
    down_store.start()
    sum_end(2)
    sum_end(3)
    attention_flow.take_final()
    for copy in attention_stores:
        copy.start()
    down_flow.sent(False)
    for shard_flow in (output_flow, attention_flow, gain_flow):
        shard_flow.sent()
    for half in range(2):
        up_flow.final_copy(half, half).wait_send()
    for offset in range(1, size):
        share_copy(offset).wait_send()
    for step in range(1, size):
        for way in range(2):

            @pl.when(away(way) <= step - 1)
            def _():
                for piece in range(PIECES):
                    sum_copy(step, piece, way, 0).wait_send()

    for copy in [up_store, down_store, output_store] + attention_stores:
        copy.wait()
    for piece in range(PIECES):
        for copy in token_stores(piece):
            copy.wait()


def back(
    branch_cot,
    grad_attended,
    query_rot,
    key_rot,
    value_rows,
    query_hat,
    key_hat,
    cosine,
    sine,
    down_near,
    up_near,
    up_early,
    attended,
    attention_full,
    rows_all,
    grad_hidden,
    *small,
):
    size = lax.axis_size("tensor")
    own_rows, model_width = grad_hidden.shape
    group_rows = size * own_rows
    height = model_width // 8
    local_width, units = attended.shape[1], down_near.shape[1]
    low_type, wide_type = jnp.bfloat16, jnp.float32
    anywhere = pl.BlockSpec(memory_space=pl.ANY)
    inside = pl.BlockSpec(memory_space=pltpu.VMEM)
    dma = pltpu.SemaphoreType.DMA
    by_device = (size, own_rows, local_width)

    def shape(*dims):
        return jax.ShapeDtypeStruct(dims, wide_type)

    def low_shape(*dims):
        return jax.ShapeDtypeStruct(dims, low_type)

    return pl.pallas_call(
        functools.partial(back_kernel, size),
        out_shape=[
            shape(own_rows, model_width),
            low_shape(height, units),
            low_shape(units, height),
            low_shape(local_width, height),
            *[low_shape(height, local_width)] * 3,
            shape(32, 128),
        ],
        in_specs=[anywhere] * 16 + [inside] * len(small),
        out_specs=[anywhere] * 7 + [inside],
        scratch_shapes=[
            pltpu.VMEM((group_rows, model_width), low_type),
            pltpu.VMEM((group_rows, local_width), low_type),
            pltpu.VMEM((model_width, 3 * local_width), low_type),
            pltpu.VMEM((group_rows, 3 * local_width), low_type),
            pltpu.VMEM((8 * 32, 128), wide_type),
            pltpu.VMEM((size, 8, model_width // 2), wide_type),
            pltpu.VMEM((own_rows, model_width), wide_type),
            pltpu.VMEM((size, own_rows, model_width), low_type),
            pltpu.VMEM((2, size - 1, own_rows, model_width), low_type),
            pltpu.VMEM((4 * height, units), low_type),
            pltpu.VMEM((7 * height, units), low_type),
            pltpu.VMEM((4 * height, local_width), low_type),
            pltpu.VMEM((7 * height, local_width), low_type),
            pltpu.VMEM((7 * height, 3 * local_width), low_type),
            pltpu.VMEM((4 * 32, 128), wide_type),
            pltpu.VMEM((7 * 32, 128), wide_type),
            pltpu.VMEM((3 * height, units), low_type),
            pltpu.VMEM((2 * group_rows, 256), wide_type),
            pltpu.VMEM((units, height), low_type),
            pltpu.VMEM((local_width, height), low_type),
            dma((15 + size,)),
            dma((1 + PIECES, 8)),
            dma((size - 1,)),
            dma((size - 1,)),
            dma((2, size - 1, PIECES)),
            dma((2, size - 1, PIECES)),
            dma((5, 10)),
            dma((5, 10)),
        ],
        compiler_params=pltpu.CompilerParams(
            collective_id=2, has_side_effects=True, vmem_limit_bytes=VMEM_BYTES
        ),
        cost_estimate=pl.CostEstimate(
            flops=2 * group_rows * model_width * (units + 8 * local_width),
            bytes_accessed=48 << 20,
            transcendentals=group_rows**2 * local_width // 128,
        ),
        name="back",
    )(
        branch_cot,
        grad_attended,
        query_rot.reshape(by_device),
        key_rot.reshape(by_device),
        value_rows.reshape(by_device),
        query_hat.reshape(by_device),
        key_hat.reshape(by_device),
        cosine,
        sine,
        down_near,
        up_near,
        up_early,
        attended,
        attention_full,
        rows_all,
        grad_hidden,
        *small,
    )


def finish_kernel(count, *refs):
    sources, gain, refs = refs[:count], refs[count], refs[count + 1 :]
    targets, head_outs, norm_outs = refs[:count], refs[count : count + 2], refs[count + 2 : count + 4]
    buffers, sem = refs[count + 4 : 2 * count + 4], refs[-1]
    wides = list(refs[2 * count + 4 : -1])
    outgoing = [buffer if buffer.dtype == jnp.float32 else wides.pop(0) for buffer in buffers]
    loads, stores = [], []
    for place, (source, buffer, wider, target) in enumerate(
        zip(sources, buffers, outgoing, targets)
    ):
        rows = source.shape[0] // 2
        for half in range(2):
            span = pl.ds(half * rows, rows)
            here = buffer.at[span, :], wider.at[span, :]
            loads.append(
                pltpu.make_async_copy(source.at[span, :], here[0], sem.at[half, place])
            )
            stores.append(
                (here, pltpu.make_async_copy(here[1], target.at[span, :], sem.at[2 + half, place]))
            )
    for copy in loads[:WINDOW]:
        copy.start()
    heads, channels = head_outs[0].shape
    shift = lax.rem(128 - lax.axis_index("dp") * channels, 128)
    own = pltpu.roll(gain[pl.ds(0, 2 * heads), :], shift, 1)
    lines = norm_outs[0].shape[0]
    for kind in range(2):
        head_outs[kind][...] = own[kind * heads : (kind + 1) * heads, :channels]
        at = 2 * heads + kind * lines
        norm_outs[kind][...] = gain[pl.ds(at, lines), :]
    for place, (load, (here, store)) in enumerate(zip(loads, stores)):
        load.wait()
        if place + WINDOW < len(loads):
            loads[place + WINDOW].start()
        if here[0].dtype != here[1].dtype:
            widen(*here)
        store.start()
    for _, copy in stores:
        copy.wait()


def widen(source, target):
    def step(index):
        span = pl.ds(pl.multiple_of(index * STRIP, STRIP), STRIP)
        target[span, :] = wide(source[span, :])

    each(source.shape[0] // STRIP, step)


def finish(gain_part, head_shape, lines, *arrays):
    anywhere = pl.BlockSpec(memory_space=pl.ANY)
    inside = pl.BlockSpec(memory_space=pltpu.VMEM)
    count = len(arrays)
    return pl.pallas_call(
        functools.partial(finish_kernel, count),
        out_shape=[
            *(jax.ShapeDtypeStruct(array.shape, jnp.float32) for array in arrays),
            *[jax.ShapeDtypeStruct(head_shape, jnp.float32)] * 2,
            *[jax.ShapeDtypeStruct((lines, 128), jnp.float32)] * 2,
        ],
        in_specs=[anywhere] * count + [inside],
        out_specs=[anywhere] * count + [inside] * 4,
        scratch_shapes=[
            *(pltpu.VMEM(array.shape, array.dtype) for array in arrays),
            *(pltpu.VMEM(array.shape, jnp.float32) for array in arrays if array.dtype != jnp.float32),
            pltpu.SemaphoreType.DMA((4, count)),
        ],
        compiler_params=pltpu.CompilerParams(vmem_limit_bytes=VMEM_BYTES),
        name="finish",
    )(*arrays, gain_part)


def local(
    tokens,
    positions,
    cotangent,
    query_weight,
    key_weight,
    value_weight,
    output_weight,
    gate_weight,
    up_weight,
    down_weight,
    query_gain,
    key_gain,
    attention_gain,
    feedforward_gain,
):
    data_size = lax.axis_size("dp")
    data_index = lax.axis_index("dp")
    high_count = data_size // 8
    width = attention_gain.shape[0]
    channels, local_heads = query_gain.shape

    def high_block(low_bits, place):
        return low_bits + 8 * ((data_index // 8) ^ place)

    def grouped(array_in):
        if high_count == 1:
            return array_in
        return jnp.concatenate(
            [
                lax.dynamic_slice_in_dim(array_in, high_block(low_bits, place) * width, width, -1)
                for low_bits in range(8)
                for place in range(high_count)
            ],
            -1,
        )

    def ungrouped(array_in):
        if high_count == 1:
            return array_in
        return jnp.concatenate(
            [
                lax.dynamic_slice_in_dim(
                    array_in,
                    (low_bits * high_count + ((data_index // 8) ^ high_bits)) * width,
                    width,
                    -1,
                )
                for high_bits in range(high_count)
                for low_bits in range(8)
            ],
            -1,
        )

    head_gains = jnp.concatenate([query_gain.T, key_gain.T], 0)
    head_gains = lax.dynamic_update_slice_in_dim(
        jnp.zeros((2 * local_heads, channels * data_size), head_gains.dtype),
        head_gains,
        data_index * channels,
        1,
    )
    for bit in range(3, bits_of(data_size)):
        head_gains = head_gains + swap(head_gains, 1 << bit)
    gain_lines = [
        head_gains,
        gather_high(attention_gain[None], 1).reshape(-1, 128),
        gather_high(feedforward_gain[None], 1).reshape(-1, 128),
    ]
    line_count = sum(lines.shape[0] for lines in gain_lines)
    gain_shard = jnp.pad(jnp.concatenate(gain_lines, 0), ((0, 32 - line_count), (0, 0)))
    (
        rows_all,
        attention_full,
        output_full,
        gate_full,
        attended,
        query_rot,
        key_rot,
        value_rows,
        query_hat,
        key_hat,
        cosine,
        sine,
        stats,
        query_scale,
        key_scale,
        attention_scale,
        feedforward_scale,
    ) = front(
        grouped(tokens),
        gather_high(query_weight, 0),
        gather_high(key_weight, 0),
        gather_high(value_weight, 0),
        gather_high(output_weight, 1),
        gather_high(gate_weight, 0),
        gain_shard,
        positions,
    )
    (
        branch_cot,
        grad_attended,
        block_grouped,
        grad_hidden,
        grad_gate,
        up_near,
        up_early,
        down_near,
        attention_gain_part,
        feedforward_gain_part,
    ) = middle(
        attended,
        rows_all,
        grouped(cotangent),
        attention_scale,
        feedforward_scale,
        output_full,
        gate_full,
        gather_high(up_weight, 0),
        gather_high(down_weight, 1),
    )
    (
        tokens_part,
        grad_up,
        grad_down,
        grad_output,
        grad_query,
        grad_key,
        grad_value,
        gain_part,
    ) = back(
        branch_cot,
        grad_attended,
        query_rot,
        key_rot,
        value_rows,
        query_hat,
        key_hat,
        cosine,
        sine,
        down_near,
        up_near,
        up_early,
        attended,
        attention_full,
        rows_all.reshape(-1, rows_all.shape[-1]),
        grad_hidden,
        stats,
        query_scale,
        key_scale,
        attention_gain_part,
        feedforward_gain_part,
    )
    def own_high(total, axis):
        return total if high_count == 1 else wide(scatter_high(total, axis))

    large = (
        ungrouped(block_grouped),
        ungrouped(tokens_part),
        own_high(grad_query, 0),
        own_high(grad_key, 0),
        own_high(grad_value, 0),
        own_high(grad_output, 1),
        own_high(grad_gate, 0),
        own_high(grad_up, 0),
        own_high(grad_down, 1),
    )
    if high_count == 1:
        *large, query_part, key_part, attention_part, feedforward_part = finish(
            gain_part, query_gain.shape[::-1], width // 128, *large
        )
        return (
            *large,
            query_part.T,
            key_part.T,
            attention_part.reshape(width),
            feedforward_part.reshape(width),
        )
    head_part = gain_part[: 2 * local_heads]
    for bit in range(3, bits_of(data_size)):
        head_part = head_part + swap(head_part, 1 << bit)
    head_part = lax.dynamic_slice_in_dim(head_part, data_index * channels, channels, 1)
    norm_part = gain_part[2 * local_heads : line_count].reshape(2, -1)

    return (
        *large,
        head_part[:local_heads].T,
        head_part[local_heads:].T,
        own_high(norm_part[0], 0),
        own_high(norm_part[1], 0),
    )


def solution(mesh):
    return jax.shard_map(
        local,
        mesh=mesh,
        in_specs=(
            P(("dp", "tensor"), None),
            P("dp"),
            P(("dp", "tensor"), None),
            P("dp", "tensor"),
            P("dp", "tensor"),
            P("dp", "tensor"),
            P("tensor", "dp"),
            P("dp", "tensor"),
            P("dp", "tensor"),
            P("tensor", "dp"),
            P("dp", "tensor"),
            P("dp", "tensor"),
            P("dp"),
            P("dp"),
        ),
        out_specs=(
            P(("dp", "tensor"), None),
            P(("dp", "tensor"), None),
            P("dp", "tensor"),
            P("dp", "tensor"),
            P("dp", "tensor"),
            P("tensor", "dp"),
            P("dp", "tensor"),
            P("dp", "tensor"),
            P("tensor", "dp"),
            P("dp", "tensor"),
            P("dp", "tensor"),
            P("dp"),
            P("dp"),
        ),
        check_vma=False,
    )
```

```python
import functools

import jax
import jax.numpy as jnp
import numpy as np
from jax import lax
from jax.experimental import pallas as pl
from jax.experimental.pallas import tpu as pltpu
from jax.sharding import PartitionSpec as P

EPS = 1e-06
THETA = 500000.0
MASKED = -1e30
VMEM_BYTES = 64 * 1024 * 1024 - 128 * 1024


def norm_backward(grad_in, normalized, inverse_rms, gain_values):
    scaled = grad_in * gain_values
    return inverse_rms * (scaled - normalized * jnp.mean(scaled * normalized, -1, keepdims=True))


def bits_of(size):
    return size.bit_length() - 1


def swap(array_in, mask):
    size = lax.axis_size("dp")
    return lax.ppermute(array_in, "dp", [(index, index ^ mask) for index in range(size)])


def gather_high(shard, axis):
    for bit in range(3, bits_of(lax.axis_size("dp"))):
        shard = jnp.concatenate([shard, swap(shard, 1 << bit)], axis)
    return shard


def scatter_high(total, axis):
    for bit in reversed(range(3, bits_of(lax.axis_size("dp")))):
        kept, sent = jnp.split(total, 2, axis)
        total = low(wide(kept) + wide(swap(low(sent), 1 << bit)))
    return total


def low(array_in):
    return array_in.astype(jnp.bfloat16)


def wide(array_in):
    return array_in.astype(jnp.float32)


def rows_product(left, right):
    return lax.dot_general(
        left, right, (((1,), (1,)), ((), ())), preferred_element_type=jnp.float32
    )


TILE = 256
WIDE_TILE = 512
STRIP = 16
CHUNKS = 2
HALVES = 2
PIECES = 4
WINDOW = 6


def shard_peer(mask):
    index = lax.axis_index("dp")
    return index + mask - 2 * mask * ((index // mask) % 2)


def low_place(mask):
    index = lax.axis_index("dp")
    total = 0
    for bit in (1, 2, 4):
        value = (index // bit) % 2
        total = total + bit * (1 - value if mask & bit else value)
    return total


ROUTE = {1: (1, 1), 2: (2, 2), 3: (1, 1), 4: (4, 4), 5: (1, 1), 6: (4, 2), 7: (1, 1)}
PLACES = {mask: place for place, mask in enumerate((0, 2, 4, 6, 1, 3, 5, 7))}


def column_blocks(width):
    return [
        (
            pl.ds(place * width, width),
            pl.ds(pl.multiple_of(low_place(mask) * width, width), width),
        )
        for mask, place in PLACES.items()
    ]


class ShardGather:
    def __init__(self, own, target, send_sem, recv_sem):
        self.own, self.target, self.send_sem, self.recv_sem = own, target, send_sem, recv_sem

    def copy(self, mask, half):
        route = ROUTE[mask][half]
        before = mask ^ route
        return pltpu.make_async_remote_copy(
            src_ref=self.target(PLACES[before], half) if before else self.own(half),
            dst_ref=self.target(PLACES[mask], half),
            send_sem=self.send_sem.at[mask - 1, half],
            recv_sem=self.recv_sem.at[mask - 1, half],
            device_id={"dp": shard_peer(route)},
            device_id_type=pl.DeviceIdType.MESH,
        )

    def start(self, *masks):
        for half in range(2):
            for mask in masks:
                self.copy(mask, half).start()

    def arrive(self, mask, halves=(0, 1)):
        for half in halves:
            self.copy(mask, half).wait_recv()
            for after, route in ROUTE.items():
                if after != mask and after ^ route[half] == mask:
                    self.copy(after, half).start()

    def sent(self):
        for mask in ROUTE:
            for half in range(2):
                self.copy(mask, half).wait_send()


def row_halves(buffer, height):
    def target(place, half):
        return buffer.at[pl.ds(place * height + half * (height // 2), height // 2), :]

    return target


def column_halves(buffer, width):
    height = buffer.shape[0] // 2

    def target(place, half):
        return buffer.at[pl.ds(half * height, height), pl.ds(place * width, width)]

    return target


def own_halves(shard):
    height = shard.shape[0] // 2
    return lambda half: shard.at[pl.ds(half * height, height), :]


def greet(line_devices):
    barrier = pltpu.get_barrier_semaphore()
    for mask in (1, 2, 4):
        pl.semaphore_signal(
            barrier,
            inc=1,
            device_id={"dp": shard_peer(mask)},
            device_id_type=pl.DeviceIdType.MESH,
        )
    for there, index in line_devices:

        @pl.when(there)
        def _():
            pl.semaphore_signal(
                barrier,
                inc=1,
                device_id={"tensor": index},
                device_id_type=pl.DeviceIdType.MESH,
            )


def turned_rows(row):
    return jnp.broadcast_to(row, (128, row.shape[1])).T


def column_sums(values):
    total = values[:, :128]
    for first in range(128, values.shape[1], 128):
        total = total + values[:, first : first + 128]
    return jnp.sum(total.T, 0, keepdims=True)


def ahead_of(values, first_key, first_query):
    key = first_key + lax.broadcasted_iota(jnp.int32, values.shape, 0)
    query = first_query + lax.broadcasted_iota(jnp.int32, values.shape, 1)
    return key > query


def head_span(head):
    return pl.ds(pl.multiple_of(head * 128, 128), 128)


def each(count, body):
    def step(index, carry):
        body(index)
        return carry

    lax.fori_loop(0, count, step, 0)


def front_kernel(
    size,
    tokens_hbm,
    query_hbm,
    key_hbm,
    value_hbm,
    output_hbm,
    gate_hbm,
    gain_hbm,
    positions,
    frequency,
    rows_out,
    attention_out,
    output_out,
    gate_out,
    attended_out,
    query_rot_out,
    key_rot_out,
    value_out,
    query_hat_out,
    key_hat_out,
    cosine_out,
    sine_out,
    stats,
    query_scale,
    key_scale,
    attention_scale,
    feedforward_scale,
    rows,
    weight,
    projected,
    gain,
    cosine,
    sine,
    squares,
    query_rot,
    key_rot,
    value,
    query_hat,
    key_hat,
    attended,
    load_sem,
    store_sem,
    hand_send,
    hand_recv,
    shard_send,
    shard_recv,
    square_send,
    square_recv,
):
    me = lax.axis_index("tensor")
    last = size - 1
    own_rows, model_width = rows.shape[1:]
    piece_rows = own_rows // PIECES
    local_width = query_hbm.shape[1]
    heads = local_width // 128
    everyone = True
    greet([(everyone, lax.rem(me + offset, size)) for offset in range(1, size)])
    block = model_width // 8
    token_loads = [
        pltpu.make_async_copy(
            tokens_hbm.at[:, natural], rows.at[me, :, here], load_sem.at[0, place]
        )
        for place, (here, natural) in enumerate(column_blocks(block))
    ]
    shard_rows = pl.ds(0, query_hbm.shape[0])
    loads = [
        pltpu.make_async_copy(source, target, load_sem.at[1, place])
        for place, (source, target) in enumerate(
            (
                (query_hbm, weight.at[shard_rows, pl.ds(0, local_width)]),
                (key_hbm, weight.at[shard_rows, pl.ds(local_width, local_width)]),
                (value_hbm, weight.at[shard_rows, pl.ds(2 * local_width, local_width)]),
                (gain_hbm, gain.at[pl.ds(0, gain_hbm.shape[0]), :]),
                (output_hbm, output_out.at[:, pl.ds(0, output_hbm.shape[1])]),
                (gate_hbm, gate_out.at[pl.ds(0, gate_hbm.shape[0]), :]),
            )
        )
    ]
    for copy in token_loads + loads:
        copy.start()
    attention_target = row_halves(weight, query_hbm.shape[0])
    attention_flow, output_flow, gate_flow, gain_flow = (
        ShardGather(own, target, shard_send.at[kind], shard_recv.at[kind])
        for kind, (own, target) in enumerate(
            (
                (functools.partial(attention_target, 0), attention_target),
                (own_halves(output_hbm), column_halves(output_out, output_hbm.shape[1])),
                (own_halves(gate_hbm), row_halves(gate_out, gate_hbm.shape[0])),
                (own_halves(gain_hbm), row_halves(gain, gain_hbm.shape[0])),
            )
        )
    )
    pl.semaphore_wait(pltpu.get_barrier_semaphore(), 3 + size - 1)

    def away(way):
        return me if way == 0 else last - me

    def hand_copy(hop, piece, way, origin):
        here = rows.at[origin, pl.ds(piece * piece_rows, piece_rows)]
        return pltpu.make_async_remote_copy(
            src_ref=here,
            dst_ref=here,
            send_sem=hand_send.at[way, hop - 1, piece],
            recv_sem=hand_recv.at[way, hop - 1, piece],
            device_id={"tensor": me + 1 - 2 * way},
            device_id_type=pl.DeviceIdType.MESH,
        )

    for copy in token_loads:
        copy.wait()
    for piece in range(PIECES):
        for way in range(2):

            @pl.when(away(1 - way) >= 1)
            def _():
                hand_copy(1, piece, way, me).start()

        if piece == 0:
            for copy in loads[:3]:
                copy.wait()
            attention_flow.start(2, 4, 1)
            gain_flow.start(2, 4, 1)

    def hand_on(hop, piece):
        for way in range(2):

            @pl.when(away(way) >= hop)
            def _():
                origin = me - hop if way == 0 else me + hop
                hand_copy(hop, piece, way, origin).wait_recv()
                if hop < size - 1:

                    @pl.when(away(1 - way) >= 1)
                    def _():
                        hand_copy(hop + 1, piece, way, origin).start()

    def row_store(origin):
        return pltpu.make_async_copy(rows.at[origin], rows_out.at[origin], store_sem.at[0, origin])

    whole_stores = [
        pltpu.make_async_copy(source, target, store_sem.at[1 + place // size, place % size])
        for place, (source, target) in enumerate(
            (
                (weight, attention_out),
                (cosine, cosine_out),
                (sine, sine_out),
                (query_hat, query_hat_out),
                (key_hat, key_hat_out),
                (query_rot, query_rot_out),
                (key_rot, key_rot_out),
                (value, value_out),
                (attended, attended_out),
            )
        )
    ]

    def span_of(origin):
        return pl.ds(pl.multiple_of(origin * own_rows, own_rows), own_rows)

    def square_copy(offset, origin):
        return pltpu.make_async_remote_copy(
            src_ref=squares.at[me, origin],
            dst_ref=squares.at[me, origin],
            send_sem=square_send.at[offset - 1, origin],
            recv_sem=square_recv.at[offset - 1, origin],
            device_id={"tensor": lax.rem(me + offset, size)},
            device_id_type=pl.DeviceIdType.MESH,
        )

    def project(origin):
        def step(index):
            columns = pl.ds(pl.multiple_of(index * WIDE_TILE, WIDE_TILE), WIDE_TILE)
            projected[origin, :, columns] = jnp.dot(
                rows[origin], weight[:, columns], preferred_element_type=jnp.float32
            )

        row_store(origin).start()
        each(weight.shape[1] // WIDE_TILE, step)
        queries = projected[origin, :, pl.ds(0, local_width)]
        keys = projected[origin, :, pl.ds(local_width, local_width)]
        squares[me, origin, pl.ds(0, 8), :] = jnp.concatenate(
            [
                column_sums(queries * queries),
                column_sums(keys * keys),
                jnp.zeros((6, own_rows), jnp.float32),
            ],
            0,
        )
        for offset in range(1, size):
            square_copy(offset, origin).start()

    def project_from(hop, way):
        @pl.when(away(way) >= hop)
        def _():
            project(me - hop if way == 0 else me + hop)

    def normalize(origin):
        for offset in range(1, size):
            square_copy(offset, origin).wait_recv()
        total = squares[0, origin]
        for device in range(1, size):
            total = total + squares[device, origin]
        inverse = lax.rsqrt(total / model_width + EPS)
        here = span_of(origin)
        stats[pl.ds(heads, 2), here] = inverse[:2]
        for kind, (hat, rot, scale) in enumerate(
            ((query_hat, query_rot, query_scale), (key_hat, key_rot, key_scale))
        ):
            column = turned_rows(inverse[kind : kind + 1])

            def step(head):
                span = head_span(head)
                source = head_span(head + kind * heads)
                normalized = projected[origin, :, source] * column
                hat[here, span] = low(normalized)
                scaled = normalized * scale[pl.ds(head, 1), :]
                rot[here, span] = low(
                    scaled * cosine[here, :] + pltpu.roll(scaled, 64, 1) * sine[here, :]
                )

            each(heads, step)
        value[here, :] = low(projected[origin, :, pl.ds(2 * local_width, local_width)])

    def tables():
        for origin in range(size):
            here = pl.ds(origin * own_rows, own_rows)
            angles = turned_rows(wide(positions[:, here])) * frequency[...]
            cosine[here, :] = jnp.cos(angles)
            lane = lax.broadcasted_iota(jnp.int32, angles.shape, 1)
            sine[here, :] = jnp.where(lane < 64, -1.0, 1.0) * jnp.sin(angles)

    def scales():
        for kind, scale in enumerate((query_scale, key_scale)):
            total = wide(gain[pl.ds(0, 16), :])
            for place in range(1, 8):
                total = total + wide(gain[pl.ds(place * gain_hbm.shape[0], 16), :])
            scale[...] = jnp.concatenate(
                [total[kind * heads : (kind + 1) * heads], jnp.zeros((8 - heads, 128), jnp.float32)],
                0,
            )
        for place in range(8):
            lines = wide(gain[pl.ds(place * gain_hbm.shape[0], 16), :])
            for kind, scale in enumerate((attention_scale, feedforward_scale)):
                for line in range(block // 128):
                    at = 2 * heads + kind * (block // 128) + line
                    scale[:, pl.ds(place * block + line * 128, 128)] = lines[at : at + 1]

    def attend(head):
        span = head_span(head)
        for origin in range(size):
            count = (origin + 1) * own_rows
            here = pl.ds(origin * own_rows, own_rows)
            scores = rows_product(key_rot[pl.ds(0, count), span], query_rot[here, span])
            scores = scores * (128**-0.5)
            near = scores[origin * own_rows :]
            near = jnp.where(ahead_of(near, 0, 0), MASKED, near)
            scores = jnp.concatenate([scores[: origin * own_rows], near], 0) if origin else near
            row_max = jnp.max(scores, 0, keepdims=True)
            exponent = jnp.exp(scores - row_max)
            row_total = jnp.sum(exponent, 0, keepdims=True)
            result = jnp.dot(
                value[pl.ds(0, count), span].T, low(exponent), preferred_element_type=jnp.float32
            )
            attended[here, span] = low((result * (1.0 / row_total)).T)
            stats[pl.ds(head, 1), here] = row_max + jnp.log(row_total)

    def turns(beat):
        if beat == 1:
            tables()
            for copy in whole_stores[1:3]:
                copy.start()
        elif beat == 2:
            attention_flow.arrive(2, (0,))
            attention_flow.arrive(4, (0,))
        elif beat == 3:
            attention_flow.arrive(2, (1,))
            attention_flow.arrive(4, (1,))
            output_flow.start(2, 4, 1)
            gain_flow.arrive(2)
            gain_flow.arrive(4)
        elif beat == 5:
            attention_flow.arrive(6)
            gate_flow.start(2, 4, 1)
            gain_flow.arrive(6)
        elif beat == 6:
            output_flow.arrive(2)
            output_flow.arrive(4)
            for mask in (1, 3, 5, 7):
                attention_flow.arrive(mask)
            whole_stores[0].start()
            project(me)
        elif beat == 7:
            project_from(1, 0)
        elif beat == 8:
            project_from(1, 1)
            output_flow.arrive(6)
            loads[3].wait()
            for mask in (1, 3, 5, 7):
                gain_flow.arrive(mask)
            scales()
        elif beat == 9:
            gate_flow.arrive(2, (0,))
            gate_flow.arrive(4, (0,))
        elif beat == 10:
            project_from(2, 0)
        elif beat == 11:
            project_from(2, 1)
            gate_flow.arrive(2, (1,))
            gate_flow.arrive(4, (1,))

    for beat in range(1, (size - 1) * PIECES + 1):
        if beat == (size - 1) * PIECES:
            for origin in range(1, last):
                normalize(origin)
        hand_on((beat - 1) // PIECES + 1, (beat - 1) % PIECES)
        turns(beat)
    project_from(3, 0)
    project_from(3, 1)
    gate_flow.arrive(6)
    for origin in (0, last):
        normalize(origin)
    for copy in whole_stores[3:8]:
        copy.start()
    def attend_pair(index):
        attend(2 * index)
        attend(2 * index + 1)

    each(heads // 2, attend_pair)
    whole_stores[8].start()
    for flow in (output_flow, gate_flow):
        for mask in (1, 3, 5, 7):
            flow.arrive(mask)
    for hop in range(1, size):
        for way in range(2):

            @pl.when(jnp.logical_and(away(way) >= hop - 1, away(1 - way) >= 1))
            def _():
                for piece in range(PIECES):
                    hand_copy(hop, piece, way, 0).wait_send()

    for flow in (attention_flow, output_flow, gate_flow, gain_flow):
        flow.sent()
    for offset in range(1, size):
        for origin in range(size):
            square_copy(offset, origin).wait_send()
    for copy in loads[4:]:
        copy.wait()
    for origin in range(size):
        row_store(origin).wait()
    for copy in whole_stores:
        copy.wait()


def front(
    tokens_grouped,
    query_shard,
    key_shard,
    value_shard,
    output_shard,
    gate_shard,
    gain_shard,
    positions,
):
    size = lax.axis_size("tensor")
    own_rows, model_width = tokens_grouped.shape
    local_width = query_shard.shape[1]
    group_rows = size * own_rows
    low_type, wide_type = jnp.bfloat16, jnp.float32
    anywhere = pl.BlockSpec(memory_space=pl.ANY)
    inside = pl.BlockSpec(memory_space=pltpu.VMEM)
    dma = pltpu.SemaphoreType.DMA
    hands = (2, size - 1, PIECES)
    half_head = np.arange(128, dtype=np.float32) % 64
    frequency = (np.float32(THETA) ** (-(half_head * np.float32(2.0 / 128))))[None]

    def shape(dims, kind=low_type):
        return jax.ShapeDtypeStruct(dims, kind)

    local_rows = (group_rows, local_width)
    tables = (group_rows, 128)
    return pl.pallas_call(
        functools.partial(front_kernel, size),
        out_shape=[
            shape((size, own_rows, model_width)),
            shape((model_width, 3 * local_width)),
            shape((output_shard.shape[0], model_width)),
            shape((model_width, gate_shard.shape[1])),
            *[shape(local_rows)] * 6,
            *[shape(tables, wide_type)] * 2,
            shape((8, group_rows), wide_type),
            *[shape((8, 128), wide_type)] * 2,
            *[shape((1, model_width), wide_type)] * 2,
        ],
        in_specs=[anywhere] * 7 + [inside] * 2,
        out_specs=[anywhere] * 12 + [inside] * 5,
        scratch_shapes=[
            pltpu.VMEM((size, own_rows, model_width), low_type),
            pltpu.VMEM((model_width, 3 * local_width), low_type),
            pltpu.VMEM((size, own_rows, 3 * local_width), wide_type),
            pltpu.VMEM((8 * gain_shard.shape[0], gain_shard.shape[1]), low_type),
            pltpu.VMEM(tables, wide_type),
            pltpu.VMEM(tables, wide_type),
            pltpu.VMEM((size, size, 8, own_rows), wide_type),
            *[pltpu.VMEM(local_rows, low_type)] * 6,
            dma((2, 8)),
            dma((4, size)),
            dma(hands),
            dma(hands),
            dma((4, 7, 2)),
            dma((4, 7, 2)),
            dma((size - 1, size)),
            dma((size - 1, size)),
        ],
        compiler_params=pltpu.CompilerParams(
            collective_id=0, has_side_effects=True, vmem_limit_bytes=VMEM_BYTES
        ),
        cost_estimate=pl.CostEstimate(
            flops=6 * group_rows * model_width * local_width,
            bytes_accessed=32 << 20,
            transcendentals=0,
        ),
        name="front",
    )(
        tokens_grouped,
        query_shard,
        key_shard,
        value_shard,
        output_shard,
        gate_shard,
        gain_shard,
        positions.reshape(1, group_rows),
        frequency,
    )


class ShardSum:
    def __init__(self, near, far, corner, final, send_sem, recv_sem, core_only=False, deferred=False, own=None, awaited=None):
        self.near, self.far, self.corner, self.final = near, far, corner, final
        self.core_only, self.deferred = core_only, deferred
        self.own = own or functools.partial(near, 0)
        self.awaited = awaited or ((0, 0), (0, 1), (1, 0), (1, 1))
        self.send_sem, self.recv_sem = send_sem, recv_sem

    def remote(self, source, target, place, route):
        return pltpu.make_async_remote_copy(
            src_ref=source,
            dst_ref=target,
            send_sem=self.send_sem.at[place],
            recv_sem=self.recv_sem.at[place],
            device_id={"dp": shard_peer(route)},
            device_id_type=pl.DeviceIdType.MESH,
        )

    def core_copy(self, place):
        return self.remote(self.far(place), self.near(place), place, 1)

    def corner_copy(self, half):
        return self.remote(self.near(3, half), self.corner(half), 4 + half, (4, 2)[half])

    def final_copy(self, way, half):
        return self.remote(
            self.near(1 + way, half), self.final(way, half), 6 + 2 * way + half, (2, 4)[way]
        )

    def far_terms(self, term, place, count=1):
        term(4 + place, self.far(place, None, count), False, count)
        for index in reversed(range(place, place + count)):
            self.core_copy(index).start()

    def near_terms(self, term, place, count=1):
        for index in range(place, place + count):
            self.core_copy(index).wait_recv()
        term(place, self.near(place, None, count), True, count)
        if not self.core_only:
            for index in range(place, place + count):
                self.near_ready(index)

    def near_ready(self, place):
        if place == 3:
            for half in range(2):
                self.corner_copy(half).start()
        elif place:
            self.final_copy(place - 1, 2 - place).start()

    def first_terms(self, term):
        self.far_terms(term, 3)
        self.far_terms(term, 2)
        self.near_terms(term, 3)

    def other_terms(self, term):
        self.far_terms(term, 0, 2)
        self.near_terms(term, 2)
        self.near_terms(term, 0, 2)

    def take_corner(self):
        for half in range(2):
            self.corner_copy(half).wait_recv()
            add_into(self.near(1 + half, half), self.corner(half))
            if not self.deferred:
                self.final_copy(half, half).start()

    def final_arrived(self, half):
        for way in range(2):
            if (way, half) in self.awaited:
                self.final_copy(way, half).wait_recv()

    def take_final(self):
        for half in range(2):
            self.final_arrived(half)
            add_into(self.own(half), self.final(0, half), self.final(1, half))

    def take_final_turned(self, out):
        for half in range(2):
            self.final_arrived(half)
            own, first, second = self.own(half), self.final(0, half), self.final(1, half)
            rows = own.shape[0]

            def step(index):
                span = pl.ds(pl.multiple_of(index * TILE, TILE), TILE)
                value = wide(own[:, span]) + wide(first[:, span]) + wide(second[:, span])
                out[span, pl.ds(half * rows, rows)] = low(value.T)

            each(own.shape[1] // TILE, step)

    def sent(self, core=True):
        for place in range(4) if core else ():
            self.core_copy(place).wait_send()
        for half in range(2):
            self.corner_copy(half).wait_send()
            for way in range(2):
                if way != half or not self.deferred:
                    self.final_copy(way, half).wait_send()


def add_into(target, *sources):
    def step(index):
        span = pl.ds(pl.multiple_of(index * STRIP, STRIP), STRIP)
        total = wide(target[span, :])
        for source in sources:
            total = total + wide(source[span, :])
        target[span, :] = total.astype(target.dtype)

    each(target.shape[0] // STRIP, step)


def product_term(left, right):
    def term(place, target, adds, count=1):
        height, width = target.shape
        tile = 1024 if width % 1024 == 0 and count == 1 else 512
        turned = left(place * (height // count), height).T

        def step(index, carry):
            columns = pl.ds(pl.multiple_of(index * tile, tile), tile)
            value = jnp.dot(turned, right(columns, tile), preferred_element_type=jnp.float32)
            if adds:
                value = value + wide(target[:, columns])
            target[:, columns] = value.astype(target.dtype)
            return carry

        lax.fori_loop(0, target.shape[1] // tile, step, 0)

    return term


def stacked(buffer, first, height):
    def view(place, half=None, count=1):
        at = first + place * height
        if half is None:
            return buffer.at[pl.ds(at, count * height), :]
        return buffer.at[pl.ds(at + half * (height // 2), height // 2), :]

    return view


def middle_kernel(size, *refs):
    (
        attended_hbm,
        rows_hbm,
        cotangent_hbm,
        attention_scale,
        feedforward_scale,
        output_hbm,
        gate_hbm,
        up_hbm,
        down_hbm,
        mlp_out,
        inner_out,
        mixed_cot_out,
        branch_cot_out,
        grad_attended_out,
        block_out,
        grad_hidden_out,
        gate_grad_out,
        up_near_out,
        up_early_out,
        down_near_out,
        attention_gain_out,
        feedforward_gain_out,
        attended,
        tokens,
        cotangent,
        output_weight,
        gate_weight,
        up_weight,
        down_weight,
        everyone,
        gate_act,
        up_act,
        inner,
        hidden,
        branch,
        arrived,
        partial,
        total,
        load_sem,
        store_sem,
        sum_send,
        sum_recv,
        hand_send,
        hand_recv,
        shard_send,
        shard_recv,
        grad_send,
        grad_recv,
        again_sem,
        shuffle_sem,
        free_sem,
    ) = refs
    me = lax.axis_index("tensor")
    last = size - 1
    chunk_rows, model_width = tokens.shape[1], tokens.shape[2]
    units = gate_weight.shape[1]
    half_rows = chunk_rows // HALVES
    all_rows = size * chunk_rows

    greet(((me < last, me + 1), (me > 0, me - 1)))
    first_loads = [
        pltpu.make_async_copy(source, target, load_sem.at[place])
        for place, (source, target) in enumerate(
            (
                (attended_hbm, attended),
                (output_hbm, output_weight),
                (rows_hbm.at[me], tokens),
                (gate_hbm, gate_weight),
                (up_hbm, up_weight.at[pl.ds(0, up_hbm.shape[0]), :]),
                (down_hbm, down_weight.at[:, pl.ds(0, down_hbm.shape[1])]),
            )
        )
    ]
    first_loads += [
        pltpu.make_async_copy(
            cotangent_hbm.at[pl.ds(chunk * chunk_rows, chunk_rows), natural],
            cotangent.at[chunk, :, here],
            shuffle_sem.at[chunk, place],
        )
        for chunk in range(CHUNKS)
        for place, (here, natural) in enumerate(column_blocks(model_width // 8))
    ]
    for copy in first_loads[:2]:
        copy.start()
    up_flow = ShardGather(
        own_halves(up_hbm),
        row_halves(up_weight, up_hbm.shape[0]),
        shard_send.at[0],
        shard_recv.at[0],
    )
    down_flow = ShardGather(
        own_halves(down_hbm),
        column_halves(down_weight, down_hbm.shape[1]),
        shard_send.at[1],
        shard_recv.at[1],
    )
    pl.semaphore_wait(
        pltpu.get_barrier_semaphore(), 3 + jnp.minimum(me, 1) + jnp.minimum(last - me, 1)
    )
    up_flow.start(2, 4, 1)
    down_flow.start(1)

    height = model_width // 8
    again = [
        pltpu.make_async_copy(
            mlp_out.at[chunk, origin],
            down_weight.at[pl.ds((chunk * size + origin) * chunk_rows, chunk_rows), :],
            again_sem.at[chunk, origin],
        )
        for chunk in range(CHUNKS)
        for origin in range(size)
    ]
    gate_grads, up_grads = (
        ShardSum(
            stacked(buffer, 0, height),
            stacked(down_weight, 4 * height, height),
            functools.partial(stacked(buffer, 4 * height, height), 0),
            stacked(buffer, 5 * height, height),
            grad_send.at[kind],
            grad_recv.at[kind],
            deferred=kind == 1,
        )
        for kind, buffer in enumerate((gate_weight, up_weight))
    )

    down_grads = ShardSum(
        lambda place, half=None, count=1: up_act.at[
            place // 2, pl.ds(place % 2 * height, count * height), :
        ],
        stacked(down_weight, 4 * height, height),
        None,
        None,
        grad_send.at[2],
        grad_recv.at[2],
        core_only=True,
    )
    down_again = [
        pltpu.make_async_copy(
            mixed_cot_out.at[chunk, origin],
            down_weight.at[pl.ds((chunk * size + origin) * chunk_rows, chunk_rows), :],
            again_sem.at[chunk, origin],
        )
        for chunk in range(CHUNKS)
        for origin in range(size)
    ] + [
        pltpu.make_async_copy(inner_out.at[chunk], gate_act.at[chunk], again_sem.at[chunk, size])
        for chunk in range(CHUNKS)
    ]

    def signal_free(place, mask):
        pl.semaphore_signal(
            free_sem.at[place],
            inc=1,
            device_id={"dp": shard_peer(mask)},
            device_id_type=pl.DeviceIdType.MESH,
        )

    def rows_again(first, shard_width):
        return down_weight[pl.ds(0, CHUNKS * all_rows), pl.ds(first, shard_width)]

    def grad_term(act):
        def columns_of(columns, tile):
            return act[:, :, columns].reshape(CHUNKS * all_rows, tile)

        return product_term(rows_again, columns_of)

    def weights_free():
        for place, mask in enumerate((1, 2, 4)):
            signal_free(place, mask)

    def near_store(chunk):
        return pltpu.make_async_copy(
            up_act.at[chunk],
            down_near_out.at[pl.ds(chunk * all_rows, all_rows), :],
            again_sem.at[chunk, 0],
        )

    gate_store = pltpu.make_async_copy(
        gate_weight.at[pl.ds(0, height), :], gate_grad_out, store_sem.at[6, 0]
    )
    up_stores = [
        pltpu.make_async_copy(up_weight.at[pl.ds(first, count), :], target, store_sem.at[7, place])
        for place, (first, count, target) in enumerate(
            (
                (0, 3 * height, up_near_out),
                (5 * height + height // 2, height, up_early_out),
            )
        )
    ]

    def grad_turns(tick, half):
        gate_term, up_term = grad_term(gate_act), grad_term(up_act)
        if (tick, half) == (21, 0):
            for copy in again:
                copy.wait()
            for place in range(3):
                pl.semaphore_wait(free_sem.at[place], 1)
            gate_grads.first_terms(gate_term)
        elif (tick, half) == (21, 1):
            gate_grads.far_terms(gate_term, 0, 2)
            gate_grads.near_terms(gate_term, 2)
        elif (tick, half) == (22, 0):
            gate_grads.near_terms(gate_term, 0, 2)
        elif (tick, half) == (22, 1):
            for place in range(4):
                gate_grads.core_copy(place).wait_send()
            up_grads.far_terms(up_term, 3)
            up_grads.far_terms(up_term, 2)
        elif (tick, half) == (23, 0):
            gate_grads.take_corner()
            up_grads.near_terms(up_term, 3)
            up_grads.far_terms(up_term, 0, 2)
        elif (tick, half) == (23, 1):
            up_grads.near_terms(up_term, 2)
            up_grads.near_terms(up_term, 0, 2)
            signal_free(3, 1)
            for copy in down_again:
                copy.start()
        elif (tick, half) == (24, 1):
            for copy in down_again:
                copy.wait()
            for place in range(4):
                up_grads.core_copy(place).wait_send()
            pl.semaphore_wait(free_sem.at[3], 1)
            down_grads.far_terms(gate_term, 2, 2)
        elif (tick, half) == (25, 0):
            down_grads.far_terms(gate_term, 0, 2)
        elif (tick, half) == (25, 1):
            down_grads.near_terms(gate_term, 2, 2)
            near_store(1).start()
        elif (tick, half) == (26, 0):
            up_grads.take_corner()
            up_stores[0].start()
        elif (tick, half) == (26, 1):
            down_grads.near_terms(gate_term, 0, 2)
            near_store(0).start()
            gate_grads.take_final()
            gate_store.start()

    def turns(tick, half):
        if (tick, half) == (2, 1):
            up_flow.arrive(2, (0,))
            up_flow.arrive(4, (0,))
        elif (tick, half) == (3, 0):
            up_flow.arrive(2, (1,))
            up_flow.arrive(4, (1,))
            down_flow.start(2, 4)
        elif (tick, half) == (4, 1):
            up_flow.arrive(6)
        elif (tick, half) == (5, 0):
            down_flow.arrive(2, (0,))
            down_flow.arrive(4, (0,))
        elif (tick, half) == (6, 0):
            down_flow.arrive(2, (1,))
            down_flow.arrive(4, (1,))
        elif (tick, half) == (7, 0):
            down_flow.arrive(6)

    attention_gain_out[...] = jnp.zeros_like(attention_gain_out)
    feedforward_gain_out[...] = jnp.zeros_like(feedforward_gain_out)

    def half_span(half):
        return pl.ds(half * half_rows, half_rows)

    def strips(half, body):
        def step(index, carry):
            body(
                pl.ds(pl.multiple_of(half * half_rows + index * STRIP, STRIP), STRIP),
                pl.ds(pl.multiple_of(index * STRIP, STRIP), STRIP),
            )
            return carry

        lax.fori_loop(0, half_rows // STRIP, step, 0)

    def sum_copy(chunk, step, half, way, dest):
        return pltpu.make_async_remote_copy(
            src_ref=partial.at[chunk, dest, half_span(half)],
            dst_ref=arrived.at[way, chunk, step - 1, half_span(half)],
            send_sem=sum_send.at[way, chunk, step - 1, half],
            recv_sem=sum_recv.at[way, chunk, step - 1, half],
            device_id={"tensor": me + 1 - 2 * way},
            device_id_type=pl.DeviceIdType.MESH,
        )

    def hand_copy(chunk, hop, half, way, origin):
        rows = everyone.at[origin, chunk, half_span(half)]
        return pltpu.make_async_remote_copy(
            src_ref=rows,
            dst_ref=rows,
            send_sem=hand_send.at[way, chunk, hop - 1, half],
            recv_sem=hand_recv.at[way, chunk, hop - 1, half],
            device_id={"tensor": me + 1 - 2 * way},
            device_id_type=pl.DeviceIdType.MESH,
        )

    def away(way):
        return me if way == 0 else last - me

    def sum_step(chunk, step, half):
        for way in range(2):
            distance = away(way)

            @pl.when(distance <= step - 1)
            def _():
                dest = me + size - step if way == 0 else me - size + step
                if step > 1:

                    @pl.when(distance >= 1)
                    def _():
                        sum_copy(chunk, step - 1, half, way, dest).wait_recv()

                        def add(rows, _):
                            partial[chunk, dest, rows] = low(
                                wide(partial[chunk, dest, rows])
                                + wide(arrived[way, chunk, step - 2, rows])
                            )

                        strips(half, add)

                sum_copy(chunk, step, half, way, dest).start()

    def sum_end(chunk, half):
        def begin(rows, here):
            total[here] = wide(partial[chunk, me, rows])

        strips(half, begin)
        for way in range(2):

            @pl.when(away(way) >= 1)
            def _():
                sum_copy(chunk, size - 1, half, way, me).wait_recv()

                def add(rows, here):
                    total[here] = total[here] + wide(arrived[way, chunk, size - 2, rows])

                strips(half, add)

    def sum_sent(chunk):
        for step in range(1, size):
            for way in range(2):

                @pl.when(away(way) <= step - 1)
                def _():
                    for half in range(HALVES):
                        sum_copy(chunk, step, half, way, 0).wait_send()

    def hand_first(chunk, half):
        for way in range(2):

            @pl.when(away(1 - way) >= 1)
            def _():
                hand_copy(chunk, 1, half, way, me).start()

    def hand_on(chunk, hop, half):
        for way in range(2):

            @pl.when(away(way) >= hop)
            def _():
                origin = me - hop if way == 0 else me + hop
                hand_copy(chunk, hop, half, way, origin).wait_recv()
                if hop < size - 1:

                    @pl.when(away(1 - way) >= 1)
                    def _():
                        hand_copy(chunk, hop + 1, half, way, origin).start()

    def hand_sent(chunk):
        for hop in range(1, size):
            for way in range(2):

                @pl.when(jnp.logical_and(away(way) >= hop - 1, away(1 - way) >= 1))
                def _():
                    for half in range(HALVES):
                        hand_copy(chunk, hop, half, way, 0).wait_send()

    def inverse_rms(values):
        return lax.rsqrt(jnp.mean(values * values, -1, keepdims=True) + EPS)

    def fold(values):
        return values[:8] + values[8:]

    def own_rows(chunk, stage, half):
        def after_branch(rows, here):
            value = total[here]
            branch[chunk, rows] = value
            state = wide(tokens[chunk, rows]) + value * inverse_rms(value) * attention_scale[...]
            hidden[chunk, rows] = state
            everyone[me, chunk, rows] = low(state)

        def after_mixed(rows, here):
            value = total[here]
            inverse = inverse_rms(value)
            normalized = value * inverse
            hidden[chunk, rows] = hidden[chunk, rows] + normalized * feedforward_scale[...]
            grad = wide(cotangent[chunk, rows])
            feedforward_gain_out[...] += fold(grad * normalized)
            everyone[me, chunk, rows] = low(
                norm_backward(grad, normalized, inverse, feedforward_scale[...])
            )

        def after_gradient(rows, here):
            grad = total[here] + wide(cotangent[chunk, rows])
            value = branch[chunk, rows]
            inverse = inverse_rms(value)
            normalized = value * inverse
            branch[chunk, rows] = grad
            attention_gain_out[...] += fold(grad * normalized)
            everyone[me, chunk, rows] = low(
                norm_backward(grad, normalized, inverse, attention_scale[...])
            )

        strips(half, (after_branch, after_mixed, after_gradient)[stage])

    def gathered(chunk):
        return everyone[:, chunk].reshape(all_rows, model_width)

    def tiles(first, end, body):
        def step(index, carry):
            body(pl.ds(pl.multiple_of(index * WIDE_TILE, WIDE_TILE), WIDE_TILE))
            return carry

        lax.fori_loop(first, end, step, 0)

    def store(kind, chunk):
        source, target = (
            (everyone.at[:, chunk], mlp_out.at[chunk]),
            (inner, inner_out.at[chunk]),
            (everyone.at[:, chunk], mixed_cot_out.at[chunk]),
            (everyone.at[:, chunk], branch_cot_out.at[:, chunk]),
            (attended.at[:, chunk], grad_attended_out.at[:, chunk]),
            (branch.at[chunk], grad_hidden_out.at[chunk]),
        )[kind]
        return pltpu.make_async_copy(source, target, store_sem.at[kind, chunk])

    def block_stores(chunk):
        return [
            pltpu.make_async_copy(
                hidden.at[chunk, :, here],
                block_out.at[pl.ds(chunk * chunk_rows, chunk_rows), natural],
                shuffle_sem.at[chunk, place],
            )
            for place, (here, natural) in enumerate(column_blocks(model_width // 8))
        ]

    def put_partial(chunk, columns, values):
        partial[chunk, :, :, columns] = low(values).reshape(size, chunk_rows, WIDE_TILE)

    def branch_terms(chunk):
        def tile(columns):
            rows = attended[:, chunk].reshape(all_rows, attended.shape[-1])
            put_partial(
                chunk,
                columns,
                jnp.dot(rows, output_weight[:, columns], preferred_element_type=jnp.float32),
            )

        tiles(0, model_width // WIDE_TILE, tile)

    def gate_tile(chunk):
        def tile(columns):
            rows = gathered(chunk)
            gate = jnp.dot(rows, gate_weight[:, columns], preferred_element_type=jnp.float32)
            up = jnp.dot(rows, up_weight[:, columns], preferred_element_type=jnp.float32)
            gate_act[chunk, :, columns] = low(gate)
            up_act[chunk, :, columns] = low(up)
            inner[:, columns] = low(gate * jax.nn.sigmoid(gate) * up)

        return tile

    def down_tile(chunk):
        def tile(columns):
            put_partial(
                chunk,
                columns,
                jnp.dot(inner[...], down_weight[:, columns], preferred_element_type=jnp.float32),
            )

        return tile

    def grad_inner_tile(chunk):
        def tile(columns):
            grad = rows_product(gathered(chunk), down_weight[columns, :])
            gate = wide(gate_act[chunk, :, columns])
            up = wide(up_act[chunk, :, columns])
            sigmoid = jax.nn.sigmoid(gate)
            gate_act[chunk, :, columns] = low(
                grad * up * sigmoid * (1.0 + gate * (1.0 - sigmoid))
            )
            up_act[chunk, :, columns] = low(grad * gate * sigmoid)

        return tile

    def grad_inner_half_tile(chunk, half):
        spans = [
            pl.ds(origin * chunk_rows + half * half_rows, half_rows) for origin in range(size)
        ]

        def tile(columns):
            rows = everyone[:, chunk, half_span(half)].reshape(size * half_rows, model_width)
            grad = rows_product(rows, down_weight[columns, :])
            gate = wide(jnp.concatenate([gate_act[chunk, span, columns] for span in spans], 0))
            up = wide(jnp.concatenate([up_act[chunk, span, columns] for span in spans], 0))
            sigmoid = jax.nn.sigmoid(gate)
            for_gate = low(grad * up * sigmoid * (1.0 + gate * (1.0 - sigmoid)))
            for_up = low(grad * gate * sigmoid)
            for origin, span in enumerate(spans):
                here = slice(origin * half_rows, (origin + 1) * half_rows)
                gate_act[chunk, span, columns] = for_gate[here]
                up_act[chunk, span, columns] = for_up[here]

        return tile

    def grad_input_tile(chunk):
        def tile(columns):
            put_partial(
                chunk,
                columns,
                rows_product(gate_act[chunk], gate_weight[columns, :])
                + rows_product(up_act[chunk], up_weight[columns, :]),
            )

        return tile

    unit_tiles, width_tiles = units // WIDE_TILE, model_width // WIDE_TILE

    def forward_piece(chunk, piece):
        if piece == 0:
            if chunk == 0:
                for mask in (1, 3, 5, 7):
                    up_flow.arrive(mask)
                for copy in first_loads[3:6]:
                    copy.wait()
            store(0, chunk).start()
            tiles(0, unit_tiles // 2, gate_tile(chunk))
        elif piece == 1:
            tiles(unit_tiles // 2, unit_tiles, gate_tile(chunk))
            store(1, chunk).start()
            sum_sent(chunk)
            hand_sent(chunk)
        else:
            if chunk == 0:
                for mask in (1, 3, 5, 7):
                    down_flow.arrive(mask)
            tiles(0, width_tiles, down_tile(chunk))
            store(0, chunk).wait()
            store(1, chunk).wait()

    def backward_piece(chunk, piece):
        if piece == 0:
            store(2, chunk).start()
            for copy in block_stores(chunk):
                copy.start()
            tiles(0, unit_tiles // 2, grad_inner_half_tile(chunk, 1))
            tiles(unit_tiles // 2, unit_tiles, grad_inner_tile(chunk))
            if chunk == CHUNKS - 1:
                down_flow.sent()
                for copy in again:
                    copy.start()
        elif piece == 1:
            sum_sent(chunk)
            hand_sent(chunk)
            tiles(0, width_tiles // 2, grad_input_tile(chunk))
        else:
            tiles(width_tiles // 2, width_tiles, grad_input_tile(chunk))
            store(2, chunk).wait()
            for copy in block_stores(chunk):
                copy.wait()
            if chunk == CHUNKS - 1:
                up_flow.sent()
                weights_free()

    def end_piece(chunk, piece):
        if piece == 0:
            store(3, chunk).start()
            store(5, chunk).start()
            for first in range(0, attended.shape[-1], TILE):
                columns = pl.ds(first, TILE)
                value = rows_product(gathered(chunk), output_weight[columns, :])
                attended[:, chunk, :, columns] = low(value).reshape(size, chunk_rows, TILE)
            store(4, chunk).start()

    first_loads[0].wait()
    first_loads[1].wait()
    for copy in first_loads[2:]:
        copy.start()
    branch_terms(0)
    first_loads[2].wait()
    for copy in first_loads[6:]:
        copy.wait()
    bases = {
        (chunk, stage): (CHUNKS * stage + chunk) * size
        for stage in range(3)
        for chunk in range(CHUNKS)
    }
    ticks = max(bases.values()) + 2 * size
    for tick in range(1, ticks + 1):
        for half in range(HALVES):
            for (chunk, stage), base in bases.items():
                at = tick - base
                if size < at < 2 * size:
                    hand_on(chunk, at - size, half)
            for (chunk, stage), base in bases.items():
                at = tick - base
                if 1 <= at < size:
                    sum_step(chunk, at, half)
                elif at == size:
                    sum_end(chunk, half)
                    own_rows(chunk, stage, half)
                    hand_first(chunk, half)
            turns(tick, half)
            if tick == 1 and half == 1:
                branch_terms(1)
            for (chunk, stage), base in bases.items():
                piece = (tick - base - 2 * size + 1) * HALVES + half - 1
                if piece == -1 and stage == 1:
                    tiles(0, unit_tiles // 2, grad_inner_half_tile(chunk, 0))
                elif 0 <= piece < 3:
                    (forward_piece, backward_piece, end_piece)[stage](chunk, piece)
            grad_turns(tick, half)
    for half in range(2):
        up_grads.final_copy(1 - half, half).wait_recv()
    up_stores[1].start()
    gate_grads.sent(False)
    up_grads.sent(False)
    for place in range(4):
        down_grads.core_copy(place).wait_send()
    for chunk in range(CHUNKS):
        sum_sent(chunk)
        hand_sent(chunk)
        store(3, chunk).wait()
        store(4, chunk).wait()
        store(5, chunk).wait()
        near_store(chunk).wait()
    for copy in [gate_store] + up_stores:
        copy.wait()


def middle(
    attended,
    rows_all,
    cotangent_grouped,
    attention_scale,
    feedforward_scale,
    output_full,
    gate_full,
    up_shard,
    down_shard,
):
    size = lax.axis_size("tensor")
    own_rows, model_width = cotangent_grouped.shape
    chunk_rows = own_rows // CHUNKS
    all_rows = size * chunk_rows
    half_rows = chunk_rows // HALVES
    heads_width = attended.shape[1]
    units = gate_full.shape[1]
    chunked = (CHUNKS, chunk_rows, model_width)
    lined = (CHUNKS, size, chunk_rows, model_width)
    low_type, wide_type = jnp.bfloat16, jnp.float32

    def shape(dims, kind=low_type):
        return jax.ShapeDtypeStruct(dims, kind)

    anywhere = pl.BlockSpec(memory_space=pl.ANY)
    inside = pl.BlockSpec(memory_space=pltpu.VMEM)
    dma = pltpu.SemaphoreType.DMA
    flops = 2 * CHUNKS * all_rows * model_width * (2 * heads_width + 6 * units)
    outs = pl.pallas_call(
        functools.partial(middle_kernel, size),
        out_shape=[
            shape(lined),
            shape((CHUNKS, all_rows, units)),
            shape(lined),
            shape((size, CHUNKS, chunk_rows, model_width)),
            shape((size, CHUNKS, chunk_rows, heads_width)),
            shape((own_rows, model_width), wide_type),
            shape(chunked, wide_type),
            shape((model_width // 8, units)),
            shape((3 * model_width // 8, units)),
            shape((model_width // 8, units)),
            shape((model_width // 2, units)),
            shape((8, model_width), wide_type),
            shape((8, model_width), wide_type),
        ],
        in_specs=[anywhere] * 3 + [inside] * 2 + [anywhere] * 4,
        out_specs=[anywhere] * 11 + [inside] * 2,
        scratch_shapes=[
            pltpu.VMEM((size, CHUNKS, chunk_rows, heads_width), low_type),
            pltpu.VMEM(chunked, low_type),
            pltpu.VMEM(chunked, low_type),
            pltpu.VMEM((heads_width, model_width), low_type),
            pltpu.VMEM((model_width, units), low_type),
            pltpu.VMEM((model_width, units), low_type),
            pltpu.VMEM((units, model_width), low_type),
            pltpu.VMEM((size, CHUNKS, chunk_rows, model_width), low_type),
            pltpu.VMEM((CHUNKS, all_rows, units), low_type),
            pltpu.VMEM((CHUNKS, all_rows, units), low_type),
            pltpu.VMEM((all_rows, units), low_type),
            pltpu.VMEM(chunked, wide_type),
            pltpu.VMEM(chunked, wide_type),
            pltpu.VMEM((2, CHUNKS, size - 1, chunk_rows, model_width), low_type),
            pltpu.VMEM(lined, low_type),
            pltpu.VMEM((half_rows, model_width), wide_type),
            dma((6,)),
            dma((8, CHUNKS)),
            dma((2, CHUNKS, size - 1, HALVES)),
            dma((2, CHUNKS, size - 1, HALVES)),
            dma((2, CHUNKS, size - 1, HALVES)),
            dma((2, CHUNKS, size - 1, HALVES)),
            dma((2, 7, 2)),
            dma((2, 7, 2)),
            dma((3, 10)),
            dma((3, 10)),
            dma((CHUNKS, size + 1)),
            dma((CHUNKS, 8)),
            pltpu.SemaphoreType.REGULAR((4,)),
        ],
        compiler_params=pltpu.CompilerParams(
            collective_id=1, has_side_effects=True, vmem_limit_bytes=VMEM_BYTES
        ),
        cost_estimate=pl.CostEstimate(
            flops=flops, bytes_accessed=64 << 20, transcendentals=0
        ),
        name="middle",
    )(
        attended.reshape(size, CHUNKS, chunk_rows, heads_width),
        rows_all.reshape(size, *chunked),
        cotangent_grouped,
        attention_scale,
        feedforward_scale,
        output_full,
        gate_full,
        up_shard,
        down_shard,
    )
    rows = CHUNKS * all_rows
    return (
        outs[3].reshape(rows, model_width),
        outs[4].reshape(rows, heads_width),
        outs[5],
        outs[6].reshape(own_rows, model_width),
        *outs[7:],
    )


def back_kernel(
    size,
    branch_cot_hbm,
    grad_attended_hbm,
    query_rot_hbm,
    key_rot_hbm,
    value_hbm,
    query_hat_hbm,
    key_hat_hbm,
    cosine_hbm,
    sine_hbm,
    down_near_hbm,
    up_near,
    up_early,
    attended_hbm,
    weight_hbm,
    rows_hbm,
    hidden_hbm,
    stats,
    query_scale,
    key_scale,
    attention_gain,
    feedforward_gain,
    tokens_out,
    up_out,
    down_out,
    output_out,
    query_out,
    key_out,
    value_out,
    gain_out,
    left,
    attended,
    weight,
    grad,
    gain,
    shared,
    hidden,
    partial,
    arrived,
    far,
    down_near,
    output_far,
    output_near,
    attention_near,
    gain_far,
    gain_near,
    up_final,
    wide_total,
    down_total,
    output_total,
    load_sem,
    store_sem,
    share_send,
    share_recv,
    sum_send,
    sum_recv,
    shard_send,
    shard_recv,
):
    me = lax.axis_index("tensor")
    last = size - 1
    own_rows, model_width = partial.shape[1:]
    group_rows = size * own_rows
    local_width = attended.shape[1]
    heads = local_width // 128
    piece_rows = own_rows // PIECES
    height = model_width // 8
    greet([(True, lax.rem(me + offset, size)) for offset in range(1, size)])

    def beside(index):
        return pl.ds(index * local_width, local_width)

    pairs = [
        (grad_attended_hbm, output_far),
        (key_rot_hbm, partial.at[:, :, beside(1)]),
        (query_rot_hbm, partial.at[:, :, beside(0)]),
        (value_hbm, partial.at[:, :, beside(2)]),
        (attended_hbm, attended),
        (query_hat_hbm, partial.at[:, :, beside(3)]),
        (cosine_hbm, wide_total.at[pl.ds(0, group_rows), pl.ds(0, 128)]),
        (sine_hbm, wide_total.at[pl.ds(0, group_rows), pl.ds(128, 128)]),
    ]
    pairs += [
        (key_hat_hbm.at[origin], far.at[pl.ds(3 * height, own_rows), beside(origin)])
        for origin in range(size)
    ]
    first_count = len(pairs)
    pairs += [
        (down_near_hbm, down_near.at[pl.ds(0, 4 * height), :]),
        (weight_hbm, weight),
        (branch_cot_hbm, left),
        (up_near.at[pl.ds(0, height), :], up_final.at[pl.ds(2 * height, height), :]),
        (up_early, up_final.at[pl.ds(height // 2, height), :]),
        (rows_hbm, left),
        (hidden_hbm, hidden),
    ]
    loads = [
        pltpu.make_async_copy(source, target, load_sem.at[place])
        for place, (source, target) in enumerate(pairs)
    ]
    near_load, weight_load, left_load, own_load, early_load, rows_load, hidden_load = loads[
        first_count:
    ]
    for copy in loads[:first_count]:
        copy.start()

    def flow(kind, near, far_view, shard_height):
        return ShardSum(
            stacked(near, 0, shard_height),
            far_view,
            lambda half: stacked(near, 4 * shard_height, shard_height)(0, half),
            lambda way, half: stacked(near, 5 * shard_height, shard_height)(way, half),
            shard_send.at[kind],
            shard_recv.at[kind],
        )

    down_flow = flow(0, down_near, None, height)
    output_flow = flow(1, output_near, stacked(output_far, 0, height), height)
    attention_flow = flow(
        2,
        attention_near,
        lambda place, half=None, count=1: far.at[
            pl.ds(place * height, count * height), pl.ds(0, 3 * local_width)
        ],
        height,
    )
    gain_height = gain.shape[0] // 8
    gain_flow = flow(3, gain_near, stacked(gain_far, 0, gain_height), gain_height)
    up_flow = ShardSum(
        stacked(up_near, 0, height),
        None,
        None,
        stacked(up_final, 0, height),
        shard_send.at[4],
        shard_recv.at[4],
        own=functools.partial(stacked(up_final, 2 * height, height), 0),
        awaited=((0, 0), (1, 1)),
    )

    def columns_of(source):
        return lambda first, width: source[:, pl.ds(first, width)]

    output_term = product_term(columns_of(left), lambda columns, _: attended[:, columns])
    attention_term = product_term(columns_of(left), lambda columns, _: grad[:, columns])

    def gain_term(place, target, adds, count):
        value = gain[pl.ds(place * gain_height, target.shape[0]), :]
        target[...] = value + target[...] if adds else value

    def away(way):
        return me if way == 0 else last - me

    def held(kind, head):
        return pl.ds(pl.multiple_of(kind * local_width + head * 128, 128), 128)

    score_scale = 128**-0.5
    query_grad, key_grad = pl.ds(0, 128), pl.ds(128, 128)

    def product_columns(kind, origin):
        return pl.ds((kind * size + origin) * 128, 128)

    def step_head(head):
        span = head_span(head)
        for origin in reversed(range(size)):
            count = (origin + 1) * own_rows
            here = pl.ds(origin * own_rows, own_rows)
            seen = pl.ds(0, origin + 1)
            keys = partial[seen, :, held(1, head)].reshape(count, 128)
            values = partial[seen, :, held(2, head)].reshape(count, 128)
            queries = partial[origin, :, held(0, head)]
            grad_rows = output_far[here, span]
            delta = column_sums(wide(grad_rows) * wide(attended[here, span]))
            probs = jnp.exp(
                rows_product(keys, queries) * score_scale - stats[pl.ds(head, 1), here]
            )
            near = probs[origin * own_rows :]
            near = jnp.where(ahead_of(near, 0, 0), 0.0, near)
            probs = jnp.concatenate([probs[: origin * own_rows], near], 0) if origin else near
            grad_scores = low(probs * (rows_product(values, grad_rows) - delta))
            for_values = jnp.dot(low(probs), grad_rows, preferred_element_type=jnp.float32)
            for_keys = jnp.dot(grad_scores, queries, preferred_element_type=jnp.float32)
            for_queries = jnp.dot(keys.T, grad_scores, preferred_element_type=jnp.float32)
            wide_total[pl.ds(group_rows + origin * own_rows, own_rows), query_grad] = (
                for_queries * score_scale
            ).T
            first = origin == size - 1
            at = pl.ds(group_rows, count)
            wide_total[at, key_grad] = for_keys if first else wide_total[at, key_grad] + for_keys
            for block in range(origin + 1):
                term = for_values[block * own_rows : (block + 1) * own_rows]
                columns = product_columns(2, block)
                hidden[:, columns] = term if first else hidden[:, columns] + term
        for kind, (factor, scale) in enumerate(((1.0, query_scale), (score_scale, key_scale))):
            gain_total = jnp.zeros((1, 128), jnp.float32)
            for origin in range(size):
                here = pl.ds(origin * own_rows, own_rows)
                source = wide_total[
                    pl.ds(group_rows + origin * own_rows, own_rows), (query_grad, key_grad)[kind]
                ]
                rotated = wide(low(source * factor))
                normal = rotated * wide_total[here, pl.ds(0, 128)]
                normal = normal - pltpu.roll(rotated, 64, 1) * wide_total[here, pl.ds(128, 128)]
                hats = hat_of(kind, origin, head)
                gain_total = gain_total + jnp.sum(normal * hats, 0, keepdims=True)
                normal = normal * scale[pl.ds(head, 1), :]
                grad[here, held(kind, head)] = low(normal)
                hidden[:, product_columns(kind, origin)] += normal * hats
            gain[pl.ds(kind * heads + head, 1), :] = gain_total
        for origin in range(size):
            grad[pl.ds(origin * own_rows, own_rows), held(2, head)] = low(
                hidden[:, product_columns(2, origin)]
            )

    def hat_of(kind, origin, head):
        if kind == 0:
            return wide(partial[origin, :, held(3, head)])
        return wide(far[pl.ds(3 * height, own_rows), held(origin, head)])

    def share_copy(offset):
        return pltpu.make_async_remote_copy(
            src_ref=shared.at[me],
            dst_ref=shared.at[me],
            send_sem=share_send.at[offset - 1],
            recv_sem=share_recv.at[offset - 1],
            device_id={"tensor": lax.rem(me + offset, size)},
            device_id_type=pl.DeviceIdType.MESH,
        )

    def share():
        half_width = model_width // 2
        lines = [
            jnp.concatenate(
                [column_sums(hidden[:, product_columns(kind, origin)]) for origin in range(size)],
                1,
            )
            for kind in range(2)
        ]
        for part in (attention_gain, feedforward_gain):
            total = jnp.sum(part[...], 0, keepdims=True)
            lines += [total[:, :half_width], total[:, half_width:]]
        lines.append(jnp.zeros((2, half_width), jnp.float32))
        shared[me] = jnp.concatenate(lines, 0)
        for offset in range(1, size):
            share_copy(offset).start()

    def take_shares():
        for offset in range(1, size):
            share_copy(offset).wait_recv()
        total = shared[0]
        for device in range(1, size):
            total = total + shared[device]
        for kind in range(2):
            for origin in range(size):
                here = pl.ds(origin * own_rows, own_rows)
                columns = slice(origin * own_rows, (origin + 1) * own_rows)
                inner_column = turned_rows(total[kind : kind + 1, columns] / model_width)
                inverse = turned_rows(stats[pl.ds(heads + kind, 1), here])
                for head in range(heads):
                    span = pl.ds((kind * heads + head) * 128, 128)
                    hats = hat_of(kind, origin, head)
                    grad[here, span] = low(inverse * (wide(grad[here, span]) - hats * inner_column))
        for place in range(8):
            if place:
                gain[pl.ds(place * gain_height, 8), :] = gain[pl.ds(0, 8), :]
            for kind in range(2):
                for line in range(height // 128):
                    row, first = divmod(place * height + line * 128, model_width // 2)
                    gain[
                        pl.ds(place * gain_height + 8 + kind * (height // 128) + line, 1), :
                    ] = total[2 + 2 * kind + row : 3 + 2 * kind + row, first : first + 128]

    def terms(dest, count):
        span = pl.ds(pl.multiple_of(dest * own_rows, own_rows), count * own_rows)

        def step(index):
            columns = pl.ds(pl.multiple_of(index * WIDE_TILE, WIDE_TILE), WIDE_TILE)
            value = low(rows_product(grad[span, :], weight[columns, :]))
            partial[pl.ds(dest, count), :, columns] = value.reshape(count, own_rows, WIDE_TILE)

        each(model_width // WIDE_TILE, step)

    low_side = 1 - 2 * me // size

    def first_terms():
        terms(last * low_side, 1)

    def other_terms():
        terms(1 - low_side, last)

    def span_of(piece):
        return pl.ds(piece * piece_rows, piece_rows)

    def sum_copy(step, piece, way, dest):
        return pltpu.make_async_remote_copy(
            src_ref=partial.at[dest, span_of(piece)],
            dst_ref=arrived.at[way, step - 1, span_of(piece)],
            send_sem=sum_send.at[way, step - 1, piece],
            recv_sem=sum_recv.at[way, step - 1, piece],
            device_id={"tensor": me + 1 - 2 * way},
            device_id_type=pl.DeviceIdType.MESH,
        )

    def sum_step(step, *pieces):
        for piece in pieces:
            for way in range(2):
                distance = away(way)

                @pl.when(distance <= step - 1)
                def _():
                    dest = me + size - step if way == 0 else me - size + step
                    if step > 1:

                        @pl.when(distance >= 1)
                        def _():
                            sum_copy(step - 1, piece, way, dest).wait_recv()
                            add_into(
                                partial.at[dest, span_of(piece)],
                                arrived.at[way, step - 2, span_of(piece)],
                            )

                    sum_copy(step, piece, way, dest).start()

    def token_stores(piece):
        return [
            pltpu.make_async_copy(
                hidden.at[span_of(piece), here],
                tokens_out.at[span_of(piece), natural],
                store_sem.at[1 + piece, place],
            )
            for place, (here, natural) in enumerate(column_blocks(height))
        ]

    def sum_end(*pieces):
        for piece in pieces:
            add_into(hidden.at[span_of(piece)], partial.at[me, span_of(piece)])
            for way in range(2):

                @pl.when(away(way) >= 1)
                def _():
                    sum_copy(size - 1, piece, way, me).wait_recv()
                    add_into(
                        hidden.at[span_of(piece)], arrived.at[way, size - 2, span_of(piece)]
                    )

            for copy in token_stores(piece):
                copy.start()

    up_store = pltpu.make_async_copy(
        up_final.at[pl.ds(2 * height, height), :], up_out, store_sem.at[0, 0]
    )
    down_store = pltpu.make_async_copy(down_total, down_out, store_sem.at[0, 1])
    output_store = pltpu.make_async_copy(output_total, output_out, store_sem.at[0, 2])
    attention_stores = [
        pltpu.make_async_copy(
            attention_near.at[pl.ds(0, height), beside(kind)], out, store_sem.at[0, 3 + kind]
        )
        for kind, out in enumerate((query_out, key_out, value_out))
    ]

    gain[...] = jnp.zeros_like(gain)
    hidden[...] = jnp.zeros_like(hidden)
    pl.semaphore_wait(pltpu.get_barrier_semaphore(), 3 + size - 1)
    for half in range(2):
        up_flow.final_copy(half, half).start()
    for copy in loads[:first_count]:
        copy.wait()
    for copy in (near_load, left_load, weight_load, own_load, early_load):
        copy.start()
    def step_pair(index):
        step_head(2 * index)
        step_head(2 * index + 1)

    each(heads // 4, step_pair)
    near_load.wait()
    for place in (3, 1, 2):
        down_flow.near_ready(place)
    each(heads // 4, lambda index: step_pair(heads // 4 + index))
    share()
    hidden_load.start()
    left_load.wait()
    output_flow.first_terms(output_term)
    take_shares()
    weight_load.wait()
    first_terms()
    sum_step(1, *range(PIECES))
    output_flow.other_terms(output_term)
    rows_load.start()
    down_flow.take_corner()
    other_terms()
    sum_step(2, 0)
    own_load.wait()
    early_load.wait()
    up_flow.take_final()
    up_store.start()
    gain_flow.first_terms(gain_term)
    gain_flow.other_terms(gain_term)
    rows_load.wait()
    attention_flow.first_terms(attention_term)
    sum_step(2, 1)
    output_flow.take_corner()
    sum_step(2, 2)
    attention_flow.other_terms(attention_term)
    sum_step(2, 3)
    sum_step(3, 0)
    gain_flow.take_corner()
    sum_step(3, 1)
    sum_step(3, 2)
    sum_step(3, 3)
    hidden_load.wait()
    attention_flow.take_corner()
    output_flow.take_final_turned(output_total)
    output_store.start()
    gain_flow.take_final()
    gain_out[...] = gain_near[pl.ds(0, gain_height), :]
    sum_end(0)
    sum_end(1)
    down_flow.take_final_turned(down_total)
    down_store.start()
    sum_end(2)
    attention_flow.take_final()
    for copy in attention_stores:
        copy.start()
    sum_end(3)
    down_flow.sent(False)
    for shard_flow in (output_flow, attention_flow, gain_flow):
        shard_flow.sent()
    for half in range(2):
        up_flow.final_copy(half, half).wait_send()
    for offset in range(1, size):
        share_copy(offset).wait_send()
    for step in range(1, size):
        for way in range(2):

            @pl.when(away(way) <= step - 1)
            def _():
                for piece in range(PIECES):
                    sum_copy(step, piece, way, 0).wait_send()

    for copy in [up_store, down_store, output_store] + attention_stores:
        copy.wait()
    for piece in range(PIECES):
        for copy in token_stores(piece):
            copy.wait()


def back(
    branch_cot,
    grad_attended,
    query_rot,
    key_rot,
    value_rows,
    query_hat,
    key_hat,
    cosine,
    sine,
    down_near,
    up_near,
    up_early,
    attended,
    attention_full,
    rows_all,
    grad_hidden,
    *small,
):
    size = lax.axis_size("tensor")
    own_rows, model_width = grad_hidden.shape
    group_rows = size * own_rows
    height = model_width // 8
    local_width, units = attended.shape[1], down_near.shape[1]
    low_type, wide_type = jnp.bfloat16, jnp.float32
    anywhere = pl.BlockSpec(memory_space=pl.ANY)
    inside = pl.BlockSpec(memory_space=pltpu.VMEM)
    dma = pltpu.SemaphoreType.DMA
    by_device = (size, own_rows, local_width)

    def shape(*dims):
        return jax.ShapeDtypeStruct(dims, wide_type)

    def low_shape(*dims):
        return jax.ShapeDtypeStruct(dims, low_type)

    return pl.pallas_call(
        functools.partial(back_kernel, size),
        out_shape=[
            shape(own_rows, model_width),
            low_shape(height, units),
            low_shape(units, height),
            low_shape(local_width, height),
            *[low_shape(height, local_width)] * 3,
            shape(32, 128),
        ],
        in_specs=[anywhere] * 16 + [inside] * len(small),
        out_specs=[anywhere] * 7 + [inside],
        scratch_shapes=[
            pltpu.VMEM((group_rows, model_width), low_type),
            pltpu.VMEM((group_rows, local_width), low_type),
            pltpu.VMEM((model_width, 3 * local_width), low_type),
            pltpu.VMEM((group_rows, 3 * local_width), low_type),
            pltpu.VMEM((8 * 32, 128), wide_type),
            pltpu.VMEM((size, 8, model_width // 2), wide_type),
            pltpu.VMEM((own_rows, model_width), wide_type),
            pltpu.VMEM((size, own_rows, model_width), low_type),
            pltpu.VMEM((2, size - 1, own_rows, model_width), low_type),
            pltpu.VMEM((4 * height, units), low_type),
            pltpu.VMEM((7 * height, units), low_type),
            pltpu.VMEM((4 * height, local_width), low_type),
            pltpu.VMEM((7 * height, local_width), low_type),
            pltpu.VMEM((7 * height, 3 * local_width), low_type),
            pltpu.VMEM((4 * 32, 128), wide_type),
            pltpu.VMEM((7 * 32, 128), wide_type),
            pltpu.VMEM((3 * height, units), low_type),
            pltpu.VMEM((2 * group_rows, 256), wide_type),
            pltpu.VMEM((units, height), low_type),
            pltpu.VMEM((local_width, height), low_type),
            dma((15 + size,)),
            dma((1 + PIECES, 8)),
            dma((size - 1,)),
            dma((size - 1,)),
            dma((2, size - 1, PIECES)),
            dma((2, size - 1, PIECES)),
            dma((5, 10)),
            dma((5, 10)),
        ],
        compiler_params=pltpu.CompilerParams(
            collective_id=2, has_side_effects=True, vmem_limit_bytes=VMEM_BYTES
        ),
        cost_estimate=pl.CostEstimate(
            flops=2 * group_rows * model_width * (units + 8 * local_width),
            bytes_accessed=48 << 20,
            transcendentals=group_rows**2 * local_width // 128,
        ),
        name="back",
    )(
        branch_cot,
        grad_attended,
        query_rot.reshape(by_device),
        key_rot.reshape(by_device),
        value_rows.reshape(by_device),
        query_hat.reshape(by_device),
        key_hat.reshape(by_device),
        cosine,
        sine,
        down_near,
        up_near,
        up_early,
        attended,
        attention_full,
        rows_all,
        grad_hidden,
        *small,
    )


def finish_kernel(count, *refs):
    sources, gain, refs = refs[:count], refs[count], refs[count + 1 :]
    targets, head_outs, norm_outs = refs[:count], refs[count : count + 2], refs[count + 2 : count + 4]
    buffers, sem = refs[count + 4 : 2 * count + 4], refs[-1]
    wides = list(refs[2 * count + 4 : -1])
    outgoing = [buffer if buffer.dtype == jnp.float32 else wides.pop(0) for buffer in buffers]
    loads, stores = [], []
    for place, (source, buffer, wider, target) in enumerate(
        zip(sources, buffers, outgoing, targets)
    ):
        rows = source.shape[0] // 2
        for half in range(2):
            span = pl.ds(half * rows, rows)
            here = buffer.at[span, :], wider.at[span, :]
            loads.append(
                pltpu.make_async_copy(source.at[span, :], here[0], sem.at[half, place])
            )
            stores.append(
                (here, pltpu.make_async_copy(here[1], target.at[span, :], sem.at[2 + half, place]))
            )
    for copy in loads[:WINDOW]:
        copy.start()
    heads, channels = head_outs[0].shape
    shift = lax.rem(128 - lax.axis_index("dp") * channels, 128)
    own = pltpu.roll(gain[pl.ds(0, 2 * heads), :], shift, 1)
    lines = norm_outs[0].shape[0]
    for kind in range(2):
        head_outs[kind][...] = own[kind * heads : (kind + 1) * heads, :channels]
        at = 2 * heads + kind * lines
        norm_outs[kind][...] = gain[pl.ds(at, lines), :]
    for place, (load, (here, store)) in enumerate(zip(loads, stores)):
        load.wait()
        if place + WINDOW < len(loads):
            loads[place + WINDOW].start()
        if here[0].dtype != here[1].dtype:
            widen(*here)
        store.start()
    for _, copy in stores:
        copy.wait()


def widen(source, target):
    def step(index):
        span = pl.ds(pl.multiple_of(index * STRIP, STRIP), STRIP)
        target[span, :] = wide(source[span, :])

    each(source.shape[0] // STRIP, step)


def finish(gain_part, head_shape, lines, *arrays):
    anywhere = pl.BlockSpec(memory_space=pl.ANY)
    inside = pl.BlockSpec(memory_space=pltpu.VMEM)
    count = len(arrays)
    return pl.pallas_call(
        functools.partial(finish_kernel, count),
        out_shape=[
            *(jax.ShapeDtypeStruct(array.shape, jnp.float32) for array in arrays),
            *[jax.ShapeDtypeStruct(head_shape, jnp.float32)] * 2,
            *[jax.ShapeDtypeStruct((lines, 128), jnp.float32)] * 2,
        ],
        in_specs=[anywhere] * count + [inside],
        out_specs=[anywhere] * count + [inside] * 4,
        scratch_shapes=[
            *(pltpu.VMEM(array.shape, array.dtype) for array in arrays),
            *(pltpu.VMEM(array.shape, jnp.float32) for array in arrays if array.dtype != jnp.float32),
            pltpu.SemaphoreType.DMA((4, count)),
        ],
        compiler_params=pltpu.CompilerParams(vmem_limit_bytes=VMEM_BYTES),
        name="finish",
    )(*arrays, gain_part)


def local(
    tokens,
    positions,
    cotangent,
    query_weight,
    key_weight,
    value_weight,
    output_weight,
    gate_weight,
    up_weight,
    down_weight,
    query_gain,
    key_gain,
    attention_gain,
    feedforward_gain,
):
    data_size = lax.axis_size("dp")
    data_index = lax.axis_index("dp")
    high_count = data_size // 8
    width = attention_gain.shape[0]
    channels, local_heads = query_gain.shape

    def high_block(low_bits, place):
        return low_bits + 8 * ((data_index // 8) ^ place)

    def grouped(array_in):
        if high_count == 1:
            return array_in
        return jnp.concatenate(
            [
                lax.dynamic_slice_in_dim(array_in, high_block(low_bits, place) * width, width, -1)
                for low_bits in range(8)
                for place in range(high_count)
            ],
            -1,
        )

    def ungrouped(array_in):
        if high_count == 1:
            return array_in
        return jnp.concatenate(
            [
                lax.dynamic_slice_in_dim(
                    array_in,
                    (low_bits * high_count + ((data_index // 8) ^ high_bits)) * width,
                    width,
                    -1,
                )
                for high_bits in range(high_count)
                for low_bits in range(8)
            ],
            -1,
        )

    head_gains = jnp.concatenate([query_gain.T, key_gain.T], 0)
    head_gains = lax.dynamic_update_slice_in_dim(
        jnp.zeros((2 * local_heads, channels * data_size), head_gains.dtype),
        head_gains,
        data_index * channels,
        1,
    )
    for bit in range(3, bits_of(data_size)):
        head_gains = head_gains + swap(head_gains, 1 << bit)
    gain_lines = [
        head_gains,
        gather_high(attention_gain[None], 1).reshape(-1, 128),
        gather_high(feedforward_gain[None], 1).reshape(-1, 128),
    ]
    line_count = sum(lines.shape[0] for lines in gain_lines)
    gain_shard = jnp.pad(jnp.concatenate(gain_lines, 0), ((0, 32 - line_count), (0, 0)))
    (
        rows_all,
        attention_full,
        output_full,
        gate_full,
        attended,
        query_rot,
        key_rot,
        value_rows,
        query_hat,
        key_hat,
        cosine,
        sine,
        stats,
        query_scale,
        key_scale,
        attention_scale,
        feedforward_scale,
    ) = front(
        grouped(tokens),
        gather_high(query_weight, 0),
        gather_high(key_weight, 0),
        gather_high(value_weight, 0),
        gather_high(output_weight, 1),
        gather_high(gate_weight, 0),
        gain_shard,
        positions,
    )
    (
        branch_cot,
        grad_attended,
        block_grouped,
        grad_hidden,
        grad_gate,
        up_near,
        up_early,
        down_near,
        attention_gain_part,
        feedforward_gain_part,
    ) = middle(
        attended,
        rows_all,
        grouped(cotangent),
        attention_scale,
        feedforward_scale,
        output_full,
        gate_full,
        gather_high(up_weight, 0),
        gather_high(down_weight, 1),
    )
    (
        tokens_part,
        grad_up,
        grad_down,
        grad_output,
        grad_query,
        grad_key,
        grad_value,
        gain_part,
    ) = back(
        branch_cot,
        grad_attended,
        query_rot,
        key_rot,
        value_rows,
        query_hat,
        key_hat,
        cosine,
        sine,
        down_near,
        up_near,
        up_early,
        attended,
        attention_full,
        rows_all.reshape(-1, rows_all.shape[-1]),
        grad_hidden,
        stats,
        query_scale,
        key_scale,
        attention_gain_part,
        feedforward_gain_part,
    )
    def own_high(total, axis):
        return total if high_count == 1 else wide(scatter_high(total, axis))

    large = (
        ungrouped(block_grouped),
        ungrouped(tokens_part),
        own_high(grad_query, 0),
        own_high(grad_key, 0),
        own_high(grad_value, 0),
        own_high(grad_output, 1),
        own_high(grad_gate, 0),
        own_high(grad_up, 0),
        own_high(grad_down, 1),
    )
    if high_count == 1:
        *large, query_part, key_part, attention_part, feedforward_part = finish(
            gain_part, query_gain.shape[::-1], width // 128, *large
        )
        return (
            *large,
            query_part.T,
            key_part.T,
            attention_part.reshape(width),
            feedforward_part.reshape(width),
        )
    head_part = gain_part[: 2 * local_heads]
    for bit in range(3, bits_of(data_size)):
        head_part = head_part + swap(head_part, 1 << bit)
    head_part = lax.dynamic_slice_in_dim(head_part, data_index * channels, channels, 1)
    norm_part = gain_part[2 * local_heads : line_count].reshape(2, -1)

    return (
        *large,
        head_part[:local_heads].T,
        head_part[local_heads:].T,
        own_high(norm_part[0], 0),
        own_high(norm_part[1], 0),
    )


def solution(mesh):
    return jax.shard_map(
        local,
        mesh=mesh,
        in_specs=(
            P(("dp", "tensor"), None),
            P("dp"),
            P(("dp", "tensor"), None),
            P("dp", "tensor"),
            P("dp", "tensor"),
            P("dp", "tensor"),
            P("tensor", "dp"),
            P("dp", "tensor"),
            P("dp", "tensor"),
            P("tensor", "dp"),
            P("dp", "tensor"),
            P("dp", "tensor"),
            P("dp"),
            P("dp"),
        ),
        out_specs=(
            P(("dp", "tensor"), None),
            P(("dp", "tensor"), None),
            P("dp", "tensor"),
            P("dp", "tensor"),
            P("dp", "tensor"),
            P("tensor", "dp"),
            P("dp", "tensor"),
            P("dp", "tensor"),
            P("tensor", "dp"),
            P("dp", "tensor"),
            P("dp", "tensor"),
            P("dp"),
            P("dp"),
        ),
        check_vma=False,
    )
```
